32 devices in a mesh: dp: 8 (over y, x, core), head: 4 (over z).
Axes of the slice: x: 2, y: 2, z: 4, core: 2. Of those that a mesh axis runs over, the one named last changes fastest.
Arguments:
- tokens: bfloat16 [12288, 768], P(('dp', 'head')), may hold values from -6 to 6
- lengths: int32 [8, 4], P('dp'), may hold values from 1 to 1533, as said below
- ln1_gain: float32 [768], replicated, may hold values from 0.5 to 1.5
- ln1_bias: float32 [768], replicated, may hold values from -3 to 3
- w_qkv: bfloat16 [768, 2304], replicated, may hold values from -0.21875 to 0.21875
- bias_q: float32 [768], replicated, may hold values from -3 to 3
- bias_v: float32 [768], replicated, may hold values from -3 to 3
- w_out: bfloat16 [768, 768], replicated, may hold values from -3.5 to 3.5
- bias_out: float32 [768], replicated, may hold values from -3 to 3
- ln2_gain: float32 [768], replicated, may hold values from 0.5 to 1.5
- ln2_bias: float32 [768], replicated, may hold values from -3 to 3
- w_fc: bfloat16 [768, 3072], replicated, may hold values from -0.21875 to 0.21875
- bias_fc: float32 [3072], replicated, may hold values from -3 to 3
- w_proj: bfloat16 [3072, 768], replicated, may hold values from -0.625 to 0.625
- bias_proj: float32 [768], replicated, may hold values from -3 to 3
- cotangent: bfloat16 [12288, 768], P(('dp', 'head')), may hold values from -6 to 6
Outputs:
- block_output: float32 [12288, 768], P(('dp', 'head'))
- grad_tokens: float32 [12288, 768], P(('dp', 'head'))
- grad_ln1_gain: float32 [768], replicated
- grad_ln1_bias: float32 [768], replicated
- grad_w_qkv: float32 [768, 2304], P('dp')
- grad_bias_q: float32 [768], replicated
- grad_bias_v: float32 [768], replicated
- grad_w_out: float32 [768, 768], P('dp')
- grad_bias_out: float32 [768], replicated
- grad_ln2_gain: float32 [768], replicated
- grad_ln2_bias: float32 [768], replicated
- grad_w_fc: float32 [768, 3072], P(None, 'dp')
- grad_bias_fc: float32 [3072], replicated
- grad_w_proj: float32 [3072, 768], P('dp')
- grad_bias_proj: float32 [768], replicated
The draws below stay inside these ranges and needn't reach their ends.
Inputs may be any that keep to these rules, and one draw needn't show every extreme that they name: Each row of lengths adds up to 1536; one sequence of each row holds at least 1248 tokens.
All inputs are finite; a program needn't handle non-finite values.
Results may differ from the reference program's by a relative error of at most 0.012.
Values may be sent and summed in bfloat16 or wider, within the bound.
A program may use at most 192 MiB of HBM per device.

```python
import math
import jax
import jax.numpy as jnp
from jax import lax

HEADS = 12
HEAD_DIM = 64
FF = 3072
TOK_DEV = 384
SEQS = 4
D = 768
GROUP_TOK = 1536
GROUPS = 8
TOKENS = 12288


def draw_lengths(key, part):
    key = jax.random.fold_in(key, 11)
    short_key, place_key, group_key = jax.random.split(key, 3)
    shorts = jax.random.randint(short_key, (GROUPS, SEQS), 1, TOK_DEV // 4 + 1, dtype=jnp.int32)
    single_group = jax.random.randint(group_key, (), 0, GROUPS, dtype=jnp.int32)
    in_single = jnp.arange(GROUPS, dtype=jnp.int32)[:, None] == single_group
    shorts = jnp.where(in_single, 1, shorts).astype(jnp.int32)
    chosen = jax.random.randint(place_key, (GROUPS, 1), 0, SEQS, dtype=jnp.int32)
    marked = jnp.arange(SEQS, dtype=jnp.int32)[None, :] == chosen
    others = jnp.sum(jnp.where(marked, 0, shorts), axis=1, keepdims=True).astype(jnp.int32)
    return jnp.where(marked, GROUP_TOK - others, shorts).astype(jnp.int32)


def levels(key, shape, pieces, smallest, top_value):
    loudness, own = 1.0, jax.random.fold_in(key, 6)
    for axis_at, parts in pieces:
        heights = jnp.exp(jax.random.uniform(jax.random.fold_in(own, axis_at), (parts,), jnp.float32, smallest / len(pieces), top_value / len(pieces)))
        loudness = loudness * jnp.repeat(heights, shape[axis_at] // parts).reshape([-1 if axis == axis_at else 1 for axis in range(len(shape))])
    return loudness


def centred(own_key, shape, width, bound, pieces=(), kind=jnp.bfloat16):
    values = width * jax.random.normal(own_key, shape, jnp.float32)
    if pieces:
        values = values * levels(own_key, shape, pieces, -0.22, 0.18)
    return jnp.clip(values, -bound, bound).astype(kind)


def setup_inputs(seed: int = 0) -> dict:
    key_list = jax.random.split(jax.random.key(seed), 17)
    return {
        "tokens": centred(key_list[0], (TOKENS, D), 1.0, 6.0, ((0, 32),)),
        "lengths": draw_lengths(jax.random.fold_in(key_list[16], 71), 0),
        "ln1_gain": jnp.clip(1.0 + 0.1 * jax.random.normal(key_list[2], (D,), jnp.float32), 0.5, 1.5),
        "ln1_bias": centred(key_list[3], (D,), 0.5, 3.0, (), jnp.float32),
        "w_qkv": centred(key_list[4], (D, 3 * D), D ** -0.5, 0.21875),
        "bias_q": centred(key_list[5], (D,), 0.5, 3.0, (), jnp.float32),
        "bias_v": centred(key_list[6], (D,), 0.5, 3.0, (), jnp.float32),
        "w_out": centred(key_list[7], (D, D), (max(D // 256, 1)) ** -0.5, 3.5),
        "bias_out": centred(key_list[8], (D,), 0.5, 3.0, (), jnp.float32),
        "ln2_gain": jnp.clip(1.0 + 0.1 * jax.random.normal(key_list[9], (D,), jnp.float32), 0.5, 1.5),
        "ln2_bias": centred(key_list[10], (D,), 0.5, 3.0, (), jnp.float32),
        "w_fc": centred(key_list[11], (D, FF), D ** -0.5, 0.21875),
        "bias_fc": centred(key_list[12], (FF,), 0.5, 3.0, (), jnp.float32),
        "w_proj": centred(key_list[13], (FF, D), (max(FF // 32, 1)) ** -0.5, 0.625),
        "bias_proj": centred(key_list[14], (D,), 0.5, 3.0, (), jnp.float32),
        "cotangent": centred(key_list[15], (TOKENS, D), 1.0, 6.0, ((0, 32),)),
    }


@jax.custom_vjp
def low(v):
    return lax.optimization_barrier(v.astype(jnp.bfloat16)).astype(jnp.float32)

@jax.custom_vjp
def low_back(v):
    return v

def low_keep(v):
    return (low(v), None)

def low_pass(kept, grad):
    return (grad,)

def back_keep(v):
    return (v, None)

def back_low(kept, grad):
    return (low(grad),)
low.defvjp(low_keep, low_pass)
low_back.defvjp(back_keep, back_low)
EPSILON = 1e-05
DEPTH_SCALE = 1.0 / math.sqrt(12.0)
HIGHEST = lax.Precision.HIGHEST

def matmul(left_matrix, right_matrix):
    return jnp.dot(left_matrix, right_matrix, precision=HIGHEST, preferred_element_type=jnp.float32)

def layer_norm(values, gain_vec, bias_vec):
    center = lax.optimization_barrier(jnp.mean(values, axis=-1, keepdims=True))
    centered = values - center
    spread = lax.optimization_barrier(jnp.mean(centered * centered, axis=-1, keepdims=True))
    return centered * lax.rsqrt(spread + EPSILON) * gain_vec + bias_vec

def sequence_ids(counts):
    seq_ends = jnp.cumsum(counts).astype(jnp.int32)
    places = jnp.arange(GROUP_TOK, dtype=jnp.int32)
    return lax.optimization_barrier(jnp.sum((places[:, None] >= seq_ends[None, :]).astype(jnp.int32), axis=1)).astype(jnp.int32)

def attend(query_heads, key_heads, value_heads, seq_ids):
    block_size = min(512, GROUP_TOK)
    places = jnp.arange(GROUP_TOK, dtype=jnp.int32)
    score_scale = HEAD_DIM ** (-0.5)

    def one_block(block_index):
        offset = (block_index * block_size).astype(jnp.int32)
        query_block = lax.dynamic_slice_in_dim(query_heads, offset, block_size, 0)
        block_ids = lax.dynamic_slice_in_dim(seq_ids, offset, block_size, 0)
        rows_here = offset + jnp.arange(block_size, dtype=jnp.int32)
        allowed = (places[None, :] <= rows_here[:, None]) & (seq_ids[None, :] == block_ids[:, None])
        raw_scores = jnp.einsum('qhd,khd->hqk', query_block, key_heads, precision=HIGHEST)
        scores = jnp.where(allowed[None], low_back(raw_scores) * score_scale, -1e+30)
        largest = lax.optimization_barrier(jnp.max(scores, axis=-1, keepdims=True))
        weights = jnp.exp(scores - largest)
        soft_weights = weights / lax.optimization_barrier(jnp.sum(weights, axis=-1, keepdims=True))
        return jnp.einsum('hqk,khd->qhd', low(soft_weights), value_heads, precision=HIGHEST)
    blocks = lax.map(jax.checkpoint(one_block), jnp.arange(GROUP_TOK // block_size, dtype=jnp.int32))
    return blocks.reshape(GROUP_TOK, HEADS * HEAD_DIM)

def block_forward(source, seq_ids, params):
    ln1_gain, ln1_bias, w_qkv, bias_q, bias_v, w_out, bias_out, ln2_gain, ln2_bias, w_fc, bias_fc, w_proj, bias_proj = params
    normed = low(layer_norm(source, ln1_gain, ln1_bias))
    offsets = jnp.concatenate([bias_q, jnp.zeros_like(bias_q), bias_v])
    mixed_rows = low(low_back(matmul(normed, w_qkv) + offsets))
    shaped = mixed_rows.reshape(GROUP_TOK, 3, HEADS, HEAD_DIM)
    attended = low(low_back(attend(shaped[:, 0], shaped[:, 1], shaped[:, 2], seq_ids)))
    middle = source + DEPTH_SCALE * (low_back(matmul(attended, w_out)) + bias_out)
    second = low(layer_norm(middle, ln2_gain, ln2_bias))
    hidden = low(jax.nn.gelu(low_back(matmul(second, w_fc)) + bias_fc, approximate=True))
    return middle + DEPTH_SCALE * (low_back(matmul(hidden, w_proj)) + bias_proj)

def reference(tokens, lengths, ln1_gain, ln1_bias, w_qkv, bias_q, bias_v, w_out, bias_out, ln2_gain, ln2_bias, w_fc, bias_fc, w_proj, bias_proj, cotangent):
    params = tuple((member.astype(jnp.float32) for member in (ln1_gain, ln1_bias, w_qkv, bias_q, bias_v, w_out, bias_out, ln2_gain, ln2_bias, w_fc, bias_fc, w_proj, bias_proj)))
    sources = tokens.astype(jnp.float32).reshape(GROUPS, GROUP_TOK, HEADS * HEAD_DIM)
    seed_grads = cotangent.astype(jnp.float32).reshape(GROUPS, GROUP_TOK, HEADS * HEAD_DIM)

    def group_step(totals, inputs):
        source, counts, seed_grad = inputs
        seq_ids = sequence_ids(counts)
        result, pullback = jax.vjp(lambda values, weights: block_forward(values, seq_ids, weights), source, params)
        grad_source, grad_params = pullback(seed_grad)
        totals = jax.tree.map(lambda running, adding: running + adding, totals, grad_params)
        return (totals, (result, grad_source))
    empty_grads = tuple((jnp.zeros_like(member) for member in params))
    totals, (results, source_grads) = lax.scan(group_step, empty_grads, (sources, lengths, seed_grads))
    grad_scale = 1.0 / math.sqrt(TOKENS)
    return (results.reshape(TOKENS, HEADS * HEAD_DIM), source_grads.reshape(TOKENS, HEADS * HEAD_DIM), totals[0] * grad_scale, totals[1] * grad_scale, totals[2] * grad_scale, totals[3] * grad_scale, totals[4] * grad_scale, totals[5] * grad_scale, totals[6] * grad_scale, totals[7] * grad_scale, totals[8] * grad_scale, totals[9] * grad_scale, totals[10] * grad_scale, totals[11] * grad_scale, totals[12] * grad_scale)
```

```python
import math

import jax
import jax.numpy as jnp
from jax import lax
from jax.sharding import PartitionSpec as P

HEAD_DIM = 64


EPSILON = 1e-05
DEPTH_SCALE = 1.0 / math.sqrt(12.0)


def layer_norm(values, gain_vec, bias_vec):
    center = jnp.mean(values, axis=-1, keepdims=True)
    centered = values - center
    spread = jnp.mean(centered * centered, axis=-1, keepdims=True)
    return centered * lax.rsqrt(spread + EPSILON) * gain_vec + bias_vec


def contract_rows(left_matrix, right_matrix):
    return lax.dot_general(
        left_matrix, right_matrix, (((0,), (0,)), ((), ())), preferred_element_type=jnp.float32
    )


def contract_cols(left_matrix, right_matrix):
    return lax.dot_general(
        left_matrix, right_matrix, (((1,), (1,)), ((), ())), preferred_element_type=jnp.float32
    )


def sequence_ids(counts, group_tok):
    seq_ends = jnp.cumsum(counts)
    places = jnp.arange(group_tok, dtype=jnp.int32)
    return jnp.sum((places[:, None] >= seq_ends[None, :]).astype(jnp.int32), axis=1)


def block_weights(query_block, key_heads, seq_ids, offset):
    group_tok = key_heads.shape[0]
    block_size = query_block.shape[0]
    places = jnp.arange(group_tok, dtype=jnp.int32)
    rows_here = offset + jnp.arange(block_size, dtype=jnp.int32)
    block_ids = lax.dynamic_slice_in_dim(seq_ids, offset, block_size, 0)
    allowed = (places[None, :] <= rows_here[:, None]) & (seq_ids[None, :] == block_ids[:, None])
    raw_scores = jnp.einsum(
        "qhd,khd->hqk", query_block, key_heads, preferred_element_type=jnp.float32
    )
    scores = jnp.where(allowed[None], raw_scores * HEAD_DIM ** (-0.5), -1e30)
    largest = jnp.max(scores, axis=-1, keepdims=True)
    weights = jnp.exp(scores - largest)
    return weights / jnp.sum(weights, axis=-1, keepdims=True)


def split_heads(group_mixed):
    group_tok, _three, part_width = group_mixed.shape
    head_count = part_width // HEAD_DIM
    shaped = group_mixed.reshape(group_tok, 3, head_count, HEAD_DIM)
    return (shaped[:, 0], shaped[:, 1], shaped[:, 2])


def attention_forward(group_mixed, seq_ids):
    group_tok = group_mixed.shape[0]
    part_width = group_mixed.shape[2]
    query_heads, key_heads, value_heads = split_heads(group_mixed)
    block_size = min(512, group_tok)

    def one_block(block_index):
        offset = block_index * block_size
        query_block = lax.dynamic_slice_in_dim(query_heads, offset, block_size, 0)
        soft_weights = block_weights(query_block, key_heads, seq_ids, offset)
        return jnp.einsum(
            "hqk,khd->qhd",
            soft_weights.astype(jnp.bfloat16),
            value_heads,
            preferred_element_type=jnp.float32,
        )

    blocks = lax.map(one_block, jnp.arange(group_tok // block_size, dtype=jnp.int32))
    return blocks.reshape(group_tok, part_width)


def attention_backward(group_mixed, group_grad, seq_ids):
    group_tok = group_mixed.shape[0]
    part_width = group_mixed.shape[2]
    query_heads, key_heads, value_heads = split_heads(group_mixed)
    grad_heads = group_grad.reshape(group_tok, part_width // HEAD_DIM, HEAD_DIM)
    block_size = min(512, group_tok)

    def one_block(running, block_index):
        key_grad, value_grad = running
        offset = block_index * block_size
        query_block = lax.dynamic_slice_in_dim(query_heads, offset, block_size, 0)
        grad_block = lax.dynamic_slice_in_dim(grad_heads, offset, block_size, 0)
        soft_weights = block_weights(query_block, key_heads, seq_ids, offset)
        weight_grad = jnp.einsum(
            "qhd,khd->hqk", grad_block, value_heads, preferred_element_type=jnp.float32
        )
        centre = jnp.sum(soft_weights * weight_grad, axis=-1, keepdims=True)
        score_grad = (soft_weights * (weight_grad - centre) * HEAD_DIM ** (-0.5)).astype(
            jnp.bfloat16
        )
        value_grad = value_grad + jnp.einsum(
            "hqk,qhd->khd",
            soft_weights.astype(jnp.bfloat16),
            grad_block,
            preferred_element_type=jnp.float32,
        )
        key_grad = key_grad + jnp.einsum(
            "hqk,qhd->khd", score_grad, query_block, preferred_element_type=jnp.float32
        )
        query_grad = jnp.einsum(
            "hqk,khd->qhd", score_grad, key_heads, preferred_element_type=jnp.float32
        )
        return ((key_grad, value_grad), query_grad)

    empty_grad = jnp.zeros(key_heads.shape, jnp.float32)
    (key_grad, value_grad), query_blocks = lax.scan(
        one_block, (empty_grad, empty_grad), jnp.arange(group_tok // block_size, dtype=jnp.int32)
    )
    query_grad = query_blocks.reshape(group_tok, part_width)
    stacked = jnp.stack(
        [
            query_grad,
            key_grad.reshape(group_tok, part_width),
            value_grad.reshape(group_tok, part_width),
        ],
        axis=1,
    )
    return stacked.astype(jnp.bfloat16)


def forward(source_rows, seq_ids, weight_set):
    (
        ln1_gain,
        ln1_bias,
        w_qkv,
        bias_q,
        bias_v,
        w_out,
        bias_out,
        ln2_gain,
        ln2_bias,
        w_fc,
        bias_fc,
        w_proj,
        bias_proj,
    ) = weight_set
    tok_rows, model_width = source_rows.shape
    source = source_rows.astype(jnp.float32)
    normed = layer_norm(source, ln1_gain, ln1_bias).astype(jnp.bfloat16)
    offsets = jnp.concatenate([bias_q, jnp.zeros_like(bias_q), bias_v])
    mixed_rows = (jnp.dot(normed, w_qkv, preferred_element_type=jnp.float32) + offsets).astype(
        jnp.bfloat16
    )
    group_mixed = lax.all_to_all(
        mixed_rows.reshape(tok_rows, 3, model_width),
        "head",
        split_axis=2,
        concat_axis=0,
        tiled=True,
    )
    attended = attention_forward(group_mixed, seq_ids).astype(jnp.bfloat16)
    back_rows = lax.all_to_all(attended, "head", split_axis=0, concat_axis=1, tiled=True)
    middle = source + DEPTH_SCALE * (
        jnp.dot(back_rows, w_out, preferred_element_type=jnp.float32) + bias_out
    )
    second = layer_norm(middle, ln2_gain, ln2_bias).astype(jnp.bfloat16)
    pre_act = jnp.dot(second, w_fc, preferred_element_type=jnp.float32) + bias_fc
    hidden = jax.nn.gelu(pre_act, approximate=True).astype(jnp.bfloat16)
    result = middle + DEPTH_SCALE * (
        jnp.dot(hidden, w_proj, preferred_element_type=jnp.float32) + bias_proj
    )
    return (source, normed, group_mixed, back_rows, middle, second, pre_act, hidden, result)


def gelu_tanh(inputs_pre):
    return jax.nn.gelu(inputs_pre, approximate=True)


def shards(
    tokens,
    lengths,
    ln1_gain,
    ln1_bias,
    w_qkv,
    bias_q,
    bias_v,
    w_out,
    bias_out,
    ln2_gain,
    ln2_bias,
    w_fc,
    bias_fc,
    w_proj,
    bias_proj,
    cotangent,
):
    tok_rows, model_width = tokens.shape
    group_tok = tok_rows * lax.axis_size("head")
    device_count = lax.axis_size("dp") * lax.axis_size("head")
    grad_scale = 1.0 / math.sqrt(tok_rows * device_count)
    seq_ids = sequence_ids(lengths[0], group_tok)
    weight_set = (
        ln1_gain,
        ln1_bias,
        w_qkv,
        bias_q,
        bias_v,
        w_out,
        bias_out,
        ln2_gain,
        ln2_bias,
        w_fc,
        bias_fc,
        w_proj,
        bias_proj,
    )
    kept = forward(tokens, seq_ids, weight_set)
    block_output = kept[8]
    grad_rows = cotangent.astype(jnp.float32)
    source, normed, group_mixed, back_rows, middle, second, pre_act, hidden, result = kept
    grad_bias_proj = DEPTH_SCALE * jnp.sum(grad_rows, axis=0)
    proj_grad = (DEPTH_SCALE * grad_rows).astype(jnp.bfloat16)
    grad_w_proj = contract_rows(hidden, proj_grad)
    hidden_grad = contract_cols(proj_grad, w_proj)
    gelu_value, gelu_pull = jax.vjp(gelu_tanh, pre_act)
    (pre_grad,) = gelu_pull(hidden_grad)
    grad_bias_fc = jnp.sum(pre_grad, axis=0)
    fc_grad = pre_grad.astype(jnp.bfloat16)
    grad_w_fc = contract_rows(second, fc_grad)
    second_grad = contract_cols(fc_grad, w_fc)
    norm_value, second_pull = jax.vjp(layer_norm, middle, ln2_gain, ln2_bias)
    middle_part, grad_ln2_gain, grad_ln2_bias = second_pull(second_grad)
    middle_grad = grad_rows + middle_part
    grad_bias_out = DEPTH_SCALE * jnp.sum(middle_grad, axis=0)
    out_grad = (DEPTH_SCALE * middle_grad).astype(jnp.bfloat16)
    grad_w_out = contract_rows(back_rows, out_grad)
    attended_grad = contract_cols(out_grad, w_out).astype(jnp.bfloat16)
    group_grad = lax.all_to_all(attended_grad, "head", split_axis=1, concat_axis=0, tiled=True)
    group_mixed_grad = attention_backward(group_mixed, group_grad, seq_ids)
    mixed_grad = lax.all_to_all(
        group_mixed_grad, "head", split_axis=0, concat_axis=2, tiled=True
    ).reshape(tok_rows, 3 * model_width)
    grad_w_qkv = contract_rows(normed, mixed_grad)
    grad_bias_q = jnp.sum(mixed_grad[:, :model_width], axis=0, dtype=jnp.float32)
    grad_bias_v = jnp.sum(mixed_grad[:, 2 * model_width :], axis=0, dtype=jnp.float32)
    normed_grad = contract_cols(mixed_grad, w_qkv)
    first_value, first_pull = jax.vjp(layer_norm, source, ln1_gain, ln1_bias)
    token_part, grad_ln1_gain, grad_ln1_bias = first_pull(normed_grad)
    grad_tokens = middle_grad + token_part
    mat_shares = (
        lax.psum_scatter((grad_w_qkv * grad_scale).astype(jnp.bfloat16), "dp", scatter_dimension=0, tiled=True),
        lax.psum_scatter((grad_w_out * grad_scale).astype(jnp.bfloat16), "dp", scatter_dimension=0, tiled=True),
        lax.psum_scatter((grad_w_fc * grad_scale).astype(jnp.bfloat16), "dp", scatter_dimension=1, tiled=True),
        lax.psum_scatter((grad_w_proj * grad_scale).astype(jnp.bfloat16), "dp", scatter_dimension=0, tiled=True),
    )
    qkv_total, out_total, fc_total, proj_total = (
        lax.psum(mat_shares[0].astype(jnp.bfloat16), "head").astype(jnp.float32),
        lax.psum(mat_shares[1].astype(jnp.bfloat16), "head").astype(jnp.float32),
        lax.psum(mat_shares[2].astype(jnp.bfloat16), "head").astype(jnp.float32),
        lax.psum(mat_shares[3].astype(jnp.bfloat16), "head").astype(jnp.float32),
    )
    vec_totals = lax.psum(
        (
            grad_ln1_gain * grad_scale,
            grad_ln1_bias * grad_scale,
            grad_bias_q * grad_scale,
            grad_bias_v * grad_scale,
            grad_bias_out * grad_scale,
            grad_ln2_gain * grad_scale,
            grad_ln2_bias * grad_scale,
            grad_bias_fc * grad_scale,
            grad_bias_proj * grad_scale,
        ),
        ("dp", "head"),
    )
    ln1g_total, ln1b_total, bq_total, bv_total, bout_total = (
        vec_totals[0],
        vec_totals[1],
        vec_totals[2],
        vec_totals[3],
        vec_totals[4],
    )
    ln2g_total, ln2b_total, bfc_total, bproj_total = (
        vec_totals[5],
        vec_totals[6],
        vec_totals[7],
        vec_totals[8],
    )
    return (
        block_output,
        grad_tokens,
        ln1g_total,
        ln1b_total,
        qkv_total,
        bq_total,
        bv_total,
        out_total,
        bout_total,
        ln2g_total,
        ln2b_total,
        fc_total,
        bfc_total,
        proj_total,
        bproj_total,
    )


def solution(mesh):
    return jax.shard_map(
        shards,
        mesh=mesh,
        in_specs=(
            P(("dp", "head"), None),
            P("dp", None),
            P(),
            P(),
            P(),
            P(),
            P(),
            P(),
            P(),
            P(),
            P(),
            P(),
            P(),
            P(),
            P(),
            P(("dp", "head"), None),
        ),
        out_specs=(
            P(("dp", "head"), None),
            P(("dp", "head"), None),
            P(),
            P(),
            P("dp", None),
            P(),
            P(),
            P("dp", None),
            P(),
            P(),
            P(),
            P(None, "dp"),
            P(),
            P("dp", None),
            P(),
        ),
        check_vma=False,
    )
```

```python
import functools
import math

import jax
import jax.numpy as jnp
from jax import lax
from jax.experimental import pallas as pl
from jax.experimental.pallas import tpu as pltpu
from jax.sharding import PartitionSpec as P

HEAD_DIM = 64
EPSILON = 1e-05
DEPTH_SCALE = 1.0 / math.sqrt(12.0)
LOG2E = 1.0 / math.log(2.0)
SCORE_SCALE = HEAD_DIM ** (-0.5)
GELU_K = math.sqrt(2.0 / math.pi)
GELU_A = 0.044715
TEAM = 8
QB = 256

F32 = jnp.float32
BF16 = jnp.bfloat16
MESH = pl.DeviceIdType.MESH
ANY = pl.BlockSpec(memory_space=pl.ANY)
VMEM = pl.BlockSpec(memory_space=pltpu.VMEM)
SMEM = pl.BlockSpec(memory_space=pltpu.SMEM)


def dot(a, b):
    return jnp.dot(a, b, preferred_element_type=F32)


def dot_nt(a, b):
    return lax.dot_general(a, b, (((1,), (1,)), ((), ())), preferred_element_type=F32)


def dot_tn(a, b):
    return lax.dot_general(a, b, (((0,), (0,)), ((), ())), preferred_element_type=F32)


def mult(x, m):
    return pl.multiple_of(x, m)


def place():
    dp, h = lax.axis_index("dp"), lax.axis_index("head")
    core = lax.rem(dp, 2)
    half = h // 2
    return dict(
        dp=dp,
        h=h,
        core=core,
        sib=dp + 1 - 2 * core,
        even=dp - core,
        half=half,
        served=dp - core + half,
        block=(h - 2 * half) * 2 + core,
    )


def greet(at):
    barrier = pltpu.get_barrier_semaphore()
    me = at["core"] * 4 + at["h"]
    for k in range(1, TEAM):
        other = lax.rem(me + k, TEAM)
        pl.semaphore_signal(
            barrier, inc=1, device_id=(at["even"] + other // 4, lax.rem(other, 4)), device_id_type=MESH
        )
    pl.semaphore_wait(barrier, TEAM - 1)


def remote(src, dst, send, recv, device):
    return pltpu.make_async_remote_copy(
        src_ref=src, dst_ref=dst, send_sem=send, recv_sem=recv, device_id=device, device_id_type=MESH
    )


def norm_parts(v):
    center = jnp.mean(v, axis=-1, keepdims=True)
    cent = v - center
    r = lax.rsqrt(jnp.mean(cent * cent, axis=-1, keepdims=True) + EPSILON)
    return cent * r, r


def norm_back(e, gain, n, r):
    ea = e * gain
    return r * (ea - jnp.mean(ea, axis=-1, keepdims=True) - n * jnp.mean(ea * n, axis=-1, keepdims=True))


def attend_kernel(
    tok, lens, gain, bias, bias_q, bias_v, w_qkv,
    att_o, mix_o, xg_o, ot_o, lse_o, start_o, wt_o,
    xn, xg, wwin, tbuf, wt, bcol, start_mine, start_sib, mix, kh, scores, ot,
    w_sem, st_sem, ag_send, ag_recv, fw_send, at_send, at_recv, at_local, out_sem,
):
    at = place()
    dp, h, core, sib = at["dp"], at["h"], at["core"], at["sib"]
    rows, width = tok.shape
    group = 4 * rows
    part = width // 4
    collects = core == at["half"]
    first = (h - 2 * at["half"]) * 2 * part + core * 128
    shift = mult(64 * core, 64)
    for p in range(3):
        pltpu.make_async_copy(
            w_qkv.at[:, pl.ds(mult(p * width + first, 128), 256)], wwin.at[p], w_sem.at[p]
        ).start()
    greet(at)

    places = lax.broadcasted_iota(jnp.int32, (8, group), 1)
    begin = jnp.zeros((8, group), jnp.int32)
    edge = lens[0, 0]
    for k in range(1, lens.shape[1] + 1):
        begin = jnp.where(places >= edge, edge, begin)
        if k < lens.shape[1]:
            edge = edge + lens[0, k]
    start_mine[...] = begin.astype(F32)
    st_copy = remote(start_mine, start_sib, st_sem.at[0], st_sem.at[1], (sib, h))
    st_copy.start()

    n, _ = norm_parts(tok[...].astype(F32))
    xn[...] = (n * gain[...] + bias[...]).astype(BF16)

    def shard(ref, s):
        return ref.at[pl.ds(mult(s * rows, rows), rows), :]

    def ag_copy(t):
        return remote(xn, shard(xg, h), ag_send.at[t], ag_recv.at[h], (dp, 2 * core + t))

    for t in range(2):
        @pl.when(2 * core + t != h)
        def _():
            ag_copy(t).start()

    own_fw = remote(xn, shard(xg, h), fw_send.at[0], ag_recv.at[h], (sib, h))

    @pl.when(collects)
    def _():
        own_fw.start()
        xg[pl.ds(mult(h * rows, rows), rows), :] = xn[...]

    for p in range(3):
        pltpu.make_async_copy(wwin.at[p], wwin.at[p], w_sem.at[p]).wait()
        tbuf[...] = wwin[p].T
        wt[p * part : (p + 1) * part, :] = tbuf[pl.ds(shift, part), :]
    wt_copy = pltpu.make_async_copy(wt, wt_o, out_sem.at[0])
    wt_copy.start()
    for p, vec in ((0, bias_q), (2, bias_v)):
        bcol[p] = jnp.broadcast_to(vec[:, pl.ds(mult(first, 128), 256)], (128, 256)).T
    bcol[1] = jnp.zeros((256, 128), F32)

    low = 1 - at["half"]
    order = (h, low * (1 - h) + (1 - low) * (5 - h), 1 + low, 3 * low)

    def fw_copy(d, s):
        return remote(shard(xg, s), shard(xg, s), fw_send.at[d], ag_recv.at[s], (sib, h))

    for d in range(4):
        s = order[d]
        if d == 0:
            @pl.when(jnp.logical_not(collects))
            def _():
                fw_copy(d, s).wait_recv()
        else:
            fw_copy(d, s).wait_recv()

            @pl.when(collects)
            def _():
                fw_copy(d, s).start()

        pltpu.make_async_copy(shard(xg, s), shard(xg_o, s), out_sem.at[1 + d]).start()
        here = xg[pl.ds(mult(s * rows, rows), rows), :]
        for p in range(3):
            res = dot_nt(wt[p * part : (p + 1) * part, :], here) + bcol[p, pl.ds(shift, part), :][:, :1]
            mix[p * part : (p + 1) * part, pl.ds(mult(s * rows, 128), rows)] = res.astype(BF16)
    mix_copy = pltpu.make_async_copy(mix, mix_o, out_sem.at[5])
    mix_copy.start()
    st_copy.wait_recv()
    start_o[...] = jnp.where(collects, start_mine[...], start_sib[...]).astype(jnp.int32)

    heads = part // HEAD_DIM
    scale = SCORE_SCALE * LOG2E

    def at_copy(i, s):
        src = ot.at[pl.ds(mult(i * HEAD_DIM, HEAD_DIM), HEAD_DIM), pl.ds(s * rows, rows)]
        dst = att_o.at[pl.ds(mult(at["block"] * part + i * HEAD_DIM, HEAD_DIM), HEAD_DIM), :]
        return src, dst

    def at_remote(i, s):
        src, dst = at_copy(i, s)
        return remote(src, dst, at_send.at[i * 4 + s], at_recv.at[at["block"] * heads + i], (at["served"], s))

    def stays(s):
        return jnp.logical_and(collects, h == s)

    def one_head(i, _):
        qrow, krow, vrow = (mult(p * part + i * HEAD_DIM, HEAD_DIM) for p in range(3))
        kh[...] = mix[pl.ds(krow, HEAD_DIM), :].T
        for j in range(group // QB):
            cols = slice(j * QB, (j + 1) * QB)
            q_t = mix[pl.ds(qrow, HEAD_DIM), cols]
            begins = start_o[0:1, cols]
            top = jnp.full((1, QB), -jnp.inf, F32)
            for k in range(j + 1):
                s_t = dot(kh[k * QB : (k + 1) * QB, :], q_t)
                key = lax.broadcasted_iota(jnp.int32, (QB, QB), 0)
                keep = key >= begins - k * QB
                if k == j:
                    keep = jnp.logical_and(keep, key <= lax.broadcasted_iota(jnp.int32, (QB, QB), 1))
                s_t = jnp.where(keep, s_t, -1e30)
                scores[k * QB : (k + 1) * QB, :] = s_t
                top = jnp.maximum(top, jnp.max(s_t, axis=0, keepdims=True))
            top = top * scale
            total = jnp.zeros((1, QB), F32)
            acc = jnp.zeros((HEAD_DIM, QB), F32)
            for k in range(j + 1):
                p_t = jnp.exp2(scores[k * QB : (k + 1) * QB, :] * scale - top)
                total = total + jnp.sum(p_t, axis=0, keepdims=True)
                acc = acc + dot(mix[pl.ds(vrow, HEAD_DIM), k * QB : (k + 1) * QB], p_t.astype(BF16))
            ot[pl.ds(qrow, HEAD_DIM), cols] = (acc / total).astype(BF16)
            lse_o[pl.ds(mult(i * 8, 8), 8), cols] = jnp.broadcast_to(top + jnp.log2(total), (8, QB))
        for s in range(4):
            @pl.when(stays(s))
            def _():
                pltpu.make_async_copy(*at_copy(i, s), at_local.at[i]).start()

            @pl.when(jnp.logical_not(stays(s)))
            def _():
                at_remote(i, s).start()
        return 0

    lax.fori_loop(0, heads, one_head, 0)
    ot_copy = pltpu.make_async_copy(ot, ot_o, out_sem.at[6])
    ot_copy.start()

    for t in range(2):
        @pl.when(2 * core + t != h)
        def _():
            ag_copy(t).wait_send()

    @pl.when(collects)
    def _():
        own_fw.wait_send()
        for d in range(1, 4):
            fw_copy(d, order[d]).wait_send()

    st_copy.wait_send()
    wt_copy.wait()
    mix_copy.wait()
    for d in range(4):
        pltpu.make_async_copy(shard(xg, order[d]), shard(xg_o, order[d]), out_sem.at[1 + d]).wait()
    ot_copy.wait()
    for i in range(heads):
        for s in range(4):
            @pl.when(stays(s))
            def _():
                pltpu.make_async_copy(*at_copy(i, s), at_local.at[i]).wait()

            @pl.when(jnp.logical_not(stays(s)))
            def _():
                at_remote(i, s).wait_send()
        for b in range(4):
            dst = att_o.at[pl.ds(b * part + i * HEAD_DIM, HEAD_DIM), :]
            src = ot.at[pl.ds(i * HEAD_DIM, HEAD_DIM), pl.ds(0, rows)]

            @pl.when(jnp.logical_not(jnp.logical_and(collects, at["block"] == b)))
            def _():
                remote(src, dst, at_send.at[i * 4], at_recv.at[b * heads + i], (sib, h)).wait_recv()


def attend(tokens, lengths, gain, bias, bias_q, bias_v, w_qkv):
    rows, width = tokens.shape
    group, part = 4 * rows, width // 4
    heads = part // HEAD_DIM
    dma = pltpu.SemaphoreType.DMA
    return pl.pallas_call(
        attend_kernel,
        out_shape=(
            jax.ShapeDtypeStruct((width, rows), BF16),
            jax.ShapeDtypeStruct((3 * part, group), BF16),
            jax.ShapeDtypeStruct((group, width), BF16),
            jax.ShapeDtypeStruct((part, group), BF16),
            jax.ShapeDtypeStruct((8 * heads, group), F32),
            jax.ShapeDtypeStruct((8, group), jnp.int32),
            jax.ShapeDtypeStruct((3 * part, width), BF16),
        ),
        in_specs=[VMEM, SMEM, VMEM, VMEM, VMEM, VMEM, ANY],
        out_specs=(ANY, ANY, ANY, ANY, VMEM, VMEM, ANY),
        scratch_shapes=[
            pltpu.VMEM((rows, width), BF16),
            pltpu.VMEM((group, width), BF16),
            pltpu.VMEM((3, width, 256), BF16),
            pltpu.VMEM((256, width), BF16),
            pltpu.VMEM((3 * part, width), BF16),
            pltpu.VMEM((3, 256, 128), F32),
            pltpu.VMEM((8, group), F32),
            pltpu.VMEM((8, group), F32),
            pltpu.VMEM((3 * part, group), BF16),
            pltpu.VMEM((group, HEAD_DIM), BF16),
            pltpu.VMEM((group, QB), F32),
            pltpu.VMEM((part, group), BF16),
            dma((3,)), dma((2,)), dma((2,)), dma((4,)), dma((4,)),
            dma((4 * heads,)), dma((4 * heads,)), dma((heads,)), dma((7,)),
        ],
        compiler_params=pltpu.CompilerParams(
            collective_id=0, has_side_effects=True, vmem_limit_bytes=32 << 20
        ),
        name="attend",
    )(tokens, lengths, gain[None], bias[None], bias_q[None], bias_v[None], w_qkv)


def mlp_kernel(
    grad_scale,
    att, tok, cot, b_out, gain, bias, b_fc, b_proj, w_out_h, w_fc_h, w_proj_h,
    out_o, dmid_o, dot_o, gout_o, gfc_o, gproj_o, vec_o,
    w_out, w_fc, w_proj, hid, dfc, dat, gout, gfc, gproj,
    w_sem, send, recv, local, out_sem,
):
    at = place()
    h, core = at["h"], at["core"]
    rows, width = tok.shape
    part = width // 4
    chunks = w_fc_h.shape[1] // width
    wo_copy = pltpu.make_async_copy(w_out_h, w_out, w_sem.at[0])
    wo_copy.start()

    def wf_copy(j):
        return pltpu.make_async_copy(w_fc_h.at[:, pl.ds(j * width, width)], w_fc.at[j], w_sem.at[1 + 2 * j])

    def wp_copy(j):
        return pltpu.make_async_copy(w_proj_h.at[pl.ds(j * width, width), :], w_proj.at[j], w_sem.at[2 + 2 * j])

    for j in range(chunks):
        wf_copy(j).start()
        wp_copy(j).start()
    greet(at)

    dy = cot[...].astype(F32)
    d_proj = (DEPTH_SCALE * dy).astype(BF16)
    wo_copy.wait()
    middle = tok[...].astype(F32) + DEPTH_SCALE * (dot_tn(att[...], w_out[...]) + b_out[...])
    n, r = norm_parts(middle)
    second = (n * gain[...] + bias[...]).astype(BF16)
    result = middle + DEPTH_SCALE * b_proj[...]
    d_second = jnp.zeros((rows, width), F32)
    vec_o[3:4, :] = jnp.sum(dy, axis=0, keepdims=True) * (DEPTH_SCALE * grad_scale)
    for j in range(chunks):
        wf_copy(j).wait()
        u = dot(second, w_fc[j]) + b_fc[j : j + 1, :]
        u2 = u * u
        th = jnp.tanh(GELU_K * u * (1.0 + GELU_A * u2))
        half = 0.5 * (1.0 + th)
        slope = half + 0.5 * u * (1.0 - th * th) * (GELU_K * (1.0 + 3.0 * GELU_A * u2))
        hidden = (u * half).astype(BF16)
        hid[j] = hidden
        wp_copy(j).wait()
        result = result + DEPTH_SCALE * dot(hidden, w_proj[j])
        d_pre = dot_nt(d_proj, w_proj[j]) * slope
        vec_o[4 + j : 5 + j, :] = jnp.sum(d_pre, axis=0, keepdims=True) * grad_scale
        d_fc = d_pre.astype(BF16)
        dfc[j] = d_fc
        d_second = d_second + dot_nt(d_fc, w_fc[j])
    out_o[...] = result
    vec_o[1:2, :] = jnp.sum(d_second * n, axis=0, keepdims=True) * grad_scale
    vec_o[2:3, :] = jnp.sum(d_second, axis=0, keepdims=True) * grad_scale
    d_middle = dy + norm_back(d_second, gain[...], n, r)
    dmid_o[...] = d_middle
    vec_o[0:1, :] = jnp.sum(d_middle, axis=0, keepdims=True) * (DEPTH_SCALE * grad_scale)
    d_out = (DEPTH_SCALE * d_middle).astype(BF16)
    dat[...] = dot_nt(w_out[...], d_out).astype(BF16)

    def target(b):
        return at["even"] + b % 2, 2 * core + b // 2

    def stays(b):
        return jnp.logical_and(core == b % 2, h == 2 * core + b // 2)

    dst = dot_o.at[:, pl.ds(mult(h * rows, 128), rows)]

    def da_local(b):
        return pltpu.make_async_copy(dat.at[pl.ds(b * part, part), :], dst, local)

    def da_remote(b):
        return remote(dat.at[pl.ds(b * part, part), :], dst, send.at[b], recv.at[h], target(b))

    for b in range(4):
        @pl.when(stays(b))
        def _():
            da_local(b).start()

        @pl.when(jnp.logical_not(stays(b)))
        def _():
            da_remote(b).start()

    gout[...] = (dot(att[...], d_out) * grad_scale).astype(BF16)
    go_copy = pltpu.make_async_copy(gout, gout_o, out_sem.at[0])
    go_copy.start()
    second_t = second.T
    gf_copies, gp_copies = [], []
    for j in range(chunks):
        gfc[j] = (dot(second_t, dfc[j]) * grad_scale).astype(BF16)
        gf_copies.append(
            pltpu.make_async_copy(gfc.at[j], gfc_o.at[:, pl.ds(j * width, width)], out_sem.at[1 + 2 * j])
        )
        gf_copies[-1].start()
        gproj[j] = (dot_tn(hid[j], d_proj) * grad_scale).astype(BF16)
        gp_copies.append(
            pltpu.make_async_copy(gproj.at[j], gproj_o.at[pl.ds(j * width, width), :], out_sem.at[2 + 2 * j])
        )
        gp_copies[-1].start()

    served_here = core == at["half"]
    for b in range(4):
        @pl.when(stays(b))
        def _():
            da_local(b).wait()

        @pl.when(jnp.logical_not(stays(b)))
        def _():
            da_remote(b).wait_send()
    for s in range(4):
        @pl.when(jnp.logical_not(jnp.logical_and(served_here, h == s)))
        def _():
            remote(
                dat.at[pl.ds(0, part), :], dot_o.at[:, pl.ds(s * rows, rows)], send.at[0], recv.at[s], (at["sib"], h)
            ).wait_recv()
    go_copy.wait()
    for copy in gf_copies + gp_copies:
        copy.wait()


def mlp(att, tokens, cotangent, grad_scale, b_out, gain, bias, b_fc, b_proj, w_out, w_fc, w_proj):
    rows, width = tokens.shape
    part, group = width // 4, 4 * rows
    ff = w_fc.shape[1]
    chunks = ff // width
    dma = pltpu.SemaphoreType.DMA
    return pl.pallas_call(
        functools.partial(mlp_kernel, grad_scale),
        out_shape=(
            jax.ShapeDtypeStruct((rows, width), F32),
            jax.ShapeDtypeStruct((rows, width), F32),
            jax.ShapeDtypeStruct((part, group), BF16),
            jax.ShapeDtypeStruct((width, width), BF16),
            jax.ShapeDtypeStruct((width, ff), BF16),
            jax.ShapeDtypeStruct((ff, width), BF16),
            jax.ShapeDtypeStruct((8, width), F32),
        ),
        in_specs=[VMEM] * 8 + [ANY] * 3,
        out_specs=(VMEM, VMEM, ANY, ANY, ANY, ANY, VMEM),
        scratch_shapes=[
            pltpu.VMEM((width, width), BF16),
            pltpu.VMEM((chunks, width, width), BF16),
            pltpu.VMEM((chunks, width, width), BF16),
            pltpu.VMEM((chunks, rows, width), BF16),
            pltpu.VMEM((chunks, rows, width), BF16),
            pltpu.VMEM((width, rows), BF16),
            pltpu.VMEM((width, width), BF16),
            pltpu.VMEM((chunks, width, width), BF16),
            pltpu.VMEM((chunks, width, width), BF16),
            dma((1 + 2 * chunks,)), dma((4,)), dma((4,)), dma, dma((1 + 2 * chunks,)),
        ],
        compiler_params=pltpu.CompilerParams(
            collective_id=1, has_side_effects=True, vmem_limit_bytes=56 << 20
        ),
        name="mlp",
    )(
        att, tokens, cotangent, b_out[None], gain[None], bias[None], b_fc.reshape(chunks, width), b_proj[None],
        w_out, w_fc, w_proj,
    )


def back_kernel(
    grad_scale,
    mix_h, xg_h, ot_h, lse, start, do_h, wt_h, dmid, tok, gain,
    gtok_o, gqkv_o, ln_o, bias_o,
    mix, xg, ot, do_t, wt, delta, kh, vh, qh, doh, dq, dk, dv, dmix, partial, summed, arrive, arrive2, gq,
    in_sem, sw_send, sw_recv, fin_send, fin_recv, fin_local, out_sem,
):
    at = place()
    h, core, sib = at["h"], at["core"], at["sib"]
    rows, width = tok.shape
    part, group = width // 4, 4 * rows
    heads = part // HEAD_DIM
    loads = [
        pltpu.make_async_copy(src, dst, in_sem.at[k])
        for k, (src, dst) in enumerate(((do_h, do_t), (ot_h, ot), (mix_h, mix), (wt_h, wt), (xg_h, xg)))
    ]
    for load in loads:
        load.start()
    greet(at)
    for load in loads[:3]:
        load.wait()
    scale = SCORE_SCALE * LOG2E

    def one_head(i, _):
        qrow, krow, vrow = (mult(p * part + i * HEAD_DIM, HEAD_DIM) for p in range(3))
        d_head = do_t[pl.ds(qrow, HEAD_DIM), :]
        delta[...] = jnp.broadcast_to(
            jnp.sum(d_head.astype(F32) * ot[pl.ds(qrow, HEAD_DIM), :].astype(F32), axis=0, keepdims=True), (8, group)
        )
        qh[...] = mix[pl.ds(qrow, HEAD_DIM), :].T
        kh[...] = mix[pl.ds(krow, HEAD_DIM), :].T
        vh[...] = mix[pl.ds(vrow, HEAD_DIM), :].T
        doh[...] = d_head.T
        for j in range(group // QB):
            cols = slice(j * QB, (j + 1) * QB)
            q_t = mix[pl.ds(qrow, HEAD_DIM), cols]
            do_j = do_t[pl.ds(qrow, HEAD_DIM), cols]
            begins = start[0:1, cols]
            lse_j = lse[pl.ds(mult(i * 8, 8), 8), cols][0:1]
            delta_j = delta[0:1, cols]
            acc = jnp.zeros((HEAD_DIM, QB), F32)
            for k in range(j + 1):
                keys = slice(k * QB, (k + 1) * QB)
                s_t = dot(kh[keys, :], q_t)
                key = lax.broadcasted_iota(jnp.int32, (QB, QB), 0)
                keep = key >= begins - k * QB
                if k == j:
                    keep = jnp.logical_and(keep, key <= lax.broadcasted_iota(jnp.int32, (QB, QB), 1))
                p_t = jnp.where(keep, jnp.exp2(s_t * scale - lse_j), 0.0)
                dp_t = dot(vh[keys, :], do_j)
                ds_t = (p_t * (dp_t - delta_j)).astype(BF16)
                dv_add = dot(p_t.astype(BF16), doh[cols, :])
                dk_add = dot(ds_t, qh[cols, :])
                if k == j:
                    dv[keys, :] = dv_add
                    dk[keys, :] = dk_add
                else:
                    dv[keys, :] += dv_add
                    dk[keys, :] += dk_add
                acc = acc + dot(mix[pl.ds(krow, HEAD_DIM), keys], ds_t)
            dmix[pl.ds(qrow, HEAD_DIM), cols] = (acc * SCORE_SCALE).astype(BF16)
        dmix[pl.ds(krow, HEAD_DIM), :] = (dk[...] * SCORE_SCALE).T.astype(BF16)
        dmix[pl.ds(vrow, HEAD_DIM), :] = dv[...].T.astype(BF16)
        return 0

    lax.fori_loop(0, heads, one_head, 0)
    loads[3].wait()
    loads[4].wait()

    def rows_of(s):
        return pl.ds(mult(s * rows, rows), rows)

    def part_of(s):
        return dot_tn(dmix[:, pl.ds(mult(s * rows, 128), rows)], wt[...])

    swaps = []
    for t in range(2):
        partial[t] = part_of(2 * t + 1 - core).astype(BF16)
        swaps.append(remote(partial.at[t], arrive.at[t], sw_send.at[t], sw_recv.at[t], (sib, h)))
        swaps[-1].start()

    slot = h - 2 * at["half"]

    def fin_remote(t):
        return remote(
            summed.at[t], arrive2.at[slot], fin_send.at[t], fin_recv.at[slot], (at["served"], 2 * t + core)
        )

    def fin_local_copy(t):
        return pltpu.make_async_copy(summed.at[t], arrive2.at[slot], fin_local)

    def stays(t):
        return jnp.logical_and(core == at["half"], h == 2 * t + core)

    for t in range(2):
        mine = part_of(2 * t + core)
        swaps[t].wait_recv()
        summed[t] = (mine + arrive[t].astype(F32)).astype(BF16)

        @pl.when(stays(t))
        def _():
            fin_local_copy(t).start()

        @pl.when(jnp.logical_not(stays(t)))
        def _():
            fin_remote(t).start()

    ones = jnp.ones((group, 128), BF16)
    bias_o[...] = dot(dmix[...], ones) * grad_scale
    gq[...] = (dot(dmix[...], xg[...]) * grad_scale).astype(BF16)
    gq_copy = pltpu.make_async_copy(gq, gqkv_o, out_sem)
    gq_copy.start()

    for k in range(2):
        from_me = jnp.logical_and(
            jnp.logical_and(core == at["half"], slot == k), lax.rem(h, 2) == core
        )

        @pl.when(from_me)
        def _():
            pltpu.make_async_copy(summed.at[0], arrive2.at[k], fin_local).wait()

        @pl.when(jnp.logical_not(from_me))
        def _():
            remote(summed.at[0], arrive2.at[k], fin_send.at[0], fin_recv.at[k], (sib, h)).wait_recv()
    e = arrive2[0].astype(F32) + arrive2[1].astype(F32)
    n, r = norm_parts(tok[...].astype(F32))
    gtok_o[...] = dmid[...] + norm_back(e, gain[...], n, r)
    ln_o[0:1, :] = jnp.sum(e * n, axis=0, keepdims=True) * grad_scale
    ln_o[1:2, :] = jnp.sum(e, axis=0, keepdims=True) * grad_scale
    ln_o[2:8, :] = jnp.zeros((6, width), F32)
    for t in range(2):
        swaps[t].wait_send()

        @pl.when(jnp.logical_not(stays(t)))
        def _():
            fin_remote(t).wait_send()
    gq_copy.wait()


def attend_back(mix, xg, ot, lse, start, d_ot, wt, d_middle, tokens, gain, grad_scale):
    rows, width = tokens.shape
    part, group = width // 4, 4 * rows
    dma = pltpu.SemaphoreType.DMA
    return pl.pallas_call(
        functools.partial(back_kernel, grad_scale),
        out_shape=(
            jax.ShapeDtypeStruct((rows, width), F32),
            jax.ShapeDtypeStruct((3 * part, width), BF16),
            jax.ShapeDtypeStruct((8, width), F32),
            jax.ShapeDtypeStruct((3 * part, 128), F32),
        ),
        in_specs=[ANY, ANY, ANY, VMEM, VMEM, ANY, ANY, VMEM, VMEM, VMEM],
        out_specs=(VMEM, ANY, VMEM, VMEM),
        scratch_shapes=[
            pltpu.VMEM((3 * part, group), BF16),
            pltpu.VMEM((group, width), BF16),
            pltpu.VMEM((part, group), BF16),
            pltpu.VMEM((part, group), BF16),
            pltpu.VMEM((3 * part, width), BF16),
            pltpu.VMEM((8, group), F32),
            pltpu.VMEM((group, HEAD_DIM), BF16),
            pltpu.VMEM((group, HEAD_DIM), BF16),
            pltpu.VMEM((group, HEAD_DIM), BF16),
            pltpu.VMEM((group, HEAD_DIM), BF16),
            pltpu.VMEM((HEAD_DIM, group), F32),
            pltpu.VMEM((group, HEAD_DIM), F32),
            pltpu.VMEM((group, HEAD_DIM), F32),
            pltpu.VMEM((3 * part, group), BF16),
            pltpu.VMEM((2, rows, width), BF16),
            pltpu.VMEM((2, rows, width), BF16),
            pltpu.VMEM((2, rows, width), BF16),
            pltpu.VMEM((2, rows, width), BF16),
            pltpu.VMEM((3 * part, width), BF16),
            dma((5,)), dma((2,)), dma((2,)), dma((2,)), dma((2,)), dma, dma,
        ],
        compiler_params=pltpu.CompilerParams(
            collective_id=2, has_side_effects=True, vmem_limit_bytes=48 << 20
        ),
        name="attend_back",
    )(mix, xg, ot, lse, start, d_ot, wt, d_middle, tokens, gain[None])


def shards(
    tokens, lengths, ln1_gain, ln1_bias, w_qkv, bias_q, bias_v, w_out, bias_out, ln2_gain, ln2_bias, w_fc, bias_fc,
    w_proj, bias_proj, cotangent,
):
    rows, width = tokens.shape
    part = width // 4
    device_count = lax.axis_size("dp") * lax.axis_size("head")
    grad_scale = 1.0 / math.sqrt(rows * device_count)
    att, mix, xg, ot, lse, start, wt = attend(tokens, lengths, ln1_gain, ln1_bias, bias_q, bias_v, w_qkv)
    block_output, d_middle, d_ot, g_out, g_fc, g_proj, vecs = mlp(
        att, tokens, cotangent, grad_scale, bias_out, ln2_gain, ln2_bias, bias_fc, bias_proj, w_out, w_fc, w_proj
    )
    grad_tokens, g_qkv, ln_vec, bias_vec = attend_back(
        mix, xg, ot, lse, start, d_ot, wt, d_middle, tokens, ln1_gain, grad_scale
    )
    block = lax.rem(lax.axis_index("head"), 2) * 2 + lax.rem(lax.axis_index("dp"), 2)
    wide = jnp.zeros((3, width, width), BF16)
    wide = lax.dynamic_update_slice(wide, g_qkv.reshape(3, part, width), (0, block * part, 0))
    wide = wide.reshape(3 * width, width).T
    bias_wide = lax.dynamic_update_slice(
        jnp.zeros((3, width), F32), bias_vec[:, 0].reshape(3, part), (0, block * part)
    )

    def reduce_mat(g, dim):
        share = lax.psum_scatter(g, "dp", scatter_dimension=dim, tiled=True)
        return lax.psum(share, "head").astype(F32)

    vec = lax.psum(jnp.concatenate([vecs, ln_vec[:2], bias_wide]), ("dp", "head"))
    return (
        block_output, grad_tokens, vec[8], vec[9], reduce_mat(wide, 0), vec[10], vec[12], reduce_mat(g_out, 0),
        vec[0], vec[1], vec[2], reduce_mat(g_fc, 1), vec[4:8].reshape(-1), reduce_mat(g_proj, 0), vec[3],
    )


def solution(mesh):
    rows = P(("dp", "head"), None)
    return jax.shard_map(
        shards,
        mesh=mesh,
        in_specs=(rows, P("dp", None)) + (P(),) * 13 + (rows,),
        out_specs=(
            rows, rows, P(), P(), P("dp", None), P(), P(), P("dp", None), P(), P(), P(), P(None, "dp"), P(),
            P("dp", None), P(),
        ),
        check_vma=False,
    )
```

```python
import functools
import math
import types

import jax
import jax.numpy as jnp
from jax import lax
from jax.experimental import pallas as pl
from jax.experimental.pallas import tpu as pltpu
from jax.sharding import PartitionSpec as P

HEAD_DIM = 64
EPSILON = 1e-05
DEPTH_SCALE = 1.0 / math.sqrt(12.0)
LOG2E = 1.0 / math.log(2.0)
SCORE_SCALE = HEAD_DIM ** (-0.5)
GELU_K = math.sqrt(2.0 / math.pi)
GELU_A = 0.044715
TEAM = 8
QB = 256
PIECES = 3

F32 = jnp.float32
BF16 = jnp.bfloat16
MESH = pl.DeviceIdType.MESH
ANY = pl.BlockSpec(memory_space=pl.ANY)
VMEM = pl.BlockSpec(memory_space=pltpu.VMEM)
SMEM = pl.BlockSpec(memory_space=pltpu.SMEM)


def dot(a, b):
    return jnp.dot(a, b, preferred_element_type=F32)


def dot_nt(a, b):
    return lax.dot_general(a, b, (((1,), (1,)), ((), ())), preferred_element_type=F32)


def dot_tn(a, b):
    return lax.dot_general(a, b, (((0,), (0,)), ((), ())), preferred_element_type=F32)


def mult(x, m):
    return pl.multiple_of(x, m)


def place():
    dp, h = lax.axis_index("dp"), lax.axis_index("head")
    core = lax.rem(dp, 2)
    half = h // 2
    return dict(
        dp=dp,
        h=h,
        core=core,
        sib=dp + 1 - 2 * core,
        even=dp - core,
        half=half,
        served=dp - core + half,
        block=(h - 2 * half) * 2 + core,
    )


def greet(at, chips=False):
    barrier = pltpu.get_barrier_semaphore()
    me = at["core"] * 4 + at["h"]
    others = []
    for k in range(1, TEAM):
        other = lax.rem(me + k, TEAM)
        others.append((at["even"] + other // 4, lax.rem(other, 4)))
    if chips:
        for k in range(1, 4):
            others.append((lax.rem(at["dp"] + 2 * k, 8), at["h"]))
    for other in others:
        pl.semaphore_signal(barrier, inc=1, device_id=other, device_id_type=MESH)
    pl.semaphore_wait(barrier, len(others))


def remote(src, dst, send, recv, device):
    return pltpu.make_async_remote_copy(
        src_ref=src, dst_ref=dst, send_sem=send, recv_sem=recv, device_id=device, device_id_type=MESH
    )


def norm_parts(v):
    center = jnp.mean(v, axis=-1, keepdims=True)
    cent = v - center
    r = lax.rsqrt(jnp.mean(cent * cent, axis=-1, keepdims=True) + EPSILON)
    return cent * r, r


def norm_back(e, gain, n, r):
    ea = e * gain
    return r * (ea - jnp.mean(ea, axis=-1, keepdims=True) - n * jnp.mean(ea * n, axis=-1, keepdims=True))


def attend_kernel(
    tok, lens, gain, bias, bias_q, bias_v, w_qkv,
    att_o, mix_o, xgt_o, ot_o, lse_o, start_o, wt_o,
    xn, xg, xgt, wwin, wt, bcol, start_mine, start_sib, mix, kh, scores, ot,
    w_sem, st_sem, ag_send, ag_recv, fw_send, at_send, at_recv, at_local, out_sem,
):
    at = place()
    dp, h, core, sib = at["dp"], at["h"], at["core"], at["sib"]
    rows, width = tok.shape
    group = 4 * rows
    part = width // 4
    collects = core == at["half"]
    first = (h - 2 * at["half"]) * 2 * part + core * 128
    shift = mult(64 * core, 64)
    for p in range(3):
        pltpu.make_async_copy(
            w_qkv.at[:, pl.ds(mult(p * width + first, 128), 256)], wwin.at[p], w_sem.at[p]
        ).start()
    greet(at)

    places = lax.broadcasted_iota(jnp.int32, (8, group), 1)
    begin = jnp.zeros((8, group), jnp.int32)
    edge = lens[0, 0]
    for k in range(1, lens.shape[1] + 1):
        begin = jnp.where(places >= edge, edge, begin)
        if k < lens.shape[1]:
            edge = edge + lens[0, k]
    start_mine[...] = begin.astype(F32)
    st_copy = remote(start_mine, start_sib, st_sem.at[0], st_sem.at[1], (sib, h))
    st_copy.start()

    n, _ = norm_parts(tok[...].astype(F32))
    xn[...] = (n * gain[...] + bias[...]).astype(BF16)

    def shard(ref, s):
        return ref.at[pl.ds(mult(s * rows, rows), rows), :]

    def ag_copy(t):
        return remote(xn, shard(xg, h), ag_send.at[t], ag_recv.at[h], (dp, 2 * core + t))

    for t in range(2):
        @pl.when(2 * core + t != h)
        def _():
            ag_copy(t).start()

    own_fw = remote(xn, shard(xg, h), fw_send.at[0], ag_recv.at[h], (sib, h))

    @pl.when(collects)
    def _():
        own_fw.start()
        xg[pl.ds(mult(h * rows, rows), rows), :] = xn[...]

    for p in range(3):
        pltpu.make_async_copy(wwin.at[p], wwin.at[p], w_sem.at[p]).wait()
        wt[p * 256 : (p + 1) * 256, :] = wwin[p].T
    wt_copy = pltpu.make_async_copy(wt, wt_o, out_sem.at[0])
    wt_copy.start()
    for p, vec in ((0, bias_q), (2, bias_v)):
        bcol[p] = jnp.broadcast_to(vec[:, pl.ds(mult(first, 128), 256)], (128, 256)).T
    bcol[1] = jnp.zeros((256, 128), F32)

    low = 1 - at["half"]
    order = (h, low * (1 - h) + (1 - low) * (5 - h), 1 + low, 3 * low)

    def fw_copy(d, s):
        return remote(shard(xg, s), shard(xg, s), fw_send.at[d], ag_recv.at[s], (sib, h))

    for d in range(4):
        s = order[d]
        if d == 0:
            @pl.when(jnp.logical_not(collects))
            def _():
                fw_copy(d, s).wait_recv()
        else:
            fw_copy(d, s).wait_recv()

            @pl.when(collects)
            def _():
                fw_copy(d, s).start()

        here = xg[pl.ds(mult(s * rows, rows), rows), :]
        xgt[:, pl.ds(mult(s * rows, 128), rows)] = here.T
        for p in range(3):
            res = dot_nt(wt[pl.ds(mult(p * 256 + shift, 64), part), :], here) + bcol[p, pl.ds(shift, part), :][:, :1]
            mix[p * part : (p + 1) * part, pl.ds(mult(s * rows, 128), rows)] = res.astype(BF16)
    mix_copy = pltpu.make_async_copy(mix, mix_o, out_sem.at[2])
    mix_copy.start()
    xgt_copy = pltpu.make_async_copy(xgt, xgt_o, out_sem.at[1])
    xgt_copy.start()
    st_copy.wait_recv()
    start_o[...] = jnp.where(collects, start_mine[...], start_sib[...]).astype(jnp.int32)

    heads = part // HEAD_DIM
    scale = SCORE_SCALE * LOG2E

    def at_copy(i, s):
        src = ot.at[pl.ds(mult(i * HEAD_DIM, HEAD_DIM), HEAD_DIM), pl.ds(s * rows, rows)]
        dst = att_o.at[pl.ds(mult(at["block"] * part + i * HEAD_DIM, HEAD_DIM), HEAD_DIM), :]
        return src, dst

    def at_remote(i, s):
        src, dst = at_copy(i, s)
        return remote(src, dst, at_send.at[i * 4 + s], at_recv.at[at["block"] * heads + i], (at["served"], s))

    def stays(s):
        return jnp.logical_and(collects, h == s)

    def one_head(i, _):
        qrow, krow, vrow = (mult(p * part + i * HEAD_DIM, HEAD_DIM) for p in range(3))
        kh[...] = mix[pl.ds(krow, HEAD_DIM), :].T
        for j in range(group // QB):
            cols = slice(j * QB, (j + 1) * QB)
            q_t = mix[pl.ds(qrow, HEAD_DIM), cols]
            begins = start_o[0:1, cols]
            top = jnp.full((1, QB), -jnp.inf, F32)
            for k in range(j + 1):
                s_t = dot(kh[k * QB : (k + 1) * QB, :], q_t)
                key = lax.broadcasted_iota(jnp.int32, (QB, QB), 0)
                keep = key >= begins - k * QB
                if k == j:
                    keep = jnp.logical_and(keep, key <= lax.broadcasted_iota(jnp.int32, (QB, QB), 1))
                s_t = jnp.where(keep, s_t, -1e30)
                scores[k * QB : (k + 1) * QB, :] = s_t
                top = jnp.maximum(top, jnp.max(s_t, axis=0, keepdims=True))
            top = top * scale
            total = jnp.zeros((1, QB), F32)
            acc = jnp.zeros((HEAD_DIM, QB), F32)
            for k in range(j + 1):
                p_t = jnp.exp2(scores[k * QB : (k + 1) * QB, :] * scale - top)
                total = total + jnp.sum(p_t, axis=0, keepdims=True)
                acc = acc + dot(mix[pl.ds(vrow, HEAD_DIM), k * QB : (k + 1) * QB], p_t.astype(BF16))
            ot[pl.ds(qrow, HEAD_DIM), cols] = (acc / total).astype(BF16)
            lse_o[pl.ds(mult(i * 8, 8), 8), cols] = jnp.broadcast_to(top + jnp.log2(total), (8, QB))
        for s in range(4):
            @pl.when(stays(s))
            def _():
                pltpu.make_async_copy(*at_copy(i, s), at_local.at[i]).start()

            @pl.when(jnp.logical_not(stays(s)))
            def _():
                at_remote(i, s).start()
        return 0

    lax.fori_loop(0, heads, one_head, 0)
    ot_copy = pltpu.make_async_copy(ot, ot_o, out_sem.at[3])
    ot_copy.start()

    for t in range(2):
        @pl.when(2 * core + t != h)
        def _():
            ag_copy(t).wait_send()

    @pl.when(collects)
    def _():
        own_fw.wait_send()
        for d in range(1, 4):
            fw_copy(d, order[d]).wait_send()

    st_copy.wait_send()
    wt_copy.wait()
    mix_copy.wait()
    xgt_copy.wait()
    ot_copy.wait()
    for i in range(heads):
        for s in range(4):
            @pl.when(stays(s))
            def _():
                pltpu.make_async_copy(*at_copy(i, s), at_local.at[i]).wait()

            @pl.when(jnp.logical_not(stays(s)))
            def _():
                at_remote(i, s).wait_send()
        for b in range(4):
            dst = att_o.at[pl.ds(b * part + i * HEAD_DIM, HEAD_DIM), :]
            src = ot.at[pl.ds(i * HEAD_DIM, HEAD_DIM), pl.ds(0, rows)]

            @pl.when(jnp.logical_not(jnp.logical_and(collects, at["block"] == b)))
            def _():
                remote(src, dst, at_send.at[i * 4], at_recv.at[b * heads + i], (sib, h)).wait_recv()


def attend(tokens, lengths, gain, bias, bias_q, bias_v, w_qkv):
    rows, width = tokens.shape
    group, part = 4 * rows, width // 4
    heads = part // HEAD_DIM
    dma = pltpu.SemaphoreType.DMA
    return pl.pallas_call(
        attend_kernel,
        out_shape=(
            jax.ShapeDtypeStruct((width, rows), BF16),
            jax.ShapeDtypeStruct((3 * part, group), BF16),
            jax.ShapeDtypeStruct((width, group), BF16),
            jax.ShapeDtypeStruct((part, group), BF16),
            jax.ShapeDtypeStruct((8 * heads, group), F32),
            jax.ShapeDtypeStruct((8, group), jnp.int32),
            jax.ShapeDtypeStruct((3 * 256, width), BF16),
        ),
        in_specs=[VMEM, SMEM, VMEM, VMEM, VMEM, VMEM, ANY],
        out_specs=(ANY, ANY, ANY, ANY, VMEM, VMEM, ANY),
        scratch_shapes=[
            pltpu.VMEM((rows, width), BF16),
            pltpu.VMEM((group, width), BF16),
            pltpu.VMEM((width, group), BF16),
            pltpu.VMEM((3, width, 256), BF16),
            pltpu.VMEM((3 * 256, width), BF16),
            pltpu.VMEM((3, 256, 128), F32),
            pltpu.VMEM((8, group), F32),
            pltpu.VMEM((8, group), F32),
            pltpu.VMEM((3 * part, group), BF16),
            pltpu.VMEM((group, HEAD_DIM), BF16),
            pltpu.VMEM((group, QB), F32),
            pltpu.VMEM((part, group), BF16),
            dma((3,)), dma((2,)), dma((2,)), dma((4,)), dma((4,)),
            dma((4 * heads,)), dma((4 * heads,)), dma((heads,)), dma((4,)),
        ],
        compiler_params=pltpu.CompilerParams(
            collective_id=0, has_side_effects=True, vmem_limit_bytes=32 << 20
        ),
        name="attend",
    )(tokens, lengths, gain[None], bias[None], bias_q[None], bias_v[None], w_qkv)


def mlp_kernel(
    grad_scale, paired,
    att, tok, cot, b_out, gain, bias, b_fc, b_proj, w_out_h, w_fc_h, w_proj_h,
    out_o, dmid_o, dot_o, gfc_o, gproj_o, vec_o,
    w_out, w_fc, w_proj, hid, dfc, dat, gfc, gproj, gfc_in, gproj_in,
    w_sem, send, recv, local, pair_send, pair_recv, out_sem,
):
    at = place()
    h, core = at["h"], at["core"]
    rows, width = tok.shape
    part = width // 4
    chunks = w_fc_h.shape[1] // width
    wo_copy = pltpu.make_async_copy(w_out_h, w_out, w_sem.at[0])
    wo_copy.start()

    def wf_copy(j):
        return pltpu.make_async_copy(w_fc_h.at[:, pl.ds(j * width, width)], w_fc.at[j], w_sem.at[1 + 2 * j])

    def wp_copy(j):
        return pltpu.make_async_copy(w_proj_h.at[pl.ds(j * width, width), :], w_proj.at[j], w_sem.at[2 + 2 * j])

    for j in range(chunks):
        wf_copy(j).start()
        wp_copy(j).start()
    greet(at)

    dy = cot[...].astype(F32)
    d_proj = (DEPTH_SCALE * dy).astype(BF16)
    wo_copy.wait()
    middle = tok[...].astype(F32) + DEPTH_SCALE * (dot_tn(att[...], w_out[...]) + b_out[...])
    n, r = norm_parts(middle)
    second = (n * gain[...] + bias[...]).astype(BF16)
    result = middle + DEPTH_SCALE * b_proj[...]
    d_second = jnp.zeros((rows, width), F32)
    vec_o[3:4, :] = jnp.sum(dy, axis=0, keepdims=True) * (DEPTH_SCALE * grad_scale)
    for j in range(chunks):
        wf_copy(j).wait()
        u = dot(second, w_fc[j]) + b_fc[j : j + 1, :]
        u2 = u * u
        th = jnp.tanh(GELU_K * u * (1.0 + GELU_A * u2))
        half = 0.5 * (1.0 + th)
        slope = half + 0.5 * u * (1.0 - th * th) * (GELU_K * (1.0 + 3.0 * GELU_A * u2))
        hidden = (u * half).astype(BF16)
        hid[j] = hidden
        wp_copy(j).wait()
        result = result + DEPTH_SCALE * dot(hidden, w_proj[j])
        d_pre = dot_nt(d_proj, w_proj[j]) * slope
        vec_o[4 + j : 5 + j, :] = jnp.sum(d_pre, axis=0, keepdims=True) * grad_scale
        d_fc = d_pre.astype(BF16)
        dfc[j] = d_fc
        d_second = d_second + dot_nt(d_fc, w_fc[j])
    out_o[...] = result
    vec_o[1:2, :] = jnp.sum(d_second * n, axis=0, keepdims=True) * grad_scale
    vec_o[2:3, :] = jnp.sum(d_second, axis=0, keepdims=True) * grad_scale
    d_middle = dy + norm_back(d_second, gain[...], n, r)
    dmid_o[...] = d_middle
    vec_o[0:1, :] = jnp.sum(d_middle, axis=0, keepdims=True) * (DEPTH_SCALE * grad_scale)
    d_out = (DEPTH_SCALE * d_middle).astype(BF16)
    dat[...] = dot_nt(w_out[...], d_out).astype(BF16)

    def target(b):
        return at["even"] + b % 2, 2 * core + b // 2

    def stays(b):
        return jnp.logical_and(core == b % 2, h == 2 * core + b // 2)

    dst = dot_o.at[:, pl.ds(mult(h * rows, 128), rows)]

    def da_local(b):
        return pltpu.make_async_copy(dat.at[pl.ds(b * part, part), :], dst, local)

    def da_remote(b):
        return remote(dat.at[pl.ds(b * part, part), :], dst, send.at[b], recv.at[h], target(b))

    for b in range(4):
        @pl.when(stays(b))
        def _():
            da_local(b).start()

        @pl.when(jnp.logical_not(stays(b)))
        def _():
            da_remote(b).start()

    half_rows = width // 2
    small = width // 8
    pair = 1 - core

    def pair_copy(ref, into, k, j):
        return remote(ref.at[pair, j], into.at[j], pair_send.at[k, j], pair_recv.at[k, j], (at["sib"], h))

    g_out = (dot(att[...], d_out) * grad_scale).astype(BF16)
    for j in range(chunks):
        for k in range(2):
            gfc[k, j, half_rows:, :] = g_out[(2 * j + k) * small : (2 * j + k + 1) * small]
    for j in range(chunks):
        res = (dot_tn(hid[j], d_proj) * grad_scale).astype(BF16)
        for k in range(2):
            gproj[k, j] = res[k * half_rows : (k + 1) * half_rows]
        if paired:
            pair_copy(gproj, gproj_in, 0, j).start()
        res = (dot_tn(dfc[j], second) * grad_scale).astype(BF16)
        for k in range(2):
            gfc[k, j, :half_rows, :] = res[k * half_rows : (k + 1) * half_rows]
        if paired:
            pair_copy(gfc, gfc_in, 1, j).start()
    if paired:
        for j in range(chunks):
            for k, (ref, into) in enumerate(((gproj, gproj_in), (gfc, gfc_in))):
                pair_copy(ref, into, k, j).wait_recv()
                ref[core, j] = (ref[core, j].astype(F32) + into[j].astype(F32)).astype(BF16)
        outs = [
            pltpu.make_async_copy(gproj.at[core], gproj_o, out_sem.at[0]),
            pltpu.make_async_copy(gfc.at[core], gfc_o, out_sem.at[1]),
        ]
    else:
        outs = [
            pltpu.make_async_copy(gproj, gproj_o, out_sem.at[0]),
            pltpu.make_async_copy(gfc, gfc_o, out_sem.at[1]),
        ]
    for copy in outs:
        copy.start()

    served_here = core == at["half"]
    for b in range(4):
        @pl.when(stays(b))
        def _():
            da_local(b).wait()

        @pl.when(jnp.logical_not(stays(b)))
        def _():
            da_remote(b).wait_send()
    for s in range(4):
        @pl.when(jnp.logical_not(jnp.logical_and(served_here, h == s)))
        def _():
            remote(
                dat.at[pl.ds(0, part), :], dot_o.at[:, pl.ds(s * rows, rows)], send.at[0], recv.at[s], (at["sib"], h)
            ).wait_recv()
    if paired:
        for j in range(chunks):
            for k, (ref, into) in enumerate(((gproj, gproj_in), (gfc, gfc_in))):
                pair_copy(ref, into, k, j).wait_send()
    for copy in outs:
        copy.wait()


def mlp(att, tokens, cotangent, grad_scale, paired, b_out, gain, bias, b_fc, b_proj, w_out, w_fc, w_proj):
    rows, width = tokens.shape
    part, group = width // 4, 4 * rows
    ff = w_fc.shape[1]
    chunks = ff // width
    lead = () if paired else (2,)
    dma = pltpu.SemaphoreType.DMA
    return pl.pallas_call(
        functools.partial(mlp_kernel, grad_scale, paired),
        out_shape=(
            jax.ShapeDtypeStruct((rows, width), F32),
            jax.ShapeDtypeStruct((rows, width), F32),
            jax.ShapeDtypeStruct((part, group), BF16),
            jax.ShapeDtypeStruct(lead + (chunks, width // 2 + width // 8, width), BF16),
            jax.ShapeDtypeStruct(lead + (chunks, width // 2, width), BF16),
            jax.ShapeDtypeStruct((8, width), F32),
        ),
        in_specs=[VMEM] * 8 + [ANY] * 3,
        out_specs=(VMEM, VMEM, ANY, ANY, ANY, VMEM),
        scratch_shapes=[
            pltpu.VMEM((width, width), BF16),
            pltpu.VMEM((chunks, width, width), BF16),
            pltpu.VMEM((chunks, width, width), BF16),
            pltpu.VMEM((chunks, rows, width), BF16),
            pltpu.VMEM((chunks, rows, width), BF16),
            pltpu.VMEM((width, rows), BF16),
            pltpu.VMEM((2, chunks, width // 2 + width // 8, width), BF16),
            pltpu.VMEM((2, chunks, width // 2, width), BF16),
            pltpu.VMEM((chunks, width // 2 + width // 8, width), BF16),
            pltpu.VMEM((chunks, width // 2, width), BF16),
            dma((1 + 2 * chunks,)), dma((4,)), dma((4,)), dma, dma((2, chunks)), dma((2, chunks)), dma((2,)),
        ],
        compiler_params=pltpu.CompilerParams(
            collective_id=1, has_side_effects=True, vmem_limit_bytes=56 << 20
        ),
        name="mlp",
    )(
        att, tokens, cotangent, b_out[None], gain[None], bias[None], b_fc.reshape(chunks, width), b_proj[None],
        w_out, w_fc, w_proj,
    )


def back_kernel(grad_scale, full, names, *refs):
    ref = types.SimpleNamespace(**dict(zip(names, refs, strict=True)))
    mix, do_t, ot, xgt, wt, dmix = ref.mix, ref.do_t, ref.ot, ref.xgt, ref.wt, ref.dmix
    lse, start, delta, kh, vh, qh, doh, dk, dv = (
        ref.lse, ref.start, ref.delta, ref.kh, ref.vh, ref.qh, ref.doh, ref.dk, ref.dv
    )
    partial, summed, arrive, arrive2 = ref.partial, ref.summed, ref.arrive, ref.arrive2
    sw_send, sw_recv, fin_send, fin_recv, fin_local = (
        ref.sw_send, ref.sw_recv, ref.fin_send, ref.fin_recv, ref.fin_local
    )
    at = place()
    h, core, sib = at["h"], at["core"], at["sib"]
    rows, width = ref.tok.shape
    part, group = width // 4, 4 * rows
    heads = part // HEAD_DIM
    loads = [
        pltpu.make_async_copy(src, dst, ref.in_sem.at[k])
        for k, (src, dst) in enumerate(
            ((ref.do_h, do_t), (ref.ot_h, ot), (ref.mix_h, mix), (ref.wt_h, wt), (ref.xgt_h, xgt))
        )
    ]
    for load in loads:
        load.start()
    greet(at, full)
    if full:
        sums = Sums(ref, at, grad_scale)
        sums.first()
    dmix[...] = jnp.zeros_like(dmix)
    for load in loads[:3]:
        load.wait()
    scale = SCORE_SCALE * LOG2E

    def drow(p, i):
        return pl.ds(mult(p * 256 + (core + i) * HEAD_DIM, HEAD_DIM), HEAD_DIM)

    def one_head(i, _):
        qrow, krow, vrow = (mult(p * part + i * HEAD_DIM, HEAD_DIM) for p in range(3))
        d_head = do_t[pl.ds(qrow, HEAD_DIM), :]
        delta[...] = jnp.broadcast_to(
            jnp.sum(d_head.astype(F32) * ot[pl.ds(qrow, HEAD_DIM), :].astype(F32), axis=0, keepdims=True), (8, group)
        )
        qh[...] = mix[pl.ds(qrow, HEAD_DIM), :].T
        kh[...] = mix[pl.ds(krow, HEAD_DIM), :].T
        vh[...] = mix[pl.ds(vrow, HEAD_DIM), :].T
        doh[...] = d_head.T
        for j in range(group // QB):
            cols = slice(j * QB, (j + 1) * QB)
            q_t = mix[pl.ds(qrow, HEAD_DIM), cols]
            do_j = do_t[pl.ds(qrow, HEAD_DIM), cols]
            begins = start[0:1, cols]
            lse_j = lse[pl.ds(mult(i * 8, 8), 8), cols][0:1]
            delta_j = delta[0:1, cols]
            acc = jnp.zeros((HEAD_DIM, QB), F32)
            for k in range(j + 1):
                keys = slice(k * QB, (k + 1) * QB)
                s_t = dot(kh[keys, :], q_t)
                key = lax.broadcasted_iota(jnp.int32, (QB, QB), 0)
                keep = key >= begins - k * QB
                if k == j:
                    keep = jnp.logical_and(keep, key <= lax.broadcasted_iota(jnp.int32, (QB, QB), 1))
                p_t = jnp.where(keep, jnp.exp2(s_t * scale - lse_j), 0.0)
                dp_t = dot(vh[keys, :], do_j)
                ds_t = (p_t * (dp_t - delta_j)).astype(BF16)
                dv_add = dot(p_t.astype(BF16), doh[cols, :])
                dk_add = dot(ds_t, qh[cols, :])
                if k == j:
                    dv[keys, :] = dv_add
                    dk[keys, :] = dk_add
                else:
                    dv[keys, :] += dv_add
                    dk[keys, :] += dk_add
                acc = acc + dot(mix[pl.ds(krow, HEAD_DIM), keys], ds_t)
            dmix[drow(0, i), cols] = (acc * SCORE_SCALE).astype(BF16)
        dmix[drow(1, i), :] = (dk[...] * SCORE_SCALE).T.astype(BF16)
        dmix[drow(2, i), :] = dv[...].T.astype(BF16)
        return 0

    lax.fori_loop(0, heads, one_head, 0)
    loads[3].wait()
    loads[4].wait()

    def rows_of(s):
        return pl.ds(mult(s * rows, rows), rows)

    def part_of(s):
        return dot_tn(dmix[:, pl.ds(mult(s * rows, 128), rows)], wt[...])

    swaps = []
    for t in range(2):
        partial[t] = part_of(2 * t + 1 - core).astype(BF16)
        swaps.append(remote(partial.at[t], arrive.at[t], sw_send.at[t], sw_recv.at[t], (sib, h)))
        swaps[-1].start()

    slot = h - 2 * at["half"]

    def fin_remote(t):
        return remote(
            summed.at[t], arrive2.at[slot], fin_send.at[t], fin_recv.at[slot], (at["served"], 2 * t + core)
        )

    def fin_local_copy(t):
        return pltpu.make_async_copy(summed.at[t], arrive2.at[slot], fin_local)

    def stays(t):
        return jnp.logical_and(core == at["half"], h == 2 * t + core)

    for t in range(2):
        mine = part_of(2 * t + core)
        swaps[t].wait_recv()
        summed[t] = (mine + arrive[t].astype(F32)).astype(BF16)

        @pl.when(stays(t))
        def _():
            fin_local_copy(t).start()

        @pl.when(jnp.logical_not(stays(t)))
        def _():
            fin_remote(t).start()

    vec, gq = ref.vec, ref.gq
    first = slot * 2 * part + core * 128
    vec[0:8, :] = ref.vec_in[...]
    vec[8:16, :] = jnp.zeros((8, width), F32)
    ones = jnp.ones((8, group), BF16)
    for p, k in ((0, 10), (2, 11)):
        vec[k : k + 1, pl.ds(mult(first, 128), 256)] = dot_nt(ones, dmix[p * 256 : (p + 1) * 256, :])[:1] * grad_scale
    small = width // 8
    for p in range(3):
        res = (dot_nt(xgt[...], dmix[p * 256 : (p + 1) * 256, :]) * grad_scale).astype(BF16)
        for k in range(8):
            gq[k % 2, k // 2, p * small : (p + 1) * small, :] = res[k * small : (k + 1) * small]
    if full:
        sums.second()
        sums.third()
        sums.heads_first()

    for k in range(2):
        from_me = jnp.logical_and(
            jnp.logical_and(core == at["half"], slot == k), lax.rem(h, 2) == core
        )

        @pl.when(from_me)
        def _():
            pltpu.make_async_copy(summed.at[0], arrive2.at[k], fin_local).wait()

        @pl.when(jnp.logical_not(from_me))
        def _():
            remote(summed.at[0], arrive2.at[k], fin_send.at[0], fin_recv.at[k], (sib, h)).wait_recv()
    e = arrive2[0].astype(F32) + arrive2[1].astype(F32)
    n, r = norm_parts(ref.tok[...].astype(F32))
    ref.gtok_o[...] = ref.dmid[...] + norm_back(e, ref.gain[...], n, r)
    vec[8:9, :] = jnp.sum(e * n, axis=0, keepdims=True) * grad_scale
    vec[9:10, :] = jnp.sum(e, axis=0, keepdims=True) * grad_scale
    if full:
        sums.vectors()
        sums.heads_second()
        sums.finish()
    else:
        ref.vec_o[...] = vec[...]
        gq_copy = pltpu.make_async_copy(gq, ref.gq_o, ref.out_sem)
        gq_copy.start()
        gq_copy.wait()
    for t in range(2):
        swaps[t].wait_send()

        @pl.when(jnp.logical_not(stays(t)))
        def _():
            fin_remote(t).wait_send()


class Sums:
    def __init__(self, ref, at, grad_scale):
        self.ref, self.at = ref, at
        dp, self.h, self.core = at["dp"], at["h"], at["core"]
        self.y, self.x = dp // 4, lax.rem(dp // 2, 2)
        self.flip_x, self.flip_y = dp + 2 - 4 * self.x, dp + 4 - 8 * self.y
        self.flip_xy = self.flip_x + 4 - 8 * self.y
        self.outer = self.h * (3 - self.h) == 0

    def setup(self, k):
        ref, x, y = self.ref, self.x, self.y
        if k == 0:
            return ref.s1p, ref.r1p, ref.r2p, ref.s2p, x, y, self.flip_x, self.flip_y, lambda a, b: b * 2 + a
        return ref.s1f, ref.r1f, ref.r2f, ref.s2f, y, x, self.flip_y, self.flip_x, lambda a, b: a * 2 + b

    def one(self, k, t):
        s1, r1, _, _, a, b, to, _, at = self.setup(k)
        b = 1 - b if t == 0 else b
        return remote(
            s1.at[at(1 - a, b)], r1.at[t], self.ref.one_send.at[k, t], self.ref.one_recv.at[k, t], (to, self.h)
        )

    def two(self, k):
        _, _, r2, s2, _, _, _, to, _ = self.setup(k)
        return remote(s2.at[0], r2, self.ref.two_send.at[k], self.ref.two_recv.at[k], (to, self.h))

    def kept(self, k, t):
        s1, _, _, s2, a, b, _, _, at = self.setup(k)
        b = 1 - b if t == 0 else b
        return pltpu.make_async_copy(s1.at[at(a, b)], s2.at[t], self.ref.kept_sem.at[k, t])

    def first(self):
        for t in range(2):
            for k in range(2):
                self.one(k, t).start()
        for t in range(2):
            for k in range(2):
                self.kept(k, t).start()

    def second(self):
        for k in range(2):
            _, r1, _, s2 = self.setup(k)[:4]
            self.kept(k, 0).wait()
            self.one(k, 0).wait_recv()
            s2[0] = (s2[0].astype(F32) + r1[0].astype(F32)).astype(BF16)
            self.two(k).start()

    def pieces(self):
        for k in range(2):
            s2 = self.setup(k)[3]
            length = s2.shape[1] // PIECES
            for q in range(PIECES):
                yield k, q, k * PIECES + q, slice(q * length, (q + 1) * length)

    def chain(self, k, q, m, rows, which):
        ref, h = self.ref, self.h
        s2 = self.setup(k)[3].at[1, rows]
        za, zb, zt = ((ref.zap, ref.zbp, ref.ztp) if k == 0 else (ref.zaf, ref.zbf, ref.ztf))
        dp = self.at["dp"]
        if which == "in":
            return remote(s2, za.at[rows], ref.z_send.at[0, m], ref.z_recv.at[0, m], (dp, 1 + h // 2))
        if which == "across":
            return remote(s2, zb.at[rows], ref.z_send.at[0, m], ref.z_recv.at[1, m], (dp, 3 - h))
        return remote(zt.at[rows], za.at[rows], ref.z_send.at[1, m], ref.z_recv.at[0, m], (dp, 3 * (h // 2)))

    def third(self):
        ref = self.ref
        for k in range(2):
            _, r1, r2, s2 = self.setup(k)[:4]
            self.kept(k, 1).wait()
            self.one(k, 1).wait_recv()
            self.two(k).wait_recv()
            s2[1] = (s2[1].astype(F32) + r1[1].astype(F32) + r2[...].astype(F32)).astype(BF16)

            @pl.when(self.outer)
            def _():
                for piece in self.pieces():
                    if piece[0] == k:
                        self.chain(*piece, "in").start()

        @pl.when(jnp.logical_not(self.outer))
        def _():
            for piece in self.pieces():
                k, q, m, rows = piece
                s2, za = self.setup(k)[3], ref.zap if k == 0 else ref.zaf
                self.chain(*piece, "in").wait_recv()
                s2[1, rows] = (s2[1, rows].astype(F32) + za[rows].astype(F32)).astype(BF16)
                self.chain(*piece, "across").start()

    def finish(self):
        ref = self.ref
        half_rows = ref.s1p.shape[1]

        @pl.when(jnp.logical_not(self.outer))
        def _():
            for piece in self.pieces():
                k, q, m, rows = piece
                s2 = self.setup(k)[3]
                zb, zt = (ref.zbp, ref.ztp) if k == 0 else (ref.zbf, ref.ztf)
                self.chain(*piece, "across").wait_recv()
                zt[rows] = (s2[1, rows].astype(F32) + zb[rows].astype(F32)).astype(BF16)
                self.chain(*piece, "out").start()

        @pl.when(self.outer)
        def _():
            for piece in self.pieces():
                k, q, m, rows = piece
                za, zt = (ref.zap, ref.ztp) if k == 0 else (ref.zaf, ref.ztf)
                self.chain(*piece, "out").wait_recv()
                zt[rows] = za[rows]

        ref.gproj_o[...] = ref.ztp[...].astype(F32)
        ref.gfc_o[...] = ref.ztf[0:half_rows, :].astype(F32).T
        ref.gout_o[...] = ref.ztf[half_rows:, :].astype(F32)
        for k in range(2):
            for t in range(2):
                self.one(k, t).wait_send()
            self.two(k).wait_send()
        for piece in self.pieces():
            self.chain(*piece, "in").wait_send()

        @pl.when(jnp.logical_not(self.outer))
        def _():
            for piece in self.pieces():
                self.chain(*piece, "out").wait_send()

    def swap(self):
        ref, core = self.ref, self.core
        return remote(ref.gq.at[1 - core], ref.gq_in, ref.q_send.at[0], ref.q_recv.at[0], (self.at["sib"], self.h))

    def spread(self, k):
        ref, x, y = self.ref, self.x, self.y
        to = (self.flip_x, self.flip_y, self.flip_xy)[k]
        block = (y * 2 + 1 - x, (1 - y) * 2 + x, (1 - y) * 2 + 1 - x)[k]
        return remote(ref.u.at[block], ref.u_in.at[k], ref.q_send.at[1 + k], ref.q_recv.at[1 + k], (to, self.h))

    def two_apart(self):
        ref, h = self.ref, self.h
        return remote(ref.v, ref.v_in, ref.q_send.at[4], ref.q_recv.at[4], (self.at["dp"], h + 2 - 4 * (h // 2)))

    def next_to(self):
        ref, h = self.ref, self.h
        return remote(ref.w, ref.w_in, ref.q_send.at[5], ref.q_recv.at[5], (self.at["dp"], h + 1 - 2 * lax.rem(h, 2)))

    def heads_first(self):
        ref, core = self.ref, self.core
        self.swap().start()
        self.swap().wait_recv()
        for j in range(4):
            mine, theirs = ref.gq[core, j].astype(F32), ref.gq_in[j].astype(F32)
            a, b = jnp.where(core == 0, mine, theirs), jnp.where(core == 0, theirs, mine)
            ref.u[j, :, 0:128] = a[:, 0:128].astype(BF16)
            ref.u[j, :, 128:256] = (a[:, 128:256] + b[:, 0:128]).astype(BF16)
            ref.u[j, :, 256:384] = b[:, 128:256].astype(BF16)
        for k in range(3):
            self.spread(k).start()
        for k in range(3):
            self.spread(k).wait_recv()
        total = ref.u[self.y * 2 + self.x].astype(F32)
        for k in range(3):
            total = total + ref.u_in[k].astype(F32)
        ref.v[...] = total.astype(BF16)
        self.two_apart().start()

    def heads_second(self):
        ref = self.ref
        odd = lax.rem(self.h, 2)
        small, half = ref.gqkv_o.shape[0], ref.w.shape[1]
        self.two_apart().wait_recv()
        ref.w[...] = (ref.v[...].astype(F32) + ref.v_in[...].astype(F32)).astype(BF16)
        self.next_to().start()
        self.next_to().wait_recv()
        for p in range(3):
            here = slice(p * small, (p + 1) * small)
            ref.gqkv_o[:, pl.ds(mult((2 * p + odd) * half, 128), half)] = ref.w[here, :].astype(F32)
            ref.gqkv_o[:, pl.ds(mult((2 * p + 1 - odd) * half, 128), half)] = ref.w_in[here, :].astype(F32)
        self.swap().wait_send()
        for k in range(3):
            self.spread(k).wait_send()
        self.two_apart().wait_send()
        self.next_to().wait_send()

    def vectors(self):
        ref, at, h, core = self.ref, self.at, self.h, self.core
        me = core * 4 + h

        def team(k):
            other = lax.rem(me + k, TEAM)
            return remote(
                ref.vec, ref.vec_team.at[me], ref.vt_send.at[k - 1], ref.vt_recv.at[me],
                (at["even"] + other // 4, lax.rem(other, 4)),
            )

        def team_in(k):
            other = lax.rem(me + k, TEAM)
            return remote(ref.vec, ref.vec_team.at[other], ref.vt_send.at[k - 1], ref.vt_recv.at[other], (at["sib"], h))

        for k in range(1, TEAM):
            team(k).start()
        ref.vec_team[me] = ref.vec[...]
        for k in range(1, TEAM):
            team_in(k).wait_recv()
        total = ref.vec_team[0]
        for k in range(1, TEAM):
            total = total + ref.vec_team[k]
        ref.vec2[...] = total
        here = self.y * 2 + self.x

        def chips(k):
            return remote(
                ref.vec2, ref.vec_xy.at[here], ref.vx_send.at[k], ref.vx_recv.at[here],
                ((self.flip_x, self.flip_y, self.flip_xy)[k], h),
            )

        others = (self.y * 2 + 1 - self.x, (1 - self.y) * 2 + self.x, (1 - self.y) * 2 + 1 - self.x)
        for k in range(3):
            chips(k).start()
        ref.vec_xy[here] = total
        for k in range(3):
            remote(
                ref.vec2, ref.vec_xy.at[others[k]], ref.vx_send.at[k], ref.vx_recv.at[others[k]], (at["sib"], h)
            ).wait_recv()
        ref.vec_o[...] = (ref.vec_xy[0] + ref.vec_xy[1]) + (ref.vec_xy[2] + ref.vec_xy[3])
        for k in range(1, TEAM):
            team(k).wait_send()
        for k in range(3):
            chips(k).wait_send()


def attend_back(mix, xgt, ot, lse, start, d_ot, wt, d_middle, tokens, gain, vecs, g_proj, g_fc, grad_scale, full):
    rows, width = tokens.shape
    part, group = width // 4, 4 * rows
    small, half = width // 8, width // 2
    dma = pltpu.SemaphoreType.DMA
    ins = [
        ("mix_h", mix, ANY), ("xgt_h", xgt, ANY), ("ot_h", ot, ANY), ("lse", lse, VMEM), ("start", start, VMEM),
        ("do_h", d_ot, ANY), ("wt_h", wt, ANY), ("dmid", d_middle, VMEM), ("tok", tokens, VMEM),
        ("gain", gain[None], VMEM), ("vec_in", vecs, VMEM),
    ]
    outs = [("gtok_o", (rows, width), F32, VMEM), ("vec_o", (16, width), F32, VMEM)]
    gq_shape = (2, 4, 3 * small, 256)
    scratch = [
        ("mix", (3 * part, group), BF16), ("xgt", (width, group), BF16), ("ot", (part, group), BF16),
        ("do_t", (part, group), BF16), ("wt", (3 * 256, width), BF16), ("delta", (8, group), F32),
        ("kh", (group, HEAD_DIM), BF16), ("vh", (group, HEAD_DIM), BF16), ("qh", (group, HEAD_DIM), BF16),
        ("doh", (group, HEAD_DIM), BF16), ("dk", (group, HEAD_DIM), F32), ("dv", (group, HEAD_DIM), F32),
        ("dmix", (3 * 256, group), BF16), ("partial", (2, rows, width), BF16), ("summed", (2, rows, width), BF16),
        ("arrive", (2, rows, width), BF16), ("arrive2", (2, rows, width), BF16), ("gq", gq_shape, BF16),
        ("vec", (16, width), F32),
    ]
    sems = [
        ("in_sem", (5,)), ("sw_send", (2,)), ("sw_recv", (2,)), ("fin_send", (2,)), ("fin_recv", (2,)),
        ("fin_local", ()),
    ]
    if full:
        ins += [("s1p", g_proj, ANY), ("s1f", g_fc, ANY)]
        outs += [
            ("gproj_o", (half, width), F32, VMEM), ("gfc_o", (width, half), F32, VMEM),
            ("gout_o", (small, width), F32, VMEM), ("gqkv_o", (small, 3 * width), F32, VMEM),
        ]
        for k, length in (("p", half), ("f", half + small)):
            scratch += [("r1" + k, (2, length, width), BF16), ("s2" + k, (2, length, width), BF16)]
            scratch += [(name + k, (length, width), BF16) for name in ("r2", "za", "zb", "zt")]
        scratch += [
            ("gq_in", gq_shape[1:], BF16), ("u", (4, 3 * small, half), BF16), ("u_in", (3, 3 * small, half), BF16),
            ("v", (3 * small, half), BF16), ("v_in", (3 * small, half), BF16),
            ("w", (3 * small, half), BF16), ("w_in", (3 * small, half), BF16),
            ("vec_team", (TEAM, 16, width), F32), ("vec2", (16, width), F32), ("vec_xy", (4, 16, width), F32),
        ]
        sems += [
            ("one_send", (2, 2)), ("one_recv", (2, 2)), ("two_send", (2,)), ("two_recv", (2,)), ("kept_sem", (2, 2)),
            ("z_send", (2, 2 * PIECES)), ("z_recv", (2, 2 * PIECES)), ("q_send", (6,)), ("q_recv", (6,)),
            ("vt_send", (TEAM - 1,)), ("vt_recv", (TEAM,)), ("vx_send", (3,)), ("vx_recv", (4,)),
        ]
    else:
        outs += [("gq_o", gq_shape, BF16, ANY)]
        sems += [("out_sem", ())]
    names = tuple(item[0] for item in ins + outs + scratch + sems)
    return pl.pallas_call(
        functools.partial(back_kernel, grad_scale, full, names),
        out_shape=tuple(jax.ShapeDtypeStruct(shape, kind) for _, shape, kind, _ in outs),
        in_specs=[spec for _, _, spec in ins],
        out_specs=tuple(spec for _, _, _, spec in outs),
        scratch_shapes=[pltpu.VMEM(shape, kind) for _, shape, kind in scratch] + [dma(shape) for _, shape in sems],
        compiler_params=pltpu.CompilerParams(
            collective_id=2, has_side_effects=True, vmem_limit_bytes=60 << 20
        ),
        name="attend_back",
    )(*(array for _, array, _ in ins))


def shards(
    tokens, lengths, ln1_gain, ln1_bias, w_qkv, bias_q, bias_v, w_out, bias_out, ln2_gain, ln2_bias, w_fc, bias_fc,
    w_proj, bias_proj, cotangent,
):
    rows, width = tokens.shape
    device_count = lax.axis_size("dp") * lax.axis_size("head")
    full = lax.axis_size("dp") == 8
    grad_scale = 1.0 / math.sqrt(rows * device_count)
    att, mix, xgt, ot, lse, start, wt = attend(tokens, lengths, ln1_gain, ln1_bias, bias_q, bias_v, w_qkv)
    block_output, d_middle, d_ot, g_fc, g_proj, vecs = mlp(
        att, tokens, cotangent, grad_scale, full, bias_out, ln2_gain, ln2_bias, bias_fc, bias_proj, w_out, w_fc, w_proj
    )
    grad_tokens, vec, *rest = attend_back(
        mix, xgt, ot, lse, start, d_ot, wt, d_middle, tokens, ln1_gain, vecs, g_proj, g_fc, grad_scale, full
    )
    if full:
        proj_total, fc_total, out_total, qkv_total = rest
    else:
        proj_total, fc_total, out_total, qkv_total, vec = sums_by_xla(rest[0], g_proj, g_fc, vec)
    return (
        block_output, grad_tokens, vec[8], vec[9], qkv_total, vec[10], vec[11], out_total, vec[0], vec[1], vec[2],
        fc_total, vec[4:8].reshape(-1), proj_total, vec[3],
    )


def sums_by_xla(gq, g_proj, g_fc, vec):
    _, blocks, length, width = g_proj.shape
    small = width // 8
    whole = g_proj.transpose(1, 0, 2, 3).reshape(2 * blocks * length, width)
    fc = g_fc[:, :, :length].transpose(1, 0, 2, 3).reshape(2 * blocks * length, width).T
    out = g_fc[:, :, length:].transpose(1, 0, 2, 3).reshape(width, width)
    core, odd = lax.rem(lax.axis_index("dp"), 2), lax.rem(lax.axis_index("head"), 2)
    window = gq.reshape(2, 4, 3, small, 256).transpose(1, 0, 3, 2, 4).reshape(width, 3, 256)
    qkv = lax.dynamic_update_slice(
        jnp.zeros((width, 3, width), BF16), window, (0, 0, odd * (width // 2) + core * 128)
    ).reshape(width, 3 * width)

    def reduce_mat(g, dim):
        share = lax.psum_scatter(g, "dp", scatter_dimension=dim, tiled=True)
        return lax.psum(share, "head").astype(F32)

    return reduce_mat(whole, 0), reduce_mat(fc, 1), reduce_mat(out, 0), reduce_mat(qkv, 0), lax.psum(vec, ("dp", "head"))


def solution(mesh):
    rows = P(("dp", "head"), None)
    return jax.shard_map(
        shards,
        mesh=mesh,
        in_specs=(rows, P("dp", None)) + (P(),) * 13 + (rows,),
        out_specs=(
            rows, rows, P(), P(), P("dp", None), P(), P(), P("dp", None), P(), P(), P(), P(None, "dp"), P(),
            P("dp", None), P(),
        ),
        check_vma=False,
    )
```

```python
import functools
import math
import types

import jax
import jax.numpy as jnp
from jax import lax
from jax.experimental import pallas as pl
from jax.experimental.pallas import tpu as pltpu
from jax.sharding import PartitionSpec as P

HEAD_DIM = 64
EPSILON = 1e-05
DEPTH_SCALE = 1.0 / math.sqrt(12.0)
LOG2E = 1.0 / math.log(2.0)
SCORE_SCALE = HEAD_DIM ** (-0.5)
GELU_K = math.sqrt(2.0 / math.pi)
GELU_A = 0.044715
TEAM = 8
QB = 256
PIECES = 3

F32 = jnp.float32
BF16 = jnp.bfloat16
MESH = pl.DeviceIdType.MESH
ANY = pl.BlockSpec(memory_space=pl.ANY)
VMEM = pl.BlockSpec(memory_space=pltpu.VMEM)
SMEM = pl.BlockSpec(memory_space=pltpu.SMEM)


def dot(a, b):
    return jnp.dot(a, b, preferred_element_type=F32)


def dot_nt(a, b):
    return lax.dot_general(a, b, (((1,), (1,)), ((), ())), preferred_element_type=F32)


def dot_tn(a, b):
    return lax.dot_general(a, b, (((0,), (0,)), ((), ())), preferred_element_type=F32)


def mult(x, m):
    return pl.multiple_of(x, m)


def place():
    dp, h = lax.axis_index("dp"), lax.axis_index("head")
    core = lax.rem(dp, 2)
    half = h // 2
    return dict(
        dp=dp,
        h=h,
        core=core,
        sib=dp + 1 - 2 * core,
        even=dp - core,
        half=half,
        served=dp - core + half,
        block=(h - 2 * half) * 2 + core,
    )


def greet(at, chips=False):
    barrier = pltpu.get_barrier_semaphore()
    me = at["core"] * 4 + at["h"]
    others = []
    for k in range(1, TEAM):
        other = lax.rem(me + k, TEAM)
        others.append((at["even"] + other // 4, lax.rem(other, 4)))
    if chips:
        for k in range(1, 4):
            others.append((lax.rem(at["dp"] + 2 * k, 8), at["h"]))
    for other in others:
        pl.semaphore_signal(barrier, inc=1, device_id=other, device_id_type=MESH)
    pl.semaphore_wait(barrier, len(others))


def remote(src, dst, send, recv, device):
    return pltpu.make_async_remote_copy(
        src_ref=src, dst_ref=dst, send_sem=send, recv_sem=recv, device_id=device, device_id_type=MESH
    )


def row(vec):
    return vec[...].reshape(1, vec.shape[0])


def norm_parts(v):
    center = jnp.mean(v, axis=-1, keepdims=True)
    cent = v - center
    r = lax.rsqrt(jnp.mean(cent * cent, axis=-1, keepdims=True) + EPSILON)
    return cent * r, r


def norm_back(e, gain, n, r):
    ea = e * gain
    return r * (ea - jnp.mean(ea, axis=-1, keepdims=True) - n * jnp.mean(ea * n, axis=-1, keepdims=True))


def attend_kernel(
    tok, lens, gain, bias, bias_q, bias_v, w_qkv,
    att_o, mix_o, xgt_o, ot_o, lse_o, start_o, wt_o,
    xn, xg, xgt, wwin, wt, brow, bcol, start_mine, start_sib, mix, kh, scores, ot,
    w_sem, st_sem, ag_send, ag_recv, fw_send, at_send, at_recv, at_local, out_sem,
):
    at = place()
    dp, h, core, sib = at["dp"], at["h"], at["core"], at["sib"]
    rows, width = tok.shape
    group = 4 * rows
    part = width // 4
    collects = core == at["half"]
    first = (h - 2 * at["half"]) * 2 * part + core * 128
    shift = mult(64 * core, 64)
    for p in range(3):
        pltpu.make_async_copy(
            w_qkv.at[:, pl.ds(mult(p * width + first, 128), 256)], wwin.at[p], w_sem.at[p]
        ).start()
    greet(at)

    places = lax.broadcasted_iota(jnp.int32, (8, group), 1)
    begin = jnp.zeros((8, group), jnp.int32)
    edge = lens[0, 0]
    for k in range(1, lens.shape[1] + 1):
        begin = jnp.where(places >= edge, edge, begin)
        if k < lens.shape[1]:
            edge = edge + lens[0, k]
    start_mine[...] = begin.astype(F32)
    st_copy = remote(start_mine, start_sib, st_sem.at[0], st_sem.at[1], (sib, h))
    st_copy.start()

    n, _ = norm_parts(tok[...].astype(F32))
    xn[...] = (n * row(gain) + row(bias)).astype(BF16)

    def shard(ref, s):
        return ref.at[pl.ds(mult(s * rows, rows), rows), :]

    inner, outer = 1 + core, 3 * core
    at_inner, at_outer = h == inner, h == outer

    def to_inner():
        return remote(xn, shard(xg, h), ag_send.at[0], ag_recv.at[h], (dp, inner))

    def to_outer(k, s):
        src = xn if k == 0 else shard(xg, s)
        return remote(src, shard(xg, s), ag_send.at[k], ag_recv.at[s], (dp, outer))

    @pl.when(at_inner)
    def _():
        to_outer(0, h).start()

    @pl.when(jnp.logical_not(at_inner))
    def _():
        to_inner().start()

    own_fw = remote(xn, shard(xg, h), fw_send.at[0], ag_recv.at[h], (sib, h))

    @pl.when(collects)
    def _():
        own_fw.start()
        xg[pl.ds(mult(h * rows, rows), rows), :] = xn[...]

    for p in range(3):
        pltpu.make_async_copy(wwin.at[p], wwin.at[p], w_sem.at[p]).wait()
        wt[p * 256 : (p + 1) * 256, :] = wwin[p].T
    wt_copy = pltpu.make_async_copy(wt, wt_o, out_sem.at[0])
    wt_copy.start()
    for p, vec in ((0, bias_q), (2, bias_v)):
        brow[...] = jnp.broadcast_to(row(vec), (8, width))
        bcol[p] = jnp.broadcast_to(brow[0:1, pl.ds(mult(first, 128), 256)], (128, 256)).T
    bcol[1] = jnp.zeros((256, 128), F32)

    low = 1 - at["half"]
    order = (h, low * (1 - h) + (1 - low) * (5 - h), 1 + low, 3 * low)

    def fw_copy(d, s):
        return remote(shard(xg, s), shard(xg, s), fw_send.at[d], ag_recv.at[s], (sib, h))

    for d in range(4):
        s = order[d]
        if d == 0:
            @pl.when(jnp.logical_not(collects))
            def _():
                fw_copy(d, s).wait_recv()
        else:
            fw_copy(d, s).wait_recv()

            @pl.when(collects)
            def _():
                fw_copy(d, s).start()

            if d > 1:
                @pl.when(at_inner)
                def _():
                    to_outer(d - 1, s).start()

        here = xg[pl.ds(mult(s * rows, rows), rows), :]
        xgt[:, pl.ds(mult(s * rows, 128), rows)] = here.T
        for p in range(3):
            res = dot_nt(wt[pl.ds(mult(p * 256 + shift, 64), part), :], here) + bcol[p, pl.ds(shift, part), :][:, :1]
            mix[p * part : (p + 1) * part, pl.ds(mult(s * rows, 128), rows)] = res.astype(BF16)
    mix_copy = pltpu.make_async_copy(mix, mix_o, out_sem.at[2])
    mix_copy.start()
    xgt_copy = pltpu.make_async_copy(xgt, xgt_o, out_sem.at[1])
    xgt_copy.start()
    st_copy.wait_recv()
    start_o[...] = jnp.where(collects, start_mine[...], start_sib[...]).astype(jnp.int32)

    heads = part // HEAD_DIM
    scale = SCORE_SCALE * LOG2E

    def at_copy(i, s):
        src = ot.at[pl.ds(mult(i * HEAD_DIM, HEAD_DIM), HEAD_DIM), pl.ds(s * rows, rows)]
        dst = att_o.at[pl.ds(mult(at["block"] * part + i * HEAD_DIM, HEAD_DIM), HEAD_DIM), :]
        return src, dst

    def at_remote(i, s):
        src, dst = at_copy(i, s)
        return remote(src, dst, at_send.at[i * 4 + s], at_recv.at[at["block"] * heads + i], (at["served"], s))

    def stays(s):
        return jnp.logical_and(collects, h == s)

    def one_head(i, _):
        qrow, krow, vrow = (mult(p * part + i * HEAD_DIM, HEAD_DIM) for p in range(3))
        kh[...] = mix[pl.ds(krow, HEAD_DIM), :].T
        for j in range(group // QB):
            cols = slice(j * QB, (j + 1) * QB)
            q_t = mix[pl.ds(qrow, HEAD_DIM), cols]
            begins = start_o[0:1, cols]
            top = jnp.full((1, QB), -jnp.inf, F32)
            for k in range(j + 1):
                s_t = dot(kh[k * QB : (k + 1) * QB, :], q_t)
                key = lax.broadcasted_iota(jnp.int32, (QB, QB), 0)
                keep = key >= begins - k * QB
                if k == j:
                    keep = jnp.logical_and(keep, key <= lax.broadcasted_iota(jnp.int32, (QB, QB), 1))
                s_t = jnp.where(keep, s_t, -1e30)
                scores[k * QB : (k + 1) * QB, :] = s_t
                top = jnp.maximum(top, jnp.max(s_t, axis=0, keepdims=True))
            top = top * scale
            total = jnp.zeros((1, QB), F32)
            acc = jnp.zeros((HEAD_DIM, QB), F32)
            for k in range(j + 1):
                p_t = jnp.exp2(scores[k * QB : (k + 1) * QB, :] * scale - top)
                total = total + jnp.sum(p_t, axis=0, keepdims=True)
                acc = acc + dot(mix[pl.ds(vrow, HEAD_DIM), k * QB : (k + 1) * QB], p_t.astype(BF16))
            ot[pl.ds(qrow, HEAD_DIM), cols] = (acc / total).astype(BF16)
            lse_o[pl.ds(mult(i * 8, 8), 8), cols] = jnp.broadcast_to(top + jnp.log2(total), (8, QB))
        for s in range(4):
            @pl.when(stays(s))
            def _():
                pltpu.make_async_copy(*at_copy(i, s), at_local.at[i]).start()

            @pl.when(jnp.logical_not(stays(s)))
            def _():
                at_remote(i, s).start()
        return 0

    lax.fori_loop(0, heads, one_head, 0)
    ot_copy = pltpu.make_async_copy(ot, ot_o, out_sem.at[3])
    ot_copy.start()

    @pl.when(at_inner)
    def _():
        to_outer(0, h).wait_send()
        for d in range(2, 4):
            to_outer(d - 1, order[d]).wait_send()

    @pl.when(jnp.logical_not(at_inner))
    def _():
        to_inner().wait_send()

    @pl.when(collects)
    def _():
        own_fw.wait_send()
        for d in range(1, 4):
            fw_copy(d, order[d]).wait_send()

    st_copy.wait_send()
    wt_copy.wait()
    mix_copy.wait()
    xgt_copy.wait()
    ot_copy.wait()
    for i in range(heads):
        for s in range(4):
            @pl.when(stays(s))
            def _():
                pltpu.make_async_copy(*at_copy(i, s), at_local.at[i]).wait()

            @pl.when(jnp.logical_not(stays(s)))
            def _():
                at_remote(i, s).wait_send()
        for b in range(4):
            dst = att_o.at[pl.ds(b * part + i * HEAD_DIM, HEAD_DIM), :]
            src = ot.at[pl.ds(i * HEAD_DIM, HEAD_DIM), pl.ds(0, rows)]

            @pl.when(jnp.logical_not(jnp.logical_and(collects, at["block"] == b)))
            def _():
                remote(src, dst, at_send.at[i * 4], at_recv.at[b * heads + i], (sib, h)).wait_recv()


def attend(tokens, lengths, gain, bias, bias_q, bias_v, w_qkv):
    rows, width = tokens.shape
    group, part = 4 * rows, width // 4
    heads = part // HEAD_DIM
    dma = pltpu.SemaphoreType.DMA
    return pl.pallas_call(
        attend_kernel,
        out_shape=(
            jax.ShapeDtypeStruct((width, rows), BF16),
            jax.ShapeDtypeStruct((3 * part, group), BF16),
            jax.ShapeDtypeStruct((width, group), BF16),
            jax.ShapeDtypeStruct((part, group), BF16),
            jax.ShapeDtypeStruct((8 * heads, group), F32),
            jax.ShapeDtypeStruct((8, group), jnp.int32),
            jax.ShapeDtypeStruct((3 * 256, width), BF16),
        ),
        in_specs=[VMEM, SMEM, VMEM, VMEM, VMEM, VMEM, ANY],
        out_specs=(ANY, ANY, ANY, ANY, VMEM, VMEM, ANY),
        scratch_shapes=[
            pltpu.VMEM((rows, width), BF16),
            pltpu.VMEM((group, width), BF16),
            pltpu.VMEM((width, group), BF16),
            pltpu.VMEM((3, width, 256), BF16),
            pltpu.VMEM((3 * 256, width), BF16),
            pltpu.VMEM((8, width), F32),
            pltpu.VMEM((3, 256, 128), F32),
            pltpu.VMEM((8, group), F32),
            pltpu.VMEM((8, group), F32),
            pltpu.VMEM((3 * part, group), BF16),
            pltpu.VMEM((group, HEAD_DIM), BF16),
            pltpu.VMEM((group, QB), F32),
            pltpu.VMEM((part, group), BF16),
            dma((3,)), dma((2,)), dma((3,)), dma((4,)), dma((4,)),
            dma((4 * heads,)), dma((4 * heads,)), dma((heads,)), dma((4,)),
        ],
        compiler_params=pltpu.CompilerParams(
            collective_id=0, has_side_effects=True, vmem_limit_bytes=60 << 20
        ),
        name="attend",
    )(tokens, lengths, gain, bias, bias_q, bias_v, w_qkv)


def mlp_kernel(
    grad_scale, paired,
    b_out, gain, bias, b_fc, b_proj, att_h, tok_h, cot_h, w_out_h, w_fc_h, w_proj_h,
    out_o, dmid_o, dot_o, gfc_o, gproj_o, vec_o,
    att, tok, cot,
    w_out, w_fc, w_proj, brow, dfc, dat, gfc, gproj, gfc_in, gproj_in, r1, s2, r2, s3,
    w_sem, send, recv, local, pair_send, pair_recv, one_send, one_recv, two_send, two_recv, in_sem, out_sem,
):
    at = place()
    h, core = at["h"], at["core"]
    rows, width = tok_h.shape
    part = width // 4
    chunks = w_fc_h.shape[1] // width
    wo_copy = pltpu.make_async_copy(w_out_h, w_out, w_sem.at[0])
    wo_copy.start()

    def wf_copy(j):
        return pltpu.make_async_copy(w_fc_h.at[:, pl.ds(mult(j * width, 128), width)], w_fc.at[j], w_sem.at[1 + 2 * j])

    def wp_copy(j):
        return pltpu.make_async_copy(w_proj_h.at[pl.ds(mult(j * width, 128), width), :], w_proj.at[j], w_sem.at[2 + 2 * j])

    loads = [
        pltpu.make_async_copy(src, dst, in_sem.at[k])
        for k, (src, dst) in enumerate(((cot_h, cot), (tok_h, tok), (att_h, att)))
    ]
    for load in loads:
        load.start()
    greet(at, paired)

    half_rows = width // 2
    small = width // 8
    y, x = at["dp"] // 4, lax.rem(at["dp"] // 2, 2)

    def pair_copy(ref, into, k, j):
        return remote(ref.at[1 - core, j], into.at[j], pair_send.at[k, j], pair_recv.at[k, j], (at["sib"], h))

    def pair_add(ref, into, k, j):
        pair_copy(ref, into, k, j).wait_recv()
        ref[core, j] = (ref[core, j].astype(F32) + into[j].astype(F32)).astype(BF16)

    if paired:
        order = [(1 - y) * 2 + 1 - x, y * 2 + 1 - x, (1 - y) * 2 + x, y * 2 + x]
    else:
        order = list(range(chunks))
    quarter = half_rows // 2
    flips = (at["dp"] + 2 - 4 * x, h), (at["dp"] + 4 - 8 * y, h)

    def halves(k):
        return slice(k * quarter, (k + 1) * quarter)

    def one(k, t):
        j = order[0] if t == 0 else order[1 + k]
        return remote(gproj.at[core, j, halves(k)], r1.at[k, t], one_send.at[k, t], one_recv.at[k, t], flips[k])

    def two(k):
        return remote(s2.at[k], r2.at[k], two_send.at[k], two_recv.at[k], flips[1 - k])

    def first_sum(k):
        one(k, 0).wait_recv()
        s2[k] = (gproj[core, order[2 - k], halves(k)].astype(F32) + r1[k, 0].astype(F32)).astype(BF16)
        two(k).start()

    def last_sum():
        for k in range(2):
            one(k, 1).wait_recv()
            two(k).wait_recv()
            s3[halves(k)] = (
                gproj[core, order[3], halves(k)].astype(F32) + r1[k, 1].astype(F32) + r2[k].astype(F32)
            ).astype(BF16)

    def proj_sums(step):
        if not paired:
            return
        pair_add(gproj, gproj_in, 0, order[step])
        if step == 0:
            one(0, 0).start()
            one(1, 0).start()
        elif step == 1:
            one(0, 1).start()
        elif step == 2:
            one(1, 1).start()
            first_sum(0)
            first_sum(1)

    loads[0].wait()
    dy = cot[...].astype(F32)
    d_proj = (DEPTH_SCALE * dy).astype(BF16)
    for j in order:
        wf_copy(j).start()
        wp_copy(j).start()
    wo_copy.wait()
    loads[1].wait()
    loads[2].wait()
    middle = tok[...].astype(F32) + DEPTH_SCALE * (dot_tn(att[...], w_out[...]) + row(b_out))
    n, r = norm_parts(middle)
    second = (n * row(gain) + row(bias)).astype(BF16)
    result = middle + DEPTH_SCALE * row(b_proj)
    brow[...] = jnp.broadcast_to(row(b_fc), brow.shape)
    d_second = jnp.zeros((rows, width), F32)
    vec_o[3:4, :] = jnp.sum(dy, axis=0, keepdims=True) * (DEPTH_SCALE * grad_scale)
    for step, j in enumerate(order):
        wf_copy(j).wait()
        u = dot(second, w_fc[j]) + brow[0:1, pl.ds(mult(j * width, 128), width)]
        u2 = u * u
        th = jnp.tanh(GELU_K * u * (1.0 + GELU_A * u2))
        half = 0.5 * (1.0 + th)
        slope = half + 0.5 * u * (1.0 - th * th) * (GELU_K * (1.0 + 3.0 * GELU_A * u2))
        hidden = (u * half).astype(BF16)
        wp_copy(j).wait()
        result = result + DEPTH_SCALE * dot(hidden, w_proj[j])
        d_pre = dot_nt(d_proj, w_proj[j]) * slope
        res = (dot_tn(hidden, d_proj) * grad_scale).astype(BF16)
        for k in range(2):
            gproj[k, j] = res[k * half_rows : (k + 1) * half_rows]
        if paired:
            pair_copy(gproj, gproj_in, 0, j).start()
        if step > 0:
            proj_sums(step - 1)
        vec_o[pl.ds(4 + j, 1), :] = jnp.sum(d_pre, axis=0, keepdims=True) * grad_scale
        d_fc = d_pre.astype(BF16)
        dfc[j] = d_fc
        d_second = d_second + dot_nt(d_fc, w_fc[j])
    out_o[...] = result
    vec_o[1:2, :] = jnp.sum(d_second * n, axis=0, keepdims=True) * grad_scale
    vec_o[2:3, :] = jnp.sum(d_second, axis=0, keepdims=True) * grad_scale
    d_middle = dy + norm_back(d_second, row(gain), n, r)
    dmid_o[...] = d_middle
    vec_o[0:1, :] = jnp.sum(d_middle, axis=0, keepdims=True) * (DEPTH_SCALE * grad_scale)
    d_out = (DEPTH_SCALE * d_middle).astype(BF16)
    dat[...] = dot_nt(w_out[...], d_out).astype(BF16)

    def target(b):
        return at["even"] + b % 2, 2 * core + b // 2

    def stays(b):
        return jnp.logical_and(core == b % 2, h == 2 * core + b // 2)

    dst = dot_o.at[:, pl.ds(mult(h * rows, 128), rows)]

    def da_local(b):
        return pltpu.make_async_copy(dat.at[pl.ds(b * part, part), :], dst, local)

    def da_remote(b):
        return remote(dat.at[pl.ds(b * part, part), :], dst, send.at[b], recv.at[h], target(b))

    for b in range(4):
        @pl.when(stays(b))
        def _():
            da_local(b).start()

        @pl.when(jnp.logical_not(stays(b)))
        def _():
            da_remote(b).start()

    g_out = (dot(att[...], d_out) * grad_scale).astype(BF16)
    for j in range(chunks):
        for k in range(2):
            gfc[k, j, half_rows:, :] = g_out[(2 * j + k) * small : (2 * j + k + 1) * small]
    proj_sums(chunks - 1)
    for j in order:
        res = (dot_tn(dfc[j], second) * grad_scale).astype(BF16)
        for k in range(2):
            gfc[k, j, :half_rows, :] = res[k * half_rows : (k + 1) * half_rows]
        if paired:
            pair_copy(gfc, gfc_in, 1, j).start()
    if paired:
        last_sum()
        for j in order:
            pair_add(gfc, gfc_in, 1, j)
        outs = [
            pltpu.make_async_copy(s3, gproj_o, out_sem.at[0]),
            pltpu.make_async_copy(gfc.at[core], gfc_o, out_sem.at[1]),
        ]
    else:
        outs = [
            pltpu.make_async_copy(gproj, gproj_o, out_sem.at[0]),
            pltpu.make_async_copy(gfc, gfc_o, out_sem.at[1]),
        ]
    for copy in outs:
        copy.start()

    served_here = core == at["half"]
    for b in range(4):
        @pl.when(stays(b))
        def _():
            da_local(b).wait()

        @pl.when(jnp.logical_not(stays(b)))
        def _():
            da_remote(b).wait_send()
    for s in range(4):
        @pl.when(jnp.logical_not(jnp.logical_and(served_here, h == s)))
        def _():
            remote(
                dat.at[pl.ds(0, part), :], dot_o.at[:, pl.ds(s * rows, rows)], send.at[0], recv.at[s], (at["sib"], h)
            ).wait_recv()
    if paired:
        for j in range(chunks):
            for k, (ref, into) in enumerate(((gproj, gproj_in), (gfc, gfc_in))):
                pair_copy(ref, into, k, j).wait_send()

        for k in range(2):
            for t in range(2):
                one(k, t).wait_send()
            two(k).wait_send()
    for copy in outs:
        copy.wait()


def mlp(att, tokens, cotangent, grad_scale, paired, b_out, gain, bias, b_fc, b_proj, w_out, w_fc, w_proj):
    rows, width = tokens.shape
    part, group = width // 4, 4 * rows
    ff = w_fc.shape[1]
    chunks = ff // width
    lead = () if paired else (2,)
    dma = pltpu.SemaphoreType.DMA
    return pl.pallas_call(
        functools.partial(mlp_kernel, grad_scale, paired),
        out_shape=(
            jax.ShapeDtypeStruct((rows, width), F32),
            jax.ShapeDtypeStruct((rows, width), F32),
            jax.ShapeDtypeStruct((part, group), BF16),
            jax.ShapeDtypeStruct(lead + (chunks, width // 2 + width // 8, width), BF16),
            jax.ShapeDtypeStruct((() if paired else (2, chunks)) + (width // 2, width), BF16),
            jax.ShapeDtypeStruct((8, width), F32),
        ),
        in_specs=[VMEM] * 5 + [ANY] * 6,
        out_specs=(VMEM, VMEM, ANY, ANY, ANY, VMEM),
        scratch_shapes=[
            pltpu.VMEM((width, rows), BF16),
            pltpu.VMEM((rows, width), BF16),
            pltpu.VMEM((rows, width), BF16),
            pltpu.VMEM((width, width), BF16),
            pltpu.VMEM((chunks, width, width), BF16),
            pltpu.VMEM((chunks, width, width), BF16),
            pltpu.VMEM((8, ff), F32),
            pltpu.VMEM((chunks, rows, width), BF16),
            pltpu.VMEM((width, rows), BF16),
            pltpu.VMEM((2, chunks, width // 2 + width // 8, width), BF16),
            pltpu.VMEM((2, chunks, width // 2, width), BF16),
            pltpu.VMEM((chunks, width // 2 + width // 8, width), BF16),
            pltpu.VMEM((chunks, width // 2, width), BF16),
            pltpu.VMEM((2, 2, width // 4, width), BF16),
            pltpu.VMEM((2, width // 4, width), BF16),
            pltpu.VMEM((2, width // 4, width), BF16),
            pltpu.VMEM((width // 2, width), BF16),
            dma((1 + 2 * chunks,)), dma((4,)), dma((4,)), dma, dma((2, chunks)), dma((2, chunks)),
            dma((2, 2)), dma((2, 2)), dma((2,)), dma((2,)), dma((3,)), dma((2,)),
        ],
        compiler_params=pltpu.CompilerParams(
            collective_id=1, has_side_effects=True, vmem_limit_bytes=60 << 20
        ),
        name="mlp",
    )(
        b_out, gain, bias, b_fc, b_proj, att, tokens, cotangent, w_out, w_fc, w_proj,
    )


def back_kernel(grad_scale, full, names, *refs):
    ref = types.SimpleNamespace(**dict(zip(names, refs, strict=True)))
    mix, do_t, ot, xgt, wt, dmix = ref.mix, ref.do_t, ref.ot, ref.xgt, ref.wt, ref.dmix
    lse, start, delta, kh, vh, qh, doh, dk, dv = (
        ref.lse, ref.start, ref.delta, ref.kh, ref.vh, ref.qh, ref.doh, ref.dk, ref.dv
    )
    partial, summed, arrive, arrive2 = ref.partial, ref.summed, ref.arrive, ref.arrive2
    sw_send, sw_recv, fin_send, fin_recv, fin_local = (
        ref.sw_send, ref.sw_recv, ref.fin_send, ref.fin_recv, ref.fin_local
    )
    at = place()
    h, core, sib = at["h"], at["core"], at["sib"]
    rows, width = ref.tok.shape
    part, group = width // 4, 4 * rows
    heads = part // HEAD_DIM
    loads = [
        pltpu.make_async_copy(src, dst, ref.in_sem.at[k])
        for k, (src, dst) in enumerate(
            (
                (ref.do_h, do_t), (ref.ot_h, ot), (ref.mix_h, mix), (ref.lse_h, lse), (ref.start_h, start),
                (ref.wt_h, wt), (ref.xgt_h, xgt), (ref.dmid_h, ref.dmid), (ref.tok_h, ref.tok),
            )
        )
    ]
    for load in loads:
        load.start()
    greet(at, full)
    if full:
        sums = Sums(ref, at, grad_scale)
        sums.first()
    dmix[...] = jnp.zeros_like(dmix)
    for load in loads[:5]:
        load.wait()
    scale = SCORE_SCALE * LOG2E

    def drow(p, i):
        return pl.ds(mult(p * 256 + (core + i) * HEAD_DIM, HEAD_DIM), HEAD_DIM)

    def one_head(i, _):
        qrow, krow, vrow = (mult(p * part + i * HEAD_DIM, HEAD_DIM) for p in range(3))
        d_head = do_t[pl.ds(qrow, HEAD_DIM), :]
        delta[...] = jnp.broadcast_to(
            jnp.sum(d_head.astype(F32) * ot[pl.ds(qrow, HEAD_DIM), :].astype(F32), axis=0, keepdims=True), (8, group)
        )
        qh[...] = mix[pl.ds(qrow, HEAD_DIM), :].T
        kh[...] = mix[pl.ds(krow, HEAD_DIM), :].T
        vh[...] = mix[pl.ds(vrow, HEAD_DIM), :].T
        doh[...] = d_head.T
        for j in range(group // QB):
            cols = slice(j * QB, (j + 1) * QB)
            q_t = mix[pl.ds(qrow, HEAD_DIM), cols]
            do_j = do_t[pl.ds(qrow, HEAD_DIM), cols]
            begins = start[0:1, cols]
            lse_j = lse[pl.ds(mult(i * 8, 8), 8), cols][0:1]
            delta_j = delta[0:1, cols]
            acc = jnp.zeros((HEAD_DIM, QB), F32)
            for k in range(j + 1):
                keys = slice(k * QB, (k + 1) * QB)
                s_t = dot(kh[keys, :], q_t)
                key = lax.broadcasted_iota(jnp.int32, (QB, QB), 0)
                keep = key >= begins - k * QB
                if k == j:
                    keep = jnp.logical_and(keep, key <= lax.broadcasted_iota(jnp.int32, (QB, QB), 1))
                p_t = jnp.where(keep, jnp.exp2(s_t * scale - lse_j), 0.0)
                dp_t = dot(vh[keys, :], do_j)
                ds_t = (p_t * (dp_t - delta_j)).astype(BF16)
                dv_add = dot(p_t.astype(BF16), doh[cols, :])
                dk_add = dot(ds_t, qh[cols, :])
                if k == j:
                    dv[keys, :] = dv_add
                    dk[keys, :] = dk_add
                else:
                    dv[keys, :] += dv_add
                    dk[keys, :] += dk_add
                acc = acc + dot(mix[pl.ds(krow, HEAD_DIM), keys], ds_t)
            dmix[drow(0, i), cols] = (acc * SCORE_SCALE).astype(BF16)
            if full and j in (2, 5):
                @pl.when(i == 1)
                def _():
                    sums.add_inner(0, (0,) if j == 2 else (1,))
            if full and j == 3:
                @pl.when(i == 2)
                def _():
                    sums.add_inner(0, (2,))
                    sums.add_across(0, (0,))
        dmix[drow(1, i), :] = (dk[...] * SCORE_SCALE).T.astype(BF16)
        dmix[drow(2, i), :] = dv[...].T.astype(BF16)
        return 0

    lax.fori_loop(0, heads, one_head, 0)
    for load in loads[5:]:
        load.wait()

    def rows_of(s):
        return pl.ds(mult(s * rows, rows), rows)

    def part_of(s):
        return dot_tn(dmix[:, pl.ds(mult(s * rows, 128), rows)], wt[...])

    swaps = []
    for t in range(2):
        partial[t] = part_of(2 * t + 1 - core).astype(BF16)
        swaps.append(remote(partial.at[t], arrive.at[t], sw_send.at[t], sw_recv.at[t], (sib, h)))
        swaps[-1].start()

    slot = h - 2 * at["half"]

    def fin_remote(t):
        return remote(
            summed.at[t], arrive2.at[slot], fin_send.at[t], fin_recv.at[slot], (at["served"], 2 * t + core)
        )

    def fin_local_copy(t):
        return pltpu.make_async_copy(summed.at[t], arrive2.at[slot], fin_local)

    def stays(t):
        return jnp.logical_and(core == at["half"], h == 2 * t + core)

    if full:
        sums.add_first(1)
        sums.add_first(2)
        sums.add_across(0, (1,))
    for t in range(2):
        mine = part_of(2 * t + core)
        swaps[t].wait_recv()
        summed[t] = (mine + arrive[t].astype(F32)).astype(BF16)

        @pl.when(stays(t))
        def _():
            fin_local_copy(t).start()

        @pl.when(jnp.logical_not(stays(t)))
        def _():
            fin_remote(t).start()

    vec, gq = ref.vec, ref.gq
    if full:
        sums.add_across(0, (2,))
    first = slot * 2 * part + core * 128
    vec[0:8, :] = ref.vec_in[...]
    vec[8:16, :] = jnp.zeros((8, width), F32)
    small = width // 8
    gain_sum = jnp.zeros((1, width), F32)
    bias_sum = jnp.zeros((1, width), F32)
    for p in range(3):
        d_cols = dmix[p * 256 : (p + 1) * 256, :]
        tok_sum = jnp.sum(d_cols.astype(F32), axis=1, keepdims=True) * grad_scale
        w_cols = wt[p * 256 : (p + 1) * 256, :].astype(F32)
        res = dot_nt(d_cols, xgt[...]) * grad_scale
        gain_sum = gain_sum + jnp.sum(w_cols * res, axis=0, keepdims=True)
        bias_sum = bias_sum + jnp.sum(w_cols * tok_sum, axis=0, keepdims=True)
        if p != 1:
            vec[10 + p // 2 : 11 + p // 2, pl.ds(mult(first, 128), 256)] = jnp.broadcast_to(tok_sum, (256, 128)).T[:1]
        res = res.astype(BF16).T
        for k in range(8):
            gq[k % 2, k // 2, p * small : (p + 1) * small, :] = res[k * small : (k + 1) * small]
    vec[8:9, :] = (gain_sum - row(ref.bias) * bias_sum) / row(ref.gain)
    vec[9:10, :] = bias_sum
    if full:
        sums.vectors_first()
        sums.heads_first()
        sums.add_second(1)
        sums.add_second(2)
        sums.heads_second()
        sums.vectors_second()
        sums.add_inner(1)
        sums.add_inner(2)

    for k in range(2):
        from_me = jnp.logical_and(
            jnp.logical_and(core == at["half"], slot == k), lax.rem(h, 2) == core
        )

        @pl.when(from_me)
        def _():
            pltpu.make_async_copy(summed.at[0], arrive2.at[k], fin_local).wait()

        @pl.when(jnp.logical_not(from_me))
        def _():
            remote(summed.at[0], arrive2.at[k], fin_send.at[0], fin_recv.at[k], (sib, h)).wait_recv()
    e = arrive2[0].astype(F32) + arrive2[1].astype(F32)
    n, r = norm_parts(ref.tok[...].astype(F32))
    ref.gtok_o[...] = ref.dmid[...] + norm_back(e, row(ref.gain), n, r)
    if full:
        sums.add_across(1)
        sums.heads_third()
        sums.add_across(2)
        sums.vectors_third()
        sums.finish()
    else:
        ref.vec_o[...] = vec[...]
        gq_copy = pltpu.make_async_copy(gq, ref.gq_o, ref.out_sem)
        gq_copy.start()
        gq_copy.wait()
    for t in range(2):
        swaps[t].wait_send()

        @pl.when(jnp.logical_not(stays(t)))
        def _():
            fin_remote(t).wait_send()


class Sums:
    def __init__(self, ref, at, grad_scale):
        self.ref, self.at = ref, at
        dp, self.h, self.core = at["dp"], at["h"], at["core"]
        self.y, self.x = dp // 4, lax.rem(dp // 2, 2)
        self.flip_x, self.flip_y = dp + 2 - 4 * self.x, dp + 4 - 8 * self.y
        self.flip_xy = self.flip_x + 4 - 8 * self.y
        self.outer = self.h * (3 - self.h) == 0

    def rows_of(self, k):
        length = self.ref.s2f.shape[1] // 2
        return slice(0, self.ref.s2p.shape[0]) if k == 0 else slice((k - 1) * length, k * length)

    def part(self, name, k, *lead):
        return getattr(self.ref, name).at[*lead, self.rows_of(k)]

    def block(self, k, t, across):
        x, y = self.x, self.y
        first, then = (y, x) if k == 2 else (x, y)
        first = 1 - first if across else first
        then = 1 - then if t == 0 else then
        return first * 2 + then if k == 2 else then * 2 + first

    def one(self, k, t):
        return remote(
            self.part("s1f", k, self.block(k, t, True)), self.part("r1f", k, t),
            self.ref.one_send.at[k, t], self.ref.one_recv.at[k, t], (self.flip_y if k == 2 else self.flip_x, self.h),
        )

    def two(self, k):
        return remote(
            self.part("s2f", k, 0), self.part("r2f", k),
            self.ref.two_send.at[k], self.ref.two_recv.at[k], (self.flip_x if k == 2 else self.flip_y, self.h),
        )

    def kept(self, k, t):
        return pltpu.make_async_copy(
            self.part("s1f", k, self.block(k, t, False)), self.part("s2f", k, t), self.ref.kept_sem.at[k, t]
        )

    def first(self):
        for t in range(2):
            for k in range(1, 3):
                self.one(k, t).start()
        came = pltpu.make_async_copy(self.ref.s3p, self.ref.s2p, self.ref.kept_sem.at[0, 0])
        came.start()
        for t in range(2):
            for k in range(1, 3):
                self.kept(k, t).start()
        came.wait()
        self.send_in(0)

    def add_first(self, k):
        ref, rows = self.ref, self.rows_of(k)
        self.kept(k, 0).wait()
        self.one(k, 0).wait_recv()
        ref.s2f[0, rows] = (ref.s2f[0, rows].astype(F32) + ref.r1f[0, rows].astype(F32)).astype(BF16)
        self.two(k).start()

    def add_second(self, k):
        ref, rows = self.ref, self.rows_of(k)
        self.kept(k, 1).wait()
        self.one(k, 1).wait_recv()
        self.two(k).wait_recv()
        ref.s2f[1, rows] = (
            ref.s2f[1, rows].astype(F32) + ref.r1f[1, rows].astype(F32) + ref.r2f[rows].astype(F32)
        ).astype(BF16)
        self.send_in(k)

    def pieces(self, k):
        rows = self.rows_of(k)
        length = (rows.stop - rows.start) // PIECES
        for q in range(PIECES):
            yield k, k * PIECES + q, slice(rows.start + q * length, rows.start + (q + 1) * length)

    def bufs(self, k):
        ref = self.ref
        return (ref.s2p, ref.zap, ref.zbp, ref.ztp) if k == 0 else (ref.s2f.at[1], ref.zaf, ref.zbf, ref.ztf)

    def chain(self, k, m, rows, which):
        ref, h = self.ref, self.h
        s2, za, zb, zt = self.bufs(k)
        dp = self.at["dp"]
        if which == "in":
            return remote(s2.at[rows], za.at[rows], ref.z_send.at[0, m], ref.z_recv.at[0, m], (dp, 1 + h // 2))
        if which == "across":
            return remote(s2.at[rows], zb.at[rows], ref.z_send.at[0, m], ref.z_recv.at[1, m], (dp, 3 - h))
        return remote(zt.at[rows], za.at[rows], ref.z_send.at[1, m], ref.z_recv.at[0, m], (dp, 3 * (h // 2)))

    def send_in(self, k):
        @pl.when(self.outer)
        def _():
            for piece in self.pieces(k):
                self.chain(*piece, "in").start()

    def add_inner(self, k, only=None):
        s2, za, _, _ = self.bufs(k)

        @pl.when(jnp.logical_not(self.outer))
        def _():
            for q, piece in enumerate(self.pieces(k)):
                if only is None or q in only:
                    rows = piece[2]
                    self.chain(*piece, "in").wait_recv()
                    s2[rows] = (s2[rows].astype(F32) + za[rows].astype(F32)).astype(BF16)
                    self.chain(*piece, "across").start()

    def add_across(self, k, only=None):
        s2, _, zb, zt = self.bufs(k)

        @pl.when(jnp.logical_not(self.outer))
        def _():
            for q, piece in enumerate(self.pieces(k)):
                if only is None or q in only:
                    rows = piece[2]
                    self.chain(*piece, "across").wait_recv()
                    zt[rows] = (s2[rows].astype(F32) + zb[rows].astype(F32)).astype(BF16)
                    self.chain(*piece, "out").start()

    def finish(self):
        @pl.when(self.outer)
        def _():
            for k in range(3):
                _, za, _, zt = self.bufs(k)
                for piece in self.pieces(k):
                    self.chain(*piece, "out").wait_recv()
                    zt[piece[2]] = za[piece[2]]

        for k in range(3):
            if k > 0:
                for t in range(2):
                    self.one(k, t).wait_send()
                self.two(k).wait_send()
            for piece in self.pieces(k):
                self.chain(*piece, "in").wait_send()

        @pl.when(jnp.logical_not(self.outer))
        def _():
            for k in range(3):
                for piece in self.pieces(k):
                    self.chain(*piece, "out").wait_send()

    def swap(self):
        ref, core = self.ref, self.core
        return remote(ref.gq.at[1 - core], ref.gq_in, ref.q_send.at[0], ref.q_recv.at[0], (self.at["sib"], self.h))

    def spread(self, k):
        ref, x, y = self.ref, self.x, self.y
        to = (self.flip_x, self.flip_y, self.flip_xy)[k]
        block = (y * 2 + 1 - x, (1 - y) * 2 + x, (1 - y) * 2 + 1 - x)[k]
        return remote(ref.u.at[block], ref.u_in.at[k], ref.q_send.at[1 + k], ref.q_recv.at[1 + k], (to, self.h))

    def two_apart(self):
        ref, h = self.ref, self.h
        return remote(ref.v, ref.v_in, ref.q_send.at[4], ref.q_recv.at[4], (self.at["dp"], h + 2 - 4 * (h // 2)))

    def next_to(self):
        ref, h = self.ref, self.h
        return remote(ref.w, ref.w_in, ref.q_send.at[5], ref.q_recv.at[5], (self.at["dp"], h + 1 - 2 * lax.rem(h, 2)))

    def heads_first(self):
        ref, core = self.ref, self.core
        self.swap().start()
        self.swap().wait_recv()
        for j in range(4):
            mine, theirs = ref.gq[core, j].astype(F32), ref.gq_in[j].astype(F32)
            a, b = jnp.where(core == 0, mine, theirs), jnp.where(core == 0, theirs, mine)
            ref.u[j, :, 0:128] = a[:, 0:128].astype(BF16)
            ref.u[j, :, 128:256] = (a[:, 128:256] + b[:, 0:128]).astype(BF16)
            ref.u[j, :, 256:384] = b[:, 128:256].astype(BF16)
        for k in range(3):
            self.spread(k).start()

    def heads_second(self):
        ref = self.ref
        for k in range(3):
            self.spread(k).wait_recv()
        total = ref.u[self.y * 2 + self.x].astype(F32)
        for k in range(3):
            total = total + ref.u_in[k].astype(F32)
        ref.v[...] = total.astype(BF16)
        self.two_apart().start()

    def heads_third(self):
        ref = self.ref
        self.two_apart().wait_recv()
        ref.w[...] = (ref.v[...].astype(F32) + ref.v_in[...].astype(F32)).astype(BF16)
        self.next_to().start()
        self.next_to().wait_recv()
        self.swap().wait_send()
        for k in range(3):
            self.spread(k).wait_send()
        self.two_apart().wait_send()
        self.next_to().wait_send()

    def team(self, k):
        ref, at = self.ref, self.at
        me = self.core * 4 + self.h
        other = lax.rem(me + k, TEAM)
        return remote(
            ref.vec, ref.vec_team.at[me], ref.vt_send.at[k - 1], ref.vt_recv.at[me],
            (at["even"] + other // 4, lax.rem(other, 4)),
        )

    def chips(self, k):
        ref = self.ref
        here = self.y * 2 + self.x
        return remote(
            ref.vec2, ref.vec_xy.at[here], ref.vx_send.at[k], ref.vx_recv.at[here],
            ((self.flip_x, self.flip_y, self.flip_xy)[k], self.h),
        )

    def vectors_first(self):
        for k in range(1, TEAM):
            self.team(k).start()
        self.ref.vec_team[self.core * 4 + self.h] = self.ref.vec[...]

    def vectors_second(self):
        ref, h = self.ref, self.h
        me = self.core * 4 + h
        for k in range(1, TEAM):
            other = lax.rem(me + k, TEAM)
            remote(
                ref.vec, ref.vec_team.at[other], ref.vt_send.at[k - 1], ref.vt_recv.at[other], (self.at["sib"], h)
            ).wait_recv()
        total = ref.vec_team[0]
        for k in range(1, TEAM):
            total = total + ref.vec_team[k]
        ref.vec2[...] = total
        for k in range(3):
            self.chips(k).start()
        ref.vec_xy[self.y * 2 + self.x] = total

    def vectors_third(self):
        ref, x, y = self.ref, self.x, self.y
        others = (y * 2 + 1 - x, (1 - y) * 2 + x, (1 - y) * 2 + 1 - x)
        for k in range(3):
            remote(
                ref.vec2, ref.vec_xy.at[others[k]], ref.vx_send.at[k], ref.vx_recv.at[others[k]],
                (self.at["sib"], self.h),
            ).wait_recv()
        ref.vec_o[...] = (ref.vec_xy[0] + ref.vec_xy[1]) + (ref.vec_xy[2] + ref.vec_xy[3])
        for k in range(1, TEAM):
            self.team(k).wait_send()
        for k in range(3):
            self.chips(k).wait_send()


def attend_back(
    mix, xgt, ot, lse, start, d_ot, wt, d_middle, tokens, gain, bias, vecs, g_proj, g_fc, grad_scale,
    full,
):
    rows, width = tokens.shape
    part, group = width // 4, 4 * rows
    small, half = width // 8, width // 2
    dma = pltpu.SemaphoreType.DMA
    ins = [
        ("mix_h", mix, ANY), ("xgt_h", xgt, ANY), ("ot_h", ot, ANY), ("lse_h", lse, ANY), ("start_h", start, ANY),
        ("do_h", d_ot, ANY), ("wt_h", wt, ANY), ("dmid_h", d_middle, ANY), ("tok_h", tokens, ANY),
        ("gain", gain, VMEM), ("bias", bias, VMEM), ("vec_in", vecs, VMEM),
    ]
    outs = [("gtok_o", (rows, width), F32, VMEM), ("vec_o", (16, width), F32, VMEM)]
    gq_shape = (2, 4, 3 * small, 256)
    scratch = [
        ("mix", (3 * part, group), BF16), ("xgt", (width, group), BF16), ("ot", (part, group), BF16),
        ("do_t", (part, group), BF16), ("wt", (3 * 256, width), BF16), ("delta", (8, group), F32),
        ("kh", (group, HEAD_DIM), BF16), ("vh", (group, HEAD_DIM), BF16), ("qh", (group, HEAD_DIM), BF16),
        ("doh", (group, HEAD_DIM), BF16), ("dk", (group, HEAD_DIM), F32), ("dv", (group, HEAD_DIM), F32),
        ("dmix", (3 * 256, group), BF16), ("partial", (2, rows, width), BF16), ("summed", (2, rows, width), BF16),
        ("arrive", (2, rows, width), BF16), ("arrive2", (2, rows, width), BF16), ("gq", gq_shape, BF16),
        ("vec", (16, width), F32), ("lse", lse.shape, F32), ("start", start.shape, jnp.int32),
        ("dmid", (rows, width), F32), ("tok", (rows, width), BF16),
    ]
    sems = [
        ("in_sem", (9,)), ("sw_send", (2,)), ("sw_recv", (2,)), ("fin_send", (2,)), ("fin_recv", (2,)),
        ("fin_local", ()),
    ]
    if full:
        ins += [("s3p", g_proj, ANY), ("s1f", g_fc, ANY)]
        outs += [
            ("ztp", (half, width), BF16, VMEM), ("ztf", (half + small, width), BF16, VMEM),
            ("w", (3 * small, half), BF16, VMEM), ("w_in", (3 * small, half), BF16, VMEM),
        ]
        scratch += [(name, (half, width), BF16) for name in ("s2p", "zap", "zbp")]
        scratch += [(name, (2, half + small, width), BF16) for name in ("r1f", "s2f")]
        scratch += [(name, (half + small, width), BF16) for name in ("r2f", "zaf", "zbf")]
        scratch += [
            ("gq_in", gq_shape[1:], BF16), ("u", (4, 3 * small, half), BF16), ("u_in", (3, 3 * small, half), BF16),
            ("v", (3 * small, half), BF16), ("v_in", (3 * small, half), BF16),
            ("vec_team", (TEAM, 16, width), F32), ("vec2", (16, width), F32), ("vec_xy", (4, 16, width), F32),
        ]
        sems += [
            ("one_send", (3, 2)), ("one_recv", (3, 2)), ("two_send", (3,)), ("two_recv", (3,)), ("kept_sem", (3, 2)),
            ("z_send", (2, 3 * PIECES)), ("z_recv", (2, 3 * PIECES)), ("q_send", (6,)), ("q_recv", (6,)),
            ("vt_send", (TEAM - 1,)), ("vt_recv", (TEAM,)), ("vx_send", (3,)), ("vx_recv", (4,)),
        ]
    else:
        outs += [("gq_o", gq_shape, BF16, ANY)]
        sems += [("out_sem", ())]
    names = tuple(item[0] for item in ins + outs + scratch + sems)
    return pl.pallas_call(
        functools.partial(back_kernel, grad_scale, full, names),
        out_shape=tuple(jax.ShapeDtypeStruct(shape, kind) for _, shape, kind, _ in outs),
        in_specs=[spec for _, _, spec in ins],
        out_specs=tuple(spec for _, _, _, spec in outs),
        scratch_shapes=[pltpu.VMEM(shape, kind) for _, shape, kind in scratch] + [dma(shape) for _, shape in sems],
        compiler_params=pltpu.CompilerParams(
            collective_id=2, has_side_effects=True, vmem_limit_bytes=60 << 20
        ),
        name="attend_back",
    )(*(array for _, array, _ in ins))


def emit_kernel(names, *refs):
    ref = types.SimpleNamespace(**dict(zip(names, refs, strict=True)))
    through = ((ref.out, ref.out_o), (ref.gtok, ref.gtok_o))
    loads = [pltpu.make_async_copy(src, ref.buf.at[k], ref.sem.at[k]) for k, (src, _) in enumerate(through)]
    stores = [pltpu.make_async_copy(ref.buf.at[k], dst, ref.sem.at[k]) for k, (_, dst) in enumerate(through)]
    for load in loads:
        load.start()
    half, width = ref.ztp.shape
    small = ref.gout_o.shape[0]
    odd = lax.rem(lax.axis_index("head"), 2)
    ref.gproj_o[...] = ref.ztp[...].astype(F32)
    ref.gfc_o[...] = ref.ztf[0:half, :].astype(F32).T
    ref.gout_o[...] = ref.ztf[half:, :].astype(F32)
    for p in range(3):
        here = slice(p * small, (p + 1) * small)
        ref.gqkv_o[:, pl.ds(mult((2 * p + odd) * half, 128), half)] = ref.w[here, :].astype(F32)
        ref.gqkv_o[:, pl.ds(mult((2 * p + 1 - odd) * half, 128), half)] = ref.w_in[here, :].astype(F32)
    for load, store in zip(loads, stores):
        load.wait()
        store.start()
    for k, name in enumerate(VECTORS):
        if name and name != "fc_b":
            getattr(ref, name)[...] = ref.vec[k].reshape(width)
    ref.fc_b[...] = jnp.concatenate([ref.vec[4 + k : 5 + k, :] for k in range(4)], axis=1).reshape(4 * width)
    for store in stores:
        store.wait()


VECTORS = ("out_b", "ln2_g", "ln2_b", "proj_b", "fc_b", "", "", "", "ln1_g", "ln1_b", "q_b", "v_b")


def emit(out, gtok, vec, ztp, ztf, w, w_in):
    rows, width = out.shape
    half, small = width // 2, width // 8
    ins = [
        ("out", out, ANY), ("gtok", gtok, ANY), ("vec", vec, VMEM), ("ztp", ztp, VMEM), ("ztf", ztf, VMEM),
        ("w", w, VMEM), ("w_in", w_in, VMEM),
    ]
    outs = [
        ("out_o", (rows, width), ANY), ("gtok_o", (rows, width), ANY), ("ln1_g", (width,), VMEM),
        ("ln1_b", (width,), VMEM), ("gqkv_o", (small, 3 * width), VMEM), ("q_b", (width,), VMEM),
        ("v_b", (width,), VMEM), ("gout_o", (small, width), VMEM), ("out_b", (width,), VMEM),
        ("ln2_g", (width,), VMEM), ("ln2_b", (width,), VMEM), ("gfc_o", (width, half), VMEM),
        ("fc_b", (4 * width,), VMEM), ("gproj_o", (half, width), VMEM), ("proj_b", (width,), VMEM),
    ]
    return pl.pallas_call(
        functools.partial(emit_kernel, tuple(item[0] for item in ins + outs) + ("buf", "sem")),
        out_shape=tuple(jax.ShapeDtypeStruct(shape, F32) for _, shape, _ in outs),
        in_specs=[spec for _, _, spec in ins],
        out_specs=tuple(spec for _, _, spec in outs),
        scratch_shapes=[pltpu.VMEM((2, rows, width), F32), pltpu.SemaphoreType.DMA((2,))],
        compiler_params=pltpu.CompilerParams(vmem_limit_bytes=60 << 20),
        name="emit",
    )(*(array for _, array, _ in ins))


def shards(
    tokens, lengths, ln1_gain, ln1_bias, w_qkv, bias_q, bias_v, w_out, bias_out, ln2_gain, ln2_bias, w_fc, bias_fc,
    w_proj, bias_proj, cotangent,
):
    rows, width = tokens.shape
    device_count = lax.axis_size("dp") * lax.axis_size("head")
    full = lax.axis_size("dp") == 8
    grad_scale = 1.0 / math.sqrt(rows * device_count)
    att, mix, xgt, ot, lse, start, wt = attend(tokens, lengths, ln1_gain, ln1_bias, bias_q, bias_v, w_qkv)
    block_output, d_middle, d_ot, g_fc, g_proj, vecs = mlp(
        att, tokens, cotangent, grad_scale, full, bias_out, ln2_gain, ln2_bias, bias_fc, bias_proj, w_out, w_fc, w_proj
    )
    grad_tokens, vec, *rest = attend_back(
        mix, xgt, ot, lse, start, d_ot, wt, d_middle, tokens, ln1_gain, ln1_bias, vecs, g_proj, g_fc, grad_scale,
        full,
    )
    if full:
        return emit(block_output, grad_tokens, vec, *rest)
    proj_total, fc_total, out_total, qkv_total, vec = sums_by_xla(rest[0], g_proj, g_fc, vec)
    return (
        block_output, grad_tokens, vec[8], vec[9], qkv_total, vec[10], vec[11], out_total, vec[0], vec[1], vec[2],
        fc_total, vec[4:8].reshape(-1), proj_total, vec[3],
    )


def sums_by_xla(gq, g_proj, g_fc, vec):
    _, blocks, length, width = g_proj.shape
    small = width // 8
    whole = g_proj.transpose(1, 0, 2, 3).reshape(2 * blocks * length, width)
    fc = g_fc[:, :, :length].transpose(1, 0, 2, 3).reshape(2 * blocks * length, width).T
    out = g_fc[:, :, length:].transpose(1, 0, 2, 3).reshape(width, width)
    core, odd = lax.rem(lax.axis_index("dp"), 2), lax.rem(lax.axis_index("head"), 2)
    window = gq.reshape(2, 4, 3, small, 256).transpose(1, 0, 3, 2, 4).reshape(width, 3, 256)
    qkv = lax.dynamic_update_slice(
        jnp.zeros((width, 3, width), BF16), window, (0, 0, odd * (width // 2) + core * 128)
    ).reshape(width, 3 * width)

    def reduce_mat(g, dim):
        share = lax.psum_scatter(g, "dp", scatter_dimension=dim, tiled=True)
        return lax.psum(share, "head").astype(F32)

    return reduce_mat(whole, 0), reduce_mat(fc, 1), reduce_mat(out, 0), reduce_mat(qkv, 0), lax.psum(vec, ("dp", "head"))


def solution(mesh):
    rows = P(("dp", "head"), None)
    return jax.shard_map(
        shards,
        mesh=mesh,
        in_specs=(rows, P("dp", None)) + (P(),) * 13 + (rows,),
        out_specs=(
            rows, rows, P(), P(), P("dp", None), P(), P(), P("dp", None), P(), P(), P(), P(None, "dp"), P(),
            P("dp", None), P(),
        ),
        check_vma=False,
    )
```

```python
import functools
import math
import types

import jax
import jax.numpy as jnp
from jax import lax
from jax.experimental import pallas as pl
from jax.experimental.pallas import tpu as pltpu
from jax.sharding import PartitionSpec as P

HEAD_DIM = 64
EPSILON = 1e-05
DEPTH_SCALE = 1.0 / math.sqrt(12.0)
LOG2E = 1.0 / math.log(2.0)
SCORE_SCALE = HEAD_DIM ** (-0.5)
GELU_K = math.sqrt(2.0 / math.pi)
GELU_A = 0.044715
TEAM = 8
QB = 256
PIECES = 3

F32 = jnp.float32
BF16 = jnp.bfloat16
MESH = pl.DeviceIdType.MESH
ANY = pl.BlockSpec(memory_space=pl.ANY)
VMEM = pl.BlockSpec(memory_space=pltpu.VMEM)
SMEM = pl.BlockSpec(memory_space=pltpu.SMEM)


def dot(a, b):
    return jnp.dot(a, b, preferred_element_type=F32)


def dot_nt(a, b):
    return lax.dot_general(a, b, (((1,), (1,)), ((), ())), preferred_element_type=F32)


def dot_tn(a, b):
    return lax.dot_general(a, b, (((0,), (0,)), ((), ())), preferred_element_type=F32)


def mult(x, m):
    return pl.multiple_of(x, m)


def place():
    dp, h = lax.axis_index("dp"), lax.axis_index("head")
    core = lax.rem(dp, 2)
    half = h // 2
    return dict(
        dp=dp,
        h=h,
        core=core,
        sib=dp + 1 - 2 * core,
        even=dp - core,
        half=half,
        served=dp - core + half,
        block=(h - 2 * half) * 2 + core,
    )


def greet(at, chips=False):
    barrier = pltpu.get_barrier_semaphore()
    me = at["core"] * 4 + at["h"]
    others = []
    for k in range(1, TEAM):
        other = lax.rem(me + k, TEAM)
        others.append((at["even"] + other // 4, lax.rem(other, 4)))
    if chips:
        for k in range(1, 4):
            others.append((lax.rem(at["dp"] + 2 * k, 8), at["h"]))
    for other in others:
        pl.semaphore_signal(barrier, inc=1, device_id=other, device_id_type=MESH)
    pl.semaphore_wait(barrier, len(others))


def remote(src, dst, send, recv, device):
    return pltpu.make_async_remote_copy(
        src_ref=src, dst_ref=dst, send_sem=send, recv_sem=recv, device_id=device, device_id_type=MESH
    )


def row(vec):
    return vec[...].reshape(1, vec.shape[0])


def norm_parts(v):
    center = jnp.mean(v, axis=-1, keepdims=True)
    cent = v - center
    r = lax.rsqrt(jnp.mean(cent * cent, axis=-1, keepdims=True) + EPSILON)
    return cent * r, r


def norm_back(e, gain, n, r):
    ea = e * gain
    return r * (ea - jnp.mean(ea, axis=-1, keepdims=True) - n * jnp.mean(ea * n, axis=-1, keepdims=True))


def attend_kernel(
    tok, lens, gain, bias, bias_q, bias_v, w_qkv,
    att_o, mix_o, xgt_o, ot_o, lse_o, start_o, wt_o,
    xn, xg, xgt, wwin, wt, brow, bcol, start_mine, start_sib, mix, kh, scores, ot,
    w_sem, st_sem, ag_send, ag_recv, fw_send, at_send, at_recv, at_local, out_sem,
):
    at = place()
    dp, h, core, sib = at["dp"], at["h"], at["core"], at["sib"]
    rows, width = tok.shape
    group = 4 * rows
    part = width // 4
    collects = core == at["half"]
    first = (h - 2 * at["half"]) * 2 * part + core * 128
    shift = mult(64 * core, 64)
    for p in range(3):
        pltpu.make_async_copy(
            w_qkv.at[:, pl.ds(mult(p * width + first, 128), 256)], wwin.at[p], w_sem.at[p]
        ).start()
    greet(at)

    places = lax.broadcasted_iota(jnp.int32, (8, group), 1)
    begin = jnp.zeros((8, group), jnp.int32)
    edge = lens[0, 0]
    for k in range(1, lens.shape[1] + 1):
        begin = jnp.where(places >= edge, edge, begin)
        if k < lens.shape[1]:
            edge = edge + lens[0, k]
    start_mine[...] = begin.astype(F32)
    st_copy = remote(start_mine, start_sib, st_sem.at[0], st_sem.at[1], (sib, h))
    st_copy.start()

    n, _ = norm_parts(tok[...].astype(F32))
    xn[...] = (n * row(gain) + row(bias)).astype(BF16)

    inner, outer = 1 + core, 3 * core
    at_inner, at_outer = h == inner, h == outer

    length = rows // PIECES

    def piece(ref, s, q):
        return ref.at[pl.ds(mult(s * rows + q * length, length), length), :]

    def to_inner(q):
        return remote(piece(xn, 0, q), piece(xg, h, q), ag_send.at[q], ag_recv.at[h, q], (dp, inner))

    def to_outer(k, s, q):
        src = piece(xn, 0, q) if k == 0 else piece(xg, s, q)
        return remote(src, piece(xg, s, q), ag_send.at[k * PIECES + q], ag_recv.at[s, q], (dp, outer))

    def to_sib(d, s, q):
        src = piece(xn, 0, q) if d == 0 else piece(xg, s, q)
        return remote(src, piece(xg, s, q), fw_send.at[d * PIECES + q], ag_recv.at[s, q], (sib, h))

    @pl.when(at_inner)
    def _():
        for q in range(PIECES):
            to_outer(0, h, q).start()

    @pl.when(jnp.logical_not(at_inner))
    def _():
        for q in range(PIECES):
            to_inner(q).start()

    @pl.when(collects)
    def _():
        for q in range(PIECES):
            to_sib(0, h, q).start()
        xg[pl.ds(mult(h * rows, rows), rows), :] = xn[...]

    for p in range(3):
        pltpu.make_async_copy(wwin.at[p], wwin.at[p], w_sem.at[p]).wait()
        wt[p * 256 : (p + 1) * 256, :] = wwin[p].T
    wt_copy = pltpu.make_async_copy(wt, wt_o, out_sem.at[0])
    wt_copy.start()
    for p, vec in ((0, bias_q), (2, bias_v)):
        brow[...] = jnp.broadcast_to(row(vec), (8, width))
        bcol[p] = jnp.broadcast_to(brow[0:1, pl.ds(mult(first, 128), 256)], (128, 256)).T
    bcol[1] = jnp.zeros((256, 128), F32)

    low = 1 - at["half"]
    order = (h, low * (1 - h) + (1 - low) * (5 - h), 1 + low, 3 * low)

    def project(s):
        here = xg[pl.ds(mult(s * rows, rows), rows), :]
        xgt[:, pl.ds(mult(s * rows, 128), rows)] = here.T
        for p in range(3):
            res = dot_nt(wt[pl.ds(mult(p * 256 + shift, 64), part), :], here) + bcol[p, pl.ds(shift, part), :][:, :1]
            mix[p * part : (p + 1) * part, pl.ds(mult(s * rows, 128), rows)] = res.astype(BF16)

    @pl.when(jnp.logical_not(collects))
    def _():
        for q in range(PIECES):
            to_sib(1, h, q).wait_recv()

    project(h)
    for q in range(PIECES):
        for d in range(1, 4):
            s = order[d]
            to_sib(d, s, q).wait_recv()

            @pl.when(collects)
            def _():
                to_sib(d, s, q).start()

            if d > 1:
                @pl.when(at_inner)
                def _():
                    to_outer(d - 1, s, q).start()

            if q == PIECES - 1:
                project(s)
    mix_copy = pltpu.make_async_copy(mix, mix_o, out_sem.at[2])
    mix_copy.start()
    xgt_copy = pltpu.make_async_copy(xgt, xgt_o, out_sem.at[1])
    xgt_copy.start()
    st_copy.wait_recv()
    start_o[...] = jnp.where(collects, start_mine[...], start_sib[...]).astype(jnp.int32)

    heads = part // HEAD_DIM
    scale = SCORE_SCALE * LOG2E

    def at_copy(i, s):
        src = ot.at[pl.ds(mult(i * HEAD_DIM, HEAD_DIM), HEAD_DIM), pl.ds(s * rows, rows)]
        dst = att_o.at[pl.ds(mult(at["block"] * part + i * HEAD_DIM, HEAD_DIM), HEAD_DIM), :]
        return src, dst

    def at_remote(i, s):
        src, dst = at_copy(i, s)
        return remote(src, dst, at_send.at[i * 4 + s], at_recv.at[at["block"] * heads + i], (at["served"], s))

    def stays(s):
        return jnp.logical_and(collects, h == s)

    def one_head(i, _):
        qrow, krow, vrow = (mult(p * part + i * HEAD_DIM, HEAD_DIM) for p in range(3))
        kh[...] = mix[pl.ds(krow, HEAD_DIM), :].T
        for j in range(group // QB):
            cols = slice(j * QB, (j + 1) * QB)
            q_t = mix[pl.ds(qrow, HEAD_DIM), cols]
            begins = start_o[0:1, cols]
            top = jnp.full((1, QB), -jnp.inf, F32)
            for k in range(j + 1):
                s_t = dot(kh[k * QB : (k + 1) * QB, :], q_t)
                key = lax.broadcasted_iota(jnp.int32, (QB, QB), 0)
                keep = key >= begins - k * QB
                if k == j:
                    keep = jnp.logical_and(keep, key <= lax.broadcasted_iota(jnp.int32, (QB, QB), 1))
                s_t = jnp.where(keep, s_t, -1e30)
                scores[k * QB : (k + 1) * QB, :] = s_t
                top = jnp.maximum(top, jnp.max(s_t, axis=0, keepdims=True))
            top = top * scale
            total = jnp.zeros((1, QB), F32)
            acc = jnp.zeros((HEAD_DIM, QB), F32)
            for k in range(j + 1):
                p_t = jnp.exp2(scores[k * QB : (k + 1) * QB, :] * scale - top)
                total = total + jnp.sum(p_t, axis=0, keepdims=True)
                acc = acc + dot(mix[pl.ds(vrow, HEAD_DIM), k * QB : (k + 1) * QB], p_t.astype(BF16))
            ot[pl.ds(qrow, HEAD_DIM), cols] = (acc / total).astype(BF16)
            lse_o[pl.ds(mult(i * 8, 8), 8), cols] = jnp.broadcast_to(top + jnp.log2(total), (8, QB))
        for s in range(4):
            @pl.when(stays(s))
            def _():
                pltpu.make_async_copy(*at_copy(i, s), at_local.at[i]).start()

            @pl.when(jnp.logical_not(stays(s)))
            def _():
                at_remote(i, s).start()
        return 0

    lax.fori_loop(0, heads, one_head, 0)
    ot_copy = pltpu.make_async_copy(ot, ot_o, out_sem.at[3])
    ot_copy.start()

    @pl.when(at_inner)
    def _():
        for q in range(PIECES):
            for d in range(1, 4):
                to_outer(d - 1, order[d], q).wait_send()

    @pl.when(jnp.logical_not(at_inner))
    def _():
        for q in range(PIECES):
            to_inner(q).wait_send()

    @pl.when(collects)
    def _():
        for q in range(PIECES):
            for d in range(4):
                to_sib(d, order[d], q).wait_send()

    st_copy.wait_send()
    wt_copy.wait()
    mix_copy.wait()
    xgt_copy.wait()
    ot_copy.wait()
    for i in range(heads):
        for s in range(4):
            @pl.when(stays(s))
            def _():
                pltpu.make_async_copy(*at_copy(i, s), at_local.at[i]).wait()

            @pl.when(jnp.logical_not(stays(s)))
            def _():
                at_remote(i, s).wait_send()
        for b in range(4):
            dst = att_o.at[pl.ds(b * part + i * HEAD_DIM, HEAD_DIM), :]
            src = ot.at[pl.ds(i * HEAD_DIM, HEAD_DIM), pl.ds(0, rows)]

            @pl.when(jnp.logical_not(jnp.logical_and(collects, at["block"] == b)))
            def _():
                remote(src, dst, at_send.at[i * 4], at_recv.at[b * heads + i], (sib, h)).wait_recv()


def attend(tokens, lengths, gain, bias, bias_q, bias_v, w_qkv):
    rows, width = tokens.shape
    group, part = 4 * rows, width // 4
    heads = part // HEAD_DIM
    dma = pltpu.SemaphoreType.DMA
    return pl.pallas_call(
        attend_kernel,
        out_shape=(
            jax.ShapeDtypeStruct((width, rows), BF16),
            jax.ShapeDtypeStruct((3 * part, group), BF16),
            jax.ShapeDtypeStruct((width, group), BF16),
            jax.ShapeDtypeStruct((part, group), BF16),
            jax.ShapeDtypeStruct((8 * heads, group), F32),
            jax.ShapeDtypeStruct((8, group), jnp.int32),
            jax.ShapeDtypeStruct((3 * 256, width), BF16),
        ),
        in_specs=[VMEM, SMEM, VMEM, VMEM, VMEM, VMEM, ANY],
        out_specs=(ANY, ANY, ANY, ANY, VMEM, VMEM, ANY),
        scratch_shapes=[
            pltpu.VMEM((rows, width), BF16),
            pltpu.VMEM((group, width), BF16),
            pltpu.VMEM((width, group), BF16),
            pltpu.VMEM((3, width, 256), BF16),
            pltpu.VMEM((3 * 256, width), BF16),
            pltpu.VMEM((8, width), F32),
            pltpu.VMEM((3, 256, 128), F32),
            pltpu.VMEM((8, group), F32),
            pltpu.VMEM((8, group), F32),
            pltpu.VMEM((3 * part, group), BF16),
            pltpu.VMEM((group, HEAD_DIM), BF16),
            pltpu.VMEM((group, QB), F32),
            pltpu.VMEM((part, group), BF16),
            dma((3,)), dma((2,)), dma((3 * PIECES,)), dma((4, PIECES)), dma((4 * PIECES,)),
            dma((4 * heads,)), dma((4 * heads,)), dma((heads,)), dma((4,)),
        ],
        compiler_params=pltpu.CompilerParams(
            collective_id=0, has_side_effects=True, vmem_limit_bytes=60 << 20
        ),
        name="attend",
    )(tokens, lengths, gain, bias, bias_q, bias_v, w_qkv)


def mlp_kernel(
    grad_scale, paired,
    b_out, gain, bias, b_fc, b_proj, att_h, tok_h, cot_h, w_out_h, w_fc_h, w_proj_h,
    out_o, dmid_o, dot_o, gfc_o, gproj_o, vec_o,
    att, tok, cot,
    w_out, w_fc, w_proj, brow, dfc, dat, gfc, gproj, gfc_in, gproj_in, r1, s2, r2, s3,
    w_sem, send, recv, local, pair_send, pair_recv, one_send, one_recv, two_send, two_recv, in_sem, out_sem,
):
    at = place()
    h, core = at["h"], at["core"]
    rows, width = tok_h.shape
    part = width // 4
    chunks = w_fc_h.shape[1] // width
    wo_copy = pltpu.make_async_copy(w_out_h, w_out, w_sem.at[0])
    wo_copy.start()

    def wf_copy(j):
        return pltpu.make_async_copy(w_fc_h.at[:, pl.ds(mult(j * width, 128), width)], w_fc.at[j], w_sem.at[1 + 2 * j])

    def wp_copy(j):
        return pltpu.make_async_copy(w_proj_h.at[pl.ds(mult(j * width, 128), width), :], w_proj.at[j], w_sem.at[2 + 2 * j])

    loads = [
        pltpu.make_async_copy(src, dst, in_sem.at[k])
        for k, (src, dst) in enumerate(((cot_h, cot), (tok_h, tok), (att_h, att)))
    ]
    for load in loads:
        load.start()
    greet(at, paired)

    half_rows = width // 2
    small = width // 8
    y, x = at["dp"] // 4, lax.rem(at["dp"] // 2, 2)

    def pair_copy(ref, into, k, j):
        return remote(ref.at[1 - core, j], into.at[j], pair_send.at[k, j], pair_recv.at[k, j], (at["sib"], h))

    def pair_add(ref, into, k, j):
        pair_copy(ref, into, k, j).wait_recv()
        ref[core, j] = (ref[core, j].astype(F32) + into[j].astype(F32)).astype(BF16)

    if paired:
        order = [(1 - y) * 2 + 1 - x, y * 2 + 1 - x, (1 - y) * 2 + x, y * 2 + x]
    else:
        order = list(range(chunks))
    quarter = half_rows // 2
    flips = (at["dp"] + 2 - 4 * x, h), (at["dp"] + 4 - 8 * y, h)

    def halves(k):
        return slice(k * quarter, (k + 1) * quarter)

    def one(k, t):
        j = order[0] if t == 0 else order[1 + k]
        return remote(gproj.at[core, j, halves(k)], r1.at[k, t], one_send.at[k, t], one_recv.at[k, t], flips[k])

    def two(k):
        return remote(s2.at[k], r2.at[k], two_send.at[k], two_recv.at[k], flips[1 - k])

    def first_sum(k):
        one(k, 0).wait_recv()
        s2[k] = (gproj[core, order[2 - k], halves(k)].astype(F32) + r1[k, 0].astype(F32)).astype(BF16)
        two(k).start()

    def last_sum():
        for k in range(2):
            one(k, 1).wait_recv()
            two(k).wait_recv()
            s3[halves(k)] = (
                gproj[core, order[3], halves(k)].astype(F32) + r1[k, 1].astype(F32) + r2[k].astype(F32)
            ).astype(BF16)

    def proj_sums(step):
        if not paired:
            return
        pair_add(gproj, gproj_in, 0, order[step])
        if step == 0:
            one(0, 0).start()
            one(1, 0).start()
        elif step == 1:
            one(0, 1).start()
        elif step == 2:
            one(1, 1).start()
            first_sum(0)
            first_sum(1)

    loads[0].wait()
    dy = cot[...].astype(F32)
    d_proj = (DEPTH_SCALE * dy).astype(BF16)
    for j in order:
        wf_copy(j).start()
        wp_copy(j).start()
    wo_copy.wait()
    loads[1].wait()
    loads[2].wait()
    middle = tok[...].astype(F32) + DEPTH_SCALE * (dot_tn(att[...], w_out[...]) + row(b_out))
    n, r = norm_parts(middle)
    second = (n * row(gain) + row(bias)).astype(BF16)
    result = middle + DEPTH_SCALE * row(b_proj)
    brow[...] = jnp.broadcast_to(row(b_fc), brow.shape)
    d_second = jnp.zeros((rows, width), F32)
    vec_o[3:4, :] = jnp.sum(dy, axis=0, keepdims=True) * (DEPTH_SCALE * grad_scale)
    for step, j in enumerate(order):
        wf_copy(j).wait()
        u = dot(second, w_fc[j]) + brow[0:1, pl.ds(mult(j * width, 128), width)]
        u2 = u * u
        th = jnp.tanh(GELU_K * u * (1.0 + GELU_A * u2))
        half = 0.5 * (1.0 + th)
        slope = half + 0.5 * u * (1.0 - th * th) * (GELU_K * (1.0 + 3.0 * GELU_A * u2))
        hidden = (u * half).astype(BF16)
        wp_copy(j).wait()
        result = result + DEPTH_SCALE * dot(hidden, w_proj[j])
        d_pre = dot_nt(d_proj, w_proj[j]) * slope
        res = (dot_tn(hidden, d_proj) * grad_scale).astype(BF16)
        for k in range(2):
            gproj[k, j] = res[k * half_rows : (k + 1) * half_rows]
        if paired:
            pair_copy(gproj, gproj_in, 0, j).start()
        if step > 0:
            proj_sums(step - 1)
        vec_o[pl.ds(4 + j, 1), :] = jnp.sum(d_pre, axis=0, keepdims=True) * grad_scale
        d_fc = d_pre.astype(BF16)
        dfc[j] = d_fc
        d_second = d_second + dot_nt(d_fc, w_fc[j])
    out_o[...] = result
    vec_o[1:2, :] = jnp.sum(d_second * n, axis=0, keepdims=True) * grad_scale
    vec_o[2:3, :] = jnp.sum(d_second, axis=0, keepdims=True) * grad_scale
    d_middle = dy + norm_back(d_second, row(gain), n, r)
    dmid_o[...] = d_middle
    vec_o[0:1, :] = jnp.sum(d_middle, axis=0, keepdims=True) * (DEPTH_SCALE * grad_scale)
    d_out = (DEPTH_SCALE * d_middle).astype(BF16)
    dat[...] = dot_nt(w_out[...], d_out).astype(BF16)

    def target(b):
        return at["even"] + b % 2, 2 * core + b // 2

    def stays(b):
        return jnp.logical_and(core == b % 2, h == 2 * core + b // 2)

    dst = dot_o.at[:, pl.ds(mult(h * rows, 128), rows)]

    def da_local(b):
        return pltpu.make_async_copy(dat.at[pl.ds(b * part, part), :], dst, local)

    def da_remote(b):
        return remote(dat.at[pl.ds(b * part, part), :], dst, send.at[b], recv.at[h], target(b))

    for b in range(4):
        @pl.when(stays(b))
        def _():
            da_local(b).start()

        @pl.when(jnp.logical_not(stays(b)))
        def _():
            da_remote(b).start()

    g_out = (dot(att[...], d_out) * grad_scale).astype(BF16)
    for j in range(chunks):
        for k in range(2):
            gfc[k, j, half_rows:, :] = g_out[(2 * j + k) * small : (2 * j + k + 1) * small]
    proj_sums(chunks - 1)
    for j in order:
        res = (dot_tn(dfc[j], second) * grad_scale).astype(BF16)
        for k in range(2):
            gfc[k, j, :half_rows, :] = res[k * half_rows : (k + 1) * half_rows]
        if paired:
            pair_copy(gfc, gfc_in, 1, j).start()
    if paired:
        last_sum()
        for j in order:
            pair_add(gfc, gfc_in, 1, j)
        outs = [
            pltpu.make_async_copy(s3, gproj_o, out_sem.at[0]),
            pltpu.make_async_copy(gfc.at[core], gfc_o, out_sem.at[1]),
        ]
    else:
        outs = [
            pltpu.make_async_copy(gproj, gproj_o, out_sem.at[0]),
            pltpu.make_async_copy(gfc, gfc_o, out_sem.at[1]),
        ]
    for copy in outs:
        copy.start()

    served_here = core == at["half"]
    for b in range(4):
        @pl.when(stays(b))
        def _():
            da_local(b).wait()

        @pl.when(jnp.logical_not(stays(b)))
        def _():
            da_remote(b).wait_send()
    for s in range(4):
        @pl.when(jnp.logical_not(jnp.logical_and(served_here, h == s)))
        def _():
            remote(
                dat.at[pl.ds(0, part), :], dot_o.at[:, pl.ds(s * rows, rows)], send.at[0], recv.at[s], (at["sib"], h)
            ).wait_recv()
    if paired:
        for j in range(chunks):
            for k, (ref, into) in enumerate(((gproj, gproj_in), (gfc, gfc_in))):
                pair_copy(ref, into, k, j).wait_send()

        for k in range(2):
            for t in range(2):
                one(k, t).wait_send()
            two(k).wait_send()
    for copy in outs:
        copy.wait()


def mlp(att, tokens, cotangent, grad_scale, paired, b_out, gain, bias, b_fc, b_proj, w_out, w_fc, w_proj):
    rows, width = tokens.shape
    part, group = width // 4, 4 * rows
    ff = w_fc.shape[1]
    chunks = ff // width
    lead = () if paired else (2,)
    dma = pltpu.SemaphoreType.DMA
    return pl.pallas_call(
        functools.partial(mlp_kernel, grad_scale, paired),
        out_shape=(
            jax.ShapeDtypeStruct((rows, width), F32),
            jax.ShapeDtypeStruct((rows, width), F32),
            jax.ShapeDtypeStruct((part, group), BF16),
            jax.ShapeDtypeStruct(lead + (chunks, width // 2 + width // 8, width), BF16),
            jax.ShapeDtypeStruct((() if paired else (2, chunks)) + (width // 2, width), BF16),
            jax.ShapeDtypeStruct((8, width), F32),
        ),
        in_specs=[VMEM] * 5 + [ANY] * 6,
        out_specs=(VMEM, VMEM, ANY, ANY, ANY, VMEM),
        scratch_shapes=[
            pltpu.VMEM((width, rows), BF16),
            pltpu.VMEM((rows, width), BF16),
            pltpu.VMEM((rows, width), BF16),
            pltpu.VMEM((width, width), BF16),
            pltpu.VMEM((chunks, width, width), BF16),
            pltpu.VMEM((chunks, width, width), BF16),
            pltpu.VMEM((8, ff), F32),
            pltpu.VMEM((chunks, rows, width), BF16),
            pltpu.VMEM((width, rows), BF16),
            pltpu.VMEM((2, chunks, width // 2 + width // 8, width), BF16),
            pltpu.VMEM((2, chunks, width // 2, width), BF16),
            pltpu.VMEM((chunks, width // 2 + width // 8, width), BF16),
            pltpu.VMEM((chunks, width // 2, width), BF16),
            pltpu.VMEM((2, 2, width // 4, width), BF16),
            pltpu.VMEM((2, width // 4, width), BF16),
            pltpu.VMEM((2, width // 4, width), BF16),
            pltpu.VMEM((width // 2, width), BF16),
            dma((1 + 2 * chunks,)), dma((4,)), dma((4,)), dma, dma((2, chunks)), dma((2, chunks)),
            dma((2, 2)), dma((2, 2)), dma((2,)), dma((2,)), dma((3,)), dma((2,)),
        ],
        compiler_params=pltpu.CompilerParams(
            collective_id=1, has_side_effects=True, vmem_limit_bytes=60 << 20
        ),
        name="mlp",
    )(
        b_out, gain, bias, b_fc, b_proj, att, tokens, cotangent, w_out, w_fc, w_proj,
    )


def back_kernel(grad_scale, full, names, *refs):
    ref = types.SimpleNamespace(**dict(zip(names, refs, strict=True)))
    mix, do_t, ot, xgt, wt, dmix = ref.mix, ref.do_t, ref.ot, ref.xgt, ref.wt, ref.dmix
    lse, start, delta, kh, vh, qh, doh, dk, dv = (
        ref.lse, ref.start, ref.delta, ref.kh, ref.vh, ref.qh, ref.doh, ref.dk, ref.dv
    )
    partial, summed, arrive, arrive2 = ref.partial, ref.summed, ref.arrive, ref.arrive2
    sw_send, sw_recv, fin_send, fin_recv, fin_local = (
        ref.sw_send, ref.sw_recv, ref.fin_send, ref.fin_recv, ref.fin_local
    )
    at = place()
    dp, h, core, sib = at["dp"], at["h"], at["core"], at["sib"]
    rows, width = ref.tok.shape
    part, group = width // 4, 4 * rows
    heads = part // HEAD_DIM
    loads = [
        pltpu.make_async_copy(src, dst, ref.in_sem.at[k])
        for k, (src, dst) in enumerate(
            (
                (ref.do_h, do_t), (ref.ot_h, ot), (ref.mix_h, mix), (ref.lse_h, lse), (ref.start_h, start),
                (ref.wt_h, wt), (ref.xgt_h, xgt), (ref.dmid_h, ref.dmid), (ref.tok_h, ref.tok),
            )
        )
    ]
    for load in loads:
        load.start()
    @pl.when(core != at["half"])
    def _():
        arrive2[1] = jnp.zeros(arrive2.shape[1:], BF16)

    greet(at, full)
    if full:
        sums = Sums(ref, at, grad_scale)
        sums.first()
    dmix[...] = jnp.zeros_like(dmix)
    for load in loads[:5]:
        load.wait()
    scale = SCORE_SCALE * LOG2E

    def drow(p, i):
        return pl.ds(mult(p * 256 + (core + i) * HEAD_DIM, HEAD_DIM), HEAD_DIM)

    def one_head(i, _):
        qrow, krow, vrow = (mult(p * part + i * HEAD_DIM, HEAD_DIM) for p in range(3))
        d_head = do_t[pl.ds(qrow, HEAD_DIM), :]
        delta[...] = jnp.broadcast_to(
            jnp.sum(d_head.astype(F32) * ot[pl.ds(qrow, HEAD_DIM), :].astype(F32), axis=0, keepdims=True), (8, group)
        )
        qh[...] = mix[pl.ds(qrow, HEAD_DIM), :].T
        kh[...] = mix[pl.ds(krow, HEAD_DIM), :].T
        vh[...] = mix[pl.ds(vrow, HEAD_DIM), :].T
        doh[...] = d_head.T
        for j in range(group // QB):
            cols = slice(j * QB, (j + 1) * QB)
            q_t = mix[pl.ds(qrow, HEAD_DIM), cols]
            do_j = do_t[pl.ds(qrow, HEAD_DIM), cols]
            begins = start[0:1, cols]
            lse_j = lse[pl.ds(mult(i * 8, 8), 8), cols][0:1]
            delta_j = delta[0:1, cols]
            acc = jnp.zeros((HEAD_DIM, QB), F32)
            for k in range(j + 1):
                keys = slice(k * QB, (k + 1) * QB)
                s_t = dot(kh[keys, :], q_t)
                key = lax.broadcasted_iota(jnp.int32, (QB, QB), 0)
                keep = key >= begins - k * QB
                if k == j:
                    keep = jnp.logical_and(keep, key <= lax.broadcasted_iota(jnp.int32, (QB, QB), 1))
                p_t = jnp.where(keep, jnp.exp2(s_t * scale - lse_j), 0.0)
                dp_t = dot(vh[keys, :], do_j)
                ds_t = (p_t * (dp_t - delta_j)).astype(BF16)
                dv_add = dot(p_t.astype(BF16), doh[cols, :])
                dk_add = dot(ds_t, qh[cols, :])
                if k == j:
                    dv[keys, :] = dv_add
                    dk[keys, :] = dk_add
                else:
                    dv[keys, :] += dv_add
                    dk[keys, :] += dk_add
                acc = acc + dot(mix[pl.ds(krow, HEAD_DIM), keys], ds_t)
            dmix[drow(0, i), cols] = (acc * SCORE_SCALE).astype(BF16)
            if full and j in (2, 5):
                @pl.when(i == 1)
                def _():
                    sums.add_inner(0, (0,) if j == 2 else (1,))
            if full and j == 3:
                @pl.when(i == 2)
                def _():
                    sums.add_inner(0, (2,))
                    sums.add_across(0, (0,))
        dmix[drow(1, i), :] = (dk[...] * SCORE_SCALE).T.astype(BF16)
        dmix[drow(2, i), :] = dv[...].T.astype(BF16)
        return 0

    lax.fori_loop(0, heads, one_head, 0)
    for load in loads[5:]:
        load.wait()

    def rows_of(s):
        return pl.ds(mult(s * rows, rows), rows)

    def part_of(s):
        return dot_tn(dmix[:, pl.ds(mult(s * rows, 128), rows)], wt[...])

    slot, inner = h - 2 * at["half"], 1 + at["half"]
    at_inner = h == inner
    ways = (1 - at["half"], at["half"])
    length = rows // PIECES
    swaps = []
    for k in range(2):
        partial[k] = part_of(2 * ways[k] + 1 - core).astype(BF16)
        swaps.append(remote(partial.at[k], arrive.at[k], sw_send.at[k], sw_recv.at[k], (sib, h)))
        swaps[-1].start()

    def far_in(q):
        here = slice(q * length, (q + 1) * length)
        return remote(summed.at[0, here], ref.far.at[here], ref.far_send.at[q], ref.far_recv.at[q], (dp, inner))

    def far_out(q):
        here = slice(q * length, (q + 1) * length)
        return remote(
            summed.at[0, here], arrive2.at[0, here], ref.far_send.at[q], ref.out_recv.at[q],
            (at["served"], 2 * ways[0] + core),
        )

    def near_remote():
        return remote(summed.at[1], arrive2.at[slot], fin_send, fin_recv.at[slot], (at["served"], 2 * ways[1] + core))

    def near_local():
        return pltpu.make_async_copy(summed.at[1], arrive2.at[slot], fin_local)

    stays = jnp.logical_and(core == at["half"], h == 2 * ways[1] + core)
    if full:
        sums.add_first(1)
        sums.add_first(2)
        sums.add_across(0, (1, 2))
    for k in range(2):
        mine = part_of(2 * ways[k] + core)
        swaps[k].wait_recv()
        summed[k] = (mine + arrive[k].astype(F32)).astype(BF16)
        if k == 0:
            @pl.when(jnp.logical_not(at_inner))
            def _():
                for q in range(PIECES):
                    far_in(q).start()
        else:
            @pl.when(stays)
            def _():
                near_local().start()

            @pl.when(jnp.logical_not(stays))
            def _():
                near_remote().start()

    def pass_on():
        @pl.when(at_inner)
        def _():
            for q in range(PIECES):
                here = slice(q * length, (q + 1) * length)
                far_in(q).wait_recv()
                summed[0, here] = (summed[0, here].astype(F32) + ref.far[here].astype(F32)).astype(BF16)
                far_out(q).start()

    vec, gq = ref.vec, ref.gq
    first = slot * 2 * part + core * 128
    vec[0:8, :] = ref.vec_in[...]
    vec[8:16, :] = jnp.zeros((8, width), F32)
    small = width // 8
    gain_sum = jnp.zeros((1, width), F32)
    bias_sum = jnp.zeros((1, width), F32)
    for p in range(3):
        d_cols = dmix[p * 256 : (p + 1) * 256, :]
        tok_sum = jnp.sum(d_cols.astype(F32), axis=1, keepdims=True) * grad_scale
        w_cols = wt[p * 256 : (p + 1) * 256, :].astype(F32)
        res = dot_nt(d_cols, xgt[...]) * grad_scale
        gain_sum = gain_sum + jnp.sum(w_cols * res, axis=0, keepdims=True)
        bias_sum = bias_sum + jnp.sum(w_cols * tok_sum, axis=0, keepdims=True)
        if p != 1:
            vec[10 + p // 2 : 11 + p // 2, pl.ds(mult(first, 128), 256)] = jnp.broadcast_to(tok_sum, (256, 128)).T[:1]
        res = res.astype(BF16).T
        for k in range(8):
            gq[k % 2, k // 2, p * small : (p + 1) * small, :] = res[k * small : (k + 1) * small]
    vec[8:9, :] = (gain_sum - row(ref.bias) * bias_sum) / row(ref.gain)
    vec[9:10, :] = bias_sum
    if full:
        sums.vectors_first()
        sums.heads_first()
        sums.heads_second()
        sums.vectors_second()
        sums.add_second(1)
    pass_on()
    if full:
        sums.add_second(2)
        sums.heads_third()
        sums.add_inner(1)
        sums.vectors_third()
        sums.add_inner(2)
        sums.add_across(1)

    owner_far = core != at["half"]

    @pl.when(owner_far)
    def _():
        for q in range(PIECES):
            far = slice(q * length, (q + 1) * length)
            remote(
                summed.at[0, far], arrive2.at[0, far], ref.far_send.at[q], ref.out_recv.at[q], (sib, h)
            ).wait_recv()

    @pl.when(jnp.logical_not(owner_far))
    def _():
        for k in range(2):
            from_me = jnp.logical_and(slot == k, lax.rem(h, 2) == core)

            @pl.when(from_me)
            def _():
                pltpu.make_async_copy(summed.at[1], arrive2.at[k], fin_local).wait()

            @pl.when(jnp.logical_not(from_me))
            def _():
                remote(summed.at[1], arrive2.at[k], fin_send, fin_recv.at[k], (sib, h)).wait_recv()

    e = arrive2[0].astype(F32) + arrive2[1].astype(F32)
    n, r = norm_parts(ref.tok[...].astype(F32))
    ref.gtok_o[...] = ref.dmid[...] + norm_back(e, row(ref.gain), n, r)
    if full:
        sums.heads_fourth()
        sums.add_across(2)
        sums.vectors_fourth()
        sums.heads_last()
        sums.vectors_last()
        sums.finish()
    else:
        ref.vec_o[...] = vec[...]
        gq_copy = pltpu.make_async_copy(gq, ref.gq_o, ref.out_sem)
        gq_copy.start()
        gq_copy.wait()
    for k in range(2):
        swaps[k].wait_send()
    for q in range(PIECES):
        far_in(q).wait_send()

    @pl.when(jnp.logical_not(stays))
    def _():
        near_remote().wait_send()


class Sums:
    def __init__(self, ref, at, grad_scale):
        self.ref, self.at = ref, at
        dp, self.h, self.core = at["dp"], at["h"], at["core"]
        self.y, self.x = dp // 4, lax.rem(dp // 2, 2)
        self.flip_x, self.flip_y = dp + 2 - 4 * self.x, dp + 4 - 8 * self.y
        self.flip_xy = self.flip_x + 4 - 8 * self.y
        self.outer = self.h * (3 - self.h) == 0

    def rows_of(self, k):
        length = self.ref.s2f.shape[1] // 2
        return slice(0, self.ref.s2p.shape[0]) if k == 0 else slice((k - 1) * length, k * length)

    def part(self, name, k, *lead):
        return getattr(self.ref, name).at[*lead, self.rows_of(k)]

    def block(self, k, t, across):
        x, y = self.x, self.y
        first, then = (y, x) if k == 2 else (x, y)
        first = 1 - first if across else first
        then = 1 - then if t == 0 else then
        return first * 2 + then if k == 2 else then * 2 + first

    def one(self, k, t):
        return remote(
            self.part("s1f", k, self.block(k, t, True)), self.part("r1f", k, t),
            self.ref.one_send.at[k, t], self.ref.one_recv.at[k, t], (self.flip_y if k == 2 else self.flip_x, self.h),
        )

    def two(self, k):
        return remote(
            self.part("s2f", k, 0), self.part("r2f", k),
            self.ref.two_send.at[k], self.ref.two_recv.at[k], (self.flip_x if k == 2 else self.flip_y, self.h),
        )

    def kept(self, k, t):
        return pltpu.make_async_copy(
            self.part("s1f", k, self.block(k, t, False)), self.part("s2f", k, t), self.ref.kept_sem.at[k, t]
        )

    def first(self):
        for t in range(2):
            for k in range(1, 3):
                self.one(k, t).start()
        came = pltpu.make_async_copy(self.ref.s3p, self.ref.s2p, self.ref.kept_sem.at[0, 0])
        came.start()
        for t in range(2):
            for k in range(1, 3):
                self.kept(k, t).start()
        came.wait()
        self.send_in(0)

    def add_first(self, k):
        ref, rows = self.ref, self.rows_of(k)
        self.kept(k, 0).wait()
        self.one(k, 0).wait_recv()
        ref.s2f[0, rows] = (ref.s2f[0, rows].astype(F32) + ref.r1f[0, rows].astype(F32)).astype(BF16)
        self.two(k).start()

    def add_second(self, k):
        ref, rows = self.ref, self.rows_of(k)
        self.kept(k, 1).wait()
        self.one(k, 1).wait_recv()
        self.two(k).wait_recv()
        ref.s2f[1, rows] = (
            ref.s2f[1, rows].astype(F32) + ref.r1f[1, rows].astype(F32) + ref.r2f[rows].astype(F32)
        ).astype(BF16)
        self.send_in(k)

    def pieces(self, k):
        rows = self.rows_of(k)
        length = (rows.stop - rows.start) // PIECES
        for q in range(PIECES):
            yield k, k * PIECES + q, slice(rows.start + q * length, rows.start + (q + 1) * length)

    def bufs(self, k):
        ref = self.ref
        return (ref.s2p, ref.zap, ref.zbp, ref.ztp) if k == 0 else (ref.s2f.at[1], ref.zaf, ref.zbf, ref.ztf)

    def chain(self, k, m, rows, which):
        ref, h = self.ref, self.h
        s2, za, zb, zt = self.bufs(k)
        dp = self.at["dp"]
        if which == "in":
            return remote(s2.at[rows], za.at[rows], ref.z_send.at[0, m], ref.z_recv.at[0, m], (dp, 1 + h // 2))
        if which == "across":
            return remote(s2.at[rows], zb.at[rows], ref.z_send.at[0, m], ref.z_recv.at[1, m], (dp, 3 - h))
        return remote(zt.at[rows], za.at[rows], ref.z_send.at[1, m], ref.z_recv.at[0, m], (dp, 3 * (h // 2)))

    def send_in(self, k):
        @pl.when(self.outer)
        def _():
            for piece in self.pieces(k):
                self.chain(*piece, "in").start()

    def add_inner(self, k, only=None):
        s2, za, _, _ = self.bufs(k)

        @pl.when(jnp.logical_not(self.outer))
        def _():
            for q, piece in enumerate(self.pieces(k)):
                if only is None or q in only:
                    rows = piece[2]
                    self.chain(*piece, "in").wait_recv()
                    s2[rows] = (s2[rows].astype(F32) + za[rows].astype(F32)).astype(BF16)
                    self.chain(*piece, "across").start()

    def add_across(self, k, only=None):
        s2, _, zb, zt = self.bufs(k)

        @pl.when(jnp.logical_not(self.outer))
        def _():
            for q, piece in enumerate(self.pieces(k)):
                if only is None or q in only:
                    rows = piece[2]
                    self.chain(*piece, "across").wait_recv()
                    zt[rows] = (s2[rows].astype(F32) + zb[rows].astype(F32)).astype(BF16)
                    self.chain(*piece, "out").start()

    def finish(self):
        @pl.when(self.outer)
        def _():
            for k in range(3):
                _, za, _, zt = self.bufs(k)
                for piece in self.pieces(k):
                    self.chain(*piece, "out").wait_recv()
                    zt[piece[2]] = za[piece[2]]

        for k in range(3):
            if k > 0:
                for t in range(2):
                    self.one(k, t).wait_send()
                self.two(k).wait_send()
            for piece in self.pieces(k):
                self.chain(*piece, "in").wait_send()

        @pl.when(jnp.logical_not(self.outer))
        def _():
            for k in range(3):
                for piece in self.pieces(k):
                    self.chain(*piece, "out").wait_send()

    def swap(self):
        ref, core = self.ref, self.core
        return remote(ref.gq.at[1 - core], ref.gq_in, ref.q_send.at[0], ref.q_recv.at[0], (self.at["sib"], self.h))

    def spread(self, k):
        ref, x, y = self.ref, self.x, self.y
        to = (self.flip_x, self.flip_y, self.flip_xy)[k]
        block = (y * 2 + 1 - x, (1 - y) * 2 + x, (1 - y) * 2 + 1 - x)[k]
        return remote(ref.u.at[block], ref.u_in.at[k], ref.q_send.at[1 + k], ref.q_recv.at[1 + k], (to, self.h))

    def two_apart(self):
        ref, h = self.ref, self.h
        return remote(ref.v, ref.v_in, ref.q_send.at[4], ref.q_recv.at[4], (self.at["dp"], h + 2 - 4 * (h // 2)))

    def next_to(self):
        ref, h = self.ref, self.h
        return remote(ref.w, ref.w_in, ref.q_send.at[5], ref.q_recv.at[5], (self.at["dp"], h + 1 - 2 * lax.rem(h, 2)))

    def heads_first(self):
        self.swap().start()

    def heads_second(self):
        ref, core = self.ref, self.core
        self.swap().wait_recv()
        for j in range(4):
            mine, theirs = ref.gq[core, j].astype(F32), ref.gq_in[j].astype(F32)
            a, b = jnp.where(core == 0, mine, theirs), jnp.where(core == 0, theirs, mine)
            ref.u[j, :, 0:128] = a[:, 0:128].astype(BF16)
            ref.u[j, :, 128:256] = (a[:, 128:256] + b[:, 0:128]).astype(BF16)
            ref.u[j, :, 256:384] = b[:, 128:256].astype(BF16)
        for k in range(3):
            self.spread(k).start()

    def heads_third(self):
        ref = self.ref
        for k in range(3):
            self.spread(k).wait_recv()
        total = ref.u[self.y * 2 + self.x].astype(F32)
        for k in range(3):
            total = total + ref.u_in[k].astype(F32)
        ref.v[...] = total.astype(BF16)
        self.two_apart().start()

    def heads_fourth(self):
        ref = self.ref
        self.two_apart().wait_recv()
        ref.w[...] = (ref.v[...].astype(F32) + ref.v_in[...].astype(F32)).astype(BF16)
        self.next_to().start()

    def heads_last(self):
        self.next_to().wait_recv()
        self.swap().wait_send()
        for k in range(3):
            self.spread(k).wait_send()
        self.two_apart().wait_send()
        self.next_to().wait_send()

    def rows8(self, ref, core):
        return ref.at[pl.ds(mult(core * 8, 8), 8), :]

    def vec_sib(self):
        ref = self.ref
        return remote(
            self.rows8(ref.vec, 1 - self.core), ref.vec_sib, ref.vs_send.at[0], ref.vs_recv.at[0], (self.at["sib"], self.h)
        )

    def vec_z(self, k):
        ref = self.ref
        return remote(
            ref.vec1, ref.vec_z.at[self.h], ref.vz_send.at[k - 1], ref.vz_recv.at[self.h],
            (self.at["dp"], lax.rem(self.h + k, 4)),
        )

    def vec_chips(self, k):
        ref = self.ref
        here = self.y * 2 + self.x
        return remote(
            ref.vec2, ref.vec_xy.at[here], ref.vx_send.at[k], ref.vx_recv.at[here],
            ((self.flip_x, self.flip_y, self.flip_xy)[k], self.h),
        )

    def vec_total(self):
        ref = self.ref
        return remote(
            ref.vec3, self.rows8(ref.vec_all, self.core), ref.vs_send.at[1], ref.vs_recv.at[1], (self.at["sib"], self.h)
        )

    def vectors_first(self):
        self.vec_sib().start()

    def vectors_second(self):
        ref = self.ref
        self.vec_sib().wait_recv()
        ref.vec1[...] = ref.vec[pl.ds(mult(self.core * 8, 8), 8), :] + ref.vec_sib[...]
        for k in range(1, 4):
            self.vec_z(k).start()
        ref.vec_z[self.h] = ref.vec1[...]

    def vectors_third(self):
        ref = self.ref
        for k in range(1, 4):
            other = lax.rem(self.h + k, 4)
            remote(
                ref.vec1, ref.vec_z.at[other], ref.vz_send.at[k - 1], ref.vz_recv.at[other], (self.at["sib"], self.h)
            ).wait_recv()
        ref.vec2[...] = (ref.vec_z[0] + ref.vec_z[1]) + (ref.vec_z[2] + ref.vec_z[3])
        for k in range(3):
            self.vec_chips(k).start()
        ref.vec_xy[self.y * 2 + self.x] = ref.vec2[...]

    def vectors_fourth(self):
        ref, x, y = self.ref, self.x, self.y
        others = (y * 2 + 1 - x, (1 - y) * 2 + x, (1 - y) * 2 + 1 - x)
        for k in range(3):
            remote(
                ref.vec2, ref.vec_xy.at[others[k]], ref.vx_send.at[k], ref.vx_recv.at[others[k]],
                (self.at["sib"], self.h),
            ).wait_recv()
        ref.vec3[...] = (ref.vec_xy[0] + ref.vec_xy[1]) + (ref.vec_xy[2] + ref.vec_xy[3])
        self.vec_total().start()
        ref.vec_all[pl.ds(mult(self.core * 8, 8), 8), :] = ref.vec3[...]

    def vectors_last(self):
        ref = self.ref
        self.vec_total().wait_recv()
        ref.vec_o[...] = ref.vec_all[...]
        self.vec_sib().wait_send()
        self.vec_total().wait_send()
        for k in range(1, 4):
            self.vec_z(k).wait_send()
        for k in range(3):
            self.vec_chips(k).wait_send()


def attend_back(
    mix, xgt, ot, lse, start, d_ot, wt, d_middle, tokens, gain, bias, vecs, g_proj, g_fc, grad_scale,
    full,
):
    rows, width = tokens.shape
    part, group = width // 4, 4 * rows
    small, half = width // 8, width // 2
    dma = pltpu.SemaphoreType.DMA
    ins = [
        ("mix_h", mix, ANY), ("xgt_h", xgt, ANY), ("ot_h", ot, ANY), ("lse_h", lse, ANY), ("start_h", start, ANY),
        ("do_h", d_ot, ANY), ("wt_h", wt, ANY), ("dmid_h", d_middle, ANY), ("tok_h", tokens, ANY),
        ("gain", gain, VMEM), ("bias", bias, VMEM), ("vec_in", vecs, VMEM),
    ]
    outs = [("gtok_o", (rows, width), F32, VMEM), ("vec_o", (16, width), F32, VMEM)]
    gq_shape = (2, 4, 3 * small, 256)
    scratch = [
        ("mix", (3 * part, group), BF16), ("xgt", (width, group), BF16), ("ot", (part, group), BF16),
        ("do_t", (part, group), BF16), ("wt", (3 * 256, width), BF16), ("delta", (8, group), F32),
        ("kh", (group, HEAD_DIM), BF16), ("vh", (group, HEAD_DIM), BF16), ("qh", (group, HEAD_DIM), BF16),
        ("doh", (group, HEAD_DIM), BF16), ("dk", (group, HEAD_DIM), F32), ("dv", (group, HEAD_DIM), F32),
        ("dmix", (3 * 256, group), BF16), ("partial", (2, rows, width), BF16), ("summed", (2, rows, width), BF16),
        ("arrive", (2, rows, width), BF16), ("arrive2", (2, rows, width), BF16), ("far", (rows, width), BF16), ("gq", gq_shape, BF16),
        ("vec", (16, width), F32), ("lse", lse.shape, F32), ("start", start.shape, jnp.int32),
        ("dmid", (rows, width), F32), ("tok", (rows, width), BF16),
    ]
    sems = [
        ("in_sem", (9,)), ("sw_send", (2,)), ("sw_recv", (2,)), ("fin_send", ()), ("fin_recv", (2,)), ("fin_local", ()),
        ("far_send", (PIECES,)), ("far_recv", (PIECES,)), ("out_recv", (PIECES,)),
    ]
    if full:
        ins += [("s3p", g_proj, ANY), ("s1f", g_fc, ANY)]
        outs += [
            ("ztp", (half, width), BF16, VMEM), ("ztf", (half + small, width), BF16, VMEM),
            ("w", (3 * small, half), BF16, VMEM), ("w_in", (3 * small, half), BF16, VMEM),
        ]
        scratch += [(name, (half, width), BF16) for name in ("s2p", "zap", "zbp")]
        scratch += [(name, (2, half + small, width), BF16) for name in ("r1f", "s2f")]
        scratch += [(name, (half + small, width), BF16) for name in ("r2f", "zaf", "zbf")]
        scratch += [
            ("gq_in", gq_shape[1:], BF16), ("u", (4, 3 * small, half), BF16), ("u_in", (3, 3 * small, half), BF16),
            ("v", (3 * small, half), BF16), ("v_in", (3 * small, half), BF16),
            ("vec_sib", (8, width), F32), ("vec1", (8, width), F32), ("vec2", (8, width), F32), ("vec3", (8, width), F32),
            ("vec_z", (4, 8, width), F32), ("vec_xy", (4, 8, width), F32), ("vec_all", (16, width), F32),
        ]
        sems += [
            ("one_send", (3, 2)), ("one_recv", (3, 2)), ("two_send", (3,)), ("two_recv", (3,)), ("kept_sem", (3, 2)),
            ("z_send", (2, 3 * PIECES)), ("z_recv", (2, 3 * PIECES)), ("q_send", (6,)), ("q_recv", (6,)),
            ("vs_send", (2,)), ("vs_recv", (2,)), ("vz_send", (3,)), ("vz_recv", (4,)), ("vx_send", (3,)), ("vx_recv", (4,)),
        ]
    else:
        outs += [("gq_o", gq_shape, BF16, ANY)]
        sems += [("out_sem", ())]
    names = tuple(item[0] for item in ins + outs + scratch + sems)
    return pl.pallas_call(
        functools.partial(back_kernel, grad_scale, full, names),
        out_shape=tuple(jax.ShapeDtypeStruct(shape, kind) for _, shape, kind, _ in outs),
        in_specs=[spec for _, _, spec in ins],
        out_specs=tuple(spec for _, _, _, spec in outs),
        scratch_shapes=[pltpu.VMEM(shape, kind) for _, shape, kind in scratch] + [dma(shape) for _, shape in sems],
        compiler_params=pltpu.CompilerParams(
            collective_id=2, has_side_effects=True, vmem_limit_bytes=60 << 20
        ),
        name="attend_back",
    )(*(array for _, array, _ in ins))


def emit_kernel(names, *refs):
    ref = types.SimpleNamespace(**dict(zip(names, refs, strict=True)))
    through = ((ref.out, ref.out_o), (ref.gtok, ref.gtok_o))
    loads = [pltpu.make_async_copy(src, ref.buf.at[k], ref.sem.at[k]) for k, (src, _) in enumerate(through)]
    stores = [pltpu.make_async_copy(ref.buf.at[k], dst, ref.sem.at[k]) for k, (_, dst) in enumerate(through)]
    for load in loads:
        load.start()
    half, width = ref.ztp.shape
    small = ref.gout_o.shape[0]
    odd = lax.rem(lax.axis_index("head"), 2)
    ref.gproj_o[...] = ref.ztp[...].astype(F32)
    ref.gfc_o[...] = ref.ztf[0:half, :].astype(F32).T
    ref.gout_o[...] = ref.ztf[half:, :].astype(F32)
    for p in range(3):
        here = slice(p * small, (p + 1) * small)
        ref.gqkv_o[:, pl.ds(mult((2 * p + odd) * half, 128), half)] = ref.w[here, :].astype(F32)
        ref.gqkv_o[:, pl.ds(mult((2 * p + 1 - odd) * half, 128), half)] = ref.w_in[here, :].astype(F32)
    for load, store in zip(loads, stores):
        load.wait()
        store.start()
    for k, name in enumerate(VECTORS):
        if name and name != "fc_b":
            getattr(ref, name)[...] = ref.vec[k].reshape(width)
    ref.fc_b[...] = jnp.concatenate([ref.vec[4 + k : 5 + k, :] for k in range(4)], axis=1).reshape(4 * width)
    for store in stores:
        store.wait()


VECTORS = ("out_b", "ln2_g", "ln2_b", "proj_b", "fc_b", "", "", "", "ln1_g", "ln1_b", "q_b", "v_b")


def emit(out, gtok, vec, ztp, ztf, w, w_in):
    rows, width = out.shape
    half, small = width // 2, width // 8
    ins = [
        ("out", out, ANY), ("gtok", gtok, ANY), ("vec", vec, VMEM), ("ztp", ztp, VMEM), ("ztf", ztf, VMEM),
        ("w", w, VMEM), ("w_in", w_in, VMEM),
    ]
    outs = [
        ("out_o", (rows, width), ANY), ("gtok_o", (rows, width), ANY), ("ln1_g", (width,), VMEM),
        ("ln1_b", (width,), VMEM), ("gqkv_o", (small, 3 * width), VMEM), ("q_b", (width,), VMEM),
        ("v_b", (width,), VMEM), ("gout_o", (small, width), VMEM), ("out_b", (width,), VMEM),
        ("ln2_g", (width,), VMEM), ("ln2_b", (width,), VMEM), ("gfc_o", (width, half), VMEM),
        ("fc_b", (4 * width,), VMEM), ("gproj_o", (half, width), VMEM), ("proj_b", (width,), VMEM),
    ]
    return pl.pallas_call(
        functools.partial(emit_kernel, tuple(item[0] for item in ins + outs) + ("buf", "sem")),
        out_shape=tuple(jax.ShapeDtypeStruct(shape, F32) for _, shape, _ in outs),
        in_specs=[spec for _, _, spec in ins],
        out_specs=tuple(spec for _, _, spec in outs),
        scratch_shapes=[pltpu.VMEM((2, rows, width), F32), pltpu.SemaphoreType.DMA((2,))],
        compiler_params=pltpu.CompilerParams(vmem_limit_bytes=60 << 20),
        name="emit",
    )(*(array for _, array, _ in ins))


def shards(
    tokens, lengths, ln1_gain, ln1_bias, w_qkv, bias_q, bias_v, w_out, bias_out, ln2_gain, ln2_bias, w_fc, bias_fc,
    w_proj, bias_proj, cotangent,
):
    rows, width = tokens.shape
    device_count = lax.axis_size("dp") * lax.axis_size("head")
    full = lax.axis_size("dp") == 8
    grad_scale = 1.0 / math.sqrt(rows * device_count)
    att, mix, xgt, ot, lse, start, wt = attend(tokens, lengths, ln1_gain, ln1_bias, bias_q, bias_v, w_qkv)
    block_output, d_middle, d_ot, g_fc, g_proj, vecs = mlp(
        att, tokens, cotangent, grad_scale, full, bias_out, ln2_gain, ln2_bias, bias_fc, bias_proj, w_out, w_fc, w_proj
    )
    grad_tokens, vec, *rest = attend_back(
        mix, xgt, ot, lse, start, d_ot, wt, d_middle, tokens, ln1_gain, ln1_bias, vecs, g_proj, g_fc, grad_scale,
        full,
    )
    if full:
        return emit(block_output, grad_tokens, vec, *rest)
    proj_total, fc_total, out_total, qkv_total, vec = sums_by_xla(rest[0], g_proj, g_fc, vec)
    return (
        block_output, grad_tokens, vec[8], vec[9], qkv_total, vec[10], vec[11], out_total, vec[0], vec[1], vec[2],
        fc_total, vec[4:8].reshape(-1), proj_total, vec[3],
    )


def sums_by_xla(gq, g_proj, g_fc, vec):
    _, blocks, length, width = g_proj.shape
    small = width // 8
    whole = g_proj.transpose(1, 0, 2, 3).reshape(2 * blocks * length, width)
    fc = g_fc[:, :, :length].transpose(1, 0, 2, 3).reshape(2 * blocks * length, width).T
    out = g_fc[:, :, length:].transpose(1, 0, 2, 3).reshape(width, width)
    core, odd = lax.rem(lax.axis_index("dp"), 2), lax.rem(lax.axis_index("head"), 2)
    window = gq.reshape(2, 4, 3, small, 256).transpose(1, 0, 3, 2, 4).reshape(width, 3, 256)
    qkv = lax.dynamic_update_slice(
        jnp.zeros((width, 3, width), BF16), window, (0, 0, odd * (width // 2) + core * 128)
    ).reshape(width, 3 * width)

    def reduce_mat(g, dim):
        share = lax.psum_scatter(g, "dp", scatter_dimension=dim, tiled=True)
        return lax.psum(share, "head").astype(F32)

    return reduce_mat(whole, 0), reduce_mat(fc, 1), reduce_mat(out, 0), reduce_mat(qkv, 0), lax.psum(vec, ("dp", "head"))


def solution(mesh):
    rows = P(("dp", "head"), None)
    return jax.shard_map(
        shards,
        mesh=mesh,
        in_specs=(rows, P("dp", None)) + (P(),) * 13 + (rows,),
        out_specs=(
            rows, rows, P(), P(), P("dp", None), P(), P(), P("dp", None), P(), P(), P(), P(None, "dp"), P(),
            P("dp", None), P(),
        ),
        check_vma=False,
    )
```

```python
import functools
import math
import types

import jax
import jax.numpy as jnp
from jax import lax
from jax.experimental import pallas as pl
from jax.experimental.pallas import tpu as pltpu
from jax.sharding import PartitionSpec as P

DP, HEAD = "dp", "head"
HEAD_DIM = 64
EPSILON = 1e-05
DEPTH_SCALE = 1.0 / math.sqrt(12.0)
LOG2E = 1.0 / math.log(2.0)
SCORE_SCALE = HEAD_DIM ** (-0.5)
GELU_K = math.sqrt(2.0 / math.pi)
GELU_A = 0.044715
TEAM = 8
QB = 256
VMEM_LIMIT = 63 << 20
PIECES = 3

INWARD, ACROSS, OUTWARD = range(3)

F32 = jnp.float32
BF16 = jnp.bfloat16
MESH = pl.DeviceIdType.MESH
ANY = pl.BlockSpec(memory_space=pl.ANY)
VMEM = pl.BlockSpec(memory_space=pltpu.VMEM)
SMEM = pl.BlockSpec(memory_space=pltpu.SMEM)


def dot(a, b):
    return jnp.dot(a, b, preferred_element_type=F32)


def dot_nt(a, b):
    return lax.dot_general(a, b, (((1,), (1,)), ((), ())), preferred_element_type=F32)


def dot_tn(a, b):
    return lax.dot_general(a, b, (((0,), (0,)), ((), ())), preferred_element_type=F32)


def mult(x, m):
    return pl.multiple_of(x, m)


def place():
    dp, h = lax.axis_index(DP), lax.axis_index(HEAD)
    core = lax.rem(dp, 2)
    half = h // 2
    return types.SimpleNamespace(
        dp=dp,
        h=h,
        core=core,
        sib=dp + 1 - 2 * core,
        even=dp - core,
        half=half,
        served=dp - core + half,
        block=(h - 2 * half) * 2 + core,
    )


def greet(at, chips=False):
    barrier = pltpu.get_barrier_semaphore()
    me = at.core * 4 + at.h
    others = []
    for k in range(1, TEAM):
        other = lax.rem(me + k, TEAM)
        others.append((at.even + other // 4, lax.rem(other, 4)))
    if chips:
        for k in range(1, 4):
            others.append((lax.rem(at.dp + 2 * k, 8), at.h))
    for other in others:
        pl.semaphore_signal(barrier, inc=1, device_id=other, device_id_type=MESH)
    pl.semaphore_wait(barrier, len(others))


def scoped(body, **buffers):
    pl.run_scoped(
        lambda *refs: body(named(buffers, refs)), *(pltpu.VMEM(shape, kind) for shape, kind in buffers.values())
    )


def named(names, refs):
    return types.SimpleNamespace(**dict(zip(names, refs, strict=True)))


def remote(src, dst, send, recv, device):
    return pltpu.make_async_remote_copy(
        src_ref=src, dst_ref=dst, send_sem=send, recv_sem=recv, device_id=device, device_id_type=MESH
    )


def row(vec):
    return vec[...].reshape(1, vec.shape[0])


def norm_parts(v):
    center = jnp.mean(v, axis=-1, keepdims=True)
    cent = v - center
    r = lax.rsqrt(jnp.mean(cent * cent, axis=-1, keepdims=True) + EPSILON)
    return cent * r, r


def norm_back(e, gain, n, r):
    ea = e * gain
    return r * (ea - jnp.mean(ea, axis=-1, keepdims=True) - n * jnp.mean(ea * n, axis=-1, keepdims=True))


def block_kernel(grad_scale, full, names, *refs):
    ref = named(names, refs)
    at = place()
    rows, width = ref.tok.shape
    group, part, chunks = 4 * rows, width // 4, ref.gfc.shape[1]
    heads = part // HEAD_DIM
    sums = Sums(ref, at) if full else None
    tok_copy = pltpu.make_async_copy(ref.tok_h, ref.tok, ref.in_sem.at[0])
    tok_copy.start()

    @pl.when(at.core != at.half)
    def _():
        ref.arrive2[1] = jnp.zeros((rows, width), BF16)

    scoped(
        lambda buf: attend(ref, buf, at, tok_copy, full),
        xn=((rows, width), BF16), wwin=((3, width, 256), BF16), brow=((8, width), F32),
        bcol=((3, 256, 128), F32), kh=((group, HEAD_DIM), BF16), scores=((group, QB), F32),
    )
    scoped(
        lambda buf: feed_forward(ref, buf, at, sums, grad_scale),
        cot=((rows, width), BF16), w_out=((width, width), BF16), w_fc=((2, width, width), BF16),
        w_proj=((2, width, width), BF16), brow=((8, chunks * width), F32),
        dfc=((chunks, rows, width), BF16), gproj=((2, chunks, width // 2, width), BF16),
        out=((rows, width), F32),
    )
    scoped(
        lambda buf: attend_back(ref, buf, at, sums, grad_scale),
        kh=((heads, group, HEAD_DIM), BF16), vh=((heads, group, HEAD_DIM), BF16),
        qh=((heads, group, HEAD_DIM), BF16), doh=((heads, group, HEAD_DIM), BF16),
        dk=((heads, group, HEAD_DIM), F32), dv=((heads, group, HEAD_DIM), F32),
        dq=((heads, HEAD_DIM, group), F32), delta=((8 * heads, group), F32), dmix=((3 * 256, group), BF16), partial=((2, rows, width), BF16),
        summed=((2, rows, width), BF16), gtok=((rows, width), F32),
        gq=((2, 4, 3 * (width // 8), 256), BF16), u=((4, 3 * (width // 8), width // 2), BF16),
    )


def attend(ref, buf, at, tok_copy, full):
    dp, h, core, sib = at.dp, at.h, at.core, at.sib
    rows, width = ref.tok.shape
    group, part = 4 * rows, width // 4
    heads = part // HEAD_DIM
    xn, xg, xgt, wwin, wt, mix, ot, lens = buf.xn, ref.xg, ref.xgt, buf.wwin, ref.wt, ref.mix, ref.ot, ref.lens
    collects = core == at.half
    first = (h - 2 * at.half) * 2 * part + core * 128
    shift = mult(64 * core, 64)
    ag_send, ag_recv, fw_send, st_sem, w_sem = ref.ag_send, ref.ag_recv, ref.fw_send, ref.st_sem, ref.w_sem
    for p in range(3):
        pltpu.make_async_copy(
            ref.w_qkv.at[:, pl.ds(mult(p * width + first, 128), 256)], wwin.at[p], w_sem.at[p]
        ).start()
    greet(at, full)
    tok_copy.wait()
    n, _ = norm_parts(ref.tok[...].astype(F32))
    xn[...] = (n * row(ref.gain1) + row(ref.bias1)).astype(BF16)

    inner, outer = 1 + core, 3 * core
    at_inner, at_outer = h == inner, h == outer

    length = rows // PIECES

    def piece(ref, s, q):
        return ref.at[pl.ds(mult(s * rows + q * length, length), length), :]

    def to_inner(q):
        return remote(piece(xn, 0, q), piece(xg, h, q), ag_send.at[q], ag_recv.at[h, q], (dp, inner))

    def to_outer(k, s, q):
        src = piece(xn, 0, q) if k == 0 else piece(xg, s, q)
        return remote(src, piece(xg, s, q), ag_send.at[k * PIECES + q], ag_recv.at[s, q], (dp, outer))

    def to_sib(d, s, q):
        src = piece(xn, 0, q) if d == 0 else piece(xg, s, q)
        return remote(src, piece(xg, s, q), fw_send.at[d * PIECES + q], ag_recv.at[s, q], (sib, h))

    @pl.when(at_inner)
    def _():
        for q in range(PIECES):
            to_outer(0, h, q).start()

    @pl.when(jnp.logical_not(at_inner))
    def _():
        for q in range(PIECES):
            to_inner(q).start()

    @pl.when(collects)
    def _():
        for q in range(PIECES):
            to_sib(0, h, q).start()
        xg[pl.ds(mult(h * rows, rows), rows), :] = xn[...]

    places = lax.broadcasted_iota(jnp.int32, (8, group), 1)
    begin = jnp.zeros((8, group), jnp.int32)
    edge = lens[0, 0]
    for k in range(1, lens.shape[1] + 1):
        begin = jnp.where(places >= edge, edge, begin)
        if k < lens.shape[1]:
            edge = edge + lens[0, k]
    ref.start_mine[...] = begin.astype(F32)
    st_copy = remote(ref.start_mine, ref.start_sib, st_sem.at[0], st_sem.at[1], (sib, h))
    st_copy.start()

    for p in range(3):
        pltpu.make_async_copy(wwin.at[p], wwin.at[p], w_sem.at[p]).wait()
        wt[p * 256 : (p + 1) * 256, :] = wwin[p].T
    for p, vec in ((0, ref.bias_q), (2, ref.bias_v)):
        buf.brow[...] = jnp.broadcast_to(row(vec), (8, width))
        buf.bcol[p] = jnp.broadcast_to(buf.brow[0:1, pl.ds(mult(first, 128), 256)], (128, 256)).T
    buf.bcol[1] = jnp.zeros((256, 128), F32)

    low = 1 - at.half
    order = (h, low * (1 - h) + (1 - low) * (5 - h), 1 + low, 3 * low)

    def project(s):
        here = xg[pl.ds(mult(s * rows, rows), rows), :]
        xgt[:, pl.ds(mult(s * rows, 128), rows)] = here.T
        for p in range(3):
            res = dot_nt(wt[pl.ds(mult(p * 256 + shift, 64), part), :], here) + buf.bcol[p, pl.ds(shift, part), :][:, :1]
            mix[p * part : (p + 1) * part, pl.ds(mult(s * rows, 128), rows)] = res.astype(BF16)

    @pl.when(jnp.logical_not(collects))
    def _():
        for q in range(PIECES):
            to_sib(1, h, q).wait_recv()

    project(h)
    for q in range(PIECES):
        for d in range(1, 4):
            s = order[d]
            to_sib(d, s, q).wait_recv()

            @pl.when(collects)
            def _():
                to_sib(d, s, q).start()

            if d > 1:
                @pl.when(at_inner)
                def _():
                    to_outer(d - 1, s, q).start()

            if q == PIECES - 1:
                project(s)
    st_copy.wait_recv()
    ref.start[...] = jnp.where(collects, ref.start_mine[...], ref.start_sib[...]).astype(jnp.int32)
    scale = SCORE_SCALE * LOG2E

    def one_head(i, _):
        qrow, krow, vrow = (mult(p * part + i * HEAD_DIM, HEAD_DIM) for p in range(3))
        buf.kh[...] = mix[pl.ds(krow, HEAD_DIM), :].T
        for j in range(group // QB):
            cols = slice(j * QB, (j + 1) * QB)
            q_t = mix[pl.ds(qrow, HEAD_DIM), cols]
            begins = ref.start[0:1, cols]
            top = jnp.full((1, QB), -jnp.inf, F32)
            for k in range(j + 1):
                s_t = dot(buf.kh[k * QB : (k + 1) * QB, :], q_t)
                key = lax.broadcasted_iota(jnp.int32, (QB, QB), 0)
                keep = key >= begins - k * QB
                if k == j:
                    keep = jnp.logical_and(keep, key <= lax.broadcasted_iota(jnp.int32, (QB, QB), 1))
                s_t = jnp.where(keep, s_t, -1e30)
                buf.scores[k * QB : (k + 1) * QB, :] = s_t
                top = jnp.maximum(top, jnp.max(s_t, axis=0, keepdims=True))
            top = top * scale
            total = jnp.zeros((1, QB), F32)
            acc = jnp.zeros((HEAD_DIM, QB), F32)
            for k in range(j + 1):
                p_t = jnp.exp2(buf.scores[k * QB : (k + 1) * QB, :] * scale - top)
                total = total + jnp.sum(p_t, axis=0, keepdims=True)
                acc = acc + dot(mix[pl.ds(vrow, HEAD_DIM), k * QB : (k + 1) * QB], p_t.astype(BF16))
            ot[pl.ds(qrow, HEAD_DIM), cols] = (acc / total).astype(BF16)
            ref.lse[pl.ds(mult(i * 8, 8), 8), cols] = jnp.broadcast_to(top + jnp.log2(total), (8, QB))
            for s in range(4):
                if j == ((s + 1) * rows - 1) // QB:
                    send_attended(ref, at, i, s)
        return 0

    lax.fori_loop(0, heads, one_head, 0)

    @pl.when(at_inner)
    def _():
        for q in range(PIECES):
            for d in range(1, 4):
                to_outer(d - 1, order[d], q).wait_send()

    @pl.when(jnp.logical_not(at_inner))
    def _():
        for q in range(PIECES):
            to_inner(q).wait_send()

    @pl.when(collects)
    def _():
        for q in range(PIECES):
            for d in range(4):
                to_sib(d, order[d], q).wait_send()

    st_copy.wait_send()


def attended_ends(ref, at, i, s):
    rows, width = ref.tok.shape
    src = ref.ot.at[pl.ds(mult(i * HEAD_DIM, HEAD_DIM), HEAD_DIM), pl.ds(s * rows, rows)]
    dst = ref.att.at[pl.ds(mult(at.block * (width // 4) + i * HEAD_DIM, HEAD_DIM), HEAD_DIM), :]
    return src, dst


def attended_stays(at, s):
    return jnp.logical_and(at.core == at.half, at.h == s)


def attended_local(ref, at, i, s):
    return pltpu.make_async_copy(*attended_ends(ref, at, i, s), ref.at_local.at[i])


def attended_remote(ref, at, i, s):
    src, dst = attended_ends(ref, at, i, s)
    heads = ref.at_local.shape[0]
    return remote(
        src, dst, ref.at_send.at[i * 4 + s], ref.at_recv.at[at.block * heads + i], (at.served, s)
    )


def send_attended(ref, at, i, s):
    @pl.when(attended_stays(at, s))
    def _():
        attended_local(ref, at, i, s).start()

    @pl.when(jnp.logical_not(attended_stays(at, s)))
    def _():
        attended_remote(ref, at, i, s).start()


def wait_attended(ref, at):
    rows, width = ref.tok.shape
    part, heads = width // 4, ref.at_local.shape[0]
    for i in range(heads):
        for s in range(4):
            @pl.when(attended_stays(at, s))
            def _():
                attended_local(ref, at, i, s).wait()

            @pl.when(jnp.logical_not(attended_stays(at, s)))
            def _():
                attended_remote(ref, at, i, s).wait_send()
        for b in range(4):
            dst = ref.att.at[pl.ds(b * part + i * HEAD_DIM, HEAD_DIM), :]
            src = ref.ot.at[pl.ds(i * HEAD_DIM, HEAD_DIM), pl.ds(0, rows)]

            @pl.when(jnp.logical_not(jnp.logical_and(at.core == at.half, at.block == b)))
            def _():
                remote(
                    src, dst, ref.at_send.at[i * 4], ref.at_recv.at[b * heads + i], (at.sib, at.h)
                ).wait_recv()


def feed_forward(ref, buf, at, sums, grad_scale):
    h, core = at.h, at.core
    rows, width = ref.tok.shape
    part = width // 4
    chunks = ref.gfc.shape[1]
    paired = sums is not None
    tok, att, cot, vec = ref.tok, ref.att, buf.cot, ref.vec
    w_out, w_fc, w_proj, brow, dfc, dat = buf.w_out, buf.w_fc, buf.w_proj, buf.brow, buf.dfc, ref.dat
    gfc, gproj, gfc_in, gproj_in, r1, s2, r2, s3 = (
        ref.gfc, buf.gproj, ref.gfc_in, ref.gproj_in, ref.r1, ref.s2, ref.r2, ref.s3
    )
    pair_send, pair_recv, one_send, one_recv, two_send, two_recv = (
        ref.pair_send, ref.pair_recv, ref.p1_send, ref.p1_recv, ref.p2_send, ref.p2_recv
    )
    cot_copy = pltpu.make_async_copy(ref.cot_h, cot, ref.in_sem.at[1])
    wo_copy = pltpu.make_async_copy(ref.w_out_h, w_out, ref.in_sem.at[2])
    cot_copy.start()
    wo_copy.start()

    def ff_copy(step, which):
        slot, here = step % 2, pl.ds(mult(order[step] * width, 128), width)
        if which == 0:
            return pltpu.make_async_copy(ref.w_fc_h.at[:, here], w_fc.at[slot], ref.ff_sem.at[0, slot])
        return pltpu.make_async_copy(ref.w_proj_h.at[here, :], w_proj.at[slot], ref.ff_sem.at[1, slot])

    half_rows = width // 2
    small = width // 8
    y, x = at.dp // 4, lax.rem(at.dp // 2, 2)

    def pair_copy(ref, into, k, j):
        return remote(ref.at[1 - core, j], into.at[j], pair_send.at[k, j], pair_recv.at[k, j], (at.sib, h))

    def pair_add(ref, into, k, j):
        pair_copy(ref, into, k, j).wait_recv()
        ref[core, j] = (ref[core, j].astype(F32) + into[j].astype(F32)).astype(BF16)

    if paired:
        order = [(1 - y) * 2 + 1 - x, y * 2 + 1 - x, (1 - y) * 2 + x, y * 2 + x]
    else:
        order = list(range(chunks))
    quarter = half_rows // 2
    flips = (at.dp + 2 - 4 * x, h), (at.dp + 4 - 8 * y, h)

    def halves(k):
        return slice(k * quarter, (k + 1) * quarter)

    def one(k, t):
        j = order[0] if t == 0 else order[1 + k]
        return remote(gproj.at[core, j, halves(k)], r1.at[k, t], one_send.at[k, t], one_recv.at[k, t], flips[k])

    def two(k):
        return remote(s2.at[k], r2.at[k], two_send.at[k], two_recv.at[k], flips[1 - k])

    def first_sum(k):
        one(k, 0).wait_recv()
        s2[k] = (gproj[core, order[2 - k], halves(k)].astype(F32) + r1[k, 0].astype(F32)).astype(BF16)
        two(k).start()

    def proj_sums(step):
        if not paired:
            return
        pair_add(gproj, gproj_in, 0, order[step])
        if step == 0:
            one(0, 0).start()
            one(1, 0).start()
        elif step == 1:
            one(0, 1).start()
        elif step == 2:
            first_sum(1)
            first_sum(0)
            one(1, 1).start()
        else:
            s3[...] = gproj[core, order[3]]

    for step in range(2):
        for which in range(2):
            ff_copy(step, which).start()
    vec[...] = jnp.zeros_like(vec)
    brow[...] = jnp.broadcast_to(row(ref.b_fc), brow.shape)
    cot_copy.wait()
    dy = cot[...].astype(F32)
    d_proj = (DEPTH_SCALE * dy).astype(BF16)
    wo_copy.wait()
    wait_attended(ref, at)
    middle = tok[...].astype(F32) + DEPTH_SCALE * (dot_tn(att[...], w_out[...]) + row(ref.b_out))
    n, r = norm_parts(middle)
    second = (n * row(ref.gain2) + row(ref.bias2)).astype(BF16)
    result = middle + DEPTH_SCALE * row(ref.b_proj)
    d_second = jnp.zeros((rows, width), F32)
    vec[3:4, :] = jnp.sum(dy, axis=0, keepdims=True) * (DEPTH_SCALE * grad_scale)
    for step, j in enumerate(order):
        slot = step % 2
        ff_copy(step, 0).wait()
        u = dot(second, w_fc[slot]) + brow[0:1, pl.ds(mult(j * width, 128), width)]
        u2 = u * u
        th = jnp.tanh(GELU_K * u * (1.0 + GELU_A * u2))
        half = 0.5 * (1.0 + th)
        slope = half + 0.5 * u * (1.0 - th * th) * (GELU_K * (1.0 + 3.0 * GELU_A * u2))
        hidden = (u * half).astype(BF16)
        ff_copy(step, 1).wait()
        result = result + DEPTH_SCALE * dot(hidden, w_proj[slot])
        d_pre = dot_nt(d_proj, w_proj[slot]) * slope
        res = (dot_tn(hidden, d_proj) * grad_scale).astype(BF16)
        for k in range(2):
            gproj[k, j] = res[k * half_rows : (k + 1) * half_rows]
        if paired:
            pair_copy(gproj, gproj_in, 0, j).start()
        if step > 0:
            proj_sums(step - 1)
        vec[pl.ds(4 + j, 1), :] = jnp.sum(d_pre, axis=0, keepdims=True) * grad_scale
        d_fc = d_pre.astype(BF16)
        dfc[j] = d_fc
        d_second = d_second + dot_nt(d_fc, w_fc[slot])
        if step + 2 < chunks:
            for which in range(2):
                ff_copy(step + 2, which).start()
    buf.out[...] = result
    out_copy = pltpu.make_async_copy(buf.out, ref.out_o, ref.out_sem.at[0])
    out_copy.start()
    vec[1:2, :] = jnp.sum(d_second * n, axis=0, keepdims=True) * grad_scale
    vec[2:3, :] = jnp.sum(d_second, axis=0, keepdims=True) * grad_scale
    d_middle = dy + norm_back(d_second, row(ref.gain2), n, r)
    ref.dmid[...] = d_middle
    vec[0:1, :] = jnp.sum(d_middle, axis=0, keepdims=True) * (DEPTH_SCALE * grad_scale)
    d_out = (DEPTH_SCALE * d_middle).astype(BF16)
    dat[...] = dot_nt(w_out[...], d_out).astype(BF16)

    send_d_attended(ref, at)

    def fc_sums(step):
        if not paired:
            return
        pair_add(gfc, gfc_in, 1, order[step])
        if step == 0:
            sums.one(1, 0).start()
            sums.one(2, 0).start()
        elif step < 3:
            sums.one(step, 1).start()

    g_out = (dot(att[...], d_out) * grad_scale).astype(BF16)
    for j in range(chunks):
        for k in range(2):
            gfc[k, j, half_rows:, :] = g_out[(2 * j + k) * small : (2 * j + k + 1) * small]
    proj_sums(chunks - 1)
    for step, j in enumerate(order):
        res = (dot_tn(dfc[j], second) * grad_scale).astype(BF16)
        for k in range(2):
            gfc[k, j, :half_rows, :] = res[k * half_rows : (k + 1) * half_rows]
        if paired:
            pair_copy(gfc, gfc_in, 1, j).start()
        if step > 0:
            fc_sums(step - 1)
    fc_sums(chunks - 1)
    if paired:
        for j in order:
            pair_copy(gproj, gproj_in, 0, j).wait_send()
        for k in range(2):
            for t in range(2):
                one(k, t).wait_send()
    else:
        outs = [
            pltpu.make_async_copy(gproj, ref.gproj_o, ref.out_sem.at[1]),
            pltpu.make_async_copy(gfc, ref.gfc_o, ref.out_sem.at[2]),
        ]
        for copy in outs:
            copy.start()
        for copy in outs:
            copy.wait()
    out_copy.wait()


def d_attended_part(at, i):
    b = lax.rem(2 * at.core + i, 4)
    return b, (at.even + lax.rem(b, 2), 2 * at.core + b // 2)


def d_attended_stays(at, i):
    b, _ = d_attended_part(at, i)
    return jnp.logical_and(at.core == lax.rem(b, 2), at.h == 2 * at.core + b // 2)


def d_attended_ends(ref, at, b):
    rows, width = ref.tok.shape
    part = width // 4
    src = ref.dat.at[pl.ds(mult(b * part, HEAD_DIM), part), :]
    return src, ref.do_t.at[:, pl.ds(mult(at.h * rows, 128), rows)]


def d_attended_local(ref, at, i):
    return pltpu.make_async_copy(*d_attended_ends(ref, at, d_attended_part(at, i)[0]), ref.da_local)


def d_attended_remote(ref, at, i):
    b, device = d_attended_part(at, i)
    src, dst = d_attended_ends(ref, at, b)
    return remote(src, dst, ref.da_send.at[i], ref.da_recv.at[at.h], device)


def send_d_attended(ref, at):
    for i in range(4):
        @pl.when(d_attended_stays(at, i))
        def _():
            d_attended_local(ref, at, i).start()

        @pl.when(jnp.logical_not(d_attended_stays(at, i)))
        def _():
            d_attended_remote(ref, at, i).start()


def wait_d_attended(ref, at):
    rows, width = ref.tok.shape
    part = width // 4
    served_here = at.core == at.half
    for i in range(4):
        @pl.when(d_attended_stays(at, i))
        def _():
            d_attended_local(ref, at, i).wait()

        @pl.when(jnp.logical_not(d_attended_stays(at, i)))
        def _():
            d_attended_remote(ref, at, i).wait_send()
    for s in range(4):
        @pl.when(jnp.logical_not(jnp.logical_and(served_here, at.h == s)))
        def _():
            remote(
                ref.dat.at[pl.ds(0, part), :], ref.do_t.at[:, pl.ds(s * rows, rows)], ref.da_send.at[0],
                ref.da_recv.at[s], (at.sib, at.h),
            ).wait_recv()


def attend_back(ref, buf, at, sums, grad_scale):
    full = sums is not None
    dp, h, core, sib = at.dp, at.h, at.core, at.sib
    rows, width = ref.tok.shape
    part, group = width // 4, 4 * rows
    heads = part // HEAD_DIM
    mix, do_t, ot, xgt, wt, lse, start = ref.mix, ref.do_t, ref.ot, ref.xgt, ref.wt, ref.lse, ref.start
    delta, kh, vh, qh, doh, dk, dv, dmix = buf.delta, buf.kh, buf.vh, buf.qh, buf.doh, buf.dk, buf.dv, buf.dmix
    dq = buf.dq
    partial, summed, arrive, arrive2 = buf.partial, buf.summed, ref.arrive, ref.arrive2
    sw_send, sw_recv, fin_send, fin_recv, fin_local = (
        ref.sw_send, ref.sw_recv, ref.fin_send, ref.fin_recv, ref.fin_local
    )
    dmix[...] = jnp.zeros_like(dmix)
    wait_d_attended(ref, at)
    scale = SCORE_SCALE * LOG2E

    def drow(p, i):
        return pl.ds(mult(p * 256 + (core + i) * HEAD_DIM, HEAD_DIM), HEAD_DIM)

    half = at.half
    blocks = group // QB
    far_cols = pl.ds(mult((1 - half) * (group // 2), 128), group // 2)
    near_cols = pl.ds(mult(half * (group // 2), 128), group // 2)

    def ready(i):
        qrow, krow, vrow = (mult(p * part + i * HEAD_DIM, HEAD_DIM) for p in range(3))
        d_head = do_t[pl.ds(qrow, HEAD_DIM), :]
        delta[pl.ds(mult(i * 8, 8), 8), :] = jnp.broadcast_to(
            jnp.sum(d_head.astype(F32) * ot[pl.ds(qrow, HEAD_DIM), :].astype(F32), axis=0, keepdims=True), (8, group)
        )
        qh[i] = mix[pl.ds(qrow, HEAD_DIM), :].T
        kh[i] = mix[pl.ds(krow, HEAD_DIM), :].T
        vh[i] = mix[pl.ds(vrow, HEAD_DIM), :].T
        doh[i] = d_head.T
        dq[i] = jnp.zeros((HEAD_DIM, group), F32)
        dk[i] = jnp.zeros((group, HEAD_DIM), F32)
        dv[i] = jnp.zeros((group, HEAD_DIM), F32)

    def pair(i, o, t):
        k = half * o + (1 - half) * (blocks - 1 - o - t)
        q = half * (o + t) + (1 - half) * (blocks - 1 - o)
        keys, cols = pl.ds(mult(k * QB, QB), QB), pl.ds(mult(q * QB, QB), QB)
        qrow, krow = (mult(p * part + i * HEAD_DIM, HEAD_DIM) for p in range(2))
        stats = pl.ds(mult(i * 8, 8), 8)
        s_t = dot(kh[i, keys, :], mix[pl.ds(qrow, HEAD_DIM), cols])
        key = lax.broadcasted_iota(jnp.int32, (QB, QB), 0)
        keep = key >= start[0:1, cols] - k * QB
        if t == 0:
            keep = jnp.logical_and(keep, key <= lax.broadcasted_iota(jnp.int32, (QB, QB), 1))
        p_t = jnp.where(keep, jnp.exp2(s_t * scale - lse[stats, cols][0:1]), 0.0)
        dp_t = dot(vh[i, keys, :], do_t[pl.ds(qrow, HEAD_DIM), cols])
        ds_t = (p_t * (dp_t - delta[stats, cols][0:1])).astype(BF16)
        dv[i, keys, :] += dot(p_t.astype(BF16), doh[i, cols, :])
        dk[i, keys, :] += dot(ds_t, qh[i, cols, :])
        dq[i, :, cols] += dot(mix[pl.ds(krow, HEAD_DIM), keys], ds_t)

    def done(i, cols):
        dmix[drow(0, i), cols] = (dq[i, :, cols] * SCORE_SCALE).astype(BF16)
        dmix[drow(1, i), cols] = (dk[i, cols, :] * SCORE_SCALE).T.astype(BF16)
        dmix[drow(2, i), cols] = dv[i, cols, :].T.astype(BF16)

    def far_head(i, _):
        ready(i)
        for o in range(blocks // 2):
            for t in range(blocks - o):
                pair(i, o, t)
            if full and o == 2:
                @pl.when(i == 0)
                def _():
                    sums.proj_last()

                @pl.when(i == 2)
                def _():
                    sums.add_inner(0, (0,))
        done(i, far_cols)
        return 0

    def near_head(i, _):
        for o in range(blocks // 2, blocks):
            for t in range(blocks - o):
                pair(i, o, t)
        done(i, near_cols)
        return 0

    def part_of(s):
        return dot_tn(dmix[:, pl.ds(mult(s * rows, 128), rows)], wt[...])

    slot, inner = h - 2 * at.half, 1 + at.half
    at_inner = h == inner
    ways = (1 - at.half, at.half)
    length = rows // PIECES
    def pass_on(q):
        @pl.when(at_inner)
        def _():
            here = slice(q * length, (q + 1) * length)
            far_in(q).wait_recv()
            summed[0, here] = (summed[0, here].astype(F32) + ref.far[here].astype(F32)).astype(BF16)
            far_out(q).start()

    def swap(k):
        return remote(partial.at[k], arrive.at[k], sw_send.at[k], sw_recv.at[k], (sib, h))

    def own_part(k):
        partial[k] = part_of(2 * ways[k] + 1 - core).astype(BF16)
        swap(k).start()
        mine = part_of(2 * ways[k] + core)
        swap(k).wait_recv()
        summed[k] = (mine + arrive[k].astype(F32)).astype(BF16)

    def far_in(q):
        here = slice(q * length, (q + 1) * length)
        return remote(summed.at[0, here], ref.far.at[here], ref.far_send.at[q], ref.far_recv.at[q], (dp, inner))

    def far_out(q):
        here = slice(q * length, (q + 1) * length)
        return remote(
            summed.at[0, here], arrive2.at[0, here], ref.far_send.at[q], ref.out_recv.at[q],
            (at.served, 2 * ways[0] + core),
        )

    def near_remote():
        return remote(summed.at[1], arrive2.at[slot], fin_send, fin_recv.at[slot], (at.served, 2 * ways[1] + core))

    def near_local():
        return pltpu.make_async_copy(summed.at[1], arrive2.at[slot], fin_local)

    stays = jnp.logical_and(core == at.half, h == 2 * ways[1] + core)
    lax.fori_loop(0, heads, far_head, 0)
    own_part(0)

    @pl.when(jnp.logical_not(at_inner))
    def _():
        for q in range(PIECES):
            far_in(q).start()

    if full:
        sums.add_first(1)
        sums.add_first(2)
        sums.add_inner(0, (1, 2))
    lax.fori_loop(0, heads, near_head, 0)
    vec, gq = ref.vec, buf.gq
    first = slot * 2 * part + core * 128
    small = width // 8
    gain_sum = jnp.zeros((1, width), F32)
    bias_sum = jnp.zeros((1, width), F32)
    for p in range(3):
        d_cols = dmix[p * 256 : (p + 1) * 256, :]
        tok_sum = jnp.sum(d_cols.astype(F32), axis=1, keepdims=True) * grad_scale
        w_cols = wt[p * 256 : (p + 1) * 256, :].astype(F32)
        res = dot_nt(d_cols, xgt[...]) * grad_scale
        gain_sum = gain_sum + jnp.sum(w_cols * res, axis=0, keepdims=True)
        bias_sum = bias_sum + jnp.sum(w_cols * tok_sum, axis=0, keepdims=True)
        if p != 1:
            vec[10 + p // 2 : 11 + p // 2, pl.ds(mult(first, 128), 256)] = jnp.broadcast_to(tok_sum, (256, 128)).T[:1]
        res = res.astype(BF16).T
        for k in range(8):
            gq[k % 2, k // 2, p * small : (p + 1) * small, :] = res[k * small : (k + 1) * small]
    vec[8:9, :] = (gain_sum - row(ref.bias1) * bias_sum) / row(ref.gain1)
    vec[9:10, :] = bias_sum
    def near(now):
        @pl.when(jnp.logical_and(now, stays))
        def _():
            near_local().start()

        @pl.when(jnp.logical_and(now, jnp.logical_not(stays)))
        def _():
            near_remote().start()

    if full:
        sums.vectors_first()
        sums.heads_first(gq)
        sums.add_across(0)
        sums.heads_second(gq, buf.u)
        sums.vectors_second()
    for q in range(PIECES):
        pass_on(q)
    own_part(1)
    near(at_inner)
    if full:
        sums.add_second(1)
        sums.add_second(2)
        sums.add_inner(1)
        sums.heads_third(buf.u)
        sums.add_inner(2)
    near(jnp.logical_not(at_inner))
    if full:
        sums.add_across(1)
        sums.heads_fourth()
        sums.vectors_third()
        sums.add_across(2)

    owner_far = core != at.half

    @pl.when(owner_far)
    def _():
        for q in range(PIECES):
            far = slice(q * length, (q + 1) * length)
            remote(
                summed.at[0, far], arrive2.at[0, far], ref.far_send.at[q], ref.out_recv.at[q], (sib, h)
            ).wait_recv()

    @pl.when(jnp.logical_not(owner_far))
    def _():
        for k in range(2):
            from_me = jnp.logical_and(slot == k, lax.rem(h, 2) == core)

            @pl.when(from_me)
            def _():
                pltpu.make_async_copy(summed.at[1], arrive2.at[k], fin_local).wait()

            @pl.when(jnp.logical_not(from_me))
            def _():
                remote(summed.at[1], arrive2.at[k], fin_send, fin_recv.at[k], (sib, h)).wait_recv()

    e = arrive2[0].astype(F32) + arrive2[1].astype(F32)
    n, r = norm_parts(ref.tok[...].astype(F32))
    buf.gtok[...] = ref.dmid[...] + norm_back(e, row(ref.gain1), n, r)
    gtok_copy = pltpu.make_async_copy(buf.gtok, ref.gtok_o, ref.out_sem.at[1])
    gtok_copy.start()
    if full:
        sums.vectors_fourth()
        sums.heads_last(gq, buf.u)
        sums.vectors_last()
        sums.finish()
    else:
        ref.vec_o[...] = vec[...]
        gq_copy = pltpu.make_async_copy(gq, ref.gq_o, ref.out_sem.at[2])
        gq_copy.start()
        gq_copy.wait()
    for k in range(2):
        swap(k).wait_send()
    for q in range(PIECES):
        far_in(q).wait_send()

    @pl.when(jnp.logical_not(stays))
    def _():
        near_remote().wait_send()
    gtok_copy.wait()


class Sums:
    def __init__(self, ref, at):
        self.ref, self.at = ref, at
        dp, self.h, self.core = at.dp, at.h, at.core
        self.y, self.x = dp // 4, lax.rem(dp // 2, 2)
        self.flip_x, self.flip_y = dp + 2 - 4 * self.x, dp + 4 - 8 * self.y
        self.flip_xy = self.flip_x + 4 - 8 * self.y
        self.outer = self.h * (3 - self.h) == 0

    def rows_of(self, k):
        length = self.ref.gfc.shape[2] // 2
        return slice(0, self.ref.s3.shape[0]) if k == 0 else slice((k - 1) * length, k * length)

    def block(self, k, t, across):
        x, y = self.x, self.y
        first, then = (y, x) if k == 2 else (x, y)
        first = 1 - first if across else first
        then = 1 - then if t == 0 else then
        return first * 2 + then if k == 2 else then * 2 + first

    def mine(self, k, t):
        return self.ref.gfc.at[self.core, self.block(k, t, False)]

    def one(self, k, t):
        ref, rows = self.ref, self.rows_of(k)
        return remote(
            ref.gfc.at[self.core, self.block(k, t, True), rows], ref.r1f.at[t, rows],
            ref.one_send.at[k, t], ref.one_recv.at[k, t], (self.flip_y if k == 2 else self.flip_x, self.h),
        )

    def two(self, k):
        ref, rows = self.ref, self.rows_of(k)
        return remote(
            self.mine(k, 0).at[rows], ref.r2f.at[rows],
            ref.two_send.at[k], ref.two_recv.at[k], (self.flip_x if k == 2 else self.flip_y, self.h),
        )

    def proj_in(self, k, step):
        ref, flips = self.ref, ((self.flip_x, self.h), (self.flip_y, self.h))
        if step == 1:
            return remote(ref.s2.at[k], ref.r1.at[k, 1], ref.p1_send.at[k, 1], ref.p1_recv.at[k, 1], flips[k])
        return remote(ref.s2.at[k], ref.r2.at[k], ref.p2_send.at[k], ref.p2_recv.at[k], flips[1 - k])

    def proj_last(self):
        ref = self.ref
        length = ref.r2.shape[1]
        for k in range(2):
            rows = slice(k * length, (k + 1) * length)
            self.proj_in(k, 1).wait_recv()
            self.proj_in(k, 2).wait_recv()
            ref.s3[rows] = (
                ref.s3[rows].astype(F32) + ref.r1[k, 1].astype(F32) + ref.r2[k].astype(F32)
            ).astype(BF16)
        self.send_in(0)

    def add_first(self, k):
        ref, rows, mine = self.ref, self.rows_of(k), self.mine(k, 0)
        self.one(k, 0).wait_recv()
        mine[rows] = (mine[rows].astype(F32) + ref.r1f[0, rows].astype(F32)).astype(BF16)
        self.two(k).start()

    def add_second(self, k):
        ref, rows, mine = self.ref, self.rows_of(k), self.mine(k, 1)
        self.one(k, 1).wait_recv()
        self.two(k).wait_recv()
        mine[rows] = (
            mine[rows].astype(F32) + ref.r1f[1, rows].astype(F32) + ref.r2f[rows].astype(F32)
        ).astype(BF16)
        self.send_in(k)

    def pieces(self, k):
        rows = self.rows_of(k)
        length = (rows.stop - rows.start) // PIECES
        for q in range(PIECES):
            yield k, k * PIECES + q, slice(rows.start + q * length, rows.start + (q + 1) * length)

    def bufs(self, k):
        ref = self.ref
        return (ref.s3, ref.zap, ref.zbp, ref.ztp) if k == 0 else (self.mine(k, 1), ref.zaf, ref.zbf, ref.ztf)

    def chain(self, k, m, rows, which):
        ref, h = self.ref, self.h
        s2, za, zb, zt = self.bufs(k)
        dp = self.at.dp
        if which == INWARD:
            return remote(s2.at[rows], za.at[rows], ref.z_send.at[0, m], ref.z_recv.at[0, m], (dp, 1 + h // 2))
        if which == ACROSS:
            return remote(s2.at[rows], zb.at[rows], ref.z_send.at[0, m], ref.z_recv.at[1, m], (dp, 3 - h))
        return remote(zt.at[rows], za.at[rows], ref.z_send.at[1, m], ref.z_recv.at[0, m], (dp, 3 * (h // 2)))

    def send_in(self, k):
        @pl.when(self.outer)
        def _():
            for piece in self.pieces(k):
                self.chain(*piece, INWARD).start()

    def add_inner(self, k, only=None):
        s2, za, _, _ = self.bufs(k)

        @pl.when(jnp.logical_not(self.outer))
        def _():
            for q, piece in enumerate(self.pieces(k)):
                if only is None or q in only:
                    rows = piece[2]
                    self.chain(*piece, INWARD).wait_recv()
                    s2[rows] = (s2[rows].astype(F32) + za[rows].astype(F32)).astype(BF16)
                    self.chain(*piece, ACROSS).start()

    def add_across(self, k, only=None):
        s2, _, zb, zt = self.bufs(k)

        @pl.when(jnp.logical_not(self.outer))
        def _():
            for q, piece in enumerate(self.pieces(k)):
                if only is None or q in only:
                    rows = piece[2]
                    self.chain(*piece, ACROSS).wait_recv()
                    zt[rows] = (s2[rows].astype(F32) + zb[rows].astype(F32)).astype(BF16)
                    self.chain(*piece, OUTWARD).start()

    def finish(self):
        @pl.when(self.outer)
        def _():
            for k in range(3):
                _, za, _, zt = self.bufs(k)
                for piece in self.pieces(k):
                    self.chain(*piece, OUTWARD).wait_recv()
                    zt[piece[2]] = za[piece[2]]

        for j in range(4):
            sib = (self.at.sib, self.h)
            remote(
                self.ref.gfc.at[1 - self.core, j], self.ref.gfc_in.at[j], self.ref.pair_send.at[1, j],
                self.ref.pair_recv.at[1, j], sib,
            ).wait_send()
        for k in range(2):
            self.proj_in(k, 2).wait_send()
        for k in range(3):
            if k > 0:
                for t in range(2):
                    self.one(k, t).wait_send()
                self.two(k).wait_send()
            for piece in self.pieces(k):
                self.chain(*piece, INWARD).wait_send()

        @pl.when(jnp.logical_not(self.outer))
        def _():
            for k in range(3):
                for piece in self.pieces(k):
                    self.chain(*piece, OUTWARD).wait_send()

    def swap(self, gq):
        ref, core = self.ref, self.core
        return remote(gq.at[1 - core], ref.gq_in, ref.q_send.at[0], ref.q_recv.at[0], (self.at.sib, self.h))

    def spread(self, u, k):
        ref, x, y = self.ref, self.x, self.y
        to = (self.flip_x, self.flip_y, self.flip_xy)[k]
        block = (y * 2 + 1 - x, (1 - y) * 2 + x, (1 - y) * 2 + 1 - x)[k]
        return remote(u.at[block], ref.u_in.at[k], ref.q_send.at[1 + k], ref.q_recv.at[1 + k], (to, self.h))

    def two_apart(self):
        ref, h = self.ref, self.h
        return remote(ref.v, ref.v_in, ref.q_send.at[4], ref.q_recv.at[4], (self.at.dp, h + 2 - 4 * (h // 2)))

    def next_to(self):
        ref, h = self.ref, self.h
        return remote(ref.w, ref.w_in, ref.q_send.at[5], ref.q_recv.at[5], (self.at.dp, h + 1 - 2 * lax.rem(h, 2)))

    def heads_first(self, gq):
        self.swap(gq).start()

    def heads_second(self, gq, u):
        ref, core = self.ref, self.core
        self.swap(gq).wait_recv()
        for j in range(4):
            mine, theirs = gq[core, j].astype(F32), ref.gq_in[j].astype(F32)
            a, b = jnp.where(core == 0, mine, theirs), jnp.where(core == 0, theirs, mine)
            u[j, :, 0:128] = a[:, 0:128].astype(BF16)
            u[j, :, 128:256] = (a[:, 128:256] + b[:, 0:128]).astype(BF16)
            u[j, :, 256:384] = b[:, 128:256].astype(BF16)
        for k in range(3):
            self.spread(u, k).start()

    def heads_third(self, u):
        ref = self.ref
        for k in range(3):
            self.spread(u, k).wait_recv()
        total = u[self.y * 2 + self.x].astype(F32)
        for k in range(3):
            total = total + ref.u_in[k].astype(F32)
        ref.v[...] = total.astype(BF16)
        self.two_apart().start()

    def heads_fourth(self):
        ref = self.ref
        self.two_apart().wait_recv()
        ref.w[...] = (ref.v[...].astype(F32) + ref.v_in[...].astype(F32)).astype(BF16)
        self.next_to().start()

    def heads_last(self, gq, u):
        self.next_to().wait_recv()
        self.swap(gq).wait_send()
        for k in range(3):
            self.spread(u, k).wait_send()
        self.two_apart().wait_send()
        self.next_to().wait_send()

    def rows8(self, ref, core):
        return ref.at[pl.ds(mult(core * 8, 8), 8), :]

    def vec_sib(self):
        ref = self.ref
        return remote(
            self.rows8(ref.vec, 1 - self.core), ref.vec_sib, ref.vs_send.at[0], ref.vs_recv.at[0], (self.at.sib, self.h)
        )

    def vec_z(self, k):
        ref = self.ref
        return remote(
            ref.vec1, ref.vec_z.at[self.h], ref.vz_send.at[k - 1], ref.vz_recv.at[self.h],
            (self.at.dp, lax.rem(self.h + k, 4)),
        )

    def vec_chips(self, k):
        ref = self.ref
        here = self.y * 2 + self.x
        return remote(
            ref.vec2, ref.vec_xy.at[here], ref.vx_send.at[k], ref.vx_recv.at[here],
            ((self.flip_x, self.flip_y, self.flip_xy)[k], self.h),
        )

    def vec_total(self):
        ref = self.ref
        return remote(
            ref.vec3, self.rows8(ref.vec_all, self.core), ref.vs_send.at[1], ref.vs_recv.at[1], (self.at.sib, self.h)
        )

    def vectors_first(self):
        self.vec_sib().start()

    def vectors_second(self):
        ref = self.ref
        self.vec_sib().wait_recv()
        ref.vec1[...] = ref.vec[pl.ds(mult(self.core * 8, 8), 8), :] + ref.vec_sib[...]
        for k in range(1, 4):
            self.vec_z(k).start()
        ref.vec_z[self.h] = ref.vec1[...]

    def vectors_third(self):
        ref = self.ref
        for k in range(1, 4):
            other = lax.rem(self.h + k, 4)
            remote(
                ref.vec1, ref.vec_z.at[other], ref.vz_send.at[k - 1], ref.vz_recv.at[other], (self.at.sib, self.h)
            ).wait_recv()
        ref.vec2[...] = (ref.vec_z[0] + ref.vec_z[1]) + (ref.vec_z[2] + ref.vec_z[3])
        for k in range(3):
            self.vec_chips(k).start()
        ref.vec_xy[self.y * 2 + self.x] = ref.vec2[...]

    def vectors_fourth(self):
        ref, x, y = self.ref, self.x, self.y
        others = (y * 2 + 1 - x, (1 - y) * 2 + x, (1 - y) * 2 + 1 - x)
        for k in range(3):
            remote(
                ref.vec2, ref.vec_xy.at[others[k]], ref.vx_send.at[k], ref.vx_recv.at[others[k]],
                (self.at.sib, self.h),
            ).wait_recv()
        ref.vec3[...] = (ref.vec_xy[0] + ref.vec_xy[1]) + (ref.vec_xy[2] + ref.vec_xy[3])
        self.vec_total().start()
        ref.vec_all[pl.ds(mult(self.core * 8, 8), 8), :] = ref.vec3[...]

    def vectors_last(self):
        ref = self.ref
        self.vec_total().wait_recv()
        ref.vec_o[...] = ref.vec_all[...]
        self.vec_sib().wait_send()
        self.vec_total().wait_send()
        for k in range(1, 4):
            self.vec_z(k).wait_send()
        for k in range(3):
            self.vec_chips(k).wait_send()


def block(ins, full, grad_scale):
    given = types.SimpleNamespace(**ins)
    rows, width = given.tok_h[0].shape
    group, part, small, half = 4 * rows, width // 4, width // 8, width // 2
    heads, chunks = part // HEAD_DIM, given.w_fc_h[0].shape[1] // width
    dma = pltpu.SemaphoreType.DMA
    outs = dict(out_o=((rows, width), F32, ANY), gtok_o=((rows, width), F32, ANY), vec_o=((16, width), F32, VMEM))
    gq_shape = (2, 4, 3 * small, 256)
    scratch = dict(
        tok=((rows, width), BF16), xg=((group, width), BF16), xgt=((width, group), BF16),
        wt=((3 * 256, width), BF16), mix=((3 * part, group), BF16), ot=((part, group), BF16),
        lse=((8 * heads, group), F32), start=((8, group), jnp.int32), start_mine=((8, group), F32),
        start_sib=((8, group), F32), att=((width, rows), BF16), dat=((width, rows), BF16),
        do_t=((part, group), BF16), dmid=((rows, width), F32), vec=((16, width), F32),
        gfc=((2, chunks, half + small, width), BF16), gfc_in=((chunks, half + small, width), BF16),
        gproj_in=((chunks, half, width), BF16), r1=((2, 2, width // 4, width), BF16),
        r2=((2, width // 4, width), BF16), s2=((2, width // 4, width), BF16), s3=((half, width), BF16),
        arrive=((2, rows, width), BF16), arrive2=((2, rows, width), BF16), far=((rows, width), BF16),
    )
    sems = dict(
        in_sem=(3,), w_sem=(3,), st_sem=(2,), ag_send=(3 * PIECES,), ag_recv=(4, PIECES),
        fw_send=(4 * PIECES,), at_send=(4 * heads,), at_recv=(4 * heads,), at_local=(heads,),
        ff_sem=(2, 2), da_send=(4,), da_recv=(4,), da_local=(), pair_send=(2, chunks),
        pair_recv=(2, chunks), p1_send=(2, 2), p1_recv=(2, 2), p2_send=(2,), p2_recv=(2,),
        out_sem=(3,), sw_send=(2,), sw_recv=(2,), fin_send=(), fin_recv=(2,),
        fin_local=(), far_send=(PIECES,), far_recv=(PIECES,), out_recv=(PIECES,),
    )
    if full:
        outs |= dict(
            ztp=((half, width), BF16, VMEM), ztf=((half + small, width), BF16, VMEM),
            w=((3 * small, half), BF16, VMEM), w_in=((3 * small, half), BF16, VMEM),
        )
        p_shape, f_shape = (half, width), (half + small, width)
        scratch |= dict(
            zap=(p_shape, BF16), zbp=(p_shape, BF16), r1f=((2,) + f_shape, BF16), r2f=(f_shape, BF16),
            zaf=(f_shape, BF16), zbf=(f_shape, BF16),
        )
        scratch |= dict(
            gq_in=(gq_shape[1:], BF16), u_in=((3, 3 * small, half), BF16),
            v=((3 * small, half), BF16), v_in=((3 * small, half), BF16),
            vec_sib=((8, width), F32), vec1=((8, width), F32), vec2=((8, width), F32), vec3=((8, width), F32),
            vec_z=((4, 8, width), F32), vec_xy=((4, 8, width), F32), vec_all=((16, width), F32),
        )
        sems |= dict(
            one_send=(3, 2), one_recv=(3, 2), two_send=(3,), two_recv=(3,),
            z_send=(2, 3 * PIECES), z_recv=(2, 3 * PIECES), q_send=(6,), q_recv=(6,),
            vs_send=(2,), vs_recv=(2,), vz_send=(3,), vz_recv=(4,), vx_send=(3,),
            vx_recv=(4,),
        )
    else:
        outs |= dict(
            gq_o=(gq_shape, BF16, ANY), gfc_o=((2, chunks, half + small, width), BF16, ANY),
            gproj_o=((2, chunks, half, width), BF16, ANY),
        )
    names = (*ins, *outs, *scratch, *sems)
    return pl.pallas_call(
        functools.partial(block_kernel, grad_scale, full, names),
        out_shape=tuple(jax.ShapeDtypeStruct(shape, kind) for shape, kind, _ in outs.values()),
        in_specs=[spec for _, spec in ins.values()],
        out_specs=tuple(spec for _, _, spec in outs.values()),
        scratch_shapes=[pltpu.VMEM(shape, kind) for shape, kind in scratch.values()] + [dma(shape) for shape in sems.values()],
        compiler_params=pltpu.CompilerParams(
            collective_id=0, has_side_effects=True, vmem_limit_bytes=VMEM_LIMIT
        ),
        name="block",
    )(*(array for array, _ in ins.values()))


def emit_kernel(names, *refs):
    ref = named(names, refs)
    through = ((ref.out, ref.out_o), (ref.gtok, ref.gtok_o))
    loads = [pltpu.make_async_copy(src, ref.buf.at[k], ref.sem.at[k]) for k, (src, _) in enumerate(through)]
    stores = [pltpu.make_async_copy(ref.buf.at[k], dst, ref.sem.at[k]) for k, (_, dst) in enumerate(through)]
    for load in loads:
        load.start()
    half, width = ref.ztp.shape
    small = ref.gout_o.shape[0]
    odd = lax.rem(lax.axis_index(HEAD), 2)
    ref.gproj_o[...] = ref.ztp[...].astype(F32)
    ref.gfc_o[...] = ref.ztf[0:half, :].astype(F32).T
    ref.gout_o[...] = ref.ztf[half:, :].astype(F32)
    for p in range(3):
        here = slice(p * small, (p + 1) * small)
        ref.gqkv_o[:, pl.ds(mult((2 * p + odd) * half, 128), half)] = ref.w[here, :].astype(F32)
        ref.gqkv_o[:, pl.ds(mult((2 * p + 1 - odd) * half, 128), half)] = ref.w_in[here, :].astype(F32)
    for load, store in zip(loads, stores):
        load.wait()
        store.start()
    vectors = (
        ref.out_b, ref.ln2_g, ref.ln2_b, ref.proj_b, None, None, None, None, ref.ln1_g, ref.ln1_b, ref.q_b, ref.v_b
    )
    for k, vector in enumerate(vectors):
        if vector is not None:
            vector[...] = ref.vec[k].reshape(width)
    ref.fc_b[...] = jnp.concatenate([ref.vec[4 + k : 5 + k, :] for k in range(4)], axis=1).reshape(4 * width)
    for store in stores:
        store.wait()


def emit(out, gtok, vec, ztp, ztf, w, w_in):
    rows, width = out.shape
    half, small = width // 2, width // 8
    ins = dict(
        out=(out, ANY), gtok=(gtok, ANY), vec=(vec, VMEM), ztp=(ztp, VMEM), ztf=(ztf, VMEM),
        w=(w, VMEM), w_in=(w_in, VMEM),
    )
    outs = dict(
        out_o=((rows, width), ANY), gtok_o=((rows, width), ANY), ln1_g=((width,), VMEM),
        ln1_b=((width,), VMEM), gqkv_o=((small, 3 * width), VMEM), q_b=((width,), VMEM),
        v_b=((width,), VMEM), gout_o=((small, width), VMEM), out_b=((width,), VMEM),
        ln2_g=((width,), VMEM), ln2_b=((width,), VMEM), gfc_o=((width, half), VMEM),
        fc_b=((4 * width,), VMEM), gproj_o=((half, width), VMEM), proj_b=((width,), VMEM),
    )
    scratch = dict(buf=pltpu.VMEM((2, rows, width), F32), sem=pltpu.SemaphoreType.DMA((2,)))
    return pl.pallas_call(
        functools.partial(emit_kernel, (*ins, *outs, *scratch)),
        out_shape=tuple(jax.ShapeDtypeStruct(shape, F32) for shape, _ in outs.values()),
        in_specs=[spec for _, spec in ins.values()],
        out_specs=tuple(spec for _, spec in outs.values()),
        scratch_shapes=list(scratch.values()),
        compiler_params=pltpu.CompilerParams(vmem_limit_bytes=60 << 20),
        name="emit",
    )(*(array for array, _ in ins.values()))


def shards(
    tokens, lengths, ln1_gain, ln1_bias, w_qkv, bias_q, bias_v, w_out, bias_out, ln2_gain, ln2_bias, w_fc, bias_fc,
    w_proj, bias_proj, cotangent,
):
    device_count = lax.axis_size(DP) * lax.axis_size(HEAD)
    full = lax.axis_size(DP) == 8
    ins = dict(
        lens=(lengths, SMEM), gain1=(ln1_gain, VMEM), bias1=(ln1_bias, VMEM), bias_q=(bias_q, VMEM),
        bias_v=(bias_v, VMEM), b_out=(bias_out, VMEM), gain2=(ln2_gain, VMEM), bias2=(ln2_bias, VMEM),
        b_fc=(bias_fc, VMEM), b_proj=(bias_proj, VMEM), tok_h=(tokens, ANY), cot_h=(cotangent, ANY),
        w_qkv=(w_qkv, ANY), w_out_h=(w_out, ANY), w_fc_h=(w_fc, ANY), w_proj_h=(w_proj, ANY),
    )
    block_output, grad_tokens, vec, *rest = block(ins, full, 1.0 / math.sqrt(tokens.shape[0] * device_count))
    if full:
        return emit(block_output, grad_tokens, vec, *rest)
    gq, g_fc, g_proj = rest
    proj_total, fc_total, out_total, qkv_total, vec = sums_by_xla(gq, g_proj, g_fc, vec)
    return (
        block_output, grad_tokens, vec[8], vec[9], qkv_total, vec[10], vec[11], out_total, vec[0], vec[1], vec[2],
        fc_total, vec[4:8].reshape(-1), proj_total, vec[3],
    )


def sums_by_xla(gq, g_proj, g_fc, vec):
    _, blocks, length, width = g_proj.shape
    small = width // 8
    whole = g_proj.transpose(1, 0, 2, 3).reshape(2 * blocks * length, width)
    fc = g_fc[:, :, :length].transpose(1, 0, 2, 3).reshape(2 * blocks * length, width).T
    out = g_fc[:, :, length:].transpose(1, 0, 2, 3).reshape(width, width)
    core, odd = lax.rem(lax.axis_index(DP), 2), lax.rem(lax.axis_index(HEAD), 2)
    window = gq.reshape(2, 4, 3, small, 256).transpose(1, 0, 3, 2, 4).reshape(width, 3, 256)
    qkv = lax.dynamic_update_slice(
        jnp.zeros((width, 3, width), BF16), window, (0, 0, odd * (width // 2) + core * 128)
    ).reshape(width, 3 * width)

    def reduce_mat(g, dim):
        share = lax.psum_scatter(g, DP, scatter_dimension=dim, tiled=True)
        return lax.psum(share, HEAD).astype(F32)

    return reduce_mat(whole, 0), reduce_mat(fc, 1), reduce_mat(out, 0), reduce_mat(qkv, 0), lax.psum(vec, (DP, HEAD))


def solution(mesh):
    rows = P((DP, HEAD), None)
    return jax.shard_map(
        shards,
        mesh=mesh,
        in_specs=(rows, P(DP, None)) + (P(),) * 13 + (rows,),
        out_specs=(
            rows, rows, P(), P(), P(DP, None), P(), P(), P(DP, None), P(), P(), P(), P(None, DP), P(),
            P(DP, None), P(),
        ),
        check_vma=False,
    )
```

```python
import functools
import math
import types

import jax
import jax.numpy as jnp
from jax import lax
from jax.experimental import pallas as pl
from jax.experimental.pallas import tpu as pltpu
from jax.sharding import PartitionSpec as P

DP, HEAD = "dp", "head"
HEAD_DIM = 64
EPSILON = 1e-05
DEPTH_SCALE = 1.0 / math.sqrt(12.0)
LOG2E = 1.0 / math.log(2.0)
SCORE_SCALE = HEAD_DIM ** (-0.5)
GELU_K = math.sqrt(2.0 / math.pi)
GELU_A = 0.044715
TEAM = 8
QB = 256
VMEM_LIMIT = 63 << 20
PIECES = 3

INWARD, ACROSS, OUTWARD = range(3)

F32 = jnp.float32
BF16 = jnp.bfloat16
MESH = pl.DeviceIdType.MESH
ANY = pl.BlockSpec(memory_space=pl.ANY)
VMEM = pl.BlockSpec(memory_space=pltpu.VMEM)
SMEM = pl.BlockSpec(memory_space=pltpu.SMEM)


def dot(a, b):
    return jnp.dot(a, b, preferred_element_type=F32)


def dot_nt(a, b):
    return lax.dot_general(a, b, (((1,), (1,)), ((), ())), preferred_element_type=F32)


def dot_tn(a, b):
    return lax.dot_general(a, b, (((0,), (0,)), ((), ())), preferred_element_type=F32)


def mult(x, m):
    return pl.multiple_of(x, m)


def place():
    dp, h = lax.axis_index(DP), lax.axis_index(HEAD)
    core = lax.rem(dp, 2)
    half = h // 2
    return types.SimpleNamespace(
        dp=dp,
        h=h,
        core=core,
        sib=dp + 1 - 2 * core,
        even=dp - core,
        half=half,
        served=dp - core + half,
        block=(h - 2 * half) * 2 + core,
    )


def greet(at, chips=False):
    barrier = pltpu.get_barrier_semaphore()
    me = at.core * 4 + at.h
    others = []
    for k in range(1, TEAM):
        other = lax.rem(me + k, TEAM)
        others.append((at.even + other // 4, lax.rem(other, 4)))
    if chips:
        for k in range(1, 4):
            others.append((lax.rem(at.dp + 2 * k, 8), at.h))
    for other in others:
        pl.semaphore_signal(barrier, inc=1, device_id=other, device_id_type=MESH)
    pl.semaphore_wait(barrier, len(others))


def scoped(body, **buffers):
    pl.run_scoped(
        lambda *refs: body(named(buffers, refs)), *(pltpu.VMEM(shape, kind) for shape, kind in buffers.values())
    )


def named(names, refs):
    return types.SimpleNamespace(**dict(zip(names, refs, strict=True)))


def remote(src, dst, send, recv, device):
    return pltpu.make_async_remote_copy(
        src_ref=src, dst_ref=dst, send_sem=send, recv_sem=recv, device_id=device, device_id_type=MESH
    )


def row(vec):
    return vec[...].reshape(1, vec.shape[0])


def norm_parts(v):
    center = jnp.mean(v, axis=-1, keepdims=True)
    cent = v - center
    r = lax.rsqrt(jnp.mean(cent * cent, axis=-1, keepdims=True) + EPSILON)
    return cent * r, r


def norm_back(e, gain, n, r):
    ea = e * gain
    return r * (ea - jnp.mean(ea, axis=-1, keepdims=True) - n * jnp.mean(ea * n, axis=-1, keepdims=True))


def block_kernel(grad_scale, full, names, *refs):
    ref = named(names, refs)
    at = place()
    rows, width = ref.tok.shape
    group, part, chunks = 4 * rows, width // 4, ref.gfc.shape[1]
    heads = part // HEAD_DIM
    sums = Sums(ref, at) if full else None
    tok_copy = pltpu.make_async_copy(ref.tok_h, ref.tok, ref.in_sem.at[0])
    tok_copy.start()

    @pl.when(at.core != at.half)
    def _():
        ref.arrive2[1] = jnp.zeros((rows, width), BF16)

    scoped(
        lambda buf: attend(ref, buf, at, tok_copy, full),
        xn=((rows, width), BF16), wwin=((3, width, 256), BF16), brow=((8, width), F32),
        bcol=((3, 256, 128), F32), kh=((group, HEAD_DIM), BF16), scores=((group, QB), F32),
    )
    scoped(
        lambda buf: feed_forward(ref, buf, at, sums, grad_scale),
        cot=((rows, width), BF16), w_out=((width, width), BF16), w_fc=((2, width, width), BF16),
        w_proj=((2, width, width), BF16), brow=((8, chunks * width), F32),
        dfc=((chunks, rows, width), BF16), gproj=((2, chunks, width // 2, width), BF16),
        out=((rows, width), F32),
    )
    scoped(
        lambda buf: attend_back(ref, buf, at, sums, grad_scale),
        kh=((heads, group, HEAD_DIM), BF16), vh=((heads, group, HEAD_DIM), BF16),
        qh=((heads, group, HEAD_DIM), BF16), doh=((heads, group, HEAD_DIM), BF16),
        dk=((heads, group, HEAD_DIM), F32), dv=((heads, group, HEAD_DIM), F32),
        dq=((heads, HEAD_DIM, group), F32), delta=((8 * heads, group), F32), dmix=((3 * 256, group), BF16), partial=((2, rows, width), BF16),
        summed=((2, rows, width), BF16), gtok=((rows, width), F32),
        gq=((2, 4, 3 * (width // 8), 256), BF16), u=((4, 3 * (width // 8), width // 2), BF16),
    )


def attend(ref, buf, at, tok_copy, full):
    dp, h, core, sib = at.dp, at.h, at.core, at.sib
    rows, width = ref.tok.shape
    group, part = 4 * rows, width // 4
    heads = part // HEAD_DIM
    xn, xg, xgt, wwin, wt, mix, ot, lens = buf.xn, ref.xg, ref.xgt, buf.wwin, ref.wt, ref.mix, ref.ot, ref.lens
    collects = core == at.half
    first = (h - 2 * at.half) * 2 * part + core * 128
    shift = mult(64 * core, 64)
    ag_send, ag_recv, fw_send, st_sem, w_sem = ref.ag_send, ref.ag_recv, ref.fw_send, ref.st_sem, ref.w_sem
    for p in range(3):
        pltpu.make_async_copy(
            ref.w_qkv.at[:, pl.ds(mult(p * width + first, 128), 256)], wwin.at[p], w_sem.at[p]
        ).start()
    greet(at, full)
    tok_copy.wait()
    n, _ = norm_parts(ref.tok[...].astype(F32))
    xn[...] = (n * row(ref.gain1) + row(ref.bias1)).astype(BF16)

    inner, outer = 1 + core, 3 * core
    at_inner, at_outer = h == inner, h == outer

    length = rows // PIECES

    def piece(ref, s, q):
        return ref.at[pl.ds(mult(s * rows + q * length, length), length), :]

    def to_inner(q):
        return remote(piece(xn, 0, q), piece(xg, h, q), ag_send.at[q], ag_recv.at[h, q], (dp, inner))

    def to_outer(k, s, q):
        src = piece(xn, 0, q) if k == 0 else piece(xg, s, q)
        return remote(src, piece(xg, s, q), ag_send.at[k * PIECES + q], ag_recv.at[s, q], (dp, outer))

    def to_sib(d, s, q):
        src = piece(xn, 0, q) if d == 0 else piece(xg, s, q)
        return remote(src, piece(xg, s, q), fw_send.at[d * PIECES + q], ag_recv.at[s, q], (sib, h))

    @pl.when(at_inner)
    def _():
        for q in range(PIECES):
            to_outer(0, h, q).start()

    @pl.when(jnp.logical_not(at_inner))
    def _():
        for q in range(PIECES):
            to_inner(q).start()

    @pl.when(collects)
    def _():
        for q in range(PIECES):
            to_sib(0, h, q).start()
        xg[pl.ds(mult(h * rows, rows), rows), :] = xn[...]

    places = lax.broadcasted_iota(jnp.int32, (8, group), 1)
    begin = jnp.zeros((8, group), jnp.int32)
    edge = lens[0, 0]
    for k in range(1, lens.shape[1] + 1):
        begin = jnp.where(places >= edge, edge, begin)
        if k < lens.shape[1]:
            edge = edge + lens[0, k]
    ref.start_mine[...] = begin.astype(F32)
    st_copy = remote(ref.start_mine, ref.start_sib, st_sem.at[0], st_sem.at[1], (sib, h))
    st_copy.start()

    for p in range(3):
        pltpu.make_async_copy(wwin.at[p], wwin.at[p], w_sem.at[p]).wait()
        wt[p * 256 : (p + 1) * 256, :] = wwin[p].T
    for p, vec in ((0, ref.bias_q), (2, ref.bias_v)):
        buf.brow[...] = jnp.broadcast_to(row(vec), (8, width))
        buf.bcol[p] = jnp.broadcast_to(buf.brow[0:1, pl.ds(mult(first, 128), 256)], (128, 256)).T
    buf.bcol[1] = jnp.zeros((256, 128), F32)

    low = 1 - at.half
    order = (h, low * (1 - h) + (1 - low) * (5 - h), 1 + low, 3 * low)

    def project(s):
        here = xg[pl.ds(mult(s * rows, rows), rows), :]
        xgt[:, pl.ds(mult(s * rows, 128), rows)] = here.T
        for p in range(3):
            res = dot_nt(wt[pl.ds(mult(p * 256 + shift, 64), part), :], here) + buf.bcol[p, pl.ds(shift, part), :][:, :1]
            mix[p * part : (p + 1) * part, pl.ds(mult(s * rows, 128), rows)] = res.astype(BF16)

    @pl.when(jnp.logical_not(collects))
    def _():
        for q in range(PIECES):
            to_sib(1, h, q).wait_recv()

    project(h)
    for q in range(PIECES):
        for d in (2, 3, 1):
            s = order[d]
            to_sib(d, s, q).wait_recv()

            @pl.when(collects)
            def _():
                to_sib(d, s, q).start()

            if d > 1:
                @pl.when(at_inner)
                def _():
                    to_outer(d - 1, s, q).start()

            if q == PIECES - 1:
                project(s)
    st_copy.wait_recv()
    ref.start[...] = jnp.where(collects, ref.start_mine[...], ref.start_sib[...]).astype(jnp.int32)
    scale = SCORE_SCALE * LOG2E

    def one_head(i, _):
        qrow, krow, vrow = (mult(p * part + i * HEAD_DIM, HEAD_DIM) for p in range(3))
        buf.kh[...] = mix[pl.ds(krow, HEAD_DIM), :].T
        for j in range(group // QB):
            cols = slice(j * QB, (j + 1) * QB)
            q_t = mix[pl.ds(qrow, HEAD_DIM), cols]
            begins = ref.start[0:1, cols]
            top = jnp.full((1, QB), -jnp.inf, F32)
            for k in range(j + 1):
                s_t = dot(buf.kh[k * QB : (k + 1) * QB, :], q_t)
                key = lax.broadcasted_iota(jnp.int32, (QB, QB), 0)
                keep = key >= begins - k * QB
                if k == j:
                    keep = jnp.logical_and(keep, key <= lax.broadcasted_iota(jnp.int32, (QB, QB), 1))
                s_t = jnp.where(keep, s_t, -1e30)
                buf.scores[k * QB : (k + 1) * QB, :] = s_t
                top = jnp.maximum(top, jnp.max(s_t, axis=0, keepdims=True))
            top = top * scale
            total = jnp.zeros((1, QB), F32)
            acc = jnp.zeros((HEAD_DIM, QB), F32)
            for k in range(j + 1):
                p_t = jnp.exp2(buf.scores[k * QB : (k + 1) * QB, :] * scale - top)
                total = total + jnp.sum(p_t, axis=0, keepdims=True)
                acc = acc + dot(mix[pl.ds(vrow, HEAD_DIM), k * QB : (k + 1) * QB], p_t.astype(BF16))
            ot[pl.ds(qrow, HEAD_DIM), cols] = (acc / total).astype(BF16)
            ref.lse[pl.ds(mult(i * 8, 8), 8), cols] = jnp.broadcast_to(top + jnp.log2(total), (8, QB))
            for s in range(4):
                if j == ((s + 1) * rows - 1) // QB:
                    send_attended(ref, at, i, s)
        return 0

    lax.fori_loop(0, heads, one_head, 0)

    @pl.when(at_inner)
    def _():
        for q in range(PIECES):
            for d in range(1, 4):
                to_outer(d - 1, order[d], q).wait_send()

    @pl.when(jnp.logical_not(at_inner))
    def _():
        for q in range(PIECES):
            to_inner(q).wait_send()

    @pl.when(collects)
    def _():
        for q in range(PIECES):
            for d in range(4):
                to_sib(d, order[d], q).wait_send()

    st_copy.wait_send()


def attended_ends(ref, at, i, s):
    rows, width = ref.tok.shape
    src = ref.ot.at[pl.ds(mult(i * HEAD_DIM, HEAD_DIM), HEAD_DIM), pl.ds(s * rows, rows)]
    dst = ref.att.at[pl.ds(mult(at.block * (width // 4) + i * HEAD_DIM, HEAD_DIM), HEAD_DIM), :]
    return src, dst


def attended_stays(at, s):
    return jnp.logical_and(at.core == at.half, at.h == s)


def attended_local(ref, at, i, s):
    return pltpu.make_async_copy(*attended_ends(ref, at, i, s), ref.at_local.at[i])


def attended_remote(ref, at, i, s):
    src, dst = attended_ends(ref, at, i, s)
    heads = ref.at_local.shape[0]
    return remote(
        src, dst, ref.at_send.at[i * 4 + s], ref.at_recv.at[at.block * heads + i], (at.served, s)
    )


def send_attended(ref, at, i, s):
    @pl.when(attended_stays(at, s))
    def _():
        attended_local(ref, at, i, s).start()

    @pl.when(jnp.logical_not(attended_stays(at, s)))
    def _():
        attended_remote(ref, at, i, s).start()


def wait_attended(ref, at):
    rows, width = ref.tok.shape
    part, heads = width // 4, ref.at_local.shape[0]
    for i in range(heads):
        for s in range(4):
            @pl.when(attended_stays(at, s))
            def _():
                attended_local(ref, at, i, s).wait()

            @pl.when(jnp.logical_not(attended_stays(at, s)))
            def _():
                attended_remote(ref, at, i, s).wait_send()
        for b in range(4):
            dst = ref.att.at[pl.ds(b * part + i * HEAD_DIM, HEAD_DIM), :]
            src = ref.ot.at[pl.ds(i * HEAD_DIM, HEAD_DIM), pl.ds(0, rows)]

            @pl.when(jnp.logical_not(jnp.logical_and(at.core == at.half, at.block == b)))
            def _():
                remote(
                    src, dst, ref.at_send.at[i * 4], ref.at_recv.at[b * heads + i], (at.sib, at.h)
                ).wait_recv()


def feed_forward(ref, buf, at, sums, grad_scale):
    h, core = at.h, at.core
    rows, width = ref.tok.shape
    part = width // 4
    chunks = ref.gfc.shape[1]
    paired = sums is not None
    tok, att, cot, vec = ref.tok, ref.att, buf.cot, ref.vec
    w_out, w_fc, w_proj, brow, dfc, dat = buf.w_out, buf.w_fc, buf.w_proj, buf.brow, buf.dfc, ref.dat
    gfc, gproj, gfc_in, gproj_in, r1, s2, r2, s3 = (
        ref.gfc, buf.gproj, ref.gfc_in, ref.gproj_in, ref.r1, ref.s2, ref.r2, ref.s3
    )
    pair_send, pair_recv, one_send, one_recv, two_send, two_recv = (
        ref.pair_send, ref.pair_recv, ref.p1_send, ref.p1_recv, ref.p2_send, ref.p2_recv
    )
    cot_copy = pltpu.make_async_copy(ref.cot_h, cot, ref.in_sem.at[1])
    wo_copy = pltpu.make_async_copy(ref.w_out_h, w_out, ref.in_sem.at[2])
    cot_copy.start()
    wo_copy.start()

    def ff_copy(step, which):
        slot, here = step % 2, pl.ds(mult(order[step] * width, 128), width)
        if which == 0:
            return pltpu.make_async_copy(ref.w_fc_h.at[:, here], w_fc.at[slot], ref.ff_sem.at[0, slot])
        return pltpu.make_async_copy(ref.w_proj_h.at[here, :], w_proj.at[slot], ref.ff_sem.at[1, slot])

    half_rows = width // 2
    small = width // 8
    y, x = at.dp // 4, lax.rem(at.dp // 2, 2)

    def pair_copy(ref, into, k, j):
        return remote(ref.at[1 - core, j], into.at[j], pair_send.at[k, j], pair_recv.at[k, j], (at.sib, h))

    def pair_add(ref, into, k, j):
        pair_copy(ref, into, k, j).wait_recv()
        ref[core, j] = (ref[core, j].astype(F32) + into[j].astype(F32)).astype(BF16)

    if paired:
        order = [(1 - y) * 2 + 1 - x, y * 2 + 1 - x, (1 - y) * 2 + x, y * 2 + x]
    else:
        order = list(range(chunks))
    quarter = half_rows // 2
    flips = (at.dp + 2 - 4 * x, h), (at.dp + 4 - 8 * y, h)

    def halves(k):
        return slice(k * quarter, (k + 1) * quarter)

    def one(k, t):
        j = order[0] if t == 0 else order[1 + k]
        return remote(gproj.at[core, j, halves(k)], r1.at[k, t], one_send.at[k, t], one_recv.at[k, t], flips[k])

    def two(k):
        return remote(s2.at[k], r2.at[k], two_send.at[k], two_recv.at[k], flips[1 - k])

    def first_sum(k):
        one(k, 0).wait_recv()
        s2[k] = (gproj[core, order[2 - k], halves(k)].astype(F32) + r1[k, 0].astype(F32)).astype(BF16)
        two(k).start()

    def proj_sums(step):
        if not paired:
            return
        pair_add(gproj, gproj_in, 0, order[step])
        if step == 0:
            one(0, 0).start()
            one(1, 0).start()
        elif step == 1:
            one(0, 1).start()
        elif step == 2:
            first_sum(1)
            first_sum(0)
            one(1, 1).start()
        else:
            s3[...] = gproj[core, order[3]]

    for step in range(2):
        for which in range(2):
            ff_copy(step, which).start()
    vec[...] = jnp.zeros_like(vec)
    brow[...] = jnp.broadcast_to(row(ref.b_fc), brow.shape)
    cot_copy.wait()
    dy = cot[...].astype(F32)
    d_proj = (DEPTH_SCALE * dy).astype(BF16)
    wo_copy.wait()
    wait_attended(ref, at)
    middle = tok[...].astype(F32) + DEPTH_SCALE * (dot_tn(att[...], w_out[...]) + row(ref.b_out))
    n, r = norm_parts(middle)
    second = (n * row(ref.gain2) + row(ref.bias2)).astype(BF16)
    result = middle + DEPTH_SCALE * row(ref.b_proj)
    d_second = jnp.zeros((rows, width), F32)
    vec[3:4, :] = jnp.sum(dy, axis=0, keepdims=True) * (DEPTH_SCALE * grad_scale)
    for step, j in enumerate(order):
        slot = step % 2
        ff_copy(step, 0).wait()
        u = dot(second, w_fc[slot]) + brow[0:1, pl.ds(mult(j * width, 128), width)]
        u2 = u * u
        th = jnp.tanh(GELU_K * u * (1.0 + GELU_A * u2))
        half = 0.5 * (1.0 + th)
        slope = half + 0.5 * u * (1.0 - th * th) * (GELU_K * (1.0 + 3.0 * GELU_A * u2))
        hidden = (u * half).astype(BF16)
        ff_copy(step, 1).wait()
        result = result + DEPTH_SCALE * dot(hidden, w_proj[slot])
        d_pre = dot_nt(d_proj, w_proj[slot]) * slope
        if step > 0:
            proj_sums(step - 1)
        res = (dot_tn(hidden, d_proj) * grad_scale).astype(BF16)
        for k in range(2):
            gproj[k, j] = res[k * half_rows : (k + 1) * half_rows]
        if paired:
            pair_copy(gproj, gproj_in, 0, j).start()
        vec[pl.ds(4 + j, 1), :] = jnp.sum(d_pre, axis=0, keepdims=True) * grad_scale
        d_fc = d_pre.astype(BF16)
        dfc[j] = d_fc
        d_second = d_second + dot_nt(d_fc, w_fc[slot])
        if step + 2 < chunks:
            for which in range(2):
                ff_copy(step + 2, which).start()
    buf.out[...] = result
    out_copy = pltpu.make_async_copy(buf.out, ref.out_o, ref.out_sem.at[0])
    out_copy.start()
    vec[1:2, :] = jnp.sum(d_second * n, axis=0, keepdims=True) * grad_scale
    vec[2:3, :] = jnp.sum(d_second, axis=0, keepdims=True) * grad_scale
    d_middle = dy + norm_back(d_second, row(ref.gain2), n, r)
    ref.dmid[...] = d_middle
    vec[0:1, :] = jnp.sum(d_middle, axis=0, keepdims=True) * (DEPTH_SCALE * grad_scale)
    d_out = (DEPTH_SCALE * d_middle).astype(BF16)
    dat[...] = dot_nt(w_out[...], d_out).astype(BF16)

    send_d_attended(ref, at)

    def fc_sums(step):
        if not paired:
            return
        pair_add(gfc, gfc_in, 1, order[step])
        if step == 0:
            sums.one(1, 0).start()
            sums.one(2, 0).start()
        elif step < 3:
            sums.one(step, 1).start()

    g_out = (dot(att[...], d_out) * grad_scale).astype(BF16)
    for j in range(chunks):
        for k in range(2):
            gfc[k, j, half_rows:, :] = g_out[(2 * j + k) * small : (2 * j + k + 1) * small]
    proj_sums(chunks - 1)
    for step, j in enumerate(order):
        res = (dot_tn(dfc[j], second) * grad_scale).astype(BF16)
        for k in range(2):
            gfc[k, j, :half_rows, :] = res[k * half_rows : (k + 1) * half_rows]
        if paired:
            pair_copy(gfc, gfc_in, 1, j).start()
        if step > 0:
            fc_sums(step - 1)
    fc_sums(chunks - 1)
    if paired:
        for j in order:
            pair_copy(gproj, gproj_in, 0, j).wait_send()
        for k in range(2):
            for t in range(2):
                one(k, t).wait_send()
    else:
        outs = [
            pltpu.make_async_copy(gproj, ref.gproj_o, ref.out_sem.at[1]),
            pltpu.make_async_copy(gfc, ref.gfc_o, ref.out_sem.at[2]),
        ]
        for copy in outs:
            copy.start()
        for copy in outs:
            copy.wait()
    out_copy.wait()


def d_attended_part(at, i):
    b = lax.rem(2 * at.core + i, 4)
    return b, (at.even + lax.rem(b, 2), 2 * at.core + b // 2)


def d_attended_stays(at, i):
    b, _ = d_attended_part(at, i)
    return jnp.logical_and(at.core == lax.rem(b, 2), at.h == 2 * at.core + b // 2)


def d_attended_ends(ref, at, b):
    rows, width = ref.tok.shape
    part = width // 4
    src = ref.dat.at[pl.ds(mult(b * part, HEAD_DIM), part), :]
    return src, ref.do_t.at[:, pl.ds(mult(at.h * rows, 128), rows)]


def d_attended_local(ref, at, i):
    return pltpu.make_async_copy(*d_attended_ends(ref, at, d_attended_part(at, i)[0]), ref.da_local)


def d_attended_remote(ref, at, i):
    b, device = d_attended_part(at, i)
    src, dst = d_attended_ends(ref, at, b)
    return remote(src, dst, ref.da_send.at[i], ref.da_recv.at[at.h], device)


def send_d_attended(ref, at):
    for i in range(4):
        @pl.when(d_attended_stays(at, i))
        def _():
            d_attended_local(ref, at, i).start()

        @pl.when(jnp.logical_not(d_attended_stays(at, i)))
        def _():
            d_attended_remote(ref, at, i).start()


def wait_d_attended(ref, at):
    rows, width = ref.tok.shape
    part = width // 4
    served_here = at.core == at.half
    for i in range(4):
        @pl.when(d_attended_stays(at, i))
        def _():
            d_attended_local(ref, at, i).wait()

        @pl.when(jnp.logical_not(d_attended_stays(at, i)))
        def _():
            d_attended_remote(ref, at, i).wait_send()
    for s in range(4):
        @pl.when(jnp.logical_not(jnp.logical_and(served_here, at.h == s)))
        def _():
            remote(
                ref.dat.at[pl.ds(0, part), :], ref.do_t.at[:, pl.ds(s * rows, rows)], ref.da_send.at[0],
                ref.da_recv.at[s], (at.sib, at.h),
            ).wait_recv()


def attend_back(ref, buf, at, sums, grad_scale):
    full = sums is not None
    dp, h, core, sib = at.dp, at.h, at.core, at.sib
    rows, width = ref.tok.shape
    part, group = width // 4, 4 * rows
    heads = part // HEAD_DIM
    mix, do_t, ot, xgt, wt, lse, start = ref.mix, ref.do_t, ref.ot, ref.xgt, ref.wt, ref.lse, ref.start
    delta, kh, vh, qh, doh, dk, dv, dmix = buf.delta, buf.kh, buf.vh, buf.qh, buf.doh, buf.dk, buf.dv, buf.dmix
    dq = buf.dq
    partial, summed, arrive, arrive2 = buf.partial, buf.summed, ref.arrive, ref.arrive2
    sw_send, sw_recv, fin_send, fin_recv, fin_local = (
        ref.sw_send, ref.sw_recv, ref.fin_send, ref.fin_recv, ref.fin_local
    )
    dmix[...] = jnp.zeros_like(dmix)
    wait_d_attended(ref, at)
    scale = SCORE_SCALE * LOG2E

    def drow(p, i):
        return pl.ds(mult(p * 256 + (core + i) * HEAD_DIM, HEAD_DIM), HEAD_DIM)

    half = at.half
    blocks = group // QB
    far_cols = pl.ds(mult((1 - half) * (group // 2), 128), group // 2)
    near_cols = pl.ds(mult(half * (group // 2), 128), group // 2)

    def ready(i):
        qrow, krow, vrow = (mult(p * part + i * HEAD_DIM, HEAD_DIM) for p in range(3))
        d_head = do_t[pl.ds(qrow, HEAD_DIM), :]
        delta[pl.ds(mult(i * 8, 8), 8), :] = jnp.broadcast_to(
            jnp.sum(d_head.astype(F32) * ot[pl.ds(qrow, HEAD_DIM), :].astype(F32), axis=0, keepdims=True), (8, group)
        )
        qh[i] = mix[pl.ds(qrow, HEAD_DIM), :].T
        kh[i] = mix[pl.ds(krow, HEAD_DIM), :].T
        vh[i] = mix[pl.ds(vrow, HEAD_DIM), :].T
        doh[i] = d_head.T
        dq[i] = jnp.zeros((HEAD_DIM, group), F32)
        dk[i] = jnp.zeros((group, HEAD_DIM), F32)
        dv[i] = jnp.zeros((group, HEAD_DIM), F32)

    def pair(i, o, t):
        k = half * o + (1 - half) * (blocks - 1 - o - t)
        q = half * (o + t) + (1 - half) * (blocks - 1 - o)
        keys, cols = pl.ds(mult(k * QB, QB), QB), pl.ds(mult(q * QB, QB), QB)
        qrow, krow = (mult(p * part + i * HEAD_DIM, HEAD_DIM) for p in range(2))
        stats = pl.ds(mult(i * 8, 8), 8)
        s_t = dot(kh[i, keys, :], mix[pl.ds(qrow, HEAD_DIM), cols])
        key = lax.broadcasted_iota(jnp.int32, (QB, QB), 0)
        keep = key >= start[0:1, cols] - k * QB
        if t == 0:
            keep = jnp.logical_and(keep, key <= lax.broadcasted_iota(jnp.int32, (QB, QB), 1))
        p_t = jnp.where(keep, jnp.exp2(s_t * scale - lse[stats, cols][0:1]), 0.0)
        dp_t = dot(vh[i, keys, :], do_t[pl.ds(qrow, HEAD_DIM), cols])
        ds_t = (p_t * (dp_t - delta[stats, cols][0:1])).astype(BF16)
        dv[i, keys, :] += dot(p_t.astype(BF16), doh[i, cols, :])
        dk[i, keys, :] += dot(ds_t, qh[i, cols, :])
        dq[i, :, cols] += dot(mix[pl.ds(krow, HEAD_DIM), keys], ds_t)

    def done(i, cols):
        dmix[drow(0, i), cols] = (dq[i, :, cols] * SCORE_SCALE).astype(BF16)
        dmix[drow(1, i), cols] = (dk[i, cols, :] * SCORE_SCALE).T.astype(BF16)
        dmix[drow(2, i), cols] = dv[i, cols, :].T.astype(BF16)

    def far_head(i, _):
        ready(i)
        for o in range(blocks // 2):
            for t in range(blocks - o):
                pair(i, o, t)
            if full and o == 0:
                @pl.when(i == 0)
                def _():
                    sums.proj_last()
                    sums.send_in(0, (0,))

                for q in (1, 2):
                    @pl.when(i == q)
                    def _():
                        sums.send_in(0, (q,))
            if full and o == 1:
                @pl.when(i == 2)
                def _():
                    sums.add_across(0, (0,))
            if full and o == 2:
                for q in range(3):
                    @pl.when(i == q)
                    def _():
                        sums.add_inner(0, (q,))
        done(i, far_cols)
        return 0

    def near_head(i, _):
        for o in range(blocks // 2, blocks):
            for t in range(blocks - o):
                pair(i, o, t)
        done(i, near_cols)

        @pl.when(i == 1)
        def _():
            send_far(1)

        return 0

    def part_of(s):
        return dot_tn(dmix[:, pl.ds(mult(s * rows, 128), rows)], wt[...])

    slot, inner = h - 2 * at.half, 1 + at.half
    at_inner = h == inner
    ways = (1 - at.half, at.half)
    length = rows // PIECES
    def pass_on(q):
        @pl.when(at_inner)
        def _():
            here = slice(q * length, (q + 1) * length)
            far_in(q).wait_recv()
            summed[0, here] = (summed[0, here].astype(F32) + ref.far[here].astype(F32)).astype(BF16)
            far_out(q).start()

    def swap(k):
        return remote(partial.at[k], arrive.at[k], sw_send.at[k], sw_recv.at[k], (sib, h))

    def sib_part(k):
        partial[k] = part_of(2 * ways[k] + 1 - core).astype(BF16)
        swap(k).start()

    def own_part(k):
        mine = part_of(2 * ways[k] + core)
        swap(k).wait_recv()
        summed[k] = (mine + arrive[k].astype(F32)).astype(BF16)

    def far_in(q):
        here = slice(q * length, (q + 1) * length)
        return remote(summed.at[0, here], ref.far.at[here], ref.far_send.at[q], ref.far_recv.at[q], (dp, inner))

    def far_out(q):
        here = slice(q * length, (q + 1) * length)
        return remote(
            summed.at[0, here], arrive2.at[0, here], ref.far_send.at[q], ref.out_recv.at[q],
            (at.served, 2 * ways[0] + core),
        )

    def near_remote():
        return remote(summed.at[1], arrive2.at[slot], fin_send, fin_recv.at[slot], (at.served, 2 * ways[1] + core))

    def near_local():
        return pltpu.make_async_copy(summed.at[1], arrive2.at[slot], fin_local)

    stays = jnp.logical_and(core == at.half, h == 2 * ways[1] + core)
    lax.fori_loop(0, heads, far_head, 0)
    sib_part(0)
    own_part(0)

    def send_far(q):
        @pl.when(jnp.logical_not(at_inner))
        def _():
            far_in(q).start()

    send_far(0)

    if full:
        sums.add_first(1)
        sums.add_first(2)
        sums.add_across(0, (1,))
    lax.fori_loop(0, heads, near_head, 0)
    sib_part(1)
    pass_on(0)
    vec, gq = ref.vec, buf.gq
    first = slot * 2 * part + core * 128
    small = width // 8
    gain_sum = jnp.zeros((1, width), F32)
    bias_sum = jnp.zeros((1, width), F32)
    for p in range(3):
        d_cols = dmix[p * 256 : (p + 1) * 256, :]
        tok_sum = jnp.sum(d_cols.astype(F32), axis=1, keepdims=True) * grad_scale
        w_cols = wt[p * 256 : (p + 1) * 256, :].astype(F32)
        res = dot_nt(d_cols, xgt[...]) * grad_scale
        gain_sum = gain_sum + jnp.sum(w_cols * res, axis=0, keepdims=True)
        bias_sum = bias_sum + jnp.sum(w_cols * tok_sum, axis=0, keepdims=True)
        if p != 1:
            vec[10 + p // 2 : 11 + p // 2, pl.ds(mult(first, 128), 256)] = jnp.broadcast_to(tok_sum, (256, 128)).T[:1]
        res = res.astype(BF16).T
        for k in range(8):
            gq[k % 2, k // 2, p * small : (p + 1) * small, :] = res[k * small : (k + 1) * small]
    vec[8:9, :] = (gain_sum - row(ref.bias1) * bias_sum) / row(ref.gain1)
    vec[9:10, :] = bias_sum
    def near(now):
        @pl.when(jnp.logical_and(now, stays))
        def _():
            near_local().start()

        @pl.when(jnp.logical_and(now, jnp.logical_not(stays)))
        def _():
            near_remote().start()

    send_far(2)
    if full:
        sums.vectors_first()
        sums.heads_first(gq)
    pass_on(1)
    if full:
        sums.add_across(0, (2,))
        sums.heads_second(gq, buf.u)
        sums.vectors_second()
        sums.add_second(1)
        sums.send_in(1, (0,))
    pass_on(2)
    own_part(1)
    near(at_inner)
    if full:
        sums.add_second(2)
        sums.send_in(1, (1, 2))
        sums.add_inner(1)
        sums.send_in(2)
        sums.heads_third(buf.u)
        sums.add_inner(2)
    near(jnp.logical_not(at_inner))
    if full:
        sums.add_across(1)
        sums.heads_fourth()
        sums.vectors_third()
        sums.add_across(2)

    owner_far = core != at.half

    @pl.when(owner_far)
    def _():
        for q in range(PIECES):
            far = slice(q * length, (q + 1) * length)
            remote(
                summed.at[0, far], arrive2.at[0, far], ref.far_send.at[q], ref.out_recv.at[q], (sib, h)
            ).wait_recv()

    @pl.when(jnp.logical_not(owner_far))
    def _():
        for k in range(2):
            from_me = jnp.logical_and(slot == k, lax.rem(h, 2) == core)

            @pl.when(from_me)
            def _():
                pltpu.make_async_copy(summed.at[1], arrive2.at[k], fin_local).wait()

            @pl.when(jnp.logical_not(from_me))
            def _():
                remote(summed.at[1], arrive2.at[k], fin_send, fin_recv.at[k], (sib, h)).wait_recv()

    e = arrive2[0].astype(F32) + arrive2[1].astype(F32)
    n, r = norm_parts(ref.tok[...].astype(F32))
    buf.gtok[...] = ref.dmid[...] + norm_back(e, row(ref.gain1), n, r)
    gtok_copy = pltpu.make_async_copy(buf.gtok, ref.gtok_o, ref.out_sem.at[1])
    gtok_copy.start()
    if full:
        sums.vectors_fourth()
        sums.heads_last(gq, buf.u)
        sums.vectors_last()
        sums.finish()
    else:
        ref.vec_o[...] = vec[...]
        gq_copy = pltpu.make_async_copy(gq, ref.gq_o, ref.out_sem.at[2])
        gq_copy.start()
        gq_copy.wait()
    for k in range(2):
        swap(k).wait_send()
    for q in range(PIECES):
        far_in(q).wait_send()

    @pl.when(jnp.logical_not(stays))
    def _():
        near_remote().wait_send()
    gtok_copy.wait()


class Sums:
    def __init__(self, ref, at):
        self.ref, self.at = ref, at
        dp, self.h, self.core = at.dp, at.h, at.core
        self.y, self.x = dp // 4, lax.rem(dp // 2, 2)
        self.flip_x, self.flip_y = dp + 2 - 4 * self.x, dp + 4 - 8 * self.y
        self.flip_xy = self.flip_x + 4 - 8 * self.y
        self.outer = self.h * (3 - self.h) == 0

    def rows_of(self, k):
        length = self.ref.gfc.shape[2] // 2
        return slice(0, self.ref.s3.shape[0]) if k == 0 else slice((k - 1) * length, k * length)

    def block(self, k, t, across):
        x, y = self.x, self.y
        first, then = (y, x) if k == 2 else (x, y)
        first = 1 - first if across else first
        then = 1 - then if t == 0 else then
        return first * 2 + then if k == 2 else then * 2 + first

    def mine(self, k, t):
        return self.ref.gfc.at[self.core, self.block(k, t, False)]

    def one(self, k, t):
        ref, rows = self.ref, self.rows_of(k)
        return remote(
            ref.gfc.at[self.core, self.block(k, t, True), rows], ref.r1f.at[t, rows],
            ref.one_send.at[k, t], ref.one_recv.at[k, t], (self.flip_y if k == 2 else self.flip_x, self.h),
        )

    def two(self, k):
        ref, rows = self.ref, self.rows_of(k)
        return remote(
            self.mine(k, 0).at[rows], ref.r2f.at[rows],
            ref.two_send.at[k], ref.two_recv.at[k], (self.flip_x if k == 2 else self.flip_y, self.h),
        )

    def proj_in(self, k, step):
        ref, flips = self.ref, ((self.flip_x, self.h), (self.flip_y, self.h))
        if step == 1:
            return remote(ref.s2.at[k], ref.r1.at[k, 1], ref.p1_send.at[k, 1], ref.p1_recv.at[k, 1], flips[k])
        return remote(ref.s2.at[k], ref.r2.at[k], ref.p2_send.at[k], ref.p2_recv.at[k], flips[1 - k])

    def proj_last(self):
        ref = self.ref
        length = ref.r2.shape[1]
        for k in range(2):
            rows = slice(k * length, (k + 1) * length)
            self.proj_in(k, 1).wait_recv()
            self.proj_in(k, 2).wait_recv()
            ref.s3[rows] = (
                ref.s3[rows].astype(F32) + ref.r1[k, 1].astype(F32) + ref.r2[k].astype(F32)
            ).astype(BF16)

    def add_first(self, k):
        ref, rows, mine = self.ref, self.rows_of(k), self.mine(k, 0)
        self.one(k, 0).wait_recv()
        mine[rows] = (mine[rows].astype(F32) + ref.r1f[0, rows].astype(F32)).astype(BF16)
        self.two(k).start()

    def add_second(self, k):
        ref, rows, mine = self.ref, self.rows_of(k), self.mine(k, 1)
        self.one(k, 1).wait_recv()
        self.two(k).wait_recv()
        mine[rows] = (
            mine[rows].astype(F32) + ref.r1f[1, rows].astype(F32) + ref.r2f[rows].astype(F32)
        ).astype(BF16)

    def pieces(self, k):
        rows = self.rows_of(k)
        length = (rows.stop - rows.start) // PIECES
        for q in range(PIECES):
            yield k, k * PIECES + q, slice(rows.start + q * length, rows.start + (q + 1) * length)

    def bufs(self, k):
        ref = self.ref
        return (ref.s3, ref.zap, ref.zbp, ref.ztp) if k == 0 else (self.mine(k, 1), ref.zaf, ref.zbf, ref.ztf)

    def chain(self, k, m, rows, which):
        ref, h = self.ref, self.h
        s2, za, zb, zt = self.bufs(k)
        dp = self.at.dp
        if which == INWARD:
            return remote(s2.at[rows], za.at[rows], ref.z_send.at[0, m], ref.z_recv.at[0, m], (dp, 1 + h // 2))
        if which == ACROSS:
            return remote(s2.at[rows], zb.at[rows], ref.z_send.at[0, m], ref.z_recv.at[1, m], (dp, 3 - h))
        return remote(zt.at[rows], za.at[rows], ref.z_send.at[1, m], ref.z_recv.at[0, m], (dp, 3 * (h // 2)))

    def send_in(self, k, only=None):
        @pl.when(self.outer)
        def _():
            for q, piece in enumerate(self.pieces(k)):
                if only is None or q in only:
                    self.chain(*piece, INWARD).start()

    def add_inner(self, k, only=None):
        s2, za, _, _ = self.bufs(k)

        @pl.when(jnp.logical_not(self.outer))
        def _():
            for q, piece in enumerate(self.pieces(k)):
                if only is None or q in only:
                    rows = piece[2]
                    self.chain(*piece, INWARD).wait_recv()
                    s2[rows] = (s2[rows].astype(F32) + za[rows].astype(F32)).astype(BF16)
                    self.chain(*piece, ACROSS).start()

    def add_across(self, k, only=None):
        s2, _, zb, zt = self.bufs(k)

        @pl.when(jnp.logical_not(self.outer))
        def _():
            for q, piece in enumerate(self.pieces(k)):
                if only is None or q in only:
                    rows = piece[2]
                    self.chain(*piece, ACROSS).wait_recv()
                    zt[rows] = (s2[rows].astype(F32) + zb[rows].astype(F32)).astype(BF16)
                    self.chain(*piece, OUTWARD).start()

    def finish(self):
        @pl.when(self.outer)
        def _():
            for k in range(3):
                _, za, _, zt = self.bufs(k)
                for piece in self.pieces(k):
                    self.chain(*piece, OUTWARD).wait_recv()
                    zt[piece[2]] = za[piece[2]]

        for j in range(4):
            sib = (self.at.sib, self.h)
            remote(
                self.ref.gfc.at[1 - self.core, j], self.ref.gfc_in.at[j], self.ref.pair_send.at[1, j],
                self.ref.pair_recv.at[1, j], sib,
            ).wait_send()
        for k in range(2):
            self.proj_in(k, 2).wait_send()
        for k in range(3):
            if k > 0:
                for t in range(2):
                    self.one(k, t).wait_send()
                self.two(k).wait_send()
            for piece in self.pieces(k):
                self.chain(*piece, INWARD).wait_send()

        @pl.when(jnp.logical_not(self.outer))
        def _():
            for k in range(3):
                for piece in self.pieces(k):
                    self.chain(*piece, OUTWARD).wait_send()

    def swap(self, gq):
        ref, core = self.ref, self.core
        return remote(gq.at[1 - core], ref.gq_in, ref.q_send.at[0], ref.q_recv.at[0], (self.at.sib, self.h))

    def spread(self, u, k):
        ref, x, y = self.ref, self.x, self.y
        to = (self.flip_x, self.flip_y, self.flip_xy)[k]
        block = (y * 2 + 1 - x, (1 - y) * 2 + x, (1 - y) * 2 + 1 - x)[k]
        return remote(u.at[block], ref.u_in.at[k], ref.q_send.at[1 + k], ref.q_recv.at[1 + k], (to, self.h))

    def two_apart(self):
        ref, h = self.ref, self.h
        return remote(ref.v, ref.v_in, ref.q_send.at[4], ref.q_recv.at[4], (self.at.dp, h + 2 - 4 * (h // 2)))

    def next_to(self):
        ref, h = self.ref, self.h
        return remote(ref.w, ref.w_in, ref.q_send.at[5], ref.q_recv.at[5], (self.at.dp, h + 1 - 2 * lax.rem(h, 2)))

    def heads_first(self, gq):
        self.swap(gq).start()

    def heads_second(self, gq, u):
        ref, core = self.ref, self.core
        self.swap(gq).wait_recv()
        for j in range(4):
            mine, theirs = gq[core, j].astype(F32), ref.gq_in[j].astype(F32)
            a, b = jnp.where(core == 0, mine, theirs), jnp.where(core == 0, theirs, mine)
            u[j, :, 0:128] = a[:, 0:128].astype(BF16)
            u[j, :, 128:256] = (a[:, 128:256] + b[:, 0:128]).astype(BF16)
            u[j, :, 256:384] = b[:, 128:256].astype(BF16)
        for k in range(3):
            self.spread(u, k).start()

    def heads_third(self, u):
        ref = self.ref
        for k in range(3):
            self.spread(u, k).wait_recv()
        total = u[self.y * 2 + self.x].astype(F32)
        for k in range(3):
            total = total + ref.u_in[k].astype(F32)
        ref.v[...] = total.astype(BF16)
        self.two_apart().start()

    def heads_fourth(self):
        ref = self.ref
        self.two_apart().wait_recv()
        ref.w[...] = (ref.v[...].astype(F32) + ref.v_in[...].astype(F32)).astype(BF16)
        self.next_to().start()

    def heads_last(self, gq, u):
        self.next_to().wait_recv()
        self.swap(gq).wait_send()
        for k in range(3):
            self.spread(u, k).wait_send()
        self.two_apart().wait_send()
        self.next_to().wait_send()

    def rows8(self, ref, core):
        return ref.at[pl.ds(mult(core * 8, 8), 8), :]

    def vec_sib(self):
        ref = self.ref
        return remote(
            self.rows8(ref.vec, 1 - self.core), ref.vec_sib, ref.vs_send.at[0], ref.vs_recv.at[0], (self.at.sib, self.h)
        )

    def vec_z(self, k):
        ref = self.ref
        return remote(
            ref.vec1, ref.vec_z.at[self.h], ref.vz_send.at[k - 1], ref.vz_recv.at[self.h],
            (self.at.dp, lax.rem(self.h + k, 4)),
        )

    def vec_chips(self, k):
        ref = self.ref
        here = self.y * 2 + self.x
        return remote(
            ref.vec2, ref.vec_xy.at[here], ref.vx_send.at[k], ref.vx_recv.at[here],
            ((self.flip_x, self.flip_y, self.flip_xy)[k], self.h),
        )

    def vec_total(self):
        ref = self.ref
        return remote(
            ref.vec3, self.rows8(ref.vec_all, self.core), ref.vs_send.at[1], ref.vs_recv.at[1], (self.at.sib, self.h)
        )

    def vectors_first(self):
        self.vec_sib().start()

    def vectors_second(self):
        ref = self.ref
        self.vec_sib().wait_recv()
        ref.vec1[...] = ref.vec[pl.ds(mult(self.core * 8, 8), 8), :] + ref.vec_sib[...]
        for k in range(1, 4):
            self.vec_z(k).start()
        ref.vec_z[self.h] = ref.vec1[...]

    def vectors_third(self):
        ref = self.ref
        for k in range(1, 4):
            other = lax.rem(self.h + k, 4)
            remote(
                ref.vec1, ref.vec_z.at[other], ref.vz_send.at[k - 1], ref.vz_recv.at[other], (self.at.sib, self.h)
            ).wait_recv()
        ref.vec2[...] = (ref.vec_z[0] + ref.vec_z[1]) + (ref.vec_z[2] + ref.vec_z[3])
        for k in range(3):
            self.vec_chips(k).start()
        ref.vec_xy[self.y * 2 + self.x] = ref.vec2[...]

    def vectors_fourth(self):
        ref, x, y = self.ref, self.x, self.y
        others = (y * 2 + 1 - x, (1 - y) * 2 + x, (1 - y) * 2 + 1 - x)
        for k in range(3):
            remote(
                ref.vec2, ref.vec_xy.at[others[k]], ref.vx_send.at[k], ref.vx_recv.at[others[k]],
                (self.at.sib, self.h),
            ).wait_recv()
        ref.vec3[...] = (ref.vec_xy[0] + ref.vec_xy[1]) + (ref.vec_xy[2] + ref.vec_xy[3])
        self.vec_total().start()
        ref.vec_all[pl.ds(mult(self.core * 8, 8), 8), :] = ref.vec3[...]

    def vectors_last(self):
        ref = self.ref
        self.vec_total().wait_recv()
        ref.vec_o[...] = ref.vec_all[...]
        self.vec_sib().wait_send()
        self.vec_total().wait_send()
        for k in range(1, 4):
            self.vec_z(k).wait_send()
        for k in range(3):
            self.vec_chips(k).wait_send()


def block(ins, full, grad_scale):
    given = types.SimpleNamespace(**ins)
    rows, width = given.tok_h[0].shape
    group, part, small, half = 4 * rows, width // 4, width // 8, width // 2
    heads, chunks = part // HEAD_DIM, given.w_fc_h[0].shape[1] // width
    dma = pltpu.SemaphoreType.DMA
    outs = dict(out_o=((rows, width), F32, ANY), gtok_o=((rows, width), F32, ANY), vec_o=((16, width), F32, VMEM))
    gq_shape = (2, 4, 3 * small, 256)
    scratch = dict(
        tok=((rows, width), BF16), xg=((group, width), BF16), xgt=((width, group), BF16),
        wt=((3 * 256, width), BF16), mix=((3 * part, group), BF16), ot=((part, group), BF16),
        lse=((8 * heads, group), F32), start=((8, group), jnp.int32), start_mine=((8, group), F32),
        start_sib=((8, group), F32), att=((width, rows), BF16), dat=((width, rows), BF16),
        do_t=((part, group), BF16), dmid=((rows, width), F32), vec=((16, width), F32),
        gfc=((2, chunks, half + small, width), BF16), gfc_in=((chunks, half + small, width), BF16),
        gproj_in=((chunks, half, width), BF16), r1=((2, 2, width // 4, width), BF16),
        r2=((2, width // 4, width), BF16), s2=((2, width // 4, width), BF16), s3=((half, width), BF16),
        arrive=((2, rows, width), BF16), arrive2=((2, rows, width), BF16), far=((rows, width), BF16),
    )
    sems = dict(
        in_sem=(3,), w_sem=(3,), st_sem=(2,), ag_send=(3 * PIECES,), ag_recv=(4, PIECES),
        fw_send=(4 * PIECES,), at_send=(4 * heads,), at_recv=(4 * heads,), at_local=(heads,),
        ff_sem=(2, 2), da_send=(4,), da_recv=(4,), da_local=(), pair_send=(2, chunks),
        pair_recv=(2, chunks), p1_send=(2, 2), p1_recv=(2, 2), p2_send=(2,), p2_recv=(2,),
        out_sem=(3,), sw_send=(2,), sw_recv=(2,), fin_send=(), fin_recv=(2,),
        fin_local=(), far_send=(PIECES,), far_recv=(PIECES,), out_recv=(PIECES,),
    )
    if full:
        outs |= dict(
            ztp=((half, width), BF16, VMEM), ztf=((half + small, width), BF16, VMEM),
            w=((3 * small, half), BF16, VMEM), w_in=((3 * small, half), BF16, VMEM),
        )
        p_shape, f_shape = (half, width), (half + small, width)
        scratch |= dict(
            zap=(p_shape, BF16), zbp=(p_shape, BF16), r1f=((2,) + f_shape, BF16), r2f=(f_shape, BF16),
            zaf=(f_shape, BF16), zbf=(f_shape, BF16),
        )
        scratch |= dict(
            gq_in=(gq_shape[1:], BF16), u_in=((3, 3 * small, half), BF16),
            v=((3 * small, half), BF16), v_in=((3 * small, half), BF16),
            vec_sib=((8, width), F32), vec1=((8, width), F32), vec2=((8, width), F32), vec3=((8, width), F32),
            vec_z=((4, 8, width), F32), vec_xy=((4, 8, width), F32), vec_all=((16, width), F32),
        )
        sems |= dict(
            one_send=(3, 2), one_recv=(3, 2), two_send=(3,), two_recv=(3,),
            z_send=(2, 3 * PIECES), z_recv=(2, 3 * PIECES), q_send=(6,), q_recv=(6,),
            vs_send=(2,), vs_recv=(2,), vz_send=(3,), vz_recv=(4,), vx_send=(3,),
            vx_recv=(4,),
        )
    else:
        outs |= dict(
            gq_o=(gq_shape, BF16, ANY), gfc_o=((2, chunks, half + small, width), BF16, ANY),
            gproj_o=((2, chunks, half, width), BF16, ANY),
        )
    names = (*ins, *outs, *scratch, *sems)
    return pl.pallas_call(
        functools.partial(block_kernel, grad_scale, full, names),
        out_shape=tuple(jax.ShapeDtypeStruct(shape, kind) for shape, kind, _ in outs.values()),
        in_specs=[spec for _, spec in ins.values()],
        out_specs=tuple(spec for _, _, spec in outs.values()),
        scratch_shapes=[pltpu.VMEM(shape, kind) for shape, kind in scratch.values()] + [dma(shape) for shape in sems.values()],
        compiler_params=pltpu.CompilerParams(
            collective_id=0, has_side_effects=True, vmem_limit_bytes=VMEM_LIMIT
        ),
        name="block",
    )(*(array for array, _ in ins.values()))


def emit_kernel(names, *refs):
    ref = named(names, refs)
    half, width = ref.ztp_h.shape
    small = ref.gout_o.shape[0]
    odd = lax.rem(lax.axis_index(HEAD), 2)
    reads = ((ref.ztf_h, ref.ztf), (ref.ztp_h, ref.ztp), (ref.w_h, ref.w), (ref.w_in_h, ref.w_in), (ref.out, ref.buf.at[0]),
             (ref.gtok, ref.buf.at[1]))
    loads = [pltpu.make_async_copy(src, dst, ref.in_sem.at[k]) for k, (src, dst) in enumerate(reads)]
    for load in loads:
        load.start()
    writes = ((ref.gfc, ref.gfc_o), (ref.gout, ref.gout_o), (ref.gproj, ref.gproj_o), (ref.gqkv, ref.gqkv_o),
              (ref.buf.at[0], ref.out_o), (ref.buf.at[1], ref.gtok_o))
    stores = [pltpu.make_async_copy(src, dst, ref.out_sem.at[k]) for k, (src, dst) in enumerate(writes)]
    vectors = (
        ref.out_b, ref.ln2_g, ref.ln2_b, ref.proj_b, None, None, None, None, ref.ln1_g, ref.ln1_b, ref.q_b, ref.v_b
    )
    for k, vector in enumerate(vectors):
        if vector is not None:
            vector[...] = ref.vec[k].reshape(width)
    ref.fc_b[...] = jnp.concatenate([ref.vec[4 + k : 5 + k, :] for k in range(4)], axis=1).reshape(4 * width)
    for k in (4, 5):
        loads[k].wait()
        stores[k].start()
    loads[1].wait()
    ref.gproj[...] = ref.ztp[...].astype(F32)
    stores[2].start()
    loads[0].wait()
    ref.gfc[...] = ref.ztf[0:half, :].astype(F32).T
    stores[0].start()
    ref.gout[...] = ref.ztf[half:, :].astype(F32)
    stores[1].start()
    loads[2].wait()
    loads[3].wait()
    for p in range(3):
        here = slice(p * small, (p + 1) * small)
        ref.gqkv[:, pl.ds(mult((2 * p + odd) * half, 128), half)] = ref.w[here, :].astype(F32)
        ref.gqkv[:, pl.ds(mult((2 * p + 1 - odd) * half, 128), half)] = ref.w_in[here, :].astype(F32)
    stores[3].start()
    for store in stores:
        store.wait()


def emit(out, gtok, vec, ztp, ztf, w, w_in):
    rows, width = out.shape
    half, small = width // 2, width // 8
    ins = dict(
        out=(out, ANY), gtok=(gtok, ANY), vec=(vec, VMEM), ztp_h=(ztp, ANY), ztf_h=(ztf, ANY), w_h=(w, ANY),
        w_in_h=(w_in, ANY),
    )
    outs = dict(
        out_o=((rows, width), ANY), gtok_o=((rows, width), ANY), ln1_g=((width,), VMEM),
        ln1_b=((width,), VMEM), gqkv_o=((small, 3 * width), ANY), q_b=((width,), VMEM),
        v_b=((width,), VMEM), gout_o=((small, width), ANY), out_b=((width,), VMEM),
        ln2_g=((width,), VMEM), ln2_b=((width,), VMEM), gfc_o=((width, half), ANY),
        fc_b=((4 * width,), VMEM), gproj_o=((half, width), ANY), proj_b=((width,), VMEM),
    )
    dma = pltpu.SemaphoreType.DMA
    scratch = dict(
        buf=pltpu.VMEM((2, rows, width), F32), ztp=pltpu.VMEM(ztp.shape, BF16), ztf=pltpu.VMEM(ztf.shape, BF16),
        w=pltpu.VMEM(w.shape, BF16), w_in=pltpu.VMEM(w.shape, BF16), gfc=pltpu.VMEM((width, half), F32),
        gout=pltpu.VMEM((small, width), F32), gproj=pltpu.VMEM((half, width), F32),
        gqkv=pltpu.VMEM((small, 3 * width), F32), in_sem=dma((6,)), out_sem=dma((6,)),
    )
    return pl.pallas_call(
        functools.partial(emit_kernel, (*ins, *outs, *scratch)),
        out_shape=tuple(jax.ShapeDtypeStruct(shape, F32) for shape, _ in outs.values()),
        in_specs=[spec for _, spec in ins.values()],
        out_specs=tuple(spec for _, spec in outs.values()),
        scratch_shapes=list(scratch.values()),
        compiler_params=pltpu.CompilerParams(vmem_limit_bytes=60 << 20),
        name="emit",
    )(*(array for array, _ in ins.values()))


def shards(
    tokens, lengths, ln1_gain, ln1_bias, w_qkv, bias_q, bias_v, w_out, bias_out, ln2_gain, ln2_bias, w_fc, bias_fc,
    w_proj, bias_proj, cotangent,
):
    device_count = lax.axis_size(DP) * lax.axis_size(HEAD)
    full = lax.axis_size(DP) == 8
    ins = dict(
        lens=(lengths, SMEM), gain1=(ln1_gain, VMEM), bias1=(ln1_bias, VMEM), bias_q=(bias_q, VMEM),
        bias_v=(bias_v, VMEM), b_out=(bias_out, VMEM), gain2=(ln2_gain, VMEM), bias2=(ln2_bias, VMEM),
        b_fc=(bias_fc, VMEM), b_proj=(bias_proj, VMEM), tok_h=(tokens, ANY), cot_h=(cotangent, ANY),
        w_qkv=(w_qkv, ANY), w_out_h=(w_out, ANY), w_fc_h=(w_fc, ANY), w_proj_h=(w_proj, ANY),
    )
    block_output, grad_tokens, vec, *rest = block(ins, full, 1.0 / math.sqrt(tokens.shape[0] * device_count))
    if full:
        return emit(block_output, grad_tokens, vec, *rest)
    gq, g_fc, g_proj = rest
    proj_total, fc_total, out_total, qkv_total, vec = sums_by_xla(gq, g_proj, g_fc, vec)
    return (
        block_output, grad_tokens, vec[8], vec[9], qkv_total, vec[10], vec[11], out_total, vec[0], vec[1], vec[2],
        fc_total, vec[4:8].reshape(-1), proj_total, vec[3],
    )


def sums_by_xla(gq, g_proj, g_fc, vec):
    _, blocks, length, width = g_proj.shape
    small = width // 8
    whole = g_proj.transpose(1, 0, 2, 3).reshape(2 * blocks * length, width)
    fc = g_fc[:, :, :length].transpose(1, 0, 2, 3).reshape(2 * blocks * length, width).T
    out = g_fc[:, :, length:].transpose(1, 0, 2, 3).reshape(width, width)
    core, odd = lax.rem(lax.axis_index(DP), 2), lax.rem(lax.axis_index(HEAD), 2)
    window = gq.reshape(2, 4, 3, small, 256).transpose(1, 0, 3, 2, 4).reshape(width, 3, 256)
    qkv = lax.dynamic_update_slice(
        jnp.zeros((width, 3, width), BF16), window, (0, 0, odd * (width // 2) + core * 128)
    ).reshape(width, 3 * width)

    def reduce_mat(g, dim):
        share = lax.psum_scatter(g, DP, scatter_dimension=dim, tiled=True)
        return lax.psum(share, HEAD).astype(F32)

    return reduce_mat(whole, 0), reduce_mat(fc, 1), reduce_mat(out, 0), reduce_mat(qkv, 0), lax.psum(vec, (DP, HEAD))


def solution(mesh):
    rows = P((DP, HEAD), None)
    return jax.shard_map(
        shards,
        mesh=mesh,
        in_specs=(rows, P(DP, None)) + (P(),) * 13 + (rows,),
        out_specs=(
            rows, rows, P(), P(), P(DP, None), P(), P(), P(DP, None), P(), P(), P(), P(None, DP), P(),
            P(DP, None), P(),
        ),
        check_vma=False,
    )
```

```python
import functools
import math
import types

import jax
import jax.numpy as jnp
from jax import lax
from jax.experimental import pallas as pl
from jax.experimental.pallas import tpu as pltpu
from jax.sharding import PartitionSpec as P

DP, HEAD = "dp", "head"
HEAD_DIM = 64
EPSILON = 1e-05
DEPTH_SCALE = 1.0 / math.sqrt(12.0)
LOG2E = 1.0 / math.log(2.0)
SCORE_SCALE = HEAD_DIM ** (-0.5)
GELU_K = math.sqrt(2.0 / math.pi)
GELU_A = 0.044715
TEAM = 8
QB = 256
VMEM_LIMIT = 63 << 20
PIECES = 3

INWARD, ACROSS, OUTWARD = range(3)

F32 = jnp.float32
BF16 = jnp.bfloat16
MESH = pl.DeviceIdType.MESH
ANY = pl.BlockSpec(memory_space=pl.ANY)
VMEM = pl.BlockSpec(memory_space=pltpu.VMEM)
SMEM = pl.BlockSpec(memory_space=pltpu.SMEM)


def dot(a, b):
    return jnp.dot(a, b, preferred_element_type=F32)


def dot_nt(a, b):
    return lax.dot_general(a, b, (((1,), (1,)), ((), ())), preferred_element_type=F32)


def dot_tn(a, b):
    return lax.dot_general(a, b, (((0,), (0,)), ((), ())), preferred_element_type=F32)


def mult(x, m):
    return pl.multiple_of(x, m)


def place():
    dp, h = lax.axis_index(DP), lax.axis_index(HEAD)
    core = lax.rem(dp, 2)
    half = h // 2
    return types.SimpleNamespace(
        dp=dp,
        h=h,
        core=core,
        sib=dp + 1 - 2 * core,
        even=dp - core,
        half=half,
        served=dp - core + half,
        block=(h - 2 * half) * 2 + core,
    )


def greet(at, chips=False):
    barrier = pltpu.get_barrier_semaphore()
    me = at.core * 4 + at.h
    others = []
    for k in range(1, TEAM):
        other = lax.rem(me + k, TEAM)
        others.append((at.even + other // 4, lax.rem(other, 4)))
    if chips:
        for k in range(1, 4):
            others.append((lax.rem(at.dp + 2 * k, 8), at.h))
    for other in others:
        pl.semaphore_signal(barrier, inc=1, device_id=other, device_id_type=MESH)
    return len(others)


def scoped(body, **buffers):
    pl.run_scoped(
        lambda *refs: body(named(buffers, refs)), *(pltpu.VMEM(shape, kind) for shape, kind in buffers.values())
    )


def named(names, refs):
    return types.SimpleNamespace(**dict(zip(names, refs, strict=True)))


def remote(src, dst, send, recv, device):
    return pltpu.make_async_remote_copy(
        src_ref=src, dst_ref=dst, send_sem=send, recv_sem=recv, device_id=device, device_id_type=MESH
    )


def row(vec):
    return vec[...].reshape(1, vec.shape[0])


def norm_parts(v):
    center = jnp.mean(v, axis=-1, keepdims=True)
    cent = v - center
    r = lax.rsqrt(jnp.mean(cent * cent, axis=-1, keepdims=True) + EPSILON)
    return cent * r, r


def norm_back(e, gain, n, r):
    ea = e * gain
    return r * (ea - jnp.mean(ea, axis=-1, keepdims=True) - n * jnp.mean(ea * n, axis=-1, keepdims=True))


def block_kernel(grad_scale, full, names, *refs):
    ref = named(names, refs)
    at = place()
    rows, width = ref.tok.shape
    group, part, chunks = 4 * rows, width // 4, ref.gfc.shape[1]
    heads = part // HEAD_DIM
    sums = Sums(ref, at) if full else None
    tok_copy = pltpu.make_async_copy(ref.tok_h, ref.tok, ref.in_sem.at[0])
    tok_copy.start()

    @pl.when(at.core != at.half)
    def _():
        ref.arrive2[1] = jnp.zeros((rows, width), BF16)

    scoped(
        lambda buf: attend(ref, buf, at, tok_copy, full),
        xn=((rows, width), BF16), wwin=((3, width, 256), BF16), brow=((8, width), F32),
        bcol=((3, 256, 128), F32), kh=((group, HEAD_DIM), BF16), scores=((group, QB), F32),
    )
    scoped(
        lambda buf: feed_forward(ref, buf, at, sums, grad_scale),
        cot=((rows, width), BF16), w_out=((width, width), BF16), w_fc=((2, width, width), BF16),
        w_proj=((2, width, width), BF16), brow=((8, chunks * width), F32),
        dfc=((chunks, rows, width), BF16), gproj=((2, chunks, width // 2, width), BF16),
        out=((rows, width), F32),
    )
    scoped(
        lambda buf: attend_back(ref, buf, at, sums, grad_scale),
        kh=((heads, group, HEAD_DIM), BF16), vh=((heads, group, HEAD_DIM), BF16),
        qh=((heads, group, HEAD_DIM), BF16), doh=((heads, group, HEAD_DIM), BF16),
        dk=((heads, group, HEAD_DIM), F32), dv=((heads, group, HEAD_DIM), F32),
        dq=((heads, HEAD_DIM, group), F32), delta=((8 * heads, group), F32), dmix=((3 * 256, group), BF16), partial=((2, rows, width), BF16),
        summed=((2, rows, width), BF16), gtok=((rows, width), F32),
        gq=((2, 4, 3 * (width // 8), 256), BF16), u=((4, 3 * (width // 8), width // 2), BF16),
    )


def attend(ref, buf, at, tok_copy, full):
    dp, h, core, sib = at.dp, at.h, at.core, at.sib
    rows, width = ref.tok.shape
    group, part = 4 * rows, width // 4
    heads = part // HEAD_DIM
    xn, xg, xgt, wwin, wt, mix, ot, lens = buf.xn, ref.xg, ref.xgt, buf.wwin, ref.wt, ref.mix, ref.ot, ref.lens
    collects = core == at.half
    first = (h - 2 * at.half) * 2 * part + core * 128
    shift = mult(64 * core, 64)
    ag_send, ag_recv, fw_send, st_sem, w_sem = ref.ag_send, ref.ag_recv, ref.fw_send, ref.st_sem, ref.w_sem
    for p in range(3):
        pltpu.make_async_copy(
            ref.w_qkv.at[:, pl.ds(mult(p * width + first, 128), 256)], wwin.at[p], w_sem.at[p]
        ).start()
    greeted = greet(at, full)
    tok_copy.wait()
    n, _ = norm_parts(ref.tok[...].astype(F32))
    xn[...] = (n * row(ref.gain1) + row(ref.bias1)).astype(BF16)

    for p in range(3):
        pltpu.make_async_copy(wwin.at[p], wwin.at[p], w_sem.at[p]).wait()
        wt[p * 256 : (p + 1) * 256, :] = wwin[p].T
    for p, vec in ((0, ref.bias_q), (2, ref.bias_v)):
        buf.brow[...] = jnp.broadcast_to(row(vec), (8, width))
        buf.bcol[p] = jnp.broadcast_to(buf.brow[0:1, pl.ds(mult(first, 128), 256)], (128, 256)).T
    buf.bcol[1] = jnp.zeros((256, 128), F32)

    pl.semaphore_wait(pltpu.get_barrier_semaphore(), greeted)

    inner, outer = 1 + core, 3 * core
    at_inner, at_outer = h == inner, h == outer

    length = rows // PIECES

    def piece(ref, s, q):
        return ref.at[pl.ds(mult(s * rows + q * length, length), length), :]

    def to_inner(q):
        return remote(piece(xn, 0, q), piece(xg, h, q), ag_send.at[q], ag_recv.at[h, q], (dp, inner))

    def to_outer(k, s, q):
        src = piece(xn, 0, q) if k == 0 else piece(xg, s, q)
        return remote(src, piece(xg, s, q), ag_send.at[k * PIECES + q], ag_recv.at[s, q], (dp, outer))

    def to_sib(d, s, q):
        src = piece(xn, 0, q) if d == 0 else piece(xg, s, q)
        return remote(src, piece(xg, s, q), fw_send.at[d * PIECES + q], ag_recv.at[s, q], (sib, h))

    @pl.when(at_inner)
    def _():
        for q in range(PIECES):
            to_outer(0, h, q).start()

    @pl.when(jnp.logical_not(at_inner))
    def _():
        for q in range(PIECES):
            to_inner(q).start()

    @pl.when(collects)
    def _():
        for q in range(PIECES):
            to_sib(0, h, q).start()
        xg[pl.ds(mult(h * rows, rows), rows), :] = xn[...]

    places = lax.broadcasted_iota(jnp.int32, (8, group), 1)
    begin = jnp.zeros((8, group), jnp.int32)
    edge = lens[0, 0]
    for k in range(1, lens.shape[1] + 1):
        begin = jnp.where(places >= edge, edge, begin)
        if k < lens.shape[1]:
            edge = edge + lens[0, k]
    ref.start_mine[...] = begin.astype(F32)
    st_copy = remote(ref.start_mine, ref.start_sib, st_sem.at[0], st_sem.at[1], (sib, h))
    st_copy.start()

    low = 1 - at.half
    order = (h, low * (1 - h) + (1 - low) * (5 - h), 1 + low, 3 * low)

    def project(s):
        here = xg[pl.ds(mult(s * rows, rows), rows), :]
        xgt[:, pl.ds(mult(s * rows, 128), rows)] = here.T
        for p in range(3):
            res = dot_nt(wt[pl.ds(mult(p * 256 + shift, 64), part), :], here) + buf.bcol[p, pl.ds(shift, part), :][:, :1]
            mix[p * part : (p + 1) * part, pl.ds(mult(s * rows, 128), rows)] = res.astype(BF16)

    @pl.when(jnp.logical_not(collects))
    def _():
        for q in range(PIECES):
            to_sib(1, h, q).wait_recv()

    project(h)
    for q in range(PIECES):
        for d in (2, 3, 1):
            s = order[d]
            to_sib(d, s, q).wait_recv()

            @pl.when(collects)
            def _():
                to_sib(d, s, q).start()

            if d > 1:
                @pl.when(at_inner)
                def _():
                    to_outer(d - 1, s, q).start()

            if q == PIECES - 1:
                project(s)
    st_copy.wait_recv()
    ref.start[...] = jnp.where(collects, ref.start_mine[...], ref.start_sib[...]).astype(jnp.int32)
    scale = SCORE_SCALE * LOG2E

    def one_head(i, _):
        qrow, krow, vrow = (mult(p * part + i * HEAD_DIM, HEAD_DIM) for p in range(3))
        buf.kh[...] = mix[pl.ds(krow, HEAD_DIM), :].T
        for j in range(group // QB):
            cols = slice(j * QB, (j + 1) * QB)
            q_t = mix[pl.ds(qrow, HEAD_DIM), cols]
            begins = ref.start[0:1, cols]
            top = jnp.full((1, QB), -jnp.inf, F32)
            for k in range(j + 1):
                s_t = dot(buf.kh[k * QB : (k + 1) * QB, :], q_t)
                key = lax.broadcasted_iota(jnp.int32, (QB, QB), 0)
                keep = key >= begins - k * QB
                if k == j:
                    keep = jnp.logical_and(keep, key <= lax.broadcasted_iota(jnp.int32, (QB, QB), 1))
                s_t = jnp.where(keep, s_t, -1e30)
                buf.scores[k * QB : (k + 1) * QB, :] = s_t
                top = jnp.maximum(top, jnp.max(s_t, axis=0, keepdims=True))
            top = top * scale
            total = jnp.zeros((1, QB), F32)
            acc = jnp.zeros((HEAD_DIM, QB), F32)
            for k in range(j + 1):
                p_t = jnp.exp2(buf.scores[k * QB : (k + 1) * QB, :] * scale - top)
                total = total + jnp.sum(p_t, axis=0, keepdims=True)
                acc = acc + dot(mix[pl.ds(vrow, HEAD_DIM), k * QB : (k + 1) * QB], p_t.astype(BF16))
            ot[pl.ds(qrow, HEAD_DIM), cols] = (acc / total).astype(BF16)
            ref.lse[pl.ds(mult(i * 8, 8), 8), cols] = jnp.broadcast_to(top + jnp.log2(total), (8, QB))
            for s in range(4):
                if j == ((s + 1) * rows - 1) // QB:
                    send_attended(ref, at, i, s)
        return 0

    lax.fori_loop(0, heads, one_head, 0)

    @pl.when(at_inner)
    def _():
        for q in range(PIECES):
            for d in range(1, 4):
                to_outer(d - 1, order[d], q).wait_send()

    @pl.when(jnp.logical_not(at_inner))
    def _():
        for q in range(PIECES):
            to_inner(q).wait_send()

    @pl.when(collects)
    def _():
        for q in range(PIECES):
            for d in range(4):
                to_sib(d, order[d], q).wait_send()

    st_copy.wait_send()


def attended_ends(ref, at, i, s):
    rows, width = ref.tok.shape
    src = ref.ot.at[pl.ds(mult(i * HEAD_DIM, HEAD_DIM), HEAD_DIM), pl.ds(s * rows, rows)]
    dst = ref.att.at[pl.ds(mult(at.block * (width // 4) + i * HEAD_DIM, HEAD_DIM), HEAD_DIM), :]
    return src, dst


def attended_stays(at, s):
    return jnp.logical_and(at.core == at.half, at.h == s)


def attended_local(ref, at, i, s):
    return pltpu.make_async_copy(*attended_ends(ref, at, i, s), ref.at_local.at[i])


def attended_remote(ref, at, i, s):
    src, dst = attended_ends(ref, at, i, s)
    heads = ref.at_local.shape[0]
    return remote(
        src, dst, ref.at_send.at[i * 4 + s], ref.at_recv.at[at.block * heads + i], (at.served, s)
    )


def send_attended(ref, at, i, s):
    @pl.when(attended_stays(at, s))
    def _():
        attended_local(ref, at, i, s).start()

    @pl.when(jnp.logical_not(attended_stays(at, s)))
    def _():
        attended_remote(ref, at, i, s).start()


def wait_attended(ref, at):
    rows, width = ref.tok.shape
    part, heads = width // 4, ref.at_local.shape[0]
    for i in range(heads):
        for s in range(4):
            @pl.when(attended_stays(at, s))
            def _():
                attended_local(ref, at, i, s).wait()

            @pl.when(jnp.logical_not(attended_stays(at, s)))
            def _():
                attended_remote(ref, at, i, s).wait_send()
        for b in range(4):
            dst = ref.att.at[pl.ds(b * part + i * HEAD_DIM, HEAD_DIM), :]
            src = ref.ot.at[pl.ds(i * HEAD_DIM, HEAD_DIM), pl.ds(0, rows)]

            @pl.when(jnp.logical_not(jnp.logical_and(at.core == at.half, at.block == b)))
            def _():
                remote(
                    src, dst, ref.at_send.at[i * 4], ref.at_recv.at[b * heads + i], (at.sib, at.h)
                ).wait_recv()


def feed_forward(ref, buf, at, sums, grad_scale):
    h, core = at.h, at.core
    rows, width = ref.tok.shape
    part = width // 4
    chunks = ref.gfc.shape[1]
    paired = sums is not None
    tok, att, cot, vec = ref.tok, ref.att, buf.cot, ref.vec
    w_out, w_fc, w_proj, brow, dfc, dat = buf.w_out, buf.w_fc, buf.w_proj, buf.brow, buf.dfc, ref.dat
    gfc, gproj, gfc_in, gproj_in, r1, s2, r2, s3 = (
        ref.gfc, buf.gproj, ref.gfc_in, ref.gproj_in, ref.r1, ref.s2, ref.r2, ref.s3
    )
    pair_send, pair_recv, one_send, one_recv, two_send, two_recv = (
        ref.pair_send, ref.pair_recv, ref.p1_send, ref.p1_recv, ref.p2_send, ref.p2_recv
    )
    cot_copy = pltpu.make_async_copy(ref.cot_h, cot, ref.in_sem.at[1])
    wo_copy = pltpu.make_async_copy(ref.w_out_h, w_out, ref.in_sem.at[2])
    cot_copy.start()
    wo_copy.start()

    def ff_copy(step, which):
        slot, here = step % 2, pl.ds(mult(order[step] * width, 128), width)
        if which == 0:
            return pltpu.make_async_copy(ref.w_fc_h.at[:, here], w_fc.at[slot], ref.ff_sem.at[0, slot])
        return pltpu.make_async_copy(ref.w_proj_h.at[here, :], w_proj.at[slot], ref.ff_sem.at[1, slot])

    half_rows = width // 2
    small = width // 8
    y, x = at.dp // 4, lax.rem(at.dp // 2, 2)

    def pair_copy(ref, into, k, j):
        return remote(ref.at[1 - core, j], into.at[j], pair_send.at[k, j], pair_recv.at[k, j], (at.sib, h))

    def pair_add(ref, into, k, j):
        pair_copy(ref, into, k, j).wait_recv()
        ref[core, j] = (ref[core, j].astype(F32) + into[j].astype(F32)).astype(BF16)

    if paired:
        order = [(1 - y) * 2 + 1 - x, y * 2 + 1 - x, (1 - y) * 2 + x, y * 2 + x]
    else:
        order = list(range(chunks))
    quarter = half_rows // 2
    flips = (at.dp + 2 - 4 * x, h), (at.dp + 4 - 8 * y, h)

    def halves(k):
        return slice(k * quarter, (k + 1) * quarter)

    def one(k, t):
        j = order[0] if t == 0 else order[1 + k]
        src = ref.late if (k, t) == (1, 1) else gproj.at[core, j, halves(k)]
        return remote(src, r1.at[k, t], one_send.at[k, t], one_recv.at[k, t], flips[k])

    def two(k):
        return remote(s2.at[k], r2.at[k], two_send.at[k], two_recv.at[k], flips[1 - k])

    def first_sum(k):
        one(k, 0).wait_recv()
        s2[k] = (gproj[core, order[2 - k], halves(k)].astype(F32) + r1[k, 0].astype(F32)).astype(BF16)
        two(k).start()

    def proj_sums(step):
        if not paired:
            return
        pair_add(gproj, gproj_in, 0, order[step])
        if step == 0:
            one(0, 0).start()
            one(1, 0).start()
        elif step == 1:
            one(0, 1).start()
        elif step == 2:
            first_sum(1)
            first_sum(0)
            ref.late[...] = gproj[core, order[2], halves(1)]
            one(1, 1).start()
        else:
            s3[...] = gproj[core, order[3]]

    for step in range(2):
        for which in range(2):
            ff_copy(step, which).start()
    vec[...] = jnp.zeros_like(vec)
    brow[...] = jnp.broadcast_to(row(ref.b_fc), brow.shape)
    cot_copy.wait()
    dy = cot[...].astype(F32)
    d_proj = (DEPTH_SCALE * dy).astype(BF16)
    wo_copy.wait()
    wait_attended(ref, at)
    middle = tok[...].astype(F32) + DEPTH_SCALE * (dot_tn(att[...], w_out[...]) + row(ref.b_out))
    n, r = norm_parts(middle)
    second = (n * row(ref.gain2) + row(ref.bias2)).astype(BF16)
    result = middle + DEPTH_SCALE * row(ref.b_proj)
    d_second = jnp.zeros((rows, width), F32)
    vec[3:4, :] = jnp.sum(dy, axis=0, keepdims=True) * (DEPTH_SCALE * grad_scale)
    for step, j in enumerate(order):
        slot = step % 2
        ff_copy(step, 0).wait()
        u = dot(second, w_fc[slot]) + brow[0:1, pl.ds(mult(j * width, 128), width)]
        u2 = u * u
        th = jnp.tanh(GELU_K * u * (1.0 + GELU_A * u2))
        half = 0.5 * (1.0 + th)
        slope = half + 0.5 * u * (1.0 - th * th) * (GELU_K * (1.0 + 3.0 * GELU_A * u2))
        hidden = (u * half).astype(BF16)
        ff_copy(step, 1).wait()
        result = result + DEPTH_SCALE * dot(hidden, w_proj[slot])
        d_pre = dot_nt(d_proj, w_proj[slot]) * slope
        if step > 0:
            proj_sums(step - 1)
        res = (dot_tn(hidden, d_proj) * grad_scale).astype(BF16)
        for k in range(2):
            gproj[k, j] = res[k * half_rows : (k + 1) * half_rows]
        if paired:
            pair_copy(gproj, gproj_in, 0, j).start()
        vec[pl.ds(4 + j, 1), :] = jnp.sum(d_pre, axis=0, keepdims=True) * grad_scale
        d_fc = d_pre.astype(BF16)
        dfc[j] = d_fc
        d_second = d_second + dot_nt(d_fc, w_fc[slot])
        if step + 2 < chunks:
            for which in range(2):
                ff_copy(step + 2, which).start()
    buf.out[...] = result
    out_copy = pltpu.make_async_copy(buf.out, ref.out_o, ref.out_sem.at[0])
    out_copy.start()
    vec[1:2, :] = jnp.sum(d_second * n, axis=0, keepdims=True) * grad_scale
    vec[2:3, :] = jnp.sum(d_second, axis=0, keepdims=True) * grad_scale
    d_middle = dy + norm_back(d_second, row(ref.gain2), n, r)
    ref.dmid[...] = d_middle
    vec[0:1, :] = jnp.sum(d_middle, axis=0, keepdims=True) * (DEPTH_SCALE * grad_scale)
    d_out = (DEPTH_SCALE * d_middle).astype(BF16)
    dat[...] = dot_nt(w_out[...], d_out).astype(BF16)

    send_d_attended(ref, at)

    def fc_sums(step):
        if not paired:
            return
        pair_add(gfc, gfc_in, 1, order[step])
        if step == 0:
            sums.one(1, 0).start()
            sums.one(2, 0).start()
        elif step < 3:
            sums.one(step, 1).start()

    g_out = (dot(att[...], d_out) * grad_scale).astype(BF16)
    for j in range(chunks):
        for k in range(2):
            gfc[k, j, half_rows:, :] = g_out[(2 * j + k) * small : (2 * j + k + 1) * small]
    for step, j in enumerate(order):
        if step == 1:
            proj_sums(chunks - 1)
        res = (dot_tn(dfc[j], second) * grad_scale).astype(BF16)
        for k in range(2):
            gfc[k, j, :half_rows, :] = res[k * half_rows : (k + 1) * half_rows]
        if paired:
            pair_copy(gfc, gfc_in, 1, j).start()
        if step > 1:
            fc_sums(step - 2)
    for step in (chunks - 2, chunks - 1):
        fc_sums(step)
    if paired:
        for j in order:
            pair_copy(gproj, gproj_in, 0, j).wait_send()
        for k in range(2):
            for t in range(2 - k):
                one(k, t).wait_send()
    else:
        outs = [
            pltpu.make_async_copy(gproj, ref.gproj_o, ref.out_sem.at[1]),
            pltpu.make_async_copy(gfc, ref.gfc_o, ref.out_sem.at[2]),
        ]
        for copy in outs:
            copy.start()
        for copy in outs:
            copy.wait()
    out_copy.wait()


def d_attended_part(at, i):
    b = lax.rem(2 * at.core + i, 4)
    return b, (at.even + lax.rem(b, 2), 2 * at.core + b // 2)


def d_attended_stays(at, i):
    b, _ = d_attended_part(at, i)
    return jnp.logical_and(at.core == lax.rem(b, 2), at.h == 2 * at.core + b // 2)


def d_attended_ends(ref, at, b):
    rows, width = ref.tok.shape
    part = width // 4
    src = ref.dat.at[pl.ds(mult(b * part, HEAD_DIM), part), :]
    return src, ref.do_t.at[:, pl.ds(mult(at.h * rows, 128), rows)]


def d_attended_local(ref, at, i):
    return pltpu.make_async_copy(*d_attended_ends(ref, at, d_attended_part(at, i)[0]), ref.da_local)


def d_attended_remote(ref, at, i):
    b, device = d_attended_part(at, i)
    src, dst = d_attended_ends(ref, at, b)
    return remote(src, dst, ref.da_send.at[i], ref.da_recv.at[at.h], device)


def send_d_attended(ref, at):
    for i in range(4):
        @pl.when(d_attended_stays(at, i))
        def _():
            d_attended_local(ref, at, i).start()

        @pl.when(jnp.logical_not(d_attended_stays(at, i)))
        def _():
            d_attended_remote(ref, at, i).start()


def wait_d_attended(ref, at):
    rows, width = ref.tok.shape
    part = width // 4
    served_here = at.core == at.half
    for i in range(4):
        @pl.when(d_attended_stays(at, i))
        def _():
            d_attended_local(ref, at, i).wait()

        @pl.when(jnp.logical_not(d_attended_stays(at, i)))
        def _():
            d_attended_remote(ref, at, i).wait_send()
    for s in range(4):
        @pl.when(jnp.logical_not(jnp.logical_and(served_here, at.h == s)))
        def _():
            remote(
                ref.dat.at[pl.ds(0, part), :], ref.do_t.at[:, pl.ds(s * rows, rows)], ref.da_send.at[0],
                ref.da_recv.at[s], (at.sib, at.h),
            ).wait_recv()


def attend_back(ref, buf, at, sums, grad_scale):
    full = sums is not None
    dp, h, core, sib = at.dp, at.h, at.core, at.sib
    rows, width = ref.tok.shape
    part, group = width // 4, 4 * rows
    heads = part // HEAD_DIM
    mix, do_t, ot, xgt, wt, lse, start = ref.mix, ref.do_t, ref.ot, ref.xgt, ref.wt, ref.lse, ref.start
    delta, kh, vh, qh, doh, dk, dv, dmix = buf.delta, buf.kh, buf.vh, buf.qh, buf.doh, buf.dk, buf.dv, buf.dmix
    dq = buf.dq
    partial, summed, arrive, arrive2 = buf.partial, buf.summed, ref.arrive, ref.arrive2
    sw_send, sw_recv, fin_send, fin_recv, fin_local = (
        ref.sw_send, ref.sw_recv, ref.fin_send, ref.fin_recv, ref.fin_local
    )
    dmix[...] = jnp.zeros_like(dmix)
    wait_d_attended(ref, at)
    scale = SCORE_SCALE * LOG2E

    def drow(p, i):
        return pl.ds(mult(p * 256 + (core + i) * HEAD_DIM, HEAD_DIM), HEAD_DIM)

    half = at.half
    blocks = group // QB
    far_cols = pl.ds(mult((1 - half) * (group // 2), 128), group // 2)
    near_cols = pl.ds(mult(half * (group // 2), 128), group // 2)

    def ready(i):
        qrow, krow, vrow = (mult(p * part + i * HEAD_DIM, HEAD_DIM) for p in range(3))
        d_head = do_t[pl.ds(qrow, HEAD_DIM), :]
        delta[pl.ds(mult(i * 8, 8), 8), :] = jnp.broadcast_to(
            jnp.sum(d_head.astype(F32) * ot[pl.ds(qrow, HEAD_DIM), :].astype(F32), axis=0, keepdims=True), (8, group)
        )
        qh[i] = mix[pl.ds(qrow, HEAD_DIM), :].T
        kh[i] = mix[pl.ds(krow, HEAD_DIM), :].T
        vh[i] = mix[pl.ds(vrow, HEAD_DIM), :].T
        doh[i] = d_head.T
        dq[i] = jnp.zeros((HEAD_DIM, group), F32)
        dk[i] = jnp.zeros((group, HEAD_DIM), F32)
        dv[i] = jnp.zeros((group, HEAD_DIM), F32)

    def pair(i, o, t):
        k = half * o + (1 - half) * (blocks - 1 - o - t)
        q = half * (o + t) + (1 - half) * (blocks - 1 - o)
        keys, cols = pl.ds(mult(k * QB, QB), QB), pl.ds(mult(q * QB, QB), QB)
        qrow, krow = (mult(p * part + i * HEAD_DIM, HEAD_DIM) for p in range(2))
        stats = pl.ds(mult(i * 8, 8), 8)
        s_t = dot(kh[i, keys, :], mix[pl.ds(qrow, HEAD_DIM), cols])
        key = lax.broadcasted_iota(jnp.int32, (QB, QB), 0)
        keep = key >= start[0:1, cols] - k * QB
        if t == 0:
            keep = jnp.logical_and(keep, key <= lax.broadcasted_iota(jnp.int32, (QB, QB), 1))
        p_t = jnp.where(keep, jnp.exp2(s_t * scale - lse[stats, cols][0:1]), 0.0)
        dp_t = dot(vh[i, keys, :], do_t[pl.ds(qrow, HEAD_DIM), cols])
        ds_t = (p_t * (dp_t - delta[stats, cols][0:1])).astype(BF16)
        dv[i, keys, :] += dot(p_t.astype(BF16), doh[i, cols, :])
        dk[i, keys, :] += dot(ds_t, qh[i, cols, :])
        dq[i, :, cols] += dot(mix[pl.ds(krow, HEAD_DIM), keys], ds_t)

    def done(i, cols):
        dmix[drow(0, i), cols] = (dq[i, :, cols] * SCORE_SCALE).astype(BF16)
        dmix[drow(1, i), cols] = (dk[i, cols, :] * SCORE_SCALE).T.astype(BF16)
        dmix[drow(2, i), cols] = dv[i, cols, :].T.astype(BF16)

    def far_head(i, _):
        ready(i)
        for o in range(blocks // 2):
            for t in range(blocks - o):
                pair(i, o, t)
            if full and o == 0:
                @pl.when(i == 0)
                def _():
                    sums.proj_last()
                    sums.send_in(0, (0,))

                for q in (1, 2):
                    @pl.when(i == q)
                    def _():
                        sums.send_in(0, (q,))
            if full and o == 1:
                @pl.when(i == 2)
                def _():
                    sums.add_across(0, (0,))
            if full and o == 2:
                for q in range(3):
                    @pl.when(i == q)
                    def _():
                        sums.add_inner(0, (q,))
        done(i, far_cols)
        return 0

    def near_head(i, _):
        for o in range(blocks // 2, blocks):
            for t in range(blocks - o):
                pair(i, o, t)
        done(i, near_cols)

        @pl.when(i == 1)
        def _():
            send_far(1)

        return 0

    def part_of(s):
        return dot_tn(dmix[:, pl.ds(mult(s * rows, 128), rows)], wt[...])

    slot, inner = h - 2 * at.half, 1 + at.half
    at_inner = h == inner
    ways = (1 - at.half, at.half)
    length = rows // PIECES
    def pass_on(q):
        @pl.when(at_inner)
        def _():
            here = slice(q * length, (q + 1) * length)
            far_in(q).wait_recv()
            summed[0, here] = (summed[0, here].astype(F32) + ref.far[here].astype(F32)).astype(BF16)
            far_out(q).start()

    def swap(k):
        return remote(partial.at[k], arrive.at[k], sw_send.at[k], sw_recv.at[k], (sib, h))

    def sib_part(k):
        partial[k] = part_of(2 * ways[k] + 1 - core).astype(BF16)
        swap(k).start()

    def own_part(k):
        mine = part_of(2 * ways[k] + core)
        swap(k).wait_recv()
        summed[k] = (mine + arrive[k].astype(F32)).astype(BF16)

    def far_in(q):
        here = slice(q * length, (q + 1) * length)
        return remote(summed.at[0, here], ref.far.at[here], ref.far_send.at[q], ref.far_recv.at[q], (dp, inner))

    def far_out(q):
        here = slice(q * length, (q + 1) * length)
        return remote(
            summed.at[0, here], arrive2.at[0, here], ref.far_send.at[q], ref.out_recv.at[q],
            (at.served, 2 * ways[0] + core),
        )

    def near_remote():
        return remote(summed.at[1], arrive2.at[slot], fin_send, fin_recv.at[slot], (at.served, 2 * ways[1] + core))

    def near_local():
        return pltpu.make_async_copy(summed.at[1], arrive2.at[slot], fin_local)

    stays = jnp.logical_and(core == at.half, h == 2 * ways[1] + core)
    lax.fori_loop(0, heads, far_head, 0)
    sib_part(0)
    own_part(0)

    def send_far(q):
        @pl.when(jnp.logical_not(at_inner))
        def _():
            far_in(q).start()

    send_far(0)

    if full:
        sums.add_first(1)
        sums.add_first(2)
        sums.add_across(0, (1,))
    lax.fori_loop(0, heads, near_head, 0)
    sib_part(1)
    pass_on(0)
    vec, gq = ref.vec, buf.gq
    first = slot * 2 * part + core * 128
    small = width // 8
    gain_sum = jnp.zeros((1, width), F32)
    bias_sum = jnp.zeros((1, width), F32)
    for p in range(3):
        d_cols = dmix[p * 256 : (p + 1) * 256, :]
        tok_sum = jnp.sum(d_cols.astype(F32), axis=1, keepdims=True) * grad_scale
        w_cols = wt[p * 256 : (p + 1) * 256, :].astype(F32)
        res = dot_nt(d_cols, xgt[...]) * grad_scale
        gain_sum = gain_sum + jnp.sum(w_cols * res, axis=0, keepdims=True)
        bias_sum = bias_sum + jnp.sum(w_cols * tok_sum, axis=0, keepdims=True)
        if p != 1:
            vec[10 + p // 2 : 11 + p // 2, pl.ds(mult(first, 128), 256)] = jnp.broadcast_to(tok_sum, (256, 128)).T[:1]
        res = res.astype(BF16).T
        for k in range(8):
            gq[k % 2, k // 2, p * small : (p + 1) * small, :] = res[k * small : (k + 1) * small]
    vec[8:9, :] = (gain_sum - row(ref.bias1) * bias_sum) / row(ref.gain1)
    vec[9:10, :] = bias_sum
    def near(now):
        @pl.when(jnp.logical_and(now, stays))
        def _():
            near_local().start()

        @pl.when(jnp.logical_and(now, jnp.logical_not(stays)))
        def _():
            near_remote().start()

    send_far(2)
    if full:
        sums.vectors_first()
        sums.heads_first(gq)
    pass_on(1)
    if full:
        sums.add_across(0, (2,))
        sums.heads_second(gq, buf.u)
        sums.vectors_second()
        sums.add_second(1)
        sums.send_in(1, (0,))
    pass_on(2)
    own_part(1)
    near(at_inner)
    if full:
        sums.add_second(2)
        sums.send_in(1, (1, 2))
        sums.add_inner(1)
        sums.send_in(2)
        sums.heads_third(buf.u)
        sums.add_inner(2)
    near(jnp.logical_not(at_inner))
    if full:
        sums.add_across(1)
        sums.heads_fourth()
        sums.vectors_third()
        sums.add_across(2)

    owner_far = core != at.half

    @pl.when(owner_far)
    def _():
        for q in range(PIECES):
            far = slice(q * length, (q + 1) * length)
            remote(
                summed.at[0, far], arrive2.at[0, far], ref.far_send.at[q], ref.out_recv.at[q], (sib, h)
            ).wait_recv()

    @pl.when(jnp.logical_not(owner_far))
    def _():
        for k in range(2):
            from_me = jnp.logical_and(slot == k, lax.rem(h, 2) == core)

            @pl.when(from_me)
            def _():
                pltpu.make_async_copy(summed.at[1], arrive2.at[k], fin_local).wait()

            @pl.when(jnp.logical_not(from_me))
            def _():
                remote(summed.at[1], arrive2.at[k], fin_send, fin_recv.at[k], (sib, h)).wait_recv()

    e = arrive2[0].astype(F32) + arrive2[1].astype(F32)
    n, r = norm_parts(ref.tok[...].astype(F32))
    buf.gtok[...] = ref.dmid[...] + norm_back(e, row(ref.gain1), n, r)
    gtok_copy = pltpu.make_async_copy(buf.gtok, ref.gtok_o, ref.out_sem.at[1])
    gtok_copy.start()
    if full:
        sums.vectors_fourth()
        sums.heads_last(gq, buf.u)
        sums.vectors_last()
        sums.finish()
    else:
        ref.vec_o[...] = vec[...]
        gq_copy = pltpu.make_async_copy(gq, ref.gq_o, ref.out_sem.at[2])
        gq_copy.start()
        gq_copy.wait()
    for k in range(2):
        swap(k).wait_send()
    for q in range(PIECES):
        far_in(q).wait_send()

    @pl.when(jnp.logical_not(stays))
    def _():
        near_remote().wait_send()
    gtok_copy.wait()


class Sums:
    def __init__(self, ref, at):
        self.ref, self.at = ref, at
        dp, self.h, self.core = at.dp, at.h, at.core
        self.y, self.x = dp // 4, lax.rem(dp // 2, 2)
        self.flip_x, self.flip_y = dp + 2 - 4 * self.x, dp + 4 - 8 * self.y
        self.flip_xy = self.flip_x + 4 - 8 * self.y
        self.outer = self.h * (3 - self.h) == 0

    def rows_of(self, k):
        length = self.ref.gfc.shape[2] // 2
        return slice(0, self.ref.s3.shape[0]) if k == 0 else slice((k - 1) * length, k * length)

    def block(self, k, t, across):
        x, y = self.x, self.y
        first, then = (y, x) if k == 2 else (x, y)
        first = 1 - first if across else first
        then = 1 - then if t == 0 else then
        return first * 2 + then if k == 2 else then * 2 + first

    def mine(self, k, t):
        return self.ref.gfc.at[self.core, self.block(k, t, False)]

    def one(self, k, t):
        ref, rows = self.ref, self.rows_of(k)
        return remote(
            ref.gfc.at[self.core, self.block(k, t, True), rows], ref.r1f.at[t, rows],
            ref.one_send.at[k, t], ref.one_recv.at[k, t], (self.flip_y if k == 2 else self.flip_x, self.h),
        )

    def two(self, k):
        ref, rows = self.ref, self.rows_of(k)
        return remote(
            self.mine(k, 0).at[rows], ref.r2f.at[rows],
            ref.two_send.at[k], ref.two_recv.at[k], (self.flip_x if k == 2 else self.flip_y, self.h),
        )

    def proj_in(self, k, step):
        ref, flips = self.ref, ((self.flip_x, self.h), (self.flip_y, self.h))
        if step == 1:
            return remote(ref.s2.at[k], ref.r1.at[k, 1], ref.p1_send.at[k, 1], ref.p1_recv.at[k, 1], flips[k])
        return remote(ref.s2.at[k], ref.r2.at[k], ref.p2_send.at[k], ref.p2_recv.at[k], flips[1 - k])

    def proj_last(self):
        ref = self.ref
        length = ref.r2.shape[1]
        for k in range(2):
            rows = slice(k * length, (k + 1) * length)
            self.proj_in(k, 1).wait_recv()
            self.proj_in(k, 2).wait_recv()
            ref.s3[rows] = (
                ref.s3[rows].astype(F32) + ref.r1[k, 1].astype(F32) + ref.r2[k].astype(F32)
            ).astype(BF16)

    def add_first(self, k):
        ref, rows, mine = self.ref, self.rows_of(k), self.mine(k, 0)
        self.one(k, 0).wait_recv()
        mine[rows] = (mine[rows].astype(F32) + ref.r1f[0, rows].astype(F32)).astype(BF16)
        self.two(k).start()

    def add_second(self, k):
        ref, rows, mine = self.ref, self.rows_of(k), self.mine(k, 1)
        self.one(k, 1).wait_recv()
        self.two(k).wait_recv()
        mine[rows] = (
            mine[rows].astype(F32) + ref.r1f[1, rows].astype(F32) + ref.r2f[rows].astype(F32)
        ).astype(BF16)

    def pieces(self, k):
        rows = self.rows_of(k)
        length = (rows.stop - rows.start) // PIECES
        for q in range(PIECES):
            yield k, k * PIECES + q, slice(rows.start + q * length, rows.start + (q + 1) * length)

    def bufs(self, k):
        ref = self.ref
        return (ref.s3, ref.zap, ref.zbp, ref.ztp) if k == 0 else (self.mine(k, 1), ref.zaf, ref.zbf, ref.ztf)

    def chain(self, k, m, rows, which):
        ref, h = self.ref, self.h
        s2, za, zb, zt = self.bufs(k)
        dp = self.at.dp
        if which == INWARD:
            return remote(s2.at[rows], za.at[rows], ref.z_send.at[0, m], ref.z_recv.at[0, m], (dp, 1 + h // 2))
        if which == ACROSS:
            return remote(s2.at[rows], zb.at[rows], ref.z_send.at[0, m], ref.z_recv.at[1, m], (dp, 3 - h))
        return remote(zt.at[rows], za.at[rows], ref.z_send.at[1, m], ref.z_recv.at[0, m], (dp, 3 * (h // 2)))

    def send_in(self, k, only=None):
        @pl.when(self.outer)
        def _():
            for q, piece in enumerate(self.pieces(k)):
                if only is None or q in only:
                    self.chain(*piece, INWARD).start()

    def add_inner(self, k, only=None):
        s2, za, _, _ = self.bufs(k)

        @pl.when(jnp.logical_not(self.outer))
        def _():
            for q, piece in enumerate(self.pieces(k)):
                if only is None or q in only:
                    rows = piece[2]
                    self.chain(*piece, INWARD).wait_recv()
                    s2[rows] = (s2[rows].astype(F32) + za[rows].astype(F32)).astype(BF16)
                    self.chain(*piece, ACROSS).start()

    def add_across(self, k, only=None):
        s2, _, zb, zt = self.bufs(k)

        @pl.when(jnp.logical_not(self.outer))
        def _():
            for q, piece in enumerate(self.pieces(k)):
                if only is None or q in only:
                    rows = piece[2]
                    self.chain(*piece, ACROSS).wait_recv()
                    zt[rows] = (s2[rows].astype(F32) + zb[rows].astype(F32)).astype(BF16)
                    self.chain(*piece, OUTWARD).start()

    def finish(self):
        @pl.when(self.outer)
        def _():
            for k in range(3):
                _, za, _, zt = self.bufs(k)
                for piece in self.pieces(k):
                    self.chain(*piece, OUTWARD).wait_recv()
                    zt[piece[2]] = za[piece[2]]

        for j in range(4):
            sib = (self.at.sib, self.h)
            remote(
                self.ref.gfc.at[1 - self.core, j], self.ref.gfc_in.at[j], self.ref.pair_send.at[1, j],
                self.ref.pair_recv.at[1, j], sib,
            ).wait_send()
        self.proj_in(1, 1).wait_send()
        for k in range(2):
            self.proj_in(k, 2).wait_send()
        for k in range(3):
            if k > 0:
                for t in range(2):
                    self.one(k, t).wait_send()
                self.two(k).wait_send()
            for piece in self.pieces(k):
                self.chain(*piece, INWARD).wait_send()

        @pl.when(jnp.logical_not(self.outer))
        def _():
            for k in range(3):
                for piece in self.pieces(k):
                    self.chain(*piece, OUTWARD).wait_send()

    def swap(self, gq):
        ref, core = self.ref, self.core
        return remote(gq.at[1 - core], ref.gq_in, ref.q_send.at[0], ref.q_recv.at[0], (self.at.sib, self.h))

    def spread(self, u, k):
        ref, x, y = self.ref, self.x, self.y
        to = (self.flip_x, self.flip_y, self.flip_xy)[k]
        block = (y * 2 + 1 - x, (1 - y) * 2 + x, (1 - y) * 2 + 1 - x)[k]
        return remote(u.at[block], ref.u_in.at[k], ref.q_send.at[1 + k], ref.q_recv.at[1 + k], (to, self.h))

    def two_apart(self):
        ref, h = self.ref, self.h
        return remote(ref.v, ref.v_in, ref.q_send.at[4], ref.q_recv.at[4], (self.at.dp, h + 2 - 4 * (h // 2)))

    def next_to(self):
        ref, h = self.ref, self.h
        return remote(ref.w, ref.w_in, ref.q_send.at[5], ref.q_recv.at[5], (self.at.dp, h + 1 - 2 * lax.rem(h, 2)))

    def heads_first(self, gq):
        self.swap(gq).start()

    def heads_second(self, gq, u):
        ref, core = self.ref, self.core
        self.swap(gq).wait_recv()
        for j in range(4):
            mine, theirs = gq[core, j].astype(F32), ref.gq_in[j].astype(F32)
            a, b = jnp.where(core == 0, mine, theirs), jnp.where(core == 0, theirs, mine)
            u[j, :, 0:128] = a[:, 0:128].astype(BF16)
            u[j, :, 128:256] = (a[:, 128:256] + b[:, 0:128]).astype(BF16)
            u[j, :, 256:384] = b[:, 128:256].astype(BF16)
        for k in range(3):
            self.spread(u, k).start()

    def heads_third(self, u):
        ref = self.ref
        for k in range(3):
            self.spread(u, k).wait_recv()
        total = u[self.y * 2 + self.x].astype(F32)
        for k in range(3):
            total = total + ref.u_in[k].astype(F32)
        ref.v[...] = total.astype(BF16)
        self.two_apart().start()

    def heads_fourth(self):
        ref = self.ref
        self.two_apart().wait_recv()
        ref.w[...] = (ref.v[...].astype(F32) + ref.v_in[...].astype(F32)).astype(BF16)
        self.next_to().start()

    def heads_last(self, gq, u):
        self.next_to().wait_recv()
        self.swap(gq).wait_send()
        for k in range(3):
            self.spread(u, k).wait_send()
        self.two_apart().wait_send()
        self.next_to().wait_send()

    def rows8(self, ref, core):
        return ref.at[pl.ds(mult(core * 8, 8), 8), :]

    def vec_sib(self):
        ref = self.ref
        return remote(
            self.rows8(ref.vec, 1 - self.core), ref.vec_sib, ref.vs_send.at[0], ref.vs_recv.at[0], (self.at.sib, self.h)
        )

    def vec_z(self, k):
        ref = self.ref
        return remote(
            ref.vec1, ref.vec_z.at[self.h], ref.vz_send.at[k - 1], ref.vz_recv.at[self.h],
            (self.at.dp, lax.rem(self.h + k, 4)),
        )

    def vec_chips(self, k):
        ref = self.ref
        here = self.y * 2 + self.x
        return remote(
            ref.vec2, ref.vec_xy.at[here], ref.vx_send.at[k], ref.vx_recv.at[here],
            ((self.flip_x, self.flip_y, self.flip_xy)[k], self.h),
        )

    def vec_total(self):
        ref = self.ref
        return remote(
            ref.vec3, self.rows8(ref.vec_all, self.core), ref.vs_send.at[1], ref.vs_recv.at[1], (self.at.sib, self.h)
        )

    def vectors_first(self):
        self.vec_sib().start()

    def vectors_second(self):
        ref = self.ref
        self.vec_sib().wait_recv()
        ref.vec1[...] = ref.vec[pl.ds(mult(self.core * 8, 8), 8), :] + ref.vec_sib[...]
        for k in range(1, 4):
            self.vec_z(k).start()
        ref.vec_z[self.h] = ref.vec1[...]

    def vectors_third(self):
        ref = self.ref
        for k in range(1, 4):
            other = lax.rem(self.h + k, 4)
            remote(
                ref.vec1, ref.vec_z.at[other], ref.vz_send.at[k - 1], ref.vz_recv.at[other], (self.at.sib, self.h)
            ).wait_recv()
        ref.vec2[...] = (ref.vec_z[0] + ref.vec_z[1]) + (ref.vec_z[2] + ref.vec_z[3])
        for k in range(3):
            self.vec_chips(k).start()
        ref.vec_xy[self.y * 2 + self.x] = ref.vec2[...]

    def vectors_fourth(self):
        ref, x, y = self.ref, self.x, self.y
        others = (y * 2 + 1 - x, (1 - y) * 2 + x, (1 - y) * 2 + 1 - x)
        for k in range(3):
            remote(
                ref.vec2, ref.vec_xy.at[others[k]], ref.vx_send.at[k], ref.vx_recv.at[others[k]],
                (self.at.sib, self.h),
            ).wait_recv()
        ref.vec3[...] = (ref.vec_xy[0] + ref.vec_xy[1]) + (ref.vec_xy[2] + ref.vec_xy[3])
        self.vec_total().start()
        ref.vec_all[pl.ds(mult(self.core * 8, 8), 8), :] = ref.vec3[...]

    def vectors_last(self):
        ref = self.ref
        self.vec_total().wait_recv()
        ref.vec_o[...] = ref.vec_all[...]
        self.vec_sib().wait_send()
        self.vec_total().wait_send()
        for k in range(1, 4):
            self.vec_z(k).wait_send()
        for k in range(3):
            self.vec_chips(k).wait_send()


def block(ins, full, grad_scale):
    given = types.SimpleNamespace(**ins)
    rows, width = given.tok_h[0].shape
    group, part, small, half = 4 * rows, width // 4, width // 8, width // 2
    heads, chunks = part // HEAD_DIM, given.w_fc_h[0].shape[1] // width
    dma = pltpu.SemaphoreType.DMA
    outs = dict(out_o=((rows, width), F32, ANY), gtok_o=((rows, width), F32, ANY), vec_o=((16, width), F32, VMEM))
    gq_shape = (2, 4, 3 * small, 256)
    scratch = dict(
        tok=((rows, width), BF16), xg=((group, width), BF16), xgt=((width, group), BF16),
        wt=((3 * 256, width), BF16), mix=((3 * part, group), BF16), ot=((part, group), BF16),
        lse=((8 * heads, group), F32), start=((8, group), jnp.int32), start_mine=((8, group), F32),
        start_sib=((8, group), F32), att=((width, rows), BF16), dat=((width, rows), BF16),
        do_t=((part, group), BF16), dmid=((rows, width), F32), vec=((16, width), F32),
        gfc=((2, chunks, half + small, width), BF16), gfc_in=((chunks, half + small, width), BF16),
        gproj_in=((chunks, half, width), BF16), r1=((2, 2, width // 4, width), BF16),
        r2=((2, width // 4, width), BF16), s2=((2, width // 4, width), BF16),
        late=((width // 4, width), BF16), s3=((half, width), BF16),
        arrive=((2, rows, width), BF16), arrive2=((2, rows, width), BF16), far=((rows, width), BF16),
    )
    sems = dict(
        in_sem=(3,), w_sem=(3,), st_sem=(2,), ag_send=(3 * PIECES,), ag_recv=(4, PIECES),
        fw_send=(4 * PIECES,), at_send=(4 * heads,), at_recv=(4 * heads,), at_local=(heads,),
        ff_sem=(2, 2), da_send=(4,), da_recv=(4,), da_local=(), pair_send=(2, chunks),
        pair_recv=(2, chunks), p1_send=(2, 2), p1_recv=(2, 2), p2_send=(2,), p2_recv=(2,),
        out_sem=(3,), sw_send=(2,), sw_recv=(2,), fin_send=(), fin_recv=(2,),
        fin_local=(), far_send=(PIECES,), far_recv=(PIECES,), out_recv=(PIECES,),
    )
    if full:
        outs |= dict(
            ztp=((half, width), BF16, VMEM), ztf=((half + small, width), BF16, VMEM),
            w=((3 * small, half), BF16, VMEM), w_in=((3 * small, half), BF16, VMEM),
        )
        p_shape, f_shape = (half, width), (half + small, width)
        scratch |= dict(
            zap=(p_shape, BF16), zbp=(p_shape, BF16), r1f=((2,) + f_shape, BF16), r2f=(f_shape, BF16),
            zaf=(f_shape, BF16), zbf=(f_shape, BF16),
        )
        scratch |= dict(
            gq_in=(gq_shape[1:], BF16), u_in=((3, 3 * small, half), BF16),
            v=((3 * small, half), BF16), v_in=((3 * small, half), BF16),
            vec_sib=((8, width), F32), vec1=((8, width), F32), vec2=((8, width), F32), vec3=((8, width), F32),
            vec_z=((4, 8, width), F32), vec_xy=((4, 8, width), F32), vec_all=((16, width), F32),
        )
        sems |= dict(
            one_send=(3, 2), one_recv=(3, 2), two_send=(3,), two_recv=(3,),
            z_send=(2, 3 * PIECES), z_recv=(2, 3 * PIECES), q_send=(6,), q_recv=(6,),
            vs_send=(2,), vs_recv=(2,), vz_send=(3,), vz_recv=(4,), vx_send=(3,),
            vx_recv=(4,),
        )
    else:
        outs |= dict(
            gq_o=(gq_shape, BF16, ANY), gfc_o=((2, chunks, half + small, width), BF16, ANY),
            gproj_o=((2, chunks, half, width), BF16, ANY),
        )
    names = (*ins, *outs, *scratch, *sems)
    return pl.pallas_call(
        functools.partial(block_kernel, grad_scale, full, names),
        out_shape=tuple(jax.ShapeDtypeStruct(shape, kind) for shape, kind, _ in outs.values()),
        in_specs=[spec for _, spec in ins.values()],
        out_specs=tuple(spec for _, _, spec in outs.values()),
        scratch_shapes=[pltpu.VMEM(shape, kind) for shape, kind in scratch.values()] + [dma(shape) for shape in sems.values()],
        compiler_params=pltpu.CompilerParams(
            collective_id=0, has_side_effects=True, vmem_limit_bytes=VMEM_LIMIT
        ),
        name="block",
    )(*(array for array, _ in ins.values()))


def emit_kernel(names, *refs):
    ref = named(names, refs)
    half, width = ref.ztp_h.shape
    small = ref.gout_o.shape[0]
    odd = lax.rem(lax.axis_index(HEAD), 2)
    reads = ((ref.ztf_h, ref.ztf), (ref.ztp_h, ref.ztp), (ref.w_h, ref.w), (ref.w_in_h, ref.w_in), (ref.out, ref.buf.at[0]),
             (ref.gtok, ref.buf.at[1]))
    loads = [pltpu.make_async_copy(src, dst, ref.in_sem.at[k]) for k, (src, dst) in enumerate(reads)]
    for load in loads:
        load.start()
    writes = ((ref.gfc, ref.gfc_o), (ref.gout, ref.gout_o), (ref.gproj, ref.gproj_o), (ref.gqkv, ref.gqkv_o),
              (ref.buf.at[0], ref.out_o), (ref.buf.at[1], ref.gtok_o))
    stores = [pltpu.make_async_copy(src, dst, ref.out_sem.at[k]) for k, (src, dst) in enumerate(writes)]
    vectors = (
        ref.out_b, ref.ln2_g, ref.ln2_b, ref.proj_b, None, None, None, None, ref.ln1_g, ref.ln1_b, ref.q_b, ref.v_b
    )
    for k, vector in enumerate(vectors):
        if vector is not None:
            vector[...] = ref.vec[k].reshape(width)
    ref.fc_b[...] = jnp.concatenate([ref.vec[4 + k : 5 + k, :] for k in range(4)], axis=1).reshape(4 * width)
    for k in (4, 5):
        loads[k].wait()
        stores[k].start()
    loads[1].wait()
    ref.gproj[...] = ref.ztp[...].astype(F32)
    stores[2].start()
    loads[0].wait()
    ref.gfc[...] = ref.ztf[0:half, :].astype(F32).T
    stores[0].start()
    ref.gout[...] = ref.ztf[half:, :].astype(F32)
    stores[1].start()
    loads[2].wait()
    loads[3].wait()
    for p in range(3):
        here = slice(p * small, (p + 1) * small)
        ref.gqkv[:, pl.ds(mult((2 * p + odd) * half, 128), half)] = ref.w[here, :].astype(F32)
        ref.gqkv[:, pl.ds(mult((2 * p + 1 - odd) * half, 128), half)] = ref.w_in[here, :].astype(F32)
    stores[3].start()
    for store in stores:
        store.wait()


def emit(out, gtok, vec, ztp, ztf, w, w_in):
    rows, width = out.shape
    half, small = width // 2, width // 8
    ins = dict(
        out=(out, ANY), gtok=(gtok, ANY), vec=(vec, VMEM), ztp_h=(ztp, ANY), ztf_h=(ztf, ANY), w_h=(w, ANY),
        w_in_h=(w_in, ANY),
    )
    outs = dict(
        out_o=((rows, width), ANY), gtok_o=((rows, width), ANY), ln1_g=((width,), VMEM),
        ln1_b=((width,), VMEM), gqkv_o=((small, 3 * width), ANY), q_b=((width,), VMEM),
        v_b=((width,), VMEM), gout_o=((small, width), ANY), out_b=((width,), VMEM),
        ln2_g=((width,), VMEM), ln2_b=((width,), VMEM), gfc_o=((width, half), ANY),
        fc_b=((4 * width,), VMEM), gproj_o=((half, width), ANY), proj_b=((width,), VMEM),
    )
    dma = pltpu.SemaphoreType.DMA
    scratch = dict(
        buf=pltpu.VMEM((2, rows, width), F32), ztp=pltpu.VMEM(ztp.shape, BF16), ztf=pltpu.VMEM(ztf.shape, BF16),
        w=pltpu.VMEM(w.shape, BF16), w_in=pltpu.VMEM(w.shape, BF16), gfc=pltpu.VMEM((width, half), F32),
        gout=pltpu.VMEM((small, width), F32), gproj=pltpu.VMEM((half, width), F32),
        gqkv=pltpu.VMEM((small, 3 * width), F32), in_sem=dma((6,)), out_sem=dma((6,)),
    )
    return pl.pallas_call(
        functools.partial(emit_kernel, (*ins, *outs, *scratch)),
        out_shape=tuple(jax.ShapeDtypeStruct(shape, F32) for shape, _ in outs.values()),
        in_specs=[spec for _, spec in ins.values()],
        out_specs=tuple(spec for _, spec in outs.values()),
        scratch_shapes=list(scratch.values()),
        compiler_params=pltpu.CompilerParams(vmem_limit_bytes=60 << 20),
        name="emit",
    )(*(array for array, _ in ins.values()))


def shards(
    tokens, lengths, ln1_gain, ln1_bias, w_qkv, bias_q, bias_v, w_out, bias_out, ln2_gain, ln2_bias, w_fc, bias_fc,
    w_proj, bias_proj, cotangent,
):
    device_count = lax.axis_size(DP) * lax.axis_size(HEAD)
    full = lax.axis_size(DP) == 8
    ins = dict(
        lens=(lengths, SMEM), gain1=(ln1_gain, VMEM), bias1=(ln1_bias, VMEM), bias_q=(bias_q, VMEM),
        bias_v=(bias_v, VMEM), b_out=(bias_out, VMEM), gain2=(ln2_gain, VMEM), bias2=(ln2_bias, VMEM),
        b_fc=(bias_fc, VMEM), b_proj=(bias_proj, VMEM), tok_h=(tokens, ANY), cot_h=(cotangent, ANY),
        w_qkv=(w_qkv, ANY), w_out_h=(w_out, ANY), w_fc_h=(w_fc, ANY), w_proj_h=(w_proj, ANY),
    )
    block_output, grad_tokens, vec, *rest = block(ins, full, 1.0 / math.sqrt(tokens.shape[0] * device_count))
    if full:
        return emit(block_output, grad_tokens, vec, *rest)
    gq, g_fc, g_proj = rest
    proj_total, fc_total, out_total, qkv_total, vec = sums_by_xla(gq, g_proj, g_fc, vec)
    return (
        block_output, grad_tokens, vec[8], vec[9], qkv_total, vec[10], vec[11], out_total, vec[0], vec[1], vec[2],
        fc_total, vec[4:8].reshape(-1), proj_total, vec[3],
    )


def sums_by_xla(gq, g_proj, g_fc, vec):
    _, blocks, length, width = g_proj.shape
    small = width // 8
    whole = g_proj.transpose(1, 0, 2, 3).reshape(2 * blocks * length, width)
    fc = g_fc[:, :, :length].transpose(1, 0, 2, 3).reshape(2 * blocks * length, width).T
    out = g_fc[:, :, length:].transpose(1, 0, 2, 3).reshape(width, width)
    core, odd = lax.rem(lax.axis_index(DP), 2), lax.rem(lax.axis_index(HEAD), 2)
    window = gq.reshape(2, 4, 3, small, 256).transpose(1, 0, 3, 2, 4).reshape(width, 3, 256)
    qkv = lax.dynamic_update_slice(
        jnp.zeros((width, 3, width), BF16), window, (0, 0, odd * (width // 2) + core * 128)
    ).reshape(width, 3 * width)

    def reduce_mat(g, dim):
        share = lax.psum_scatter(g, DP, scatter_dimension=dim, tiled=True)
        return lax.psum(share, HEAD).astype(F32)

    return reduce_mat(whole, 0), reduce_mat(fc, 1), reduce_mat(out, 0), reduce_mat(qkv, 0), lax.psum(vec, (DP, HEAD))


def solution(mesh):
    rows = P((DP, HEAD), None)
    return jax.shard_map(
        shards,
        mesh=mesh,
        in_specs=(rows, P(DP, None)) + (P(),) * 13 + (rows,),
        out_specs=(
            rows, rows, P(), P(), P(DP, None), P(), P(), P(DP, None), P(), P(), P(), P(None, DP), P(),
            P(DP, None), P(),
        ),
        check_vma=False,
    )
```

```python
import functools
import math
import types

import jax
import jax.numpy as jnp
from jax import lax
from jax.experimental import pallas as pl
from jax.experimental.pallas import tpu as pltpu
from jax.sharding import PartitionSpec as P

DP, HEAD = "dp", "head"
HEAD_DIM = 64
EPSILON = 1e-05
DEPTH_SCALE = 1.0 / math.sqrt(12.0)
LOG2E = 1.0 / math.log(2.0)
SCORE_SCALE = HEAD_DIM ** (-0.5)
GELU_K = math.sqrt(2.0 / math.pi)
GELU_A = 0.044715
TEAM = 8
QB = 256
VMEM_LIMIT = 63 << 20
PIECES = 3

INWARD, ACROSS, OUTWARD = range(3)

F32 = jnp.float32
BF16 = jnp.bfloat16
MESH = pl.DeviceIdType.MESH
ANY = pl.BlockSpec(memory_space=pl.ANY)
VMEM = pl.BlockSpec(memory_space=pltpu.VMEM)
SMEM = pl.BlockSpec(memory_space=pltpu.SMEM)


def dot(a, b):
    return jnp.dot(a, b, preferred_element_type=F32)


def dot_nt(a, b):
    return lax.dot_general(a, b, (((1,), (1,)), ((), ())), preferred_element_type=F32)


def dot_tn(a, b):
    return lax.dot_general(a, b, (((0,), (0,)), ((), ())), preferred_element_type=F32)


def mult(x, m):
    return pl.multiple_of(x, m)


def place():
    dp, h = lax.axis_index(DP), lax.axis_index(HEAD)
    core = lax.rem(dp, 2)
    half = h // 2
    return types.SimpleNamespace(
        dp=dp,
        h=h,
        core=core,
        sib=dp + 1 - 2 * core,
        even=dp - core,
        half=half,
        served=dp - core + half,
        block=(h - 2 * half) * 2 + core,
    )


def greet(at, chips=False):
    barrier = pltpu.get_barrier_semaphore()
    me = at.core * 4 + at.h
    others = []
    for k in range(1, TEAM):
        other = lax.rem(me + k, TEAM)
        others.append((at.even + other // 4, lax.rem(other, 4)))
    if chips:
        for k in range(1, 4):
            others.append((lax.rem(at.dp + 2 * k, 8), at.h))
    for other in others:
        pl.semaphore_signal(barrier, inc=1, device_id=other, device_id_type=MESH)
    return len(others)


def scoped(body, **buffers):
    pl.run_scoped(
        lambda *refs: body(named(buffers, refs)), *(pltpu.VMEM(shape, kind) for shape, kind in buffers.values())
    )


def named(names, refs):
    return types.SimpleNamespace(**dict(zip(names, refs, strict=True)))


def remote(src, dst, send, recv, device):
    return pltpu.make_async_remote_copy(
        src_ref=src, dst_ref=dst, send_sem=send, recv_sem=recv, device_id=device, device_id_type=MESH
    )


def row(vec):
    return vec[...].reshape(1, vec.shape[0])


def norm_parts(v):
    center = jnp.mean(v, axis=-1, keepdims=True)
    cent = v - center
    r = lax.rsqrt(jnp.mean(cent * cent, axis=-1, keepdims=True) + EPSILON)
    return cent * r, r


def norm_back(e, gain, n, r):
    ea = e * gain
    return r * (ea - jnp.mean(ea, axis=-1, keepdims=True) - n * jnp.mean(ea * n, axis=-1, keepdims=True))


def block_kernel(grad_scale, full, names, *refs):
    ref = named(names, refs)
    at = place()
    rows, width = ref.tok.shape
    group, part, chunks = 4 * rows, width // 4, ref.gfc.shape[1]
    heads = part // HEAD_DIM
    sums = Sums(ref, at) if full else None
    tok_copy = pltpu.make_async_copy(ref.tok_h, ref.tok, ref.in_sem.at[0])
    tok_copy.start()

    @pl.when(at.core != at.half)
    def _():
        ref.arrive2[1] = jnp.zeros((rows, width), BF16)

    scoped(
        lambda buf: attend(ref, buf, at, tok_copy, full),
        xn=((rows, width), BF16), wwin=((3, width, 256), BF16), brow=((8, width), F32),
        bcol=((3, 256, 128), F32), kh=((group, HEAD_DIM), BF16), scores=((group, QB), F32),
    )
    scoped(
        lambda buf: feed_forward(ref, buf, at, sums, grad_scale),
        cot=((rows, width), BF16), w_out=((width, width), BF16), w_fc=((2, width, width), BF16),
        w_proj=((2, width, width), BF16), brow=((8, chunks * width), F32),
        dfc=((chunks, rows, width), BF16), gproj=((2, chunks, width // 2, width), BF16),
        out=((rows, width), F32),
    )
    scoped(
        lambda buf: attend_back(ref, buf, at, sums, grad_scale),
        kh=((heads, group, HEAD_DIM), BF16), vh=((heads, group, HEAD_DIM), BF16),
        qh=((heads, group, HEAD_DIM), BF16), doh=((heads, group, HEAD_DIM), BF16),
        dk=((heads, group, HEAD_DIM), F32), dv=((heads, group, HEAD_DIM), F32),
        dq=((heads, HEAD_DIM, group), F32), delta=((8 * heads, group), F32), dmix=((3 * 256, group), BF16), partial=((2, rows, width), BF16),
        summed=((2, rows, width), BF16), gtok=((rows, width), F32),
        gq=((2, 4, 3 * (width // 8), 256), BF16), u=((4, 3 * (width // 8), width // 2), BF16),
    )


def attend(ref, buf, at, tok_copy, full):
    dp, h, core, sib = at.dp, at.h, at.core, at.sib
    rows, width = ref.tok.shape
    group, part = 4 * rows, width // 4
    heads = part // HEAD_DIM
    xn, xg, xgt, wwin, wt, mix, ot, lens = buf.xn, ref.xg, ref.xgt, buf.wwin, ref.wt, ref.mix, ref.ot, ref.lens
    collects = core == at.half
    first = (h - 2 * at.half) * 2 * part + core * 128
    shift = mult(64 * core, 64)
    ag_send, ag_recv, fw_send, st_sem, w_sem = ref.ag_send, ref.ag_recv, ref.fw_send, ref.st_sem, ref.w_sem
    for p in range(3):
        pltpu.make_async_copy(
            ref.w_qkv.at[:, pl.ds(mult(p * width + first, 128), 256)], wwin.at[p], w_sem.at[p]
        ).start()
    greeted = greet(at, full)
    tok_copy.wait()
    n, _ = norm_parts(ref.tok[...].astype(F32))
    xn[...] = (n * row(ref.gain1) + row(ref.bias1)).astype(BF16)

    for p in range(3):
        pltpu.make_async_copy(wwin.at[p], wwin.at[p], w_sem.at[p]).wait()
        wt[p * 256 : (p + 1) * 256, :] = wwin[p].T
    for p, vec in ((0, ref.bias_q), (2, ref.bias_v)):
        buf.brow[...] = jnp.broadcast_to(row(vec), (8, width))
        buf.bcol[p] = jnp.broadcast_to(buf.brow[0:1, pl.ds(mult(first, 128), 256)], (128, 256)).T
    buf.bcol[1] = jnp.zeros((256, 128), F32)

    pl.semaphore_wait(pltpu.get_barrier_semaphore(), greeted)

    inner, outer = 1 + core, 3 * core
    at_inner, at_outer = h == inner, h == outer

    length = rows // PIECES

    def piece(ref, s, q):
        return ref.at[pl.ds(mult(s * rows + q * length, length), length), :]

    def to_inner(q):
        return remote(piece(xn, 0, q), piece(xg, h, q), ag_send.at[q], ag_recv.at[h, q], (dp, inner))

    def to_outer(k, s, q):
        src = piece(xn, 0, q) if k == 0 else piece(xg, s, q)
        return remote(src, piece(xg, s, q), ag_send.at[k * PIECES + q], ag_recv.at[s, q], (dp, outer))

    def to_sib(d, s, q):
        src = piece(xn, 0, q) if d == 0 else piece(xg, s, q)
        return remote(src, piece(xg, s, q), fw_send.at[d * PIECES + q], ag_recv.at[s, q], (sib, h))

    @pl.when(at_inner)
    def _():
        for q in range(PIECES):
            to_outer(0, h, q).start()

    @pl.when(jnp.logical_not(at_inner))
    def _():
        for q in range(PIECES):
            to_inner(q).start()

    @pl.when(collects)
    def _():
        for q in range(PIECES):
            to_sib(0, h, q).start()
        xg[pl.ds(mult(h * rows, rows), rows), :] = xn[...]

    places = lax.broadcasted_iota(jnp.int32, (8, group), 1)
    begin = jnp.zeros((8, group), jnp.int32)
    edge = lens[0, 0]
    for k in range(1, lens.shape[1] + 1):
        begin = jnp.where(places >= edge, edge, begin)
        if k < lens.shape[1]:
            edge = edge + lens[0, k]
    ref.start_mine[...] = begin.astype(F32)
    st_copy = remote(ref.start_mine, ref.start_sib, st_sem.at[0], st_sem.at[1], (sib, h))
    st_copy.start()

    low = 1 - at.half
    order = (h, low * (1 - h) + (1 - low) * (5 - h), 1 + low, 3 * low)

    def project(s):
        here = xg[pl.ds(mult(s * rows, rows), rows), :]
        xgt[:, pl.ds(mult(s * rows, 128), rows)] = here.T
        for p in range(3):
            res = dot_nt(wt[pl.ds(mult(p * 256 + shift, 64), part), :], here) + buf.bcol[p, pl.ds(shift, part), :][:, :1]
            mix[p * part : (p + 1) * part, pl.ds(mult(s * rows, 128), rows)] = res.astype(BF16)

    @pl.when(jnp.logical_not(collects))
    def _():
        for q in range(PIECES):
            to_sib(1, h, q).wait_recv()

    project(h)
    for q in range(PIECES):
        for d in (2, 3, 1):
            s = order[d]
            to_sib(d, s, q).wait_recv()

            @pl.when(collects)
            def _():
                to_sib(d, s, q).start()

            if d > 1:
                @pl.when(at_inner)
                def _():
                    to_outer(d - 1, s, q).start()

            if q == PIECES - 1:
                project(s)
    st_copy.wait_recv()
    ref.start[...] = jnp.where(collects, ref.start_mine[...], ref.start_sib[...]).astype(jnp.int32)
    scale = SCORE_SCALE * LOG2E

    def one_head(i, _):
        qrow, krow, vrow = (mult(p * part + i * HEAD_DIM, HEAD_DIM) for p in range(3))
        buf.kh[...] = mix[pl.ds(krow, HEAD_DIM), :].T
        for j in range(group // QB):
            cols = slice(j * QB, (j + 1) * QB)
            q_t = mix[pl.ds(qrow, HEAD_DIM), cols]
            begins = ref.start[0:1, cols]
            top = jnp.full((1, QB), -jnp.inf, F32)
            for k in range(j + 1):
                s_t = dot(buf.kh[k * QB : (k + 1) * QB, :], q_t)
                key = lax.broadcasted_iota(jnp.int32, (QB, QB), 0)
                keep = key >= begins - k * QB
                if k == j:
                    keep = jnp.logical_and(keep, key <= lax.broadcasted_iota(jnp.int32, (QB, QB), 1))
                s_t = jnp.where(keep, s_t, -1e30)
                buf.scores[k * QB : (k + 1) * QB, :] = s_t
                top = jnp.maximum(top, jnp.max(s_t, axis=0, keepdims=True))
            top = top * scale
            total = jnp.zeros((1, QB), F32)
            acc = jnp.zeros((HEAD_DIM, QB), F32)
            for k in range(j + 1):
                p_t = jnp.exp2(buf.scores[k * QB : (k + 1) * QB, :] * scale - top)
                total = total + jnp.sum(p_t, axis=0, keepdims=True)
                acc = acc + dot(mix[pl.ds(vrow, HEAD_DIM), k * QB : (k + 1) * QB], p_t.astype(BF16))
            ot[pl.ds(qrow, HEAD_DIM), cols] = (acc / total).astype(BF16)
            ref.lse[pl.ds(mult(i * 8, 8), 8), cols] = jnp.broadcast_to(top + jnp.log2(total), (8, QB))
            for s in range(4):
                if j == ((s + 1) * rows - 1) // QB:
                    send_attended(ref, at, i, s)
        return 0

    lax.fori_loop(0, heads, one_head, 0)

    @pl.when(at_inner)
    def _():
        for q in range(PIECES):
            for d in range(1, 4):
                to_outer(d - 1, order[d], q).wait_send()

    @pl.when(jnp.logical_not(at_inner))
    def _():
        for q in range(PIECES):
            to_inner(q).wait_send()

    @pl.when(collects)
    def _():
        for q in range(PIECES):
            for d in range(4):
                to_sib(d, order[d], q).wait_send()

    st_copy.wait_send()


def attended_ends(ref, at, i, s):
    rows, width = ref.tok.shape
    src = ref.ot.at[pl.ds(mult(i * HEAD_DIM, HEAD_DIM), HEAD_DIM), pl.ds(s * rows, rows)]
    dst = ref.att.at[pl.ds(mult(at.block * (width // 4) + i * HEAD_DIM, HEAD_DIM), HEAD_DIM), :]
    return src, dst


def attended_stays(at, s):
    return jnp.logical_and(at.core == at.half, at.h == s)


def attended_local(ref, at, i, s):
    return pltpu.make_async_copy(*attended_ends(ref, at, i, s), ref.at_local.at[i])


def attended_remote(ref, at, i, s):
    src, dst = attended_ends(ref, at, i, s)
    heads = ref.at_local.shape[0]
    return remote(
        src, dst, ref.at_send.at[i * 4 + s], ref.at_recv.at[at.block * heads + i], (at.served, s)
    )


def send_attended(ref, at, i, s):
    @pl.when(attended_stays(at, s))
    def _():
        attended_local(ref, at, i, s).start()

    @pl.when(jnp.logical_not(attended_stays(at, s)))
    def _():
        attended_remote(ref, at, i, s).start()


def wait_attended(ref, at):
    rows, width = ref.tok.shape
    part, heads = width // 4, ref.at_local.shape[0]
    for i in range(heads):
        for s in range(4):
            @pl.when(attended_stays(at, s))
            def _():
                attended_local(ref, at, i, s).wait()

            @pl.when(jnp.logical_not(attended_stays(at, s)))
            def _():
                attended_remote(ref, at, i, s).wait_send()
        for b in range(4):
            dst = ref.att.at[pl.ds(b * part + i * HEAD_DIM, HEAD_DIM), :]
            src = ref.ot.at[pl.ds(i * HEAD_DIM, HEAD_DIM), pl.ds(0, rows)]

            @pl.when(jnp.logical_not(jnp.logical_and(at.core == at.half, at.block == b)))
            def _():
                remote(
                    src, dst, ref.at_send.at[i * 4], ref.at_recv.at[b * heads + i], (at.sib, at.h)
                ).wait_recv()


def feed_forward(ref, buf, at, sums, grad_scale):
    h, core = at.h, at.core
    rows, width = ref.tok.shape
    part = width // 4
    chunks = ref.gfc.shape[1]
    paired = sums is not None
    tok, att, cot, vec = ref.tok, ref.att, buf.cot, ref.vec
    w_out, w_fc, w_proj, brow, dfc, dat = buf.w_out, buf.w_fc, buf.w_proj, buf.brow, buf.dfc, ref.dat
    gfc, gproj, gfc_in, gproj_in, r1, s2, r2, s3 = (
        ref.gfc, buf.gproj, ref.gfc_in, ref.gproj_in, ref.r1, ref.s2, ref.r2, ref.s3
    )
    pair_send, pair_recv, one_send, one_recv, two_send, two_recv = (
        ref.pair_send, ref.pair_recv, ref.p1_send, ref.p1_recv, ref.p2_send, ref.p2_recv
    )
    cot_copy = pltpu.make_async_copy(ref.cot_h, cot, ref.in_sem.at[1])
    wo_copy = pltpu.make_async_copy(ref.w_out_h, w_out, ref.in_sem.at[2])
    cot_copy.start()
    wo_copy.start()

    def ff_copy(step, which):
        slot, here = step % 2, pl.ds(mult(order[step] * width, 128), width)
        if which == 0:
            return pltpu.make_async_copy(ref.w_fc_h.at[:, here], w_fc.at[slot], ref.ff_sem.at[0, slot])
        return pltpu.make_async_copy(ref.w_proj_h.at[here, :], w_proj.at[slot], ref.ff_sem.at[1, slot])

    half_rows = width // 2
    small = width // 8
    y, x = at.dp // 4, lax.rem(at.dp // 2, 2)

    def pair_copy(ref, into, k, j):
        return remote(ref.at[1 - core, j], into.at[j], pair_send.at[k, j], pair_recv.at[k, j], (at.sib, h))

    def pair_add(ref, into, k, j):
        pair_copy(ref, into, k, j).wait_recv()
        ref[core, j] = (ref[core, j].astype(F32) + into[j].astype(F32)).astype(BF16)

    if paired:
        order = [(1 - y) * 2 + 1 - x, y * 2 + 1 - x, (1 - y) * 2 + x, y * 2 + x]
    else:
        order = list(range(chunks))
    quarter = half_rows // 2
    flips = (at.dp + 2 - 4 * x, h), (at.dp + 4 - 8 * y, h)

    def halves(k):
        return slice(k * quarter, (k + 1) * quarter)

    def one(k, t):
        j = order[0] if t == 0 else order[1 + k]
        src = ref.late if (k, t) == (1, 1) else gproj.at[core, j, halves(k)]
        return remote(src, r1.at[k, t], one_send.at[k, t], one_recv.at[k, t], flips[k])

    def two(k):
        return remote(s2.at[k], r2.at[k], two_send.at[k], two_recv.at[k], flips[1 - k])

    def first_sum(k):
        one(k, 0).wait_recv()
        s2[k] = (gproj[core, order[2 - k], halves(k)].astype(F32) + r1[k, 0].astype(F32)).astype(BF16)
        two(k).start()

    def proj_sums(step):
        if not paired:
            return
        pair_add(gproj, gproj_in, 0, order[step])
        if step == 0:
            one(0, 0).start()
            one(1, 0).start()
        elif step == 1:
            one(0, 1).start()
        elif step == 2:
            first_sum(1)
            first_sum(0)
            ref.late[...] = gproj[core, order[2], halves(1)]
            one(1, 1).start()
        else:
            s3[...] = gproj[core, order[3]]

    for step in range(2):
        for which in range(2):
            ff_copy(step, which).start()
    vec[...] = jnp.zeros_like(vec)
    brow[...] = jnp.broadcast_to(row(ref.b_fc), brow.shape)
    cot_copy.wait()
    dy = cot[...].astype(F32)
    d_proj = (DEPTH_SCALE * dy).astype(BF16)
    wo_copy.wait()
    wait_attended(ref, at)
    middle = tok[...].astype(F32) + DEPTH_SCALE * (dot_tn(att[...], w_out[...]) + row(ref.b_out))
    n, r = norm_parts(middle)
    second = (n * row(ref.gain2) + row(ref.bias2)).astype(BF16)
    result = middle + DEPTH_SCALE * row(ref.b_proj)
    d_second = jnp.zeros((rows, width), F32)
    vec[3:4, :] = jnp.sum(dy, axis=0, keepdims=True) * (DEPTH_SCALE * grad_scale)
    for step, j in enumerate(order):
        slot = step % 2
        ff_copy(step, 0).wait()
        u = dot(second, w_fc[slot]) + brow[0:1, pl.ds(mult(j * width, 128), width)]
        u2 = u * u
        th = jnp.tanh(GELU_K * u * (1.0 + GELU_A * u2))
        half = 0.5 * (1.0 + th)
        slope = half + 0.5 * u * (1.0 - th * th) * (GELU_K * (1.0 + 3.0 * GELU_A * u2))
        hidden = (u * half).astype(BF16)
        ff_copy(step, 1).wait()
        result = result + DEPTH_SCALE * dot(hidden, w_proj[slot])
        d_pre = dot_nt(d_proj, w_proj[slot]) * slope
        if step > 0:
            proj_sums(step - 1)
        res = (dot_tn(hidden, d_proj) * grad_scale).astype(BF16)
        for k in range(2):
            gproj[k, j] = res[k * half_rows : (k + 1) * half_rows]
        if paired:
            pair_copy(gproj, gproj_in, 0, j).start()
        vec[pl.ds(4 + j, 1), :] = jnp.sum(d_pre, axis=0, keepdims=True) * grad_scale
        d_fc = d_pre.astype(BF16)
        dfc[j] = d_fc
        d_second = d_second + dot_nt(d_fc, w_fc[slot])
        if step + 2 < chunks:
            for which in range(2):
                ff_copy(step + 2, which).start()
    buf.out[...] = result
    out_copy = pltpu.make_async_copy(buf.out, ref.out_o, ref.out_sem.at[0])
    out_copy.start()
    vec[1:2, :] = jnp.sum(d_second * n, axis=0, keepdims=True) * grad_scale
    vec[2:3, :] = jnp.sum(d_second, axis=0, keepdims=True) * grad_scale
    d_middle = dy + norm_back(d_second, row(ref.gain2), n, r)
    ref.dmid[...] = d_middle
    vec[0:1, :] = jnp.sum(d_middle, axis=0, keepdims=True) * (DEPTH_SCALE * grad_scale)
    d_out = (DEPTH_SCALE * d_middle).astype(BF16)
    dat[...] = dot_nt(w_out[...], d_out).astype(BF16)

    send_d_attended(ref, at)

    def fc_sums(step):
        if not paired:
            return
        pair_add(gfc, gfc_in, 1, order[step])
        if step == 0:
            sums.one(1, 0).start()
            sums.one(2, 0).start()
        elif step < 3:
            sums.one(step, 1).start()

    g_out = (dot(att[...], d_out) * grad_scale).astype(BF16)
    for j in range(chunks):
        for k in range(2):
            gfc[k, j, half_rows:, :] = g_out[(2 * j + k) * small : (2 * j + k + 1) * small]
    for step, j in enumerate(order):
        if step == 1:
            proj_sums(chunks - 1)
        res = (dot_tn(dfc[j], second) * grad_scale).astype(BF16)
        for k in range(2):
            gfc[k, j, :half_rows, :] = res[k * half_rows : (k + 1) * half_rows]
        if paired:
            pair_copy(gfc, gfc_in, 1, j).start()
        if step > 1:
            fc_sums(step - 2)
    for step in (chunks - 2, chunks - 1):
        fc_sums(step)
    if paired:
        for j in order:
            pair_copy(gproj, gproj_in, 0, j).wait_send()
        for k in range(2):
            for t in range(2 - k):
                one(k, t).wait_send()
    else:
        outs = [
            pltpu.make_async_copy(gproj, ref.gproj_o, ref.out_sem.at[1]),
            pltpu.make_async_copy(gfc, ref.gfc_o, ref.out_sem.at[2]),
        ]
        for copy in outs:
            copy.start()
        for copy in outs:
            copy.wait()
    out_copy.wait()


def d_attended_part(at, i):
    b = lax.rem(2 * at.core + i, 4)
    return b, (at.even + lax.rem(b, 2), 2 * at.core + b // 2)


def d_attended_stays(at, i):
    b, _ = d_attended_part(at, i)
    return jnp.logical_and(at.core == lax.rem(b, 2), at.h == 2 * at.core + b // 2)


def d_attended_ends(ref, at, b):
    rows, width = ref.tok.shape
    part = width // 4
    src = ref.dat.at[pl.ds(mult(b * part, HEAD_DIM), part), :]
    return src, ref.do_t.at[:, pl.ds(mult(at.h * rows, 128), rows)]


def d_attended_local(ref, at, i):
    return pltpu.make_async_copy(*d_attended_ends(ref, at, d_attended_part(at, i)[0]), ref.da_local)


def d_attended_remote(ref, at, i):
    b, device = d_attended_part(at, i)
    src, dst = d_attended_ends(ref, at, b)
    return remote(src, dst, ref.da_send.at[i], ref.da_recv.at[at.h], device)


def send_d_attended(ref, at):
    for i in range(4):
        @pl.when(d_attended_stays(at, i))
        def _():
            d_attended_local(ref, at, i).start()

        @pl.when(jnp.logical_not(d_attended_stays(at, i)))
        def _():
            d_attended_remote(ref, at, i).start()


def wait_d_attended(ref, at):
    rows, width = ref.tok.shape
    part = width // 4
    served_here = at.core == at.half
    for i in range(4):
        @pl.when(d_attended_stays(at, i))
        def _():
            d_attended_local(ref, at, i).wait()

        @pl.when(jnp.logical_not(d_attended_stays(at, i)))
        def _():
            d_attended_remote(ref, at, i).wait_send()
    for s in range(4):
        @pl.when(jnp.logical_not(jnp.logical_and(served_here, at.h == s)))
        def _():
            remote(
                ref.dat.at[pl.ds(0, part), :], ref.do_t.at[:, pl.ds(s * rows, rows)], ref.da_send.at[0],
                ref.da_recv.at[s], (at.sib, at.h),
            ).wait_recv()


def attend_back(ref, buf, at, sums, grad_scale):
    full = sums is not None
    dp, h, core, sib = at.dp, at.h, at.core, at.sib
    rows, width = ref.tok.shape
    part, group = width // 4, 4 * rows
    heads = part // HEAD_DIM
    mix, do_t, ot, xgt, wt, lse, start = ref.mix, ref.do_t, ref.ot, ref.xgt, ref.wt, ref.lse, ref.start
    delta, kh, vh, qh, doh, dk, dv, dmix = buf.delta, buf.kh, buf.vh, buf.qh, buf.doh, buf.dk, buf.dv, buf.dmix
    dq = buf.dq
    partial, summed, arrive, arrive2 = buf.partial, buf.summed, ref.arrive, ref.arrive2
    sw_send, sw_recv, fin_send, fin_recv, fin_local = (
        ref.sw_send, ref.sw_recv, ref.fin_send, ref.fin_recv, ref.fin_local
    )
    dmix[...] = jnp.zeros_like(dmix)
    wait_d_attended(ref, at)
    scale = SCORE_SCALE * LOG2E

    def drow(p, i):
        return pl.ds(mult(p * 256 + (core + i) * HEAD_DIM, HEAD_DIM), HEAD_DIM)

    half = at.half
    blocks = group // QB
    far_cols = pl.ds(mult((1 - half) * (group // 2), 128), group // 2)
    near_cols = pl.ds(mult(half * (group // 2), 128), group // 2)

    def ready(i):
        qrow, krow, vrow = (mult(p * part + i * HEAD_DIM, HEAD_DIM) for p in range(3))
        d_head = do_t[pl.ds(qrow, HEAD_DIM), :]
        delta[pl.ds(mult(i * 8, 8), 8), :] = jnp.broadcast_to(
            jnp.sum(d_head.astype(F32) * ot[pl.ds(qrow, HEAD_DIM), :].astype(F32), axis=0, keepdims=True), (8, group)
        )
        qh[i] = mix[pl.ds(qrow, HEAD_DIM), :].T
        kh[i] = mix[pl.ds(krow, HEAD_DIM), :].T
        vh[i] = mix[pl.ds(vrow, HEAD_DIM), :].T
        doh[i] = d_head.T
        dq[i] = jnp.zeros((HEAD_DIM, group), F32)
        dk[i] = jnp.zeros((group, HEAD_DIM), F32)
        dv[i] = jnp.zeros((group, HEAD_DIM), F32)

    def pair(i, o, t):
        k = half * o + (1 - half) * (blocks - 1 - o - t)
        q = half * (o + t) + (1 - half) * (blocks - 1 - o)
        keys, cols = pl.ds(mult(k * QB, QB), QB), pl.ds(mult(q * QB, QB), QB)
        qrow, krow = (mult(p * part + i * HEAD_DIM, HEAD_DIM) for p in range(2))
        stats = pl.ds(mult(i * 8, 8), 8)
        s_t = dot(kh[i, keys, :], mix[pl.ds(qrow, HEAD_DIM), cols])
        key = lax.broadcasted_iota(jnp.int32, (QB, QB), 0)
        keep = key >= start[0:1, cols] - k * QB
        if t == 0:
            keep = jnp.logical_and(keep, key <= lax.broadcasted_iota(jnp.int32, (QB, QB), 1))
        p_t = jnp.where(keep, jnp.exp2(s_t * scale - lse[stats, cols][0:1]), 0.0)
        dp_t = dot(vh[i, keys, :], do_t[pl.ds(qrow, HEAD_DIM), cols])
        ds_t = (p_t * (dp_t - delta[stats, cols][0:1])).astype(BF16)
        dv[i, keys, :] += dot(p_t.astype(BF16), doh[i, cols, :])
        dk[i, keys, :] += dot(ds_t, qh[i, cols, :])
        dq[i, :, cols] += dot(mix[pl.ds(krow, HEAD_DIM), keys], ds_t)

    def done(i, cols):
        dmix[drow(0, i), cols] = (dq[i, :, cols] * SCORE_SCALE).astype(BF16)
        dmix[drow(1, i), cols] = (dk[i, cols, :] * SCORE_SCALE).T.astype(BF16)
        dmix[drow(2, i), cols] = dv[i, cols, :].T.astype(BF16)

    def far_head(i, _):
        ready(i)
        for o in range(blocks // 2):
            for t in range(blocks - o):
                pair(i, o, t)
            if full and o == 0:
                @pl.when(i == 0)
                def _():
                    sums.proj_last()
                    sums.send_in(0, (0,))

                for q in (1, 2):
                    @pl.when(i == q)
                    def _():
                        sums.send_in(0, (q,))
            if full and o == 1:
                @pl.when(i == 2)
                def _():
                    sums.add_across(0, (0,))
            if full and o == 2:
                for q in range(3):
                    @pl.when(i == q)
                    def _():
                        sums.add_inner(0, (q,))
        done(i, far_cols)
        return 0

    def near_head(i, _):
        for o in range(blocks // 2, blocks):
            for t in range(blocks - o):
                pair(i, o, t)
        done(i, near_cols)

        @pl.when(i == 1)
        def _():
            send_far(1)

        return 0

    def part_of(s):
        return dot_tn(dmix[:, pl.ds(mult(s * rows, 128), rows)], wt[...])

    slot, inner = h - 2 * at.half, 1 + at.half
    at_inner = h == inner
    ways = (1 - at.half, at.half)
    length = rows // PIECES
    def pass_on(q):
        @pl.when(at_inner)
        def _():
            here = slice(q * length, (q + 1) * length)
            far_in(q).wait_recv()
            summed[0, here] = (summed[0, here].astype(F32) + ref.far[here].astype(F32)).astype(BF16)
            far_out(q).start()

    def swap(k):
        return remote(partial.at[k], arrive.at[k], sw_send.at[k], sw_recv.at[k], (sib, h))

    def sib_part(k):
        partial[k] = part_of(2 * ways[k] + 1 - core).astype(BF16)
        swap(k).start()

    def own_part(k):
        mine = part_of(2 * ways[k] + core)
        swap(k).wait_recv()
        summed[k] = (mine + arrive[k].astype(F32)).astype(BF16)

    def far_in(q):
        here = slice(q * length, (q + 1) * length)
        return remote(summed.at[0, here], ref.far.at[here], ref.far_send.at[q], ref.far_recv.at[q], (dp, inner))

    def far_out(q):
        here = slice(q * length, (q + 1) * length)
        return remote(
            summed.at[0, here], arrive2.at[0, here], ref.far_send.at[q], ref.out_recv.at[q],
            (at.served, 2 * ways[0] + core),
        )

    def near_remote():
        return remote(summed.at[1], arrive2.at[slot], fin_send, fin_recv.at[slot], (at.served, 2 * ways[1] + core))

    def near_local():
        return pltpu.make_async_copy(summed.at[1], arrive2.at[slot], fin_local)

    stays = jnp.logical_and(core == at.half, h == 2 * ways[1] + core)
    lax.fori_loop(0, heads, far_head, 0)
    sib_part(0)
    own_part(0)

    def send_far(q):
        @pl.when(jnp.logical_not(at_inner))
        def _():
            far_in(q).start()

    send_far(0)

    if full:
        sums.add_first(1)
        sums.add_first(2)
        sums.add_across(0, (1,))
    lax.fori_loop(0, heads, near_head, 0)
    send_far(2)
    sib_part(1)
    pass_on(0)
    vec, gq = ref.vec, buf.gq
    first = slot * 2 * part + core * 128
    small = width // 8
    gain_sum = jnp.zeros((1, width), F32)
    bias_sum = jnp.zeros((1, width), F32)
    for p in range(3):
        d_cols = dmix[p * 256 : (p + 1) * 256, :]
        tok_sum = jnp.sum(d_cols.astype(F32), axis=1, keepdims=True) * grad_scale
        w_cols = wt[p * 256 : (p + 1) * 256, :].astype(F32)
        res = dot_nt(d_cols, xgt[...]) * grad_scale
        gain_sum = gain_sum + jnp.sum(w_cols * res, axis=0, keepdims=True)
        bias_sum = bias_sum + jnp.sum(w_cols * tok_sum, axis=0, keepdims=True)
        if p != 1:
            vec[10 + p // 2 : 11 + p // 2, pl.ds(mult(first, 128), 256)] = jnp.broadcast_to(tok_sum, (256, 128)).T[:1]
        res = res.astype(BF16).T
        for k in range(8):
            gq[k % 2, k // 2, p * small : (p + 1) * small, :] = res[k * small : (k + 1) * small]
    vec[8:9, :] = (gain_sum - row(ref.bias1) * bias_sum) / row(ref.gain1)
    vec[9:10, :] = bias_sum
    def near(now):
        @pl.when(jnp.logical_and(now, stays))
        def _():
            near_local().start()

        @pl.when(jnp.logical_and(now, jnp.logical_not(stays)))
        def _():
            near_remote().start()

    if full:
        sums.vectors_first()
        sums.heads_first(gq)
    pass_on(1)
    if full:
        sums.add_across(0, (2,))
        sums.heads_second(gq, buf.u)
        sums.vectors_second()
        sums.add_second(1)
        sums.send_in(1, (0,))
    pass_on(2)
    own_part(1)
    near(at_inner)
    if full:
        sums.add_second(2)
        sums.send_in(1, (1, 2))
        sums.add_inner(1)
        sums.send_in(2)
        sums.heads_third(buf.u)
        sums.add_inner(2)
    near(jnp.logical_not(at_inner))
    if full:
        sums.add_across(1)
        sums.heads_fourth()
        sums.vectors_third()
        sums.add_across(2)

    owner_far = core != at.half

    @pl.when(owner_far)
    def _():
        for q in range(PIECES):
            far = slice(q * length, (q + 1) * length)
            remote(
                summed.at[0, far], arrive2.at[0, far], ref.far_send.at[q], ref.out_recv.at[q], (sib, h)
            ).wait_recv()

    @pl.when(jnp.logical_not(owner_far))
    def _():
        for k in range(2):
            from_me = jnp.logical_and(slot == k, lax.rem(h, 2) == core)

            @pl.when(from_me)
            def _():
                pltpu.make_async_copy(summed.at[1], arrive2.at[k], fin_local).wait()

            @pl.when(jnp.logical_not(from_me))
            def _():
                remote(summed.at[1], arrive2.at[k], fin_send, fin_recv.at[k], (sib, h)).wait_recv()

    e = arrive2[0].astype(F32) + arrive2[1].astype(F32)
    n, r = norm_parts(ref.tok[...].astype(F32))
    buf.gtok[...] = ref.dmid[...] + norm_back(e, row(ref.gain1), n, r)
    gtok_copy = pltpu.make_async_copy(buf.gtok, ref.gtok_o, ref.out_sem.at[1])
    gtok_copy.start()
    if full:
        sums.vectors_fourth()
        sums.heads_last(gq, buf.u)
        sums.vectors_last()
        sums.finish()
    else:
        ref.vec_o[...] = vec[...]
        gq_copy = pltpu.make_async_copy(gq, ref.gq_o, ref.out_sem.at[2])
        gq_copy.start()
        gq_copy.wait()
    for k in range(2):
        swap(k).wait_send()
    for q in range(PIECES):
        far_in(q).wait_send()

    @pl.when(jnp.logical_not(stays))
    def _():
        near_remote().wait_send()
    gtok_copy.wait()


class Sums:
    def __init__(self, ref, at):
        self.ref, self.at = ref, at
        dp, self.h, self.core = at.dp, at.h, at.core
        self.y, self.x = dp // 4, lax.rem(dp // 2, 2)
        self.flip_x, self.flip_y = dp + 2 - 4 * self.x, dp + 4 - 8 * self.y
        self.flip_xy = self.flip_x + 4 - 8 * self.y
        self.outer = self.h * (3 - self.h) == 0

    def rows_of(self, k):
        length = self.ref.gfc.shape[2] // 2
        return slice(0, self.ref.s3.shape[0]) if k == 0 else slice((k - 1) * length, k * length)

    def block(self, k, t, across):
        x, y = self.x, self.y
        first, then = (y, x) if k == 2 else (x, y)
        first = 1 - first if across else first
        then = 1 - then if t == 0 else then
        return first * 2 + then if k == 2 else then * 2 + first

    def mine(self, k, t):
        return self.ref.gfc.at[self.core, self.block(k, t, False)]

    def one(self, k, t):
        ref, rows = self.ref, self.rows_of(k)
        return remote(
            ref.gfc.at[self.core, self.block(k, t, True), rows], ref.r1f.at[t, rows],
            ref.one_send.at[k, t], ref.one_recv.at[k, t], (self.flip_y if k == 2 else self.flip_x, self.h),
        )

    def two(self, k):
        ref, rows = self.ref, self.rows_of(k)
        return remote(
            self.mine(k, 0).at[rows], ref.r2f.at[rows],
            ref.two_send.at[k], ref.two_recv.at[k], (self.flip_x if k == 2 else self.flip_y, self.h),
        )

    def proj_in(self, k, step):
        ref, flips = self.ref, ((self.flip_x, self.h), (self.flip_y, self.h))
        if step == 1:
            return remote(ref.s2.at[k], ref.r1.at[k, 1], ref.p1_send.at[k, 1], ref.p1_recv.at[k, 1], flips[k])
        return remote(ref.s2.at[k], ref.r2.at[k], ref.p2_send.at[k], ref.p2_recv.at[k], flips[1 - k])

    def proj_last(self):
        ref = self.ref
        length = ref.r2.shape[1]
        for k in range(2):
            rows = slice(k * length, (k + 1) * length)
            self.proj_in(k, 1).wait_recv()
            self.proj_in(k, 2).wait_recv()
            ref.s3[rows] = (
                ref.s3[rows].astype(F32) + ref.r1[k, 1].astype(F32) + ref.r2[k].astype(F32)
            ).astype(BF16)

    def add_first(self, k):
        ref, rows, mine = self.ref, self.rows_of(k), self.mine(k, 0)
        self.one(k, 0).wait_recv()
        mine[rows] = (mine[rows].astype(F32) + ref.r1f[0, rows].astype(F32)).astype(BF16)
        self.two(k).start()

    def add_second(self, k):
        ref, rows, mine = self.ref, self.rows_of(k), self.mine(k, 1)
        self.one(k, 1).wait_recv()
        self.two(k).wait_recv()
        mine[rows] = (
            mine[rows].astype(F32) + ref.r1f[1, rows].astype(F32) + ref.r2f[rows].astype(F32)
        ).astype(BF16)

    def pieces(self, k):
        rows = self.rows_of(k)
        length = (rows.stop - rows.start) // PIECES
        for q in range(PIECES):
            yield k, k * PIECES + q, slice(rows.start + q * length, rows.start + (q + 1) * length)

    def bufs(self, k):
        ref = self.ref
        return (ref.s3, ref.zap, ref.zbp, ref.ztp) if k == 0 else (self.mine(k, 1), ref.zaf, ref.zbf, ref.ztf)

    def chain(self, k, m, rows, which):
        ref, h = self.ref, self.h
        s2, za, zb, zt = self.bufs(k)
        dp = self.at.dp
        if which == INWARD:
            return remote(s2.at[rows], za.at[rows], ref.z_send.at[0, m], ref.z_recv.at[0, m], (dp, 1 + h // 2))
        if which == ACROSS:
            return remote(s2.at[rows], zb.at[rows], ref.z_send.at[0, m], ref.z_recv.at[1, m], (dp, 3 - h))
        return remote(zt.at[rows], za.at[rows], ref.z_send.at[1, m], ref.z_recv.at[0, m], (dp, 3 * (h // 2)))

    def send_in(self, k, only=None):
        @pl.when(self.outer)
        def _():
            for q, piece in enumerate(self.pieces(k)):
                if only is None or q in only:
                    self.chain(*piece, INWARD).start()

    def add_inner(self, k, only=None):
        s2, za, _, _ = self.bufs(k)

        @pl.when(jnp.logical_not(self.outer))
        def _():
            for q, piece in enumerate(self.pieces(k)):
                if only is None or q in only:
                    rows = piece[2]
                    self.chain(*piece, INWARD).wait_recv()
                    s2[rows] = (s2[rows].astype(F32) + za[rows].astype(F32)).astype(BF16)
                    self.chain(*piece, ACROSS).start()

    def add_across(self, k, only=None):
        s2, _, zb, zt = self.bufs(k)

        @pl.when(jnp.logical_not(self.outer))
        def _():
            for q, piece in enumerate(self.pieces(k)):
                if only is None or q in only:
                    rows = piece[2]
                    self.chain(*piece, ACROSS).wait_recv()
                    zt[rows] = (s2[rows].astype(F32) + zb[rows].astype(F32)).astype(BF16)
                    self.chain(*piece, OUTWARD).start()

    def finish(self):
        @pl.when(self.outer)
        def _():
            for k in range(3):
                _, za, _, zt = self.bufs(k)
                for piece in self.pieces(k):
                    self.chain(*piece, OUTWARD).wait_recv()
                    zt[piece[2]] = za[piece[2]]

        for j in range(4):
            sib = (self.at.sib, self.h)
            remote(
                self.ref.gfc.at[1 - self.core, j], self.ref.gfc_in.at[j], self.ref.pair_send.at[1, j],
                self.ref.pair_recv.at[1, j], sib,
            ).wait_send()
        self.proj_in(1, 1).wait_send()
        for k in range(2):
            self.proj_in(k, 2).wait_send()
        for k in range(3):
            if k > 0:
                for t in range(2):
                    self.one(k, t).wait_send()
                self.two(k).wait_send()
            for piece in self.pieces(k):
                self.chain(*piece, INWARD).wait_send()

        @pl.when(jnp.logical_not(self.outer))
        def _():
            for k in range(3):
                for piece in self.pieces(k):
                    self.chain(*piece, OUTWARD).wait_send()

    def swap(self, gq):
        ref, core = self.ref, self.core
        return remote(gq.at[1 - core], ref.gq_in, ref.q_send.at[0], ref.q_recv.at[0], (self.at.sib, self.h))

    def spread(self, u, k):
        ref, x, y = self.ref, self.x, self.y
        to = (self.flip_x, self.flip_y, self.flip_xy)[k]
        block = (y * 2 + 1 - x, (1 - y) * 2 + x, (1 - y) * 2 + 1 - x)[k]
        return remote(u.at[block], ref.u_in.at[k], ref.q_send.at[1 + k], ref.q_recv.at[1 + k], (to, self.h))

    def two_apart(self):
        ref, h = self.ref, self.h
        return remote(ref.v, ref.v_in, ref.q_send.at[4], ref.q_recv.at[4], (self.at.dp, h + 2 - 4 * (h // 2)))

    def next_to(self):
        ref, h = self.ref, self.h
        return remote(ref.w, ref.w_in, ref.q_send.at[5], ref.q_recv.at[5], (self.at.dp, h + 1 - 2 * lax.rem(h, 2)))

    def heads_first(self, gq):
        self.swap(gq).start()

    def heads_second(self, gq, u):
        ref, core = self.ref, self.core
        self.swap(gq).wait_recv()
        for j in range(4):
            mine, theirs = gq[core, j].astype(F32), ref.gq_in[j].astype(F32)
            a, b = jnp.where(core == 0, mine, theirs), jnp.where(core == 0, theirs, mine)
            u[j, :, 0:128] = a[:, 0:128].astype(BF16)
            u[j, :, 128:256] = (a[:, 128:256] + b[:, 0:128]).astype(BF16)
            u[j, :, 256:384] = b[:, 128:256].astype(BF16)
        for k in range(3):
            self.spread(u, k).start()

    def heads_third(self, u):
        ref = self.ref
        for k in range(3):
            self.spread(u, k).wait_recv()
        total = u[self.y * 2 + self.x].astype(F32)
        for k in range(3):
            total = total + ref.u_in[k].astype(F32)
        ref.v[...] = total.astype(BF16)
        self.two_apart().start()

    def heads_fourth(self):
        ref = self.ref
        self.two_apart().wait_recv()
        ref.w[...] = (ref.v[...].astype(F32) + ref.v_in[...].astype(F32)).astype(BF16)
        self.next_to().start()

    def heads_last(self, gq, u):
        self.next_to().wait_recv()
        self.swap(gq).wait_send()
        for k in range(3):
            self.spread(u, k).wait_send()
        self.two_apart().wait_send()
        self.next_to().wait_send()

    def rows8(self, ref, core):
        return ref.at[pl.ds(mult(core * 8, 8), 8), :]

    def vec_sib(self):
        ref = self.ref
        return remote(
            self.rows8(ref.vec, 1 - self.core), ref.vec_sib, ref.vs_send.at[0], ref.vs_recv.at[0], (self.at.sib, self.h)
        )

    def vec_z(self, k):
        ref = self.ref
        return remote(
            ref.vec1, ref.vec_z.at[self.h], ref.vz_send.at[k - 1], ref.vz_recv.at[self.h],
            (self.at.dp, lax.rem(self.h + k, 4)),
        )

    def vec_chips(self, k):
        ref = self.ref
        here = self.y * 2 + self.x
        return remote(
            ref.vec2, ref.vec_xy.at[here], ref.vx_send.at[k], ref.vx_recv.at[here],
            ((self.flip_x, self.flip_y, self.flip_xy)[k], self.h),
        )

    def vec_total(self):
        ref = self.ref
        return remote(
            ref.vec3, self.rows8(ref.vec_all, self.core), ref.vs_send.at[1], ref.vs_recv.at[1], (self.at.sib, self.h)
        )

    def vectors_first(self):
        self.vec_sib().start()

    def vectors_second(self):
        ref = self.ref
        self.vec_sib().wait_recv()
        ref.vec1[...] = ref.vec[pl.ds(mult(self.core * 8, 8), 8), :] + ref.vec_sib[...]
        for k in range(1, 4):
            self.vec_z(k).start()
        ref.vec_z[self.h] = ref.vec1[...]

    def vectors_third(self):
        ref = self.ref
        for k in range(1, 4):
            other = lax.rem(self.h + k, 4)
            remote(
                ref.vec1, ref.vec_z.at[other], ref.vz_send.at[k - 1], ref.vz_recv.at[other], (self.at.sib, self.h)
            ).wait_recv()
        ref.vec2[...] = (ref.vec_z[0] + ref.vec_z[1]) + (ref.vec_z[2] + ref.vec_z[3])
        for k in range(3):
            self.vec_chips(k).start()
        ref.vec_xy[self.y * 2 + self.x] = ref.vec2[...]

    def vectors_fourth(self):
        ref, x, y = self.ref, self.x, self.y
        others = (y * 2 + 1 - x, (1 - y) * 2 + x, (1 - y) * 2 + 1 - x)
        for k in range(3):
            remote(
                ref.vec2, ref.vec_xy.at[others[k]], ref.vx_send.at[k], ref.vx_recv.at[others[k]],
                (self.at.sib, self.h),
            ).wait_recv()
        ref.vec3[...] = (ref.vec_xy[0] + ref.vec_xy[1]) + (ref.vec_xy[2] + ref.vec_xy[3])
        self.vec_total().start()
        ref.vec_all[pl.ds(mult(self.core * 8, 8), 8), :] = ref.vec3[...]

    def vectors_last(self):
        ref = self.ref
        self.vec_total().wait_recv()
        ref.vec_o[...] = ref.vec_all[...]
        self.vec_sib().wait_send()
        self.vec_total().wait_send()
        for k in range(1, 4):
            self.vec_z(k).wait_send()
        for k in range(3):
            self.vec_chips(k).wait_send()


def block(ins, full, grad_scale):
    given = types.SimpleNamespace(**ins)
    rows, width = given.tok_h[0].shape
    group, part, small, half = 4 * rows, width // 4, width // 8, width // 2
    heads, chunks = part // HEAD_DIM, given.w_fc_h[0].shape[1] // width
    dma = pltpu.SemaphoreType.DMA
    outs = dict(out_o=((rows, width), F32, ANY), gtok_o=((rows, width), F32, ANY), vec_o=((16, width), F32, VMEM))
    gq_shape = (2, 4, 3 * small, 256)
    scratch = dict(
        tok=((rows, width), BF16), xg=((group, width), BF16), xgt=((width, group), BF16),
        wt=((3 * 256, width), BF16), mix=((3 * part, group), BF16), ot=((part, group), BF16),
        lse=((8 * heads, group), F32), start=((8, group), jnp.int32), start_mine=((8, group), F32),
        start_sib=((8, group), F32), att=((width, rows), BF16), dat=((width, rows), BF16),
        do_t=((part, group), BF16), dmid=((rows, width), F32), vec=((16, width), F32),
        gfc=((2, chunks, half + small, width), BF16), gfc_in=((chunks, half + small, width), BF16),
        gproj_in=((chunks, half, width), BF16), r1=((2, 2, width // 4, width), BF16),
        r2=((2, width // 4, width), BF16), s2=((2, width // 4, width), BF16),
        late=((width // 4, width), BF16), s3=((half, width), BF16),
        arrive=((2, rows, width), BF16), arrive2=((2, rows, width), BF16), far=((rows, width), BF16),
    )
    sems = dict(
        in_sem=(3,), w_sem=(3,), st_sem=(2,), ag_send=(3 * PIECES,), ag_recv=(4, PIECES),
        fw_send=(4 * PIECES,), at_send=(4 * heads,), at_recv=(4 * heads,), at_local=(heads,),
        ff_sem=(2, 2), da_send=(4,), da_recv=(4,), da_local=(), pair_send=(2, chunks),
        pair_recv=(2, chunks), p1_send=(2, 2), p1_recv=(2, 2), p2_send=(2,), p2_recv=(2,),
        out_sem=(3,), sw_send=(2,), sw_recv=(2,), fin_send=(), fin_recv=(2,),
        fin_local=(), far_send=(PIECES,), far_recv=(PIECES,), out_recv=(PIECES,),
    )
    if full:
        outs |= dict(
            ztp=((half, width), BF16, VMEM), ztf=((half + small, width), BF16, VMEM),
            w=((3 * small, half), BF16, VMEM), w_in=((3 * small, half), BF16, VMEM),
        )
        p_shape, f_shape = (half, width), (half + small, width)
        scratch |= dict(
            zap=(p_shape, BF16), zbp=(p_shape, BF16), r1f=((2,) + f_shape, BF16), r2f=(f_shape, BF16),
            zaf=(f_shape, BF16), zbf=(f_shape, BF16),
        )
        scratch |= dict(
            gq_in=(gq_shape[1:], BF16), u_in=((3, 3 * small, half), BF16),
            v=((3 * small, half), BF16), v_in=((3 * small, half), BF16),
            vec_sib=((8, width), F32), vec1=((8, width), F32), vec2=((8, width), F32), vec3=((8, width), F32),
            vec_z=((4, 8, width), F32), vec_xy=((4, 8, width), F32), vec_all=((16, width), F32),
        )
        sems |= dict(
            one_send=(3, 2), one_recv=(3, 2), two_send=(3,), two_recv=(3,),
            z_send=(2, 3 * PIECES), z_recv=(2, 3 * PIECES), q_send=(6,), q_recv=(6,),
            vs_send=(2,), vs_recv=(2,), vz_send=(3,), vz_recv=(4,), vx_send=(3,),
            vx_recv=(4,),
        )
    else:
        outs |= dict(
            gq_o=(gq_shape, BF16, ANY), gfc_o=((2, chunks, half + small, width), BF16, ANY),
            gproj_o=((2, chunks, half, width), BF16, ANY),
        )
    names = (*ins, *outs, *scratch, *sems)
    return pl.pallas_call(
        functools.partial(block_kernel, grad_scale, full, names),
        out_shape=tuple(jax.ShapeDtypeStruct(shape, kind) for shape, kind, _ in outs.values()),
        in_specs=[spec for _, spec in ins.values()],
        out_specs=tuple(spec for _, _, spec in outs.values()),
        scratch_shapes=[pltpu.VMEM(shape, kind) for shape, kind in scratch.values()] + [dma(shape) for shape in sems.values()],
        compiler_params=pltpu.CompilerParams(
            collective_id=0, has_side_effects=True, vmem_limit_bytes=VMEM_LIMIT
        ),
        name="block",
    )(*(array for array, _ in ins.values()))


def emit_kernel(names, *refs):
    ref = named(names, refs)
    half, width = ref.ztp_h.shape
    small = ref.gout_o.shape[0]
    odd = lax.rem(lax.axis_index(HEAD), 2)
    reads = ((ref.ztf_h, ref.ztf), (ref.ztp_h, ref.ztp), (ref.w_h, ref.w), (ref.w_in_h, ref.w_in), (ref.out, ref.buf.at[0]),
             (ref.gtok, ref.buf.at[1]))
    loads = [pltpu.make_async_copy(src, dst, ref.in_sem.at[k]) for k, (src, dst) in enumerate(reads)]
    for load in loads:
        load.start()
    writes = ((ref.gfc, ref.gfc_o), (ref.gout, ref.gout_o), (ref.gproj, ref.gproj_o), (ref.gqkv, ref.gqkv_o),
              (ref.buf.at[0], ref.out_o), (ref.buf.at[1], ref.gtok_o))
    stores = [pltpu.make_async_copy(src, dst, ref.out_sem.at[k]) for k, (src, dst) in enumerate(writes)]
    vectors = (
        ref.out_b, ref.ln2_g, ref.ln2_b, ref.proj_b, None, None, None, None, ref.ln1_g, ref.ln1_b, ref.q_b, ref.v_b
    )
    for k, vector in enumerate(vectors):
        if vector is not None:
            vector[...] = ref.vec[k].reshape(width)
    ref.fc_b[...] = jnp.concatenate([ref.vec[4 + k : 5 + k, :] for k in range(4)], axis=1).reshape(4 * width)
    for k in (4, 5):
        loads[k].wait()
        stores[k].start()
    loads[1].wait()
    ref.gproj[...] = ref.ztp[...].astype(F32)
    stores[2].start()
    loads[0].wait()
    ref.gfc[...] = ref.ztf[0:half, :].astype(F32).T
    stores[0].start()
    ref.gout[...] = ref.ztf[half:, :].astype(F32)
    stores[1].start()
    loads[2].wait()
    loads[3].wait()
    for p in range(3):
        here = slice(p * small, (p + 1) * small)
        ref.gqkv[:, pl.ds(mult((2 * p + odd) * half, 128), half)] = ref.w[here, :].astype(F32)
        ref.gqkv[:, pl.ds(mult((2 * p + 1 - odd) * half, 128), half)] = ref.w_in[here, :].astype(F32)
    stores[3].start()
    for store in stores:
        store.wait()


def emit(out, gtok, vec, ztp, ztf, w, w_in):
    rows, width = out.shape
    half, small = width // 2, width // 8
    ins = dict(
        out=(out, ANY), gtok=(gtok, ANY), vec=(vec, VMEM), ztp_h=(ztp, ANY), ztf_h=(ztf, ANY), w_h=(w, ANY),
        w_in_h=(w_in, ANY),
    )
    outs = dict(
        out_o=((rows, width), ANY), gtok_o=((rows, width), ANY), ln1_g=((width,), VMEM),
        ln1_b=((width,), VMEM), gqkv_o=((small, 3 * width), ANY), q_b=((width,), VMEM),
        v_b=((width,), VMEM), gout_o=((small, width), ANY), out_b=((width,), VMEM),
        ln2_g=((width,), VMEM), ln2_b=((width,), VMEM), gfc_o=((width, half), ANY),
        fc_b=((4 * width,), VMEM), gproj_o=((half, width), ANY), proj_b=((width,), VMEM),
    )
    dma = pltpu.SemaphoreType.DMA
    scratch = dict(
        buf=pltpu.VMEM((2, rows, width), F32), ztp=pltpu.VMEM(ztp.shape, BF16), ztf=pltpu.VMEM(ztf.shape, BF16),
        w=pltpu.VMEM(w.shape, BF16), w_in=pltpu.VMEM(w.shape, BF16), gfc=pltpu.VMEM((width, half), F32),
        gout=pltpu.VMEM((small, width), F32), gproj=pltpu.VMEM((half, width), F32),
        gqkv=pltpu.VMEM((small, 3 * width), F32), in_sem=dma((6,)), out_sem=dma((6,)),
    )
    return pl.pallas_call(
        functools.partial(emit_kernel, (*ins, *outs, *scratch)),
        out_shape=tuple(jax.ShapeDtypeStruct(shape, F32) for shape, _ in outs.values()),
        in_specs=[spec for _, spec in ins.values()],
        out_specs=tuple(spec for _, spec in outs.values()),
        scratch_shapes=list(scratch.values()),
        compiler_params=pltpu.CompilerParams(vmem_limit_bytes=60 << 20),
        name="emit",
    )(*(array for array, _ in ins.values()))


def shards(
    tokens, lengths, ln1_gain, ln1_bias, w_qkv, bias_q, bias_v, w_out, bias_out, ln2_gain, ln2_bias, w_fc, bias_fc,
    w_proj, bias_proj, cotangent,
):
    device_count = lax.axis_size(DP) * lax.axis_size(HEAD)
    full = lax.axis_size(DP) == 8
    ins = dict(
        lens=(lengths, SMEM), gain1=(ln1_gain, VMEM), bias1=(ln1_bias, VMEM), bias_q=(bias_q, VMEM),
        bias_v=(bias_v, VMEM), b_out=(bias_out, VMEM), gain2=(ln2_gain, VMEM), bias2=(ln2_bias, VMEM),
        b_fc=(bias_fc, VMEM), b_proj=(bias_proj, VMEM), tok_h=(tokens, ANY), cot_h=(cotangent, ANY),
        w_qkv=(w_qkv, ANY), w_out_h=(w_out, ANY), w_fc_h=(w_fc, ANY), w_proj_h=(w_proj, ANY),
    )
    block_output, grad_tokens, vec, *rest = block(ins, full, 1.0 / math.sqrt(tokens.shape[0] * device_count))
    if full:
        return emit(block_output, grad_tokens, vec, *rest)
    gq, g_fc, g_proj = rest
    proj_total, fc_total, out_total, qkv_total, vec = sums_by_xla(gq, g_proj, g_fc, vec)
    return (
        block_output, grad_tokens, vec[8], vec[9], qkv_total, vec[10], vec[11], out_total, vec[0], vec[1], vec[2],
        fc_total, vec[4:8].reshape(-1), proj_total, vec[3],
    )


def sums_by_xla(gq, g_proj, g_fc, vec):
    _, blocks, length, width = g_proj.shape
    small = width // 8
    whole = g_proj.transpose(1, 0, 2, 3).reshape(2 * blocks * length, width)
    fc = g_fc[:, :, :length].transpose(1, 0, 2, 3).reshape(2 * blocks * length, width).T
    out = g_fc[:, :, length:].transpose(1, 0, 2, 3).reshape(width, width)
    core, odd = lax.rem(lax.axis_index(DP), 2), lax.rem(lax.axis_index(HEAD), 2)
    window = gq.reshape(2, 4, 3, small, 256).transpose(1, 0, 3, 2, 4).reshape(width, 3, 256)
    qkv = lax.dynamic_update_slice(
        jnp.zeros((width, 3, width), BF16), window, (0, 0, odd * (width // 2) + core * 128)
    ).reshape(width, 3 * width)

    def reduce_mat(g, dim):
        share = lax.psum_scatter(g, DP, scatter_dimension=dim, tiled=True)
        return lax.psum(share, HEAD).astype(F32)

    return reduce_mat(whole, 0), reduce_mat(fc, 1), reduce_mat(out, 0), reduce_mat(qkv, 0), lax.psum(vec, (DP, HEAD))


def solution(mesh):
    rows = P((DP, HEAD), None)
    return jax.shard_map(
        shards,
        mesh=mesh,
        in_specs=(rows, P(DP, None)) + (P(),) * 13 + (rows,),
        out_specs=(
            rows, rows, P(), P(), P(DP, None), P(), P(), P(DP, None), P(), P(), P(), P(None, DP), P(),
            P(DP, None), P(),
        ),
        check_vma=False,
    )
```
